32 devices in a mesh: chan: 4 (over x, core), region: 8 (over z, y).
Axes of the slice: x: 2, y: 2, z: 4, core: 2. Of those that a mesh axis runs over, the one named last changes fastest.
Arguments:
- latent: bfloat16 [8, 24, 24, 12, 128], P('region'), may hold values from -6 to 6
- cond_scale: float32 [128], replicated, may hold values from 0.5 to 1.5
- cond_shift: float32 [128], replicated, may hold values from -3 to 3
- fine_weight: bfloat16 [3, 3, 3, 128, 128], replicated, may hold values from -0.109375 to 0.109375
- fine_bias: float32 [128], replicated, may hold values from -3 to 3
- proj_weight: bfloat16 [8192, 1024], P(('chan', 'region')), may hold values from -0.0625 to 0.0625
- proj_bias: float32 [1024], replicated, may hold values from -3 to 3
- bottle_weight: bfloat16 [27, 1024, 1024], P(None, 'chan'), may hold values from -0.0390625 to 0.0390625
- bottle_bias: float32 [1024], replicated, may hold values from -3 to 3
- guide: float32 [1], replicated, may hold values from 1.5 to 4
Outputs:
- guided: bfloat16 [8, 6, 6, 3, 1024], P('region', None, None, None, 'chan')
The draws below stay inside these ranges and needn't reach their ends.
All inputs are finite; a program needn't handle non-finite values.
Results may differ from the reference program's by a relative error of at most 0.012.
The reference program's roundings to bfloat16 on the way (of `slab`, `inputs`, `hidden` and `coarse`) count: a program that leaves them out, or rounds other values in their place, can miss the bound.
Values may be sent and summed in bfloat16 or wider, within the bound.
No kernel may reach another device: no remote copies, remote signals or barrier semaphores. Data moves between devices by JAX's collectives and lax.ppermute only.
A program may use at most 128 MiB of HBM per device.

```python
import jax
import jax.numpy as jnp
from jax import lax

FINE_WIDTH = 128
COARSE_WIDTH = 1024
TILE_SIDE = 12
STRIDE = 4
REGIONS_Y = 4
REGIONS_Z = 2
N_REGION = 8


def steps_of(key, dims, split, low, top_value):
    level, own = 1.0, jax.random.fold_in(key, 6)
    for position, shards_of in split:
        draws = jnp.exp(jax.random.uniform(jax.random.fold_in(own, position), (shards_of,), jnp.float32, low / len(split), top_value / len(split)))
        level = level * jnp.repeat(draws, dims[position] // shards_of).reshape([-1 if axis == position else 1 for axis in range(len(dims))])
    return level


def noise(key, shape, width, most, pieces=(), held_as=jnp.bfloat16):
    gain = steps_of(key, shape, pieces, -0.22, 0.18) if pieces else 1.0
    result = jax.random.normal(key, shape, jnp.float32) * width * gain
    return jnp.minimum(jnp.maximum(result, -most), most).astype(held_as)


def setup_inputs(seed: int = 0) -> dict:
    key_list = jax.random.split(jax.random.key(seed), 11)
    return {
        "latent": noise(key_list[0], (N_REGION, 2 * TILE_SIDE, 2 * TILE_SIDE, TILE_SIDE, FINE_WIDTH), 1.0, 6.0, ((0, 8),)),
        "cond_scale": jnp.clip(1.0 + 0.1 * jax.random.normal(key_list[1], (FINE_WIDTH,), jnp.float32), 0.5, 1.5),
        "cond_shift": noise(key_list[2], (FINE_WIDTH,), 0.5, 3.0, (), jnp.float32),
        "fine_weight": noise(key_list[3], (3, 3, 3, FINE_WIDTH, FINE_WIDTH), (27 * FINE_WIDTH) ** -0.5, 0.109375),
        "fine_bias": noise(key_list[4], (FINE_WIDTH,), 0.5, 3.0, (), jnp.float32),
        "proj_weight": noise(key_list[5], (FINE_WIDTH * STRIDE ** 3, COARSE_WIDTH), (FINE_WIDTH * STRIDE ** 3) ** -0.5, 0.0625, ((0, 32),)),
        "proj_bias": noise(key_list[6], (COARSE_WIDTH,), 0.5, 3.0, (), jnp.float32),
        "bottle_weight": noise(key_list[7], (27, COARSE_WIDTH, COARSE_WIDTH), (27 * COARSE_WIDTH) ** -0.5, 0.0390625, ((1, 4),)),
        "bottle_bias": noise(key_list[8], (COARSE_WIDTH,), 0.5, 3.0, (), jnp.float32),
        "guide": jnp.clip(jax.random.uniform(key_list[9], (1,), jnp.float32, 1.5, 4.0), 1.5, 4.0),
    }


def blocks_to_slab(array, side_x, side_y, side_z):
    count_x = array.shape[0] // (REGIONS_Y * REGIONS_Z)
    grid = array.reshape(count_x, REGIONS_Y, REGIONS_Z, side_x, side_y, side_z, array.shape[-1])
    grid = grid.transpose(0, 3, 1, 4, 2, 5, 6)
    return grid.reshape(count_x * side_x, REGIONS_Y * side_y, REGIONS_Z * side_z, array.shape[-1])


def slab_to_blocks(field, side_x, side_y, side_z):
    count_x = field.shape[0] // side_x
    grid = field.reshape(count_x, side_x, REGIONS_Y, side_y, REGIONS_Z, side_z, field.shape[-1])
    grid = grid.transpose(0, 2, 4, 1, 3, 5, 6)
    return grid.reshape(count_x * REGIONS_Y * REGIONS_Z, side_x, side_y, side_z, field.shape[-1])


def conv_three(field, kernel):
    return lax.conv_general_dilated(field, kernel, (1, 1, 1), "SAME",
                                    dimension_numbers=("NDHWC", "DHWIO", "NDHWC"),
                                    precision=lax.Precision.HIGHEST)


def reference(latent, cond_scale, cond_shift, fine_weight, fine_bias, proj_weight, proj_bias, bottle_weight, bottle_bias, guide):
    side = TILE_SIDE
    slab = blocks_to_slab(latent, 2 * side, 2 * side, side).astype(jnp.float32)
    shaped = (slab * cond_scale + cond_shift).astype(jnp.bfloat16)
    shaped = lax.optimization_barrier(shaped).astype(jnp.float32)
    inputs = jnp.stack([slab, shaped])
    hidden = jax.nn.silu(conv_three(inputs, fine_weight.astype(jnp.float32)) + fine_bias).astype(jnp.bfloat16)
    width_x, width_y, width_z = hidden.shape[1] // STRIDE, hidden.shape[2] // STRIDE, hidden.shape[3] // STRIDE
    grid = hidden.reshape(2, width_x, STRIDE, width_y, STRIDE, width_z, STRIDE, FINE_WIDTH)
    grid = grid.transpose(0, 1, 3, 5, 7, 2, 4, 6).reshape(2 * width_x * width_y * width_z, FINE_WIDTH * STRIDE ** 3)
    coarse = (jnp.dot(grid, proj_weight, preferred_element_type=jnp.float32) + proj_bias).astype(jnp.bfloat16)
    coarse = coarse.reshape(2, width_x, width_y, width_z, COARSE_WIDTH).astype(jnp.float32)
    kernel = bottle_weight.reshape(3, 3, 3, COARSE_WIDTH, COARSE_WIDTH).astype(jnp.float32)
    bottle = jax.nn.silu(conv_three(coarse, kernel) + bottle_bias)
    guided = (bottle[0] + guide[0] * (bottle[1] - bottle[0])).astype(jnp.bfloat16)
    cells = side // STRIDE
    return slab_to_blocks(guided, 2 * cells, 2 * cells, cells)
```

```python
import functools

import numpy as np

import jax
import jax.numpy as jnp
from jax import lax
from jax.experimental import pallas as pl
from jax.experimental.pallas import tpu as pltpu
from jax.sharding import PartitionSpec as P

FINE_WIDTH = 128
COARSE_WIDTH = 1024
TILE_SIDE = 12
STRIDE = 4
REGIONS_Y = 4
REGIONS_Z = 2

CELLS = TILE_SIDE // STRIDE
ACROSS = 2 * CELLS
PLANE = 2 * ACROSS * ACROSS
ROWS = CELLS * PLANE
PADDED = -(-ROWS // 16) * 16
PHASES = STRIDE + 2
SLOTS = 16
OFFSETS = STRIDE**3
LANES = 128
MIB = 2**20


def vmem(count):
    return [pl.BlockSpec(memory_space=pltpu.VMEM) for _ in range(count)]


def regroup_kernel(rows_ref, out_ref, wide):
    groups = out_ref.shape[1]
    for lane in range(wide.shape[0]):
        columns = slice(lane * LANES, (lane + 1) * LANES)
        wide[lane] = rows_ref[:, columns].astype(jnp.float32)
        for offset in range(OFFSETS):
            out_ref[offset, :, columns] = wide[
                lane, pl.ds(offset, groups, stride=OFFSETS), :
            ].astype(jnp.bfloat16)


def regroup(rows):
    groups, width = rows.shape[0] // OFFSETS, rows.shape[1]
    return pl.pallas_call(
        regroup_kernel,
        out_shape=jax.ShapeDtypeStruct((OFFSETS, groups, width), jnp.bfloat16),
        in_specs=vmem(1),
        out_specs=vmem(1)[0],
        scratch_shapes=[pltpu.VMEM((width // LANES, rows.shape[0], LANES), jnp.float32)],
        name="regroup",
    )(rows)


def fine_kernel(
    inside_ref, field_ref, scale_ref, shift_ref, weight_ref, order_ref, bias_ref, out_ref,
    taps, slab, layers, windows,
):
    side, width = 2 * TILE_SIDE, FINE_WIDTH
    half = 2 * ACROSS * side
    zero = jnp.zeros((width, width), jnp.bfloat16)
    for place in range(9):
        taps[place, 3 * width :, :width] = zero
        taps[place, :width, width:] = zero
        for step in range(3):
            block = jnp.dot(
                weight_ref[place * 3 + step], order_ref[...], preferred_element_type=jnp.float32
            ).astype(jnp.bfloat16)
            taps[place, step * width : (step + 1) * width, :width] = block
            taps[place, (step + 1) * width : (step + 2) * width, width:] = block

    scale = jnp.broadcast_to(scale_ref[...], (8, width))
    shift = jnp.broadcast_to(shift_ref[...], (8, width))
    row = lax.broadcasted_iota(jnp.int32, (8, width), 0)
    first = jnp.where(row == 0, shift * inside_ref[2], shift)
    last = jnp.where(row == side + 1 - 20, shift * inside_ref[3], shift)
    chunks = [(0, first), (8, shift), (16, shift), (4, shift), (12, shift), (20, last)]

    def fill(phase_x, carry):
        def split(cell_x, carry):
            at_x = phase_x + STRIDE * cell_x
            for at_y in range(side + 2):
                slab[at_y * SLOTS : (at_y + 1) * SLOTS, :] = field_ref[at_x, at_y].astype(jnp.float32)
            within = jnp.where(at_x == 0, inside_ref[0], 1.0)
            within = jnp.where(at_x == side + 1, inside_ref[1], within)
            for at_z in range(TILE_SIDE + 2):
                slot = (at_z + TILE_SIDE + 1) % (TILE_SIDE + 2)
                if at_z == 0:
                    factor = within * inside_ref[4]
                elif at_z == TILE_SIDE + 1:
                    factor = within * inside_ref[5]
                else:
                    factor = within
                for number, (start, added) in enumerate(chunks):
                    value = slab[pl.ds(start * SLOTS + slot, 8, stride=SLOTS), :]
                    base = number // 3 * half + number % 3 * 8
                    base = pl.multiple_of(base + cell_x * side, 8)
                    layers[at_z, pl.ds(base, 8), :] = value
                    layers[at_z, pl.ds(base + half // 2, 8), :] = value * scale + added * factor
            return carry

        lax.fori_loop(0, ACROSS, split, 0)
        for phase_y in range(PHASES):
            start = phase_y if phase_y < STRIDE else half + phase_y - STRIDE
            for phase_z in range(PHASES):
                parts = [
                    layers[phase_z + STRIDE * cell, pl.ds(start, PLANE, stride=STRIDE), :]
                    for cell in range(CELLS)
                ]
                parts.append(jnp.zeros((PADDED - ROWS, width), jnp.float32))
                windows[phase_x * PHASES + phase_y, :, phase_z * width : (phase_z + 1) * width] = (
                    jnp.concatenate(parts, axis=0).astype(jnp.bfloat16)
                )
        return carry

    lax.fori_loop(0, PHASES, fill, 0)

    bias = bias_ref[...]

    def convolve(place, carry):
        at_x, at_y = place // STRIDE, place % STRIDE
        for pair in range(STRIDE // 2):
            total = jnp.zeros((PADDED, 2 * width), jnp.float32)
            for step_x in range(3):
                for step_y in range(3):
                    total += jnp.dot(
                        windows[
                            (at_x + step_x) * PHASES + at_y + step_y,
                            :,
                            pair * 2 * width : (pair * 2 + 4) * width,
                        ],
                        taps[step_x * 3 + step_y],
                        preferred_element_type=jnp.float32,
                    )
            total = total + bias
            out_ref[place * 2 + pair] = (total / (1.0 + jnp.exp(-total))).astype(jnp.bfloat16)
        return carry

    lax.fori_loop(0, STRIDE * STRIDE, convolve, 0)


def fine_conv(inside, field, scale, shift, weight, order, bias):
    width, side = FINE_WIDTH, 2 * TILE_SIDE
    pairs = OFFSETS // 2
    return pl.pallas_call(
        fine_kernel,
        out_shape=jax.ShapeDtypeStruct((pairs, PADDED, 2 * width), jnp.bfloat16),
        in_specs=[pl.BlockSpec(memory_space=pltpu.SMEM)] + vmem(6),
        out_specs=vmem(1)[0],
        scratch_shapes=[
            pltpu.VMEM((9, 4 * width, 2 * width), jnp.bfloat16),
            pltpu.VMEM(((side + 4) * SLOTS, width), jnp.float32),
            pltpu.VMEM((TILE_SIDE + 2, 4 * ACROSS * side, width), jnp.float32),
            pltpu.VMEM((PHASES**2, PADDED, PHASES * width), jnp.bfloat16),
        ],
        compiler_params=pltpu.CompilerParams(vmem_limit_bytes=48 * MIB),
        cost_estimate=pl.CostEstimate(
            flops=2 * pairs * PADDED * 36 * width * 2 * width,
            bytes_accessed=16 * MIB,
            transcendentals=pairs * PADDED * 2 * width,
        ),
        name="fine_conv",
    )(inside, field, scale, shift, weight, order, bias)


def project_kernel(hidden_ref, weight_ref, bias_ref, out_ref, total):
    step = pl.program_id(0)
    width = weight_ref.shape[3]

    @pl.when(step == 0)
    def _():
        total[...] = jnp.zeros_like(total)

    for pair in range(hidden_ref.shape[0]):
        weight = jnp.concatenate(
            [weight_ref[:, 2 * pair + item].reshape(FINE_WIDTH, width) for item in range(2)], axis=0
        )
        total[...] += jnp.dot(hidden_ref[pair], weight, preferred_element_type=jnp.float32)

    @pl.when(step == pl.num_programs(0) - 1)
    def _():
        out_ref[...] = (total[...] + bias_ref[...]).astype(jnp.bfloat16)


def project(hidden, weight, bias):
    pairs, rows, depth = hidden.shape
    groups, _, members, width = weight.shape
    steps = 8
    return pl.pallas_call(
        project_kernel,
        out_shape=jax.ShapeDtypeStruct((rows, width), jnp.bfloat16),
        grid=(steps,),
        in_specs=[
            pl.BlockSpec((pairs // steps, rows, depth), lambda i: (i, 0, 0)),
            pl.BlockSpec((groups, 2 * pairs // steps, members, width), lambda i: (0, i, 0, 0)),
            pl.BlockSpec((1, width), lambda i: (0, 0)),
        ],
        out_specs=pl.BlockSpec((rows, width), lambda i: (0, 0)),
        scratch_shapes=[pltpu.VMEM((rows, width), jnp.float32)],
        compiler_params=pltpu.CompilerParams(vmem_limit_bytes=24 * MIB),
        cost_estimate=pl.CostEstimate(
            flops=2 * pairs * rows * depth * width, bytes_accessed=8 * MIB, transcendentals=0
        ),
        name="project",
    )(hidden, weight, bias)


def bottle_kernel(field_ref, weight_ref, out_ref, total, packed):
    step_y = pl.program_id(0)
    width = field_ref.shape[4]
    frame = ACROSS + 2
    rows = CELLS * 2 * ACROSS * frame
    chunk = 256

    @pl.when(step_y == 0)
    def _():
        for step_x in range(3):
            for step_z in range(3):
                place = step_x * 3 + step_z
                packed[:, place * width : (place + 1) * width] = (
                    field_ref[step_z : step_z + CELLS, :, step_x : step_x + ACROSS]
                    .astype(jnp.float32)
                    .reshape(rows, width)
                    .astype(jnp.bfloat16)
                )

    for start in range(0, weight_ref.shape[4], chunk):
        acc = jnp.zeros((rows, chunk), jnp.float32)
        for step_x in range(3):
            for step_z in range(3):
                place = step_x * 3 + step_z
                acc += jnp.dot(
                    packed[:, place * width : (place + 1) * width],
                    weight_ref[step_x, 0, step_z, :, start : start + chunk],
                    preferred_element_type=jnp.float32,
                )
        total[step_y, :, start : start + chunk] = acc

    @pl.when(step_y == 2)
    def _():
        share = out_ref.shape[2]
        for group in range(rows // frame):
            at = group * frame
            value = sum(total[item, at + item : at + item + ACROSS, :] for item in range(3))
            for owner in range(out_ref.shape[0]):
                out_ref[owner, group * ACROSS : (group + 1) * ACROSS, :] = value[
                    :, owner * share : (owner + 1) * share
                ]


def bottle_terms(field, weight, owners):
    frame = ACROSS + 2
    rows = CELLS * 2 * ACROSS * frame
    width = weight.shape[3]
    return pl.pallas_call(
        bottle_kernel,
        out_shape=jax.ShapeDtypeStruct((owners, ROWS, COARSE_WIDTH // owners), jnp.float32),
        grid=(3,),
        in_specs=[
            pl.BlockSpec(field.shape, lambda i: (0, 0, 0, 0, 0)),
            pl.BlockSpec((3, 1, 3, width, COARSE_WIDTH), lambda i: (0, i, 0, 0, 0)),
        ],
        out_specs=pl.BlockSpec((owners, ROWS, COARSE_WIDTH // owners), lambda i: (0, 0, 0)),
        scratch_shapes=[
            pltpu.VMEM((3, rows, COARSE_WIDTH), jnp.float32),
            pltpu.VMEM((rows, 9 * width), jnp.bfloat16),
        ],
        compiler_params=pltpu.CompilerParams(vmem_limit_bytes=32 * MIB),
        cost_estimate=pl.CostEstimate(
            flops=2 * rows * 27 * width * COARSE_WIDTH, bytes_accessed=16 * MIB, transcendentals=0
        ),
        name="bottle_terms",
    )(field, weight)


def passed(value, steps):
    count = lax.axis_size("region")
    return lax.ppermute(
        value, "region", [(at, at + steps) for at in range(max(0, -steps), min(count, count - steps))]
    )


def halo(first, last, stride, count):
    if count == 1:
        return jnp.zeros_like(last), jnp.zeros_like(first)
    place = lax.axis_index("region") // stride % count
    if count == 2:
        span = lax.axis_size("region")
        pairs = [(at, at + stride if at // stride % 2 == 0 else at - stride) for at in range(span)]
        arrived = lax.ppermute(jnp.where(place == 0, last, first), "region", pairs)
        zero = jnp.zeros_like(arrived)
        return jnp.where(place == 1, arrived, zero), jnp.where(place == 0, arrived, zero)
    below, above = passed(last, stride), passed(first, -stride)
    return (
        jnp.where(place > 0, below, jnp.zeros_like(below)),
        jnp.where(place < count - 1, above, jnp.zeros_like(above)),
    )


def gathered_projection(proj_weight):
    chans, regions = lax.axis_size("chan"), lax.axis_size("region")
    held = proj_weight.shape[0]
    width = COARSE_WIDTH // chans
    mine = lax.all_to_all(proj_weight, "chan", split_axis=1, concat_axis=0, tiled=True)
    if held % OFFSETS == 0 and chans * held // OFFSETS % 16 == 0:
        each = held // OFFSETS
        whole = lax.all_gather(regroup(mine), "region", axis=0, tiled=False)
        channel = np.arange(FINE_WIDTH).reshape(chans, regions, each).transpose(1, 0, 2)
        return whole, channel.reshape(-1)
    whole = lax.all_gather(mine.reshape(chans, held, width), "region", axis=1, tiled=True)
    whole = whole.reshape(FINE_WIDTH, OFFSETS, width).transpose(1, 0, 2)
    return whole[None], np.arange(FINE_WIDTH)


def shards(
    latent,
    cond_scale,
    cond_shift,
    fine_weight,
    fine_bias,
    proj_weight,
    proj_bias,
    bottle_weight,
    bottle_bias,
    guide,
):
    chans = lax.axis_size("chan")
    chan_place = lax.axis_index("chan")
    region = lax.axis_index("region")
    width = COARSE_WIDTH // chans
    side = 2 * TILE_SIDE
    count_x = lax.axis_size("region") // (REGIONS_Y * REGIONS_Z)
    steps = (REGIONS_Y * REGIONS_Z, REGIONS_Z, 1)
    counts = (count_x, REGIONS_Y, REGIONS_Z)
    places = [region // step % count for step, count in zip(steps, counts)]
    inside = jnp.stack(
        [
            flag
            for place, count in zip(places, counts)
            for flag in ((place > 0).astype(jnp.float32), (place < count - 1).astype(jnp.float32))
        ]
    )

    columns, channel = gathered_projection(proj_weight)
    order = np.zeros((FINE_WIDTH, FINE_WIDTH), np.float32)
    order[channel, np.arange(FINE_WIDTH)] = 1.0
    order = jnp.asarray(order, jnp.bfloat16)

    block = latent[0]
    low, high = halo(block[:, :, :1], block[:, :, -1:], steps[2], counts[2])
    spare = jnp.zeros(block.shape[:2] + (SLOTS - TILE_SIDE - 2, FINE_WIDTH), block.dtype)
    field = jnp.concatenate([block, high, low, spare], axis=2)
    low, high = halo(field[:, :1], field[:, -1:], steps[1], counts[1])
    field = jnp.concatenate([low, field, high], axis=1)
    low, high = halo(field[:1], field[-1:], steps[0], counts[0])
    field = jnp.concatenate([low, field, high], axis=0)

    bias = jnp.dot(
        fine_bias[None], order.astype(jnp.float32), precision=lax.Precision.HIGHEST
    )
    hidden = fine_conv(
        inside,
        field,
        cond_scale[None],
        cond_shift[None],
        fine_weight.reshape(27, FINE_WIDTH, FINE_WIDTH),
        order,
        jnp.concatenate([bias, bias], axis=1),
    )
    coarse = project(
        hidden, columns, lax.dynamic_slice_in_dim(proj_bias, chan_place * width, width)[None]
    )

    grid = coarse[:ROWS].reshape(CELLS, 2, ACROSS, ACROSS, width)
    low, high = halo(grid[:1], grid[-1:], steps[2], counts[2])
    grid = jnp.concatenate([low, grid, high], axis=0)
    low, high = halo(grid[:, :, :, :1], grid[:, :, :, -1:], steps[1], counts[1])
    grid = jnp.concatenate([low, grid, high], axis=3)
    low, high = halo(grid[:, :, :1], grid[:, :, -1:], steps[0], counts[0])
    grid = jnp.concatenate([low, grid, high], axis=2)

    terms = bottle_terms(grid, bottle_weight.reshape(3, 3, 3, width, COARSE_WIDTH), chans)
    terms = lax.all_to_all(terms, "chan", split_axis=0, concat_axis=0, tiled=True)
    summed = jnp.sum(terms, axis=0)
    bottle = jax.nn.silu(summed + lax.dynamic_slice_in_dim(bottle_bias, chan_place * width, width))
    bottle = bottle.reshape(CELLS, 2, ACROSS, ACROSS, width)
    guided = (bottle[:, 0] + guide[0] * (bottle[:, 1] - bottle[:, 0])).astype(jnp.bfloat16)
    return guided.transpose(1, 2, 0, 3)[None]


def solution(mesh):
    placed = (
        P("region", None, None, None, None),
        P(),
        P(),
        P(),
        P(),
        P(("chan", "region"), None),
        P(),
        P(None, "chan", None),
        P(),
        P(),
    )
    return jax.shard_map(
        shards,
        mesh=mesh,
        in_specs=placed,
        out_specs=P("region", None, None, None, "chan"),
        check_vma=False,
    )
```

```python
import functools

import numpy as np

import jax
import jax.numpy as jnp
from jax import lax
from jax.experimental import pallas as pl
from jax.experimental.pallas import tpu as pltpu
from jax.sharding import PartitionSpec as P

FINE_WIDTH = 128
COARSE_WIDTH = 1024
TILE_SIDE = 12
STRIDE = 4
REGIONS_Y = 4
REGIONS_Z = 2

CELLS = TILE_SIDE // STRIDE
ACROSS = 2 * CELLS
PLANE = 2 * ACROSS * ACROSS
ROWS = CELLS * PLANE
PADDED = -(-ROWS // 16) * 16
PHASES = STRIDE + 2
OFFSETS = STRIDE**3
LANES = 128
MIB = 2**20


def vmem(count):
    return [pl.BlockSpec(memory_space=pltpu.VMEM) for _ in range(count)]


def regroup_kernel(*refs):
    rows_refs, out_ref, wide = refs[:-2], refs[-2], refs[-1]
    held = rows_refs[0].shape[0]
    groups = out_ref.shape[1]
    for lane in range(wide.shape[0]):
        columns = slice(lane * LANES, (lane + 1) * LANES)
        for number, rows_ref in enumerate(rows_refs):
            wide[lane, number * held : (number + 1) * held, :] = rows_ref[:, columns].astype(jnp.float32)
        for offset in range(OFFSETS):
            out_ref[offset, :, columns] = wide[
                lane, pl.ds(offset, groups, stride=OFFSETS), :
            ].astype(jnp.bfloat16)


def regroup(pieces):
    held, width = pieces[0].shape
    total = len(pieces) * held
    return pl.pallas_call(
        regroup_kernel,
        out_shape=jax.ShapeDtypeStruct((OFFSETS, total // OFFSETS, width), jnp.bfloat16),
        in_specs=vmem(len(pieces)),
        out_specs=vmem(1)[0],
        scratch_shapes=[pltpu.VMEM((width // LANES, total, LANES), jnp.float32)],
        name="regroup",
    )(*pieces)


def window_kernel(
    inside_ref, field_ref, scale_ref, shift_ref, weight_ref, order_ref, windows_ref, taps_ref,
    line, layers,
):
    phase_x = pl.program_id(0)
    side, width = 2 * TILE_SIDE, FINE_WIDTH
    half = 2 * ACROSS * side

    @pl.when(phase_x == 0)
    def _():
        zero = jnp.zeros((width, width), jnp.bfloat16)
        for place in range(9):
            taps_ref[place, 3 * width :, :width] = zero
            taps_ref[place, :width, width:] = zero
            for step in range(3):
                block = jnp.dot(
                    weight_ref[place * 3 + step], order_ref[...], preferred_element_type=jnp.float32
                ).astype(jnp.bfloat16)
                taps_ref[place, step * width : (step + 1) * width, :width] = block
                taps_ref[place, (step + 1) * width : (step + 2) * width, width:] = block

    scale = jnp.broadcast_to(scale_ref[...], (8, width))
    shift = jnp.broadcast_to(shift_ref[...], (8, width))
    row = lax.broadcasted_iota(jnp.int32, (8, width), 0)
    first = jnp.where(row == 0, shift * inside_ref[2], shift)
    last = jnp.where(row == side + 1 - 20, shift * inside_ref[3], shift)
    chunks = [(0, first), (8, shift), (16, shift), (4, shift), (12, shift), (20, last)]

    def split(cell_x, carry):
        at_x = phase_x + STRIDE * cell_x
        within = jnp.where(at_x == 0, inside_ref[0], 1.0)
        within = jnp.where(at_x == side + 1, inside_ref[1], within)
        for at_z in range(TILE_SIDE + 2):
            value = field_ref[at_x, at_z].astype(jnp.float32)
            line[at_z, 0:8, :] = value[side : side + 8]
            line[at_z, 8 : side + 8, :] = value[:side]
            line[at_z, side + 8 : side + 16, :] = value[side : side + 8]
            if at_z == 0:
                factor = within * inside_ref[4]
            elif at_z == TILE_SIDE + 1:
                factor = within * inside_ref[5]
            else:
                factor = within
            for number, (start, added) in enumerate(chunks):
                value = line[at_z, pl.ds(start + 7, 8), :]
                base = number // 3 * half + number % 3 * 8
                base = pl.multiple_of(base + cell_x * side, 8)
                layers[at_z, pl.ds(base, 8), :] = value
                layers[at_z, pl.ds(base + half // 2, 8), :] = value * scale + added * factor
        return carry

    lax.fori_loop(0, ACROSS, split, 0)
    for phase_y in range(PHASES):
        start = phase_y if phase_y < STRIDE else half + phase_y - STRIDE
        for phase_z in range(PHASES):
            parts = [
                layers[phase_z + STRIDE * cell, pl.ds(start, PLANE, stride=STRIDE), :]
                for cell in range(CELLS)
            ]
            parts.append(jnp.zeros((PADDED - ROWS, width), jnp.float32))
            windows_ref[0, phase_y, :, phase_z * width : (phase_z + 1) * width] = jnp.concatenate(
                parts, axis=0
            ).astype(jnp.bfloat16)


def make_windows(inside, field, scale, shift, weight, order):
    width, side = FINE_WIDTH, 2 * TILE_SIDE

    def whole(array):
        return pl.BlockSpec(array.shape, lambda i: (0,) * array.ndim)

    return pl.pallas_call(
        window_kernel,
        out_shape=(
            jax.ShapeDtypeStruct((PHASES, PHASES, PADDED, PHASES * width), jnp.bfloat16),
            jax.ShapeDtypeStruct((9, 4 * width, 2 * width), jnp.bfloat16),
        ),
        grid=(PHASES,),
        in_specs=[pl.BlockSpec(memory_space=pltpu.SMEM)]
        + [whole(array) for array in (field, scale, shift, weight, order)],
        out_specs=(
            pl.BlockSpec((1, PHASES, PADDED, PHASES * width), lambda i: (i, 0, 0, 0)),
            pl.BlockSpec((9, 4 * width, 2 * width), lambda i: (0, 0, 0)),
        ),
        scratch_shapes=[
            pltpu.VMEM((TILE_SIDE + 2, side + 16, width), jnp.float32),
            pltpu.VMEM((TILE_SIDE + 2, 4 * ACROSS * side, width), jnp.float32),
        ],
        compiler_params=pltpu.CompilerParams(vmem_limit_bytes=40 * MIB),
        cost_estimate=pl.CostEstimate(flops=10**10, bytes_accessed=16 * MIB, transcendentals=0),
        name="windows",
    )(inside, field, scale, shift, weight, order)


def convolve_kernel(first_ref, second_ref, third_ref, taps_ref, bias_ref, out_ref):
    width = FINE_WIDTH
    bias = bias_ref[...]

    def convolve(at_y, carry):
        for pair in range(STRIDE // 2):
            total = jnp.zeros((PADDED, 2 * width), jnp.float32)
            for step_x, windows_ref in enumerate((first_ref, second_ref, third_ref)):
                for step_y in range(3):
                    total += jnp.dot(
                        windows_ref[0, at_y + step_y, :, pair * 2 * width : (pair * 2 + 4) * width],
                        taps_ref[step_x * 3 + step_y],
                        preferred_element_type=jnp.float32,
                    )
            total = total + bias
            out_ref[at_y * 2 + pair] = (total / (1.0 + jnp.exp(-total))).astype(jnp.bfloat16)
        return carry

    lax.fori_loop(0, STRIDE, convolve, 0)


def convolve(windows, taps, bias, start, count):
    width = FINE_WIDTH
    each = STRIDE * STRIDE // 2
    block = (1, PHASES, PADDED, PHASES * width)
    return pl.pallas_call(
        convolve_kernel,
        out_shape=jax.ShapeDtypeStruct((count * each, PADDED, 2 * width), jnp.bfloat16),
        grid=(count,),
        in_specs=[
            pl.BlockSpec(block, lambda i, step=step: (i + start + step, 0, 0, 0)) for step in range(3)
        ]
        + [
            pl.BlockSpec(taps.shape, lambda i: (0, 0, 0)),
            pl.BlockSpec(bias.shape, lambda i: (0, 0)),
        ],
        out_specs=pl.BlockSpec((each, PADDED, 2 * width), lambda i: (i, 0, 0)),
        compiler_params=pltpu.CompilerParams(vmem_limit_bytes=40 * MIB),
        cost_estimate=pl.CostEstimate(
            flops=2 * count * each * PADDED * 36 * width * 2 * width,
            bytes_accessed=16 * MIB,
            transcendentals=count * each * PADDED * 2 * width,
        ),
        name="convolve",
    )(windows, windows, windows, taps, bias)


def project_kernel(early_ref, late_ref, *refs):
    weight_refs, bias_ref, out_ref, total = refs[:-3], refs[-3], refs[-2], refs[-1]
    step = pl.program_id(0)
    steps = pl.num_programs(0)
    width = out_ref.shape[1]

    @pl.when(step == 0)
    def _():
        total[...] = jnp.zeros_like(total)

    def add(hidden_ref):
        acc = total[...]
        for pair in range(hidden_ref.shape[0]):
            weight = jnp.concatenate(
                [ref[2 * pair + item] for item in range(2) for ref in weight_refs], axis=0
            )
            acc += jnp.dot(hidden_ref[pair], weight, preferred_element_type=jnp.float32)
        total[...] = acc

    pl.when(step < steps // 2)(lambda: add(early_ref))
    pl.when(step >= steps // 2)(lambda: add(late_ref))

    @pl.when(step == steps - 1)
    def _():
        out_ref[...] = (total[...] + bias_ref[...]).astype(jnp.bfloat16)


def project(early, late, weights, bias):
    pairs, rows, depth = early.shape
    width = bias.shape[1]
    steps = 8
    half = steps // 2
    return pl.pallas_call(
        project_kernel,
        out_shape=jax.ShapeDtypeStruct((rows, width), jnp.bfloat16),
        grid=(steps,),
        in_specs=[
            pl.BlockSpec((pairs // half, rows, depth), lambda i: (jnp.minimum(i, half - 1), 0, 0)),
            pl.BlockSpec((pairs // half, rows, depth), lambda i: (jnp.maximum(i - half, 0), 0, 0)),
        ]
        + [
            pl.BlockSpec((OFFSETS // steps,) + weight.shape[1:], lambda i: (i, 0, 0))
            for weight in weights
        ]
        + [pl.BlockSpec((1, width), lambda i: (0, 0))],
        out_specs=pl.BlockSpec((rows, width), lambda i: (0, 0)),
        scratch_shapes=[pltpu.VMEM((rows, width), jnp.float32)],
        compiler_params=pltpu.CompilerParams(vmem_limit_bytes=56 * MIB),
        cost_estimate=pl.CostEstimate(
            flops=4 * pairs * rows * depth * width, bytes_accessed=8 * MIB, transcendentals=0
        ),
        name="project",
    )(early, late, *weights, bias)


def bottle_kernel(field_ref, weight_ref, out_ref, total, packed):
    step_y = pl.program_id(0)
    width = field_ref.shape[4]
    frame = ACROSS + 2
    rows = CELLS * 2 * ACROSS * frame
    chunk = 256

    @pl.when(step_y == 0)
    def _():
        for step_x in range(3):
            for step_z in range(3):
                place = step_x * 3 + step_z
                packed[:, place * width : (place + 1) * width] = (
                    field_ref[step_z : step_z + CELLS, :, step_x : step_x + ACROSS]
                    .astype(jnp.float32)
                    .reshape(rows, width)
                    .astype(jnp.bfloat16)
                )

    for start in range(0, weight_ref.shape[4], chunk):
        acc = jnp.zeros((rows, chunk), jnp.float32)
        for step_x in range(3):
            for step_z in range(3):
                place = step_x * 3 + step_z
                acc += jnp.dot(
                    packed[:, place * width : (place + 1) * width],
                    weight_ref[step_x, 0, step_z, :, start : start + chunk],
                    preferred_element_type=jnp.float32,
                )
        total[step_y, :, start : start + chunk] = acc

    @pl.when(step_y == 2)
    def _():
        share = out_ref.shape[2]
        for group in range(rows // frame):
            at = group * frame
            value = sum(total[item, at + item : at + item + ACROSS, :] for item in range(3))
            for owner in range(out_ref.shape[0]):
                out_ref[owner, group * ACROSS : (group + 1) * ACROSS, :] = value[
                    :, owner * share : (owner + 1) * share
                ]


def bottle_terms(field, weight, owners):
    frame = ACROSS + 2
    rows = CELLS * 2 * ACROSS * frame
    width = weight.shape[3]
    return pl.pallas_call(
        bottle_kernel,
        out_shape=jax.ShapeDtypeStruct((owners, ROWS, COARSE_WIDTH // owners), jnp.float32),
        grid=(3,),
        in_specs=[
            pl.BlockSpec(field.shape, lambda i: (0, 0, 0, 0, 0)),
            pl.BlockSpec((3, 1, 3, width, COARSE_WIDTH), lambda i: (0, i, 0, 0, 0)),
        ],
        out_specs=pl.BlockSpec((owners, ROWS, COARSE_WIDTH // owners), lambda i: (0, 0, 0)),
        scratch_shapes=[
            pltpu.VMEM((3, rows, COARSE_WIDTH), jnp.float32),
            pltpu.VMEM((rows, 9 * width), jnp.bfloat16),
        ],
        compiler_params=pltpu.CompilerParams(vmem_limit_bytes=56 * MIB),
        cost_estimate=pl.CostEstimate(
            flops=2 * rows * 27 * width * COARSE_WIDTH, bytes_accessed=16 * MIB, transcendentals=0
        ),
        name="bottle_terms",
    )(field, weight)


def passed(value, steps):
    count = lax.axis_size("region")
    return lax.ppermute(
        value, "region", [(at, at + steps) for at in range(max(0, -steps), min(count, count - steps))]
    )


def across_z(value, steps):
    count = lax.axis_size("region")
    pairs = []
    for at in range(count):
        place_y = at // REGIONS_Z % REGIONS_Y + steps
        if 0 <= place_y < REGIONS_Y:
            pairs.append((at, (at + steps * REGIONS_Z) // REGIONS_Z * REGIONS_Z + 1 - at % REGIONS_Z))
    return lax.ppermute(value, "region", pairs)


def along_y(value, steps):
    count = lax.axis_size("region")
    pairs = [
        (at, at + steps * REGIONS_Z)
        for at in range(count)
        if 0 <= at // REGIONS_Z % REGIONS_Y + steps < REGIONS_Y
    ]
    return lax.ppermute(value, "region", pairs)


def with_halos(value, dim_z, dim_y):
    upper = lax.axis_index("region") % REGIONS_Z == 1

    def edge(array, dim, last):
        size = array.shape[dim]
        return lax.slice_in_dim(array, size - 1 if last else 0, size if last else 1, axis=dim)

    def ends(array):
        zero = jnp.zeros_like(array)
        return jnp.where(upper, array, zero), jnp.where(upper, zero, array)

    face = jnp.where(upper, edge(value, dim_z, False), edge(value, dim_z, True))
    layer = across_z(face, 0)
    below = along_y(edge(value, dim_y, True), 1)
    above = along_y(edge(value, dim_y, False), -1)
    corner_below = across_z(edge(face, dim_y, True), 1)
    corner_above = across_z(edge(face, dim_y, False), -1)
    parts = []
    for middle, outer in ((value, layer), (below, corner_below), (above, corner_above)):
        low, high = ends(outer)
        parts.append(jnp.concatenate([low, middle, high], axis=dim_z))
    return parts


def with_x_halos(value, dim):
    count = lax.axis_size("region") // (REGIONS_Y * REGIONS_Z)
    size = value.shape[dim]
    first = lax.slice_in_dim(value, 0, 1, axis=dim)
    last = lax.slice_in_dim(value, size - 1, size, axis=dim)
    if count == 1:
        low, high = jnp.zeros_like(last), jnp.zeros_like(first)
    else:
        low, high = passed(last, REGIONS_Y * REGIONS_Z), passed(first, -REGIONS_Y * REGIONS_Z)
    return jnp.concatenate([low, value, high], axis=dim)


def exchange(pieces_of):
    chans = lax.axis_size("chan")
    me = lax.axis_index("chan")
    arrived = []
    for distance in range(1, chans):
        arrived.append(
            lax.ppermute(pieces_of(me ^ distance), "chan", [(at, at ^ distance) for at in range(chans)])
        )
    return [pieces_of(me)] + arrived


def around(value):
    count = lax.axis_size("region")
    ring = list(range(0, count, 2)) + list(range(1, count, 2))[::-1]
    held, sources = [value], [[0] * count]
    forward = backward = value
    for step in range(1, count // 2 + 1):
        forward = lax.ppermute(
            forward, "region", [(ring[at], ring[(at + 1) % count]) for at in range(count)]
        )
        held.append(forward)
        sources.append([-step] * count)
        if step < count - count // 2:
            backward = lax.ppermute(
                backward, "region", [(ring[(at + 1) % count], ring[at]) for at in range(count)]
            )
            held.append(backward)
            sources.append([step] * count)
    place = {region: at for at, region in enumerate(ring)}
    origin = np.array(
        [[ring[(place[region] + shift[0]) % count] for shift in sources] for region in range(count)]
    )
    return held, origin


def gathered_projection(proj_weight):
    chans, regions = lax.axis_size("chan"), lax.axis_size("region")
    held = proj_weight.shape[0]
    width = COARSE_WIDTH // chans
    if held % OFFSETS == 0 and chans * held // OFFSETS % 16 == 0:
        each = held // OFFSETS
        mine = exchange(lambda owner: lax.dynamic_slice_in_dim(proj_weight, owner * width, width, axis=1))
        pieces, origin = around(regroup(mine))
        table = np.zeros((chans, regions, len(pieces), chans, each), np.int32)
        for chan in range(chans):
            for distance in range(chans):
                first = (chan ^ distance) * regions + origin
                table[chan, :, :, distance] = first[:, :, None] * each + np.arange(each)
        table = jnp.asarray(table.reshape(chans * regions, FINE_WIDTH))
        device = lax.axis_index("chan") * regions + lax.axis_index("region")
        return pieces, lax.dynamic_index_in_dim(table, device, 0, keepdims=True)
    mine = lax.all_to_all(proj_weight, "chan", split_axis=1, concat_axis=0, tiled=True)
    whole = lax.all_gather(mine.reshape(chans, held, width), "region", axis=1, tiled=True)
    whole = whole.reshape(FINE_WIDTH, OFFSETS, width).transpose(1, 0, 2)
    return [whole], jnp.arange(FINE_WIDTH, dtype=jnp.int32)[None]


def shards(
    latent,
    cond_scale,
    cond_shift,
    fine_weight,
    fine_bias,
    proj_weight,
    proj_bias,
    bottle_weight,
    bottle_bias,
    guide,
):
    chans = lax.axis_size("chan")
    chan_place = lax.axis_index("chan")
    region = lax.axis_index("region")
    width = COARSE_WIDTH // chans
    side = 2 * TILE_SIDE
    count_x = lax.axis_size("region") // (REGIONS_Y * REGIONS_Z)
    steps = (REGIONS_Y * REGIONS_Z, REGIONS_Z, 1)
    counts = (count_x, REGIONS_Y, REGIONS_Z)
    places = [region // step % count for step, count in zip(steps, counts)]
    inside = jnp.stack(
        [
            flag
            for place, count in zip(places, counts)
            for flag in ((place > 0).astype(jnp.float32), (place < count - 1).astype(jnp.float32))
        ]
    )

    columns, channel = gathered_projection(proj_weight)
    order = lax.broadcasted_iota(jnp.int32, (FINE_WIDTH, FINE_WIDTH), 0) == channel

    body, low, high = with_halos(latent[0].transpose(0, 2, 1, 3), 1, 2)
    spare = jnp.zeros(low.shape[:2] + (6, FINE_WIDTH), low.dtype)
    field = with_x_halos(jnp.concatenate([body, high, spare, low], axis=2), 0)

    bias = jnp.sum(jnp.where(order, fine_bias[:, None], 0.0), axis=0)
    windows, taps = make_windows(
        inside,
        field,
        cond_scale[None],
        cond_shift[None],
        fine_weight.reshape(27, FINE_WIDTH, FINE_WIDTH),
        order.astype(jnp.bfloat16),
    )
    bias = jnp.concatenate([bias, bias])[None]
    half = STRIDE // 2
    early = convolve(windows, taps, bias, 0, half)
    late = convolve(windows, taps, bias, half, half)
    coarse = project(
        early, late, columns, lax.dynamic_slice_in_dim(proj_bias, chan_place * width, width)[None]
    )

    grid = coarse[:ROWS].reshape(CELLS, 2, ACROSS, ACROSS, width)
    body, low, high = with_halos(grid, 0, 3)
    field = with_x_halos(jnp.concatenate([low, body, high], axis=3), 2)

    terms = bottle_terms(field, bottle_weight.reshape(3, 3, 3, width, COARSE_WIDTH), chans)
    own = lax.dynamic_index_in_dim(terms, chan_place, 0, keepdims=False)
    _, *others = exchange(
        lambda owner: lax.dynamic_index_in_dim(terms, owner, 0, keepdims=False).astype(jnp.bfloat16)
    )
    summed = own + sum(other.astype(jnp.float32) for other in others)
    bottle = jax.nn.silu(summed + lax.dynamic_slice_in_dim(bottle_bias, chan_place * width, width))
    bottle = bottle.reshape(CELLS, 2, ACROSS, ACROSS, width)
    guided = (bottle[:, 0] + guide[0] * (bottle[:, 1] - bottle[:, 0])).astype(jnp.bfloat16)
    return guided.transpose(1, 2, 0, 3)[None]


def solution(mesh):
    placed = (
        P("region", None, None, None, None),
        P(),
        P(),
        P(),
        P(),
        P(("chan", "region"), None),
        P(),
        P(None, "chan", None),
        P(),
        P(),
    )
    return jax.shard_map(
        shards,
        mesh=mesh,
        in_specs=placed,
        out_specs=P("region", None, None, None, "chan"),
        check_vma=False,
    )
```

```python
import functools

import numpy as np

import jax
import jax.numpy as jnp
from jax import lax
from jax.experimental import pallas as pl
from jax.experimental.pallas import tpu as pltpu
from jax.sharding import PartitionSpec as P

FINE_WIDTH = 128
COARSE_WIDTH = 1024
TILE_SIDE = 12
STRIDE = 4
REGIONS_Y = 4
REGIONS_Z = 2

CELLS = TILE_SIDE // STRIDE
ACROSS = 2 * CELLS
PLANE = 2 * ACROSS * ACROSS
ROWS = CELLS * PLANE
PADDED = -(-ROWS // 16) * 16
PHASES = STRIDE + 2
OFFSETS = STRIDE**3
LANES = 128
MIB = 2**20


def vmem(count):
    return [pl.BlockSpec(memory_space=pltpu.VMEM) for _ in range(count)]


def regroup_kernel(*refs):
    rows_refs, out_ref, wide = refs[:-2], refs[-2], refs[-1]
    held = rows_refs[0].shape[0]
    groups = out_ref.shape[1]
    for lane in range(wide.shape[0]):
        columns = slice(lane * LANES, (lane + 1) * LANES)
        for number, rows_ref in enumerate(rows_refs):
            wide[lane, number * held : (number + 1) * held, :] = rows_ref[:, columns].astype(jnp.float32)
        for offset in range(OFFSETS):
            out_ref[offset, :, columns] = wide[
                lane, pl.ds(offset, groups, stride=OFFSETS), :
            ].astype(jnp.bfloat16)


def regroup(pieces):
    held, width = pieces[0].shape
    total = len(pieces) * held
    return pl.pallas_call(
        regroup_kernel,
        out_shape=jax.ShapeDtypeStruct((OFFSETS, total // OFFSETS, width), jnp.bfloat16),
        in_specs=vmem(len(pieces)),
        out_specs=vmem(1)[0],
        scratch_shapes=[pltpu.VMEM((width // LANES, total, LANES), jnp.float32)],
        name="regroup",
    )(*pieces)


def window_kernel(
    inside_ref, block_ref, layer_ref, below_ref, above_ref, outer_ref, scale_ref, shift_ref,
    weight_ref, order_ref, windows_ref, taps_ref, rows, line, layers,
):
    phase_x = pl.program_id(0)
    side, depth, width = 2 * TILE_SIDE, TILE_SIDE, FINE_WIDTH
    half = 2 * ACROSS * side

    @pl.when(phase_x == 0)
    def _():
        zero = jnp.zeros((width, width), jnp.bfloat16)
        for place in range(9):
            taps_ref[place, 3 * width :, :width] = zero
            taps_ref[place, :width, width:] = zero
            for step in range(3):
                block = jnp.dot(
                    weight_ref[place * 3 + step], order_ref[...], preferred_element_type=jnp.float32
                ).astype(jnp.bfloat16)
                taps_ref[place, step * width : (step + 1) * width, :width] = block
                taps_ref[place, (step + 1) * width : (step + 2) * width, width:] = block

        def widen(at_x, carry):
            rows[0, at_x, : depth + 1, :] = below_ref[at_x].astype(jnp.float32)
            rows[1, at_x, : depth + 1, :] = above_ref[at_x].astype(jnp.float32)
            return carry

        lax.fori_loop(0, side, widen, 0)

    scale = jnp.broadcast_to(scale_ref[...], (8, width))
    shift = jnp.broadcast_to(shift_ref[...], (8, width))
    row = lax.broadcasted_iota(jnp.int32, (8, width), 0)
    first = jnp.where(row == 0, shift * inside_ref[2], shift)
    last = jnp.where(row == side + 1 - 20, shift * inside_ref[3], shift)
    chunks = [(0, first), (8, shift), (16, shift), (4, shift), (12, shift), (20, last)]

    def split(cell_x, carry):
        at_x = phase_x + STRIDE * cell_x
        outside = jnp.logical_or(at_x == 0, at_x == side + 1)

        @pl.when(jnp.logical_not(outside))
        def _():
            at = at_x - 1
            for at_z in range(depth + 2):
                if at_z == 0:
                    flag, value, place = inside_ref[4], layer_ref[at], depth
                elif at_z == depth + 1:
                    flag, value, place = inside_ref[5], layer_ref[at], depth
                else:
                    flag, value, place = None, block_ref[at, at_z - 1], at_z - 1
                value = value.astype(jnp.float32)
                low, high = rows[0, at, place : place + 1, :], rows[1, at, place : place + 1, :]
                if flag is not None:
                    value, low, high = value * flag, low * flag, high * flag
                line[at_z, 7:8, :] = low
                line[at_z, 8 : side + 8, :] = value
                line[at_z, side + 8 : side + 9, :] = high

        @pl.when(outside)
        def _():
            end = jnp.where(at_x == 0, 0, 1)
            for at_z in range(depth + 2):
                value = outer_ref[end, at_z].astype(jnp.float32)
                line[at_z, 0:8, :] = value[side : side + 8]
                line[at_z, 8 : side + 8, :] = value[:side]
                line[at_z, side + 8 : side + 16, :] = value[side : side + 8]

        within = jnp.where(at_x == 0, inside_ref[0], 1.0)
        within = jnp.where(at_x == side + 1, inside_ref[1], within)
        for at_z in range(depth + 2):
            if at_z == 0:
                factor = within * inside_ref[4]
            elif at_z == depth + 1:
                factor = within * inside_ref[5]
            else:
                factor = within
            for number, (start, added) in enumerate(chunks):
                value = line[at_z, pl.ds(start + 7, 8), :]
                base = number // 3 * half + number % 3 * 8
                base = pl.multiple_of(base + cell_x * side, 8)
                layers[at_z, pl.ds(base, 8), :] = value
                layers[at_z, pl.ds(base + half // 2, 8), :] = value * scale + added * factor
        return carry

    lax.fori_loop(0, ACROSS, split, 0)
    for phase_y in range(PHASES):
        start = phase_y if phase_y < STRIDE else half + phase_y - STRIDE
        for phase_z in range(PHASES):
            parts = [
                layers[phase_z + STRIDE * cell, pl.ds(start, PLANE, stride=STRIDE), :]
                for cell in range(CELLS)
            ]
            parts.append(jnp.zeros((PADDED - ROWS, width), jnp.float32))
            windows_ref[0, phase_y, :, phase_z * width : (phase_z + 1) * width] = jnp.concatenate(
                parts, axis=0
            ).astype(jnp.bfloat16)


def make_windows(inside, *arrays):
    width, side = FINE_WIDTH, 2 * TILE_SIDE

    def whole(array):
        return pl.BlockSpec(array.shape, lambda i: (0,) * array.ndim)

    return pl.pallas_call(
        window_kernel,
        out_shape=(
            jax.ShapeDtypeStruct((PHASES, PHASES, PADDED, PHASES * width), jnp.bfloat16),
            jax.ShapeDtypeStruct((9, 4 * width, 2 * width), jnp.bfloat16),
        ),
        grid=(PHASES,),
        in_specs=[pl.BlockSpec(memory_space=pltpu.SMEM)] + [whole(array) for array in arrays],
        out_specs=(
            pl.BlockSpec((1, PHASES, PADDED, PHASES * width), lambda i: (i, 0, 0, 0)),
            pl.BlockSpec((9, 4 * width, 2 * width), lambda i: (0, 0, 0)),
        ),
        scratch_shapes=[
            pltpu.VMEM((2, side, 16, width), jnp.float32),
            pltpu.VMEM((TILE_SIDE + 2, side + 16, width), jnp.float32),
            pltpu.VMEM((TILE_SIDE + 2, 4 * ACROSS * side, width), jnp.float32),
        ],
        compiler_params=pltpu.CompilerParams(vmem_limit_bytes=28 * MIB),
        cost_estimate=pl.CostEstimate(flops=10**10, bytes_accessed=16 * MIB, transcendentals=0),
        name="windows",
    )(inside, *arrays)


def convolve_kernel(first_ref, second_ref, third_ref, taps_ref, bias_ref, out_ref):
    width = FINE_WIDTH
    bias = bias_ref[...]

    def convolve(at_y, carry):
        total = jnp.zeros((2 * PADDED, 2 * width), jnp.float32)
        for step_x, windows_ref in enumerate((first_ref, second_ref, third_ref)):
            for step_y in range(3):
                taken = [
                    windows_ref[0, at_y + step_y, :, pair * 2 * width : (pair * 2 + 4) * width]
                    for pair in range(2)
                ]
                total += jnp.dot(
                    jnp.concatenate(taken, axis=0),
                    taps_ref[step_x * 3 + step_y],
                    preferred_element_type=jnp.float32,
                )
        total = total + bias
        hidden = (total / (1.0 + jnp.exp(-total))).astype(jnp.bfloat16)
        for pair in range(2):
            out_ref[at_y * 2 + pair] = hidden[pair * PADDED : (pair + 1) * PADDED]
        return carry

    lax.fori_loop(0, STRIDE, convolve, 0)


def convolve(windows, taps, bias, start, count):
    width = FINE_WIDTH
    each = STRIDE * STRIDE // 2
    block = (1, PHASES, PADDED, PHASES * width)
    return pl.pallas_call(
        convolve_kernel,
        out_shape=jax.ShapeDtypeStruct((count * each, PADDED, 2 * width), jnp.bfloat16),
        grid=(count,),
        in_specs=[
            pl.BlockSpec(block, lambda i, step=step: (i + start + step, 0, 0, 0)) for step in range(3)
        ]
        + [
            pl.BlockSpec(taps.shape, lambda i: (0, 0, 0)),
            pl.BlockSpec(bias.shape, lambda i: (0, 0)),
        ],
        out_specs=pl.BlockSpec((each, PADDED, 2 * width), lambda i: (i, 0, 0)),
        compiler_params=pltpu.CompilerParams(vmem_limit_bytes=28 * MIB),
        cost_estimate=pl.CostEstimate(
            flops=2 * count * each * PADDED * 36 * width * 2 * width,
            bytes_accessed=16 * MIB,
            transcendentals=count * each * PADDED * 2 * width,
        ),
        name="convolve",
    )(windows, windows, windows, taps, bias)


def project_kernel(place_ref, early_ref, late_ref, *refs):
    weight_refs, bias_ref, out_ref, total = refs[:-3], refs[-3], refs[-2], refs[-1]
    step = pl.program_id(0)
    width = out_ref.shape[1]

    def product(hidden_ref):
        acc = jnp.zeros(total.shape, jnp.float32)
        for pair in range(hidden_ref.shape[0]):
            weight = jnp.concatenate(
                [ref[2 * pair + item] for item in range(2) for ref in weight_refs], axis=0
            )
            acc += jnp.dot(hidden_ref[pair], weight, preferred_element_type=jnp.float32)
        return acc

    @pl.when(step == 0)
    def _():
        total[...] = product(early_ref)

    @pl.when(step == 1)
    def _():
        start = pl.multiple_of(place_ref[0] * width, width)
        out_ref[...] = (total[...] + product(late_ref) + bias_ref[:, pl.ds(start, width)]).astype(
            jnp.bfloat16
        )


def project(place, early, late, weights, bias):
    pairs, rows, depth = early.shape
    width = weights[0].shape[2]
    return pl.pallas_call(
        project_kernel,
        out_shape=jax.ShapeDtypeStruct((rows, width), jnp.bfloat16),
        grid=(2,),
        in_specs=[
            pl.BlockSpec(memory_space=pltpu.SMEM),
            pl.BlockSpec(early.shape, lambda i: (0, 0, 0)),
            pl.BlockSpec(late.shape, lambda i: (0, 0, 0)),
        ]
        + [
            pl.BlockSpec((OFFSETS // 2,) + weight.shape[1:], lambda i: (i, 0, 0)) for weight in weights
        ]
        + [pl.BlockSpec(bias.shape, lambda i: (0, 0))],
        out_specs=pl.BlockSpec((rows, width), lambda i: (0, 0)),
        scratch_shapes=[pltpu.VMEM((rows, width), jnp.float32)],
        compiler_params=pltpu.CompilerParams(vmem_limit_bytes=24 * MIB),
        cost_estimate=pl.CostEstimate(
            flops=4 * pairs * rows * depth * width, bytes_accessed=8 * MIB, transcendentals=0
        ),
        name="project",
    )(place, early, late, *weights, bias)


def bottle_kernel(place_ref, field_ref, weight_ref, own_ref, *refs):
    other_refs, total, packed, dense = refs[:-3], refs[-3], refs[-2], refs[-1]
    step_y = pl.program_id(0)
    width = field_ref.shape[4]
    share = own_ref.shape[1]
    frame = ACROSS + 2
    rows = CELLS * 2 * ACROSS * frame
    chunk = 256

    @pl.when(step_y == 0)
    def _():
        for step_x in range(3):
            for step_z in range(3):
                place = step_x * 3 + step_z
                packed[:, place * width : (place + 1) * width] = (
                    field_ref[step_z : step_z + CELLS, :, step_x : step_x + ACROSS]
                    .astype(jnp.float32)
                    .reshape(rows, width)
                    .astype(jnp.bfloat16)
                )

    for start in range(0, weight_ref.shape[4], chunk):
        total[step_y, :, start : start + chunk] = jnp.dot(
            packed[...],
            weight_ref[:, 0, :, :, start : start + chunk].reshape(9 * width, chunk),
            preferred_element_type=jnp.float32,
        )

    @pl.when(step_y == 2)
    def _():
        for distance, out_ref in enumerate((own_ref,) + other_refs):
            start = pl.multiple_of((place_ref[0] ^ distance) * share, share)
            for group in range(rows // frame):
                at = group * frame
                dense[group * ACROSS : (group + 1) * ACROSS, :] = sum(
                    total[item, at + item : at + item + ACROSS, pl.ds(start, share)]
                    for item in range(3)
                )
            out_ref[...] = dense[...].astype(out_ref.dtype)


def bottle_terms(place, field, weight, owners):
    frame = ACROSS + 2
    rows = CELLS * 2 * ACROSS * frame
    width = weight.shape[3]
    share = COARSE_WIDTH // owners
    return pl.pallas_call(
        bottle_kernel,
        out_shape=[
            jax.ShapeDtypeStruct((ROWS, share), jnp.bfloat16 if distance else jnp.float32)
            for distance in range(owners)
        ],
        grid=(3,),
        in_specs=[
            pl.BlockSpec(memory_space=pltpu.SMEM),
            pl.BlockSpec(field.shape, lambda i: (0, 0, 0, 0, 0)),
            pl.BlockSpec((3, 1, 3, width, COARSE_WIDTH), lambda i: (0, i, 0, 0, 0)),
        ],
        out_specs=[pl.BlockSpec((ROWS, share), lambda i: (0, 0))] * owners,
        scratch_shapes=[
            pltpu.VMEM((3, rows, COARSE_WIDTH), jnp.float32),
            pltpu.VMEM((rows, 9 * width), jnp.bfloat16),
            pltpu.VMEM((ROWS, share), jnp.float32),
        ],
        compiler_params=pltpu.CompilerParams(vmem_limit_bytes=28 * MIB),
        cost_estimate=pl.CostEstimate(
            flops=2 * rows * 27 * width * COARSE_WIDTH, bytes_accessed=16 * MIB, transcendentals=0
        ),
        name="bottle_terms",
    )(place, field, weight)


def finish_kernel(place_ref, guide_ref, own_ref, *refs):
    other_refs, bias_ref, out_ref = refs[:-2], refs[-2], refs[-1]
    share = own_ref.shape[1]
    start = pl.multiple_of(place_ref[0] * share, share)
    value = own_ref[...] + bias_ref[:, pl.ds(start, share)]
    for other_ref in other_refs:
        value = value + other_ref[...].astype(jnp.float32)
    value = value / (1.0 + jnp.exp(-value))
    half = PLANE // 2
    for cell in range(CELLS):
        plain = value[cell * PLANE : cell * PLANE + half]
        guided = value[cell * PLANE + half : (cell + 1) * PLANE]
        out_ref[cell] = (plain + guide_ref[0] * (guided - plain)).astype(jnp.bfloat16)


def finish(place, guide, terms, bias):
    share = terms[0].shape[1]
    return pl.pallas_call(
        finish_kernel,
        out_shape=jax.ShapeDtypeStruct((CELLS, PLANE // 2, share), jnp.bfloat16),
        in_specs=[pl.BlockSpec(memory_space=pltpu.SMEM)] * 2 + vmem(len(terms) + 1),
        out_specs=vmem(1)[0],
        name="finish",
    )(place, guide, *terms, bias)


def passed(value, steps):
    count = lax.axis_size("region")
    return lax.ppermute(
        value, "region", [(at, at + steps) for at in range(max(0, -steps), min(count, count - steps))]
    )


def across_z(value):
    count = lax.axis_size("region")
    return lax.ppermute(value, "region", [(at, at ^ 1) for at in range(count)])


def along_y(value, steps):
    count = lax.axis_size("region")
    pairs = [
        (at, at + steps * REGIONS_Z)
        for at in range(count)
        if 0 <= at // REGIONS_Z % REGIONS_Y + steps < REGIONS_Y
    ]
    return lax.ppermute(value, "region", pairs)


def with_halos(value, dim_x, dim_y, dim_z):
    value = jnp.concatenate(z_ends(z_layer(value, dim_z), value, dim_z), axis=dim_z)
    value = jnp.concatenate(
        [along_y(edge(value, dim_y, True), 1), value, along_y(edge(value, dim_y, False), -1)],
        axis=dim_y,
    )
    low, high = x_layers(edge(value, dim_x, False), edge(value, dim_x, True))
    return jnp.concatenate([low, value, high], axis=dim_x)


def edge(array, dim, last):
    size = array.shape[dim]
    return lax.slice_in_dim(array, size - 1 if last else 0, size if last else 1, axis=dim)


def is_upper():
    return lax.axis_index("region") % REGIONS_Z == 1


def z_layer(value, dim):
    return across_z(jnp.where(is_upper(), edge(value, dim, False), edge(value, dim, True)))


def z_ends(layer, value, dim):
    zero = jnp.zeros_like(layer)
    return [jnp.where(is_upper(), layer, zero), value, jnp.where(is_upper(), zero, layer)]


def x_layers(first, last):
    count = lax.axis_size("region") // (REGIONS_Y * REGIONS_Z)
    if count == 1:
        return jnp.zeros_like(last), jnp.zeros_like(first)
    return passed(last, REGIONS_Y * REGIONS_Z), passed(first, -REGIONS_Y * REGIONS_Z)


def exchange(piece_at):
    chans = lax.axis_size("chan")
    return [piece_at(0)] + [
        lax.ppermute(piece_at(distance), "chan", [(at, at ^ distance) for at in range(chans)])
        for distance in range(1, chans)
    ]


def around(value):
    count = lax.axis_size("region")
    ring = list(range(0, count, 2)) + list(range(1, count, 2))[::-1]
    held, sources = [value], [[0] * count]
    forward = backward = value
    for step in range(1, count // 2 + 1):
        forward = lax.ppermute(
            forward, "region", [(ring[at], ring[(at + 1) % count]) for at in range(count)]
        )
        held.append(forward)
        sources.append([-step] * count)
        if step < count - count // 2:
            backward = lax.ppermute(
                backward, "region", [(ring[(at + 1) % count], ring[at]) for at in range(count)]
            )
            held.append(backward)
            sources.append([step] * count)
    place = {region: at for at, region in enumerate(ring)}
    origin = np.array(
        [[ring[(place[region] + shift[0]) % count] for shift in sources] for region in range(count)]
    )
    return held, origin


def gathered_projection(proj_weight):
    chans, regions = lax.axis_size("chan"), lax.axis_size("region")
    held = proj_weight.shape[0]
    width = COARSE_WIDTH // chans
    if held % OFFSETS == 0 and chans * held // OFFSETS % 16 == 0:
        each = held // OFFSETS
        me = lax.axis_index("chan")
        mine = exchange(
            lambda distance: lax.dynamic_slice_in_dim(
                proj_weight, (me ^ distance) * width, width, axis=1
            )
        )
        pieces, origin = around(regroup(mine))
        table = np.zeros((chans, regions, len(pieces), chans, each), np.int32)
        for chan in range(chans):
            for distance in range(chans):
                first = (chan ^ distance) * regions + origin
                table[chan, :, :, distance] = first[:, :, None] * each + np.arange(each)
        table = jnp.asarray(table.reshape(chans * regions, FINE_WIDTH))
        device = lax.axis_index("chan") * regions + lax.axis_index("region")
        return pieces, lax.dynamic_index_in_dim(table, device, 0, keepdims=True)
    mine = lax.all_to_all(proj_weight, "chan", split_axis=1, concat_axis=0, tiled=True)
    whole = lax.all_gather(mine.reshape(chans, held, width), "region", axis=1, tiled=True)
    whole = whole.reshape(FINE_WIDTH, OFFSETS, width).transpose(1, 0, 2)
    return [whole], jnp.arange(FINE_WIDTH, dtype=jnp.int32)[None]


def shards(
    latent,
    cond_scale,
    cond_shift,
    fine_weight,
    fine_bias,
    proj_weight,
    proj_bias,
    bottle_weight,
    bottle_bias,
    guide,
):
    chans = lax.axis_size("chan")
    chan_place = lax.axis_index("chan")
    region = lax.axis_index("region")
    width = COARSE_WIDTH // chans
    side = 2 * TILE_SIDE
    count_x = lax.axis_size("region") // (REGIONS_Y * REGIONS_Z)
    steps = (REGIONS_Y * REGIONS_Z, REGIONS_Z, 1)
    counts = (count_x, REGIONS_Y, REGIONS_Z)
    places = [region // step % count for step, count in zip(steps, counts)]
    inside = jnp.stack(
        [
            flag
            for place, count in zip(places, counts)
            for flag in ((place > 0).astype(jnp.float32), (place < count - 1).astype(jnp.float32))
        ]
    )

    columns, channel = gathered_projection(proj_weight)
    order = lax.broadcasted_iota(jnp.int32, (FINE_WIDTH, FINE_WIDTH), 0) == channel

    block = latent[0].transpose(0, 2, 1, 3)
    layer = z_layer(block, 1)
    rows = jnp.concatenate([block, layer], axis=1)
    below = along_y(rows[:, :, -1], 1)
    above = along_y(rows[:, :, 0], -1)
    ends = []
    for at in (0, -1):
        plane = jnp.concatenate(z_ends(layer[at], block[at], 0), axis=0)
        low, high = [
            jnp.concatenate(z_ends(part[at, TILE_SIDE:], part[at, :TILE_SIDE], 0), axis=0)[:, None]
            for part in (below, above)
        ]
        spare = jnp.zeros((TILE_SIDE + 2, 6, FINE_WIDTH), plane.dtype)
        ends.append(jnp.concatenate([plane, high, spare, low], axis=1))
    outer = jnp.stack(x_layers(*ends))

    bias = jnp.sum(jnp.where(order, fine_bias[:, None], 0.0), axis=0)
    windows, taps = make_windows(
        inside,
        block,
        layer[:, 0],
        below,
        above,
        outer,
        cond_scale[None],
        cond_shift[None],
        fine_weight.reshape(27, FINE_WIDTH, FINE_WIDTH),
        order.astype(jnp.bfloat16),
    )
    bias = jnp.concatenate([bias, bias])[None]
    half = STRIDE // 2
    early = convolve(windows, taps, bias, 0, half)
    late = convolve(windows, taps, bias, half, half)
    place = chan_place[None]
    coarse = project(place, early, late, columns, proj_bias[None])

    grid = coarse[:ROWS].reshape(CELLS, 2, ACROSS, ACROSS, width)
    field = with_halos(grid, 2, 3, 0)
    terms = bottle_terms(place, field, bottle_weight.reshape(3, 3, 3, width, COARSE_WIDTH), chans)
    terms = exchange(lambda distance: terms[distance])
    guided = finish(place, guide, terms, bottle_bias[None])
    return guided.reshape(CELLS, ACROSS, ACROSS, width).transpose(1, 2, 0, 3)[None]


def solution(mesh):
    placed = (
        P("region", None, None, None, None),
        P(),
        P(),
        P(),
        P(),
        P(("chan", "region"), None),
        P(),
        P(None, "chan", None),
        P(),
        P(),
    )
    return jax.shard_map(
        shards,
        mesh=mesh,
        in_specs=placed,
        out_specs=P("region", None, None, None, "chan"),
        check_vma=False,
    )
```

```python
import functools

import numpy as np

import jax
import jax.numpy as jnp
from jax import lax
from jax.experimental import pallas as pl
from jax.experimental.pallas import tpu as pltpu
from jax.sharding import PartitionSpec as P

FINE_WIDTH = 128
COARSE_WIDTH = 1024
TILE_SIDE = 12
STRIDE = 4
REGIONS_Y = 4
REGIONS_Z = 2

CELLS = TILE_SIDE // STRIDE
ACROSS = 2 * CELLS
PLANE = 2 * ACROSS * ACROSS
ROWS = CELLS * PLANE
PADDED = -(-ROWS // 16) * 16
PHASES = STRIDE + 2
OFFSETS = STRIDE**3
LANES = 128
SPREAD = 8
MIB = 2**20


def vmem(count):
    return [pl.BlockSpec(memory_space=pltpu.VMEM) for _ in range(count)]


def regroup_kernel(*refs):
    rows_refs, out_ref, wide = refs[:-2], refs[-2], refs[-1]
    held = rows_refs[0].shape[0]
    groups = out_ref.shape[1]
    for lane in range(wide.shape[0]):
        columns = slice(lane * LANES, (lane + 1) * LANES)
        for number, rows_ref in enumerate(rows_refs):
            wide[lane, number * held : (number + 1) * held, :] = rows_ref[:, columns].astype(jnp.float32)
        for offset in range(OFFSETS):
            out_ref[offset, :, columns] = wide[
                lane, pl.ds(offset, groups, stride=OFFSETS), :
            ].astype(jnp.bfloat16)


def regroup(pieces):
    held, width = pieces[0].shape
    total = len(pieces) * held
    return pl.pallas_call(
        regroup_kernel,
        out_shape=jax.ShapeDtypeStruct((OFFSETS, total // OFFSETS, width), jnp.bfloat16),
        in_specs=vmem(len(pieces)),
        out_specs=vmem(1)[0],
        scratch_shapes=[pltpu.VMEM((width // LANES, total, LANES), jnp.float32)],
        compiler_params=pltpu.CompilerParams(vmem_limit_bytes=8 * MIB),
        name="regroup",
    )(*pieces)


def split_kernel(place_ref, rows_ref, *out_refs):
    width = out_refs[0].shape[1]
    for distance, out_ref in enumerate(out_refs):
        start = pl.multiple_of((place_ref[0] ^ distance) * width, width)
        out_ref[...] = rows_ref[:, pl.ds(start, width)]


def split_columns(place, rows, owners):
    held, width = rows.shape[0], rows.shape[1] // owners
    return pl.pallas_call(
        split_kernel,
        out_shape=[jax.ShapeDtypeStruct((held, width), rows.dtype)] * owners,
        in_specs=[pl.BlockSpec(memory_space=pltpu.SMEM)] + vmem(1),
        out_specs=vmem(owners),
        compiler_params=pltpu.CompilerParams(vmem_limit_bytes=4 * MIB),
        name="split_columns",
    )(place, rows)


def faces_kernel(upper_ref, layer_ref, first_ref, last_ref, face_ref, low_ref, high_ref, wide):
    face_ref[...] = layer_ref[:, 0]

    def take(at_x, carry):
        for rows_ref, row, out_ref in ((first_ref, 0, low_ref), (last_ref, 7, high_ref)):
            for at_z in range(TILE_SIDE):
                wide[at_z : at_z + 1, :] = rows_ref[at_x, at_z].astype(jnp.float32)[row : row + 1]
            out_ref[at_x] = wide[...].astype(jnp.bfloat16)
        return carry

    wide[...] = jnp.zeros_like(wide)
    lax.fori_loop(0, layer_ref.shape[0], take, 0)


def faces(upper, block):
    side_x, depth, side_y, width = block.shape
    return pl.pallas_call(
        faces_kernel,
        out_shape=(
            jax.ShapeDtypeStruct((side_x, side_y, width), block.dtype),
            jax.ShapeDtypeStruct((side_x, 16, width), block.dtype),
            jax.ShapeDtypeStruct((side_x, 16, width), block.dtype),
        ),
        grid_spec=pltpu.PrefetchScalarGridSpec(
            num_scalar_prefetch=1,
            grid=(1,),
            in_specs=[
                pl.BlockSpec(
                    (side_x, 1, side_y, width), lambda i, upper: (0, (1 - upper[0]) * (depth - 1), 0, 0)
                ),
                pl.BlockSpec((side_x, depth, 8, width), lambda i, upper: (0, 0, 0, 0)),
                pl.BlockSpec((side_x, depth, 8, width), lambda i, upper: (0, 0, side_y // 8 - 1, 0)),
            ],
            out_specs=(
                pl.BlockSpec((side_x, side_y, width), lambda i, upper: (0, 0, 0)),
                pl.BlockSpec((side_x, 16, width), lambda i, upper: (0, 0, 0)),
                pl.BlockSpec((side_x, 16, width), lambda i, upper: (0, 0, 0)),
            ),
            scratch_shapes=[pltpu.VMEM((16, width), jnp.float32)],
        ),
        compiler_params=pltpu.CompilerParams(vmem_limit_bytes=12 * MIB),
        name="faces",
    )(upper, block, block, block)


def window_kernel(
    inside_ref, block_ref, layer_ref, below_ref, above_ref, outer_ref, scale_ref, shift_ref,
    weight_ref, order_ref, windows_ref, taps_ref, rows, line, layers,
):
    phase_x = pl.program_id(0)
    side, depth, width = 2 * TILE_SIDE, TILE_SIDE, FINE_WIDTH
    half = 2 * ACROSS * side

    @pl.when(phase_x == 0)
    def _():
        zero = jnp.zeros((width, width), jnp.bfloat16)
        for place in range(9):
            taps_ref[place, 3 * width :, :width] = zero
            taps_ref[place, :width, width:] = zero
            for step in range(3):
                block = jnp.dot(
                    weight_ref[place * 3 + step], order_ref[...], preferred_element_type=jnp.float32
                ).astype(jnp.bfloat16)
                taps_ref[place, step * width : (step + 1) * width, :width] = block
                taps_ref[place, (step + 1) * width : (step + 2) * width, width:] = block

        def widen(at_x, carry):
            rows[0, at_x] = below_ref[at_x].astype(jnp.float32)
            rows[1, at_x] = above_ref[at_x].astype(jnp.float32)
            return carry

        lax.fori_loop(0, side, widen, 0)

    scale = jnp.broadcast_to(scale_ref[...], (8, width))
    shift = jnp.broadcast_to(shift_ref[...], (8, width))
    row = lax.broadcasted_iota(jnp.int32, (8, width), 0)
    first = jnp.where(row == 0, shift * inside_ref[2], shift)
    last = jnp.where(row == side + 1 - 20, shift * inside_ref[3], shift)
    chunks = [(0, first), (8, shift), (16, shift), (4, shift), (12, shift), (20, last)]

    def split(cell_x, carry):
        at_x = phase_x + STRIDE * cell_x
        outside = jnp.logical_or(at_x == 0, at_x == side + 1)

        @pl.when(jnp.logical_not(outside))
        def _():
            at = at_x - 1
            for at_z in range(depth + 2):
                if at_z == 0:
                    flag, value, place = inside_ref[4], layer_ref[at], depth
                elif at_z == depth + 1:
                    flag, value, place = inside_ref[5], layer_ref[at], depth
                else:
                    flag, value, place = None, block_ref[at, at_z - 1], at_z - 1
                value = value.astype(jnp.float32)
                low, high = rows[0, at, place : place + 1, :], rows[1, at, place : place + 1, :]
                if flag is not None:
                    value, low, high = value * flag, low * flag, high * flag
                line[at_z, 7:8, :] = low
                line[at_z, 8 : side + 8, :] = value
                line[at_z, side + 8 : side + 9, :] = high

        @pl.when(outside)
        def _():
            end = jnp.where(at_x == 0, 0, 1)
            for at_z in range(depth + 2):
                value = outer_ref[end, at_z].astype(jnp.float32)
                line[at_z, 0:8, :] = value[side : side + 8]
                line[at_z, 8 : side + 8, :] = value[:side]
                line[at_z, side + 8 : side + 16, :] = value[side : side + 8]

        within = jnp.where(at_x == 0, inside_ref[0], 1.0)
        within = jnp.where(at_x == side + 1, inside_ref[1], within)
        for at_z in range(depth + 2):
            if at_z == 0:
                factor = within * inside_ref[4]
            elif at_z == depth + 1:
                factor = within * inside_ref[5]
            else:
                factor = within
            for number, (start, added) in enumerate(chunks):
                value = line[at_z, pl.ds(start + 7, 8), :]
                base = number // 3 * half + number % 3 * 8
                base = pl.multiple_of(base + cell_x * side, 8)
                layers[at_z, pl.ds(base, 8), :] = value
                layers[at_z, pl.ds(base + half // 2, 8), :] = value * scale + added * factor
        return carry

    lax.fori_loop(0, ACROSS, split, 0)
    for phase_y in range(PHASES):
        start = phase_y if phase_y < STRIDE else half + phase_y - STRIDE
        for phase_z in range(PHASES):
            parts = [
                layers[phase_z + STRIDE * cell, pl.ds(start, PLANE, stride=STRIDE), :]
                for cell in range(CELLS)
            ]
            parts.append(jnp.zeros((PADDED - ROWS, width), jnp.float32))
            windows_ref[0, phase_y, :, phase_z * width : (phase_z + 1) * width] = jnp.concatenate(
                parts, axis=0
            ).astype(jnp.bfloat16)


def make_windows(inside, *arrays):
    width, side = FINE_WIDTH, 2 * TILE_SIDE

    def whole(array):
        return pl.BlockSpec(array.shape, lambda i: (0,) * array.ndim)

    return pl.pallas_call(
        window_kernel,
        out_shape=(
            jax.ShapeDtypeStruct((PHASES, PHASES, PADDED, PHASES * width), jnp.bfloat16),
            jax.ShapeDtypeStruct((9, 4 * width, 2 * width), jnp.bfloat16),
        ),
        grid=(PHASES,),
        in_specs=[pl.BlockSpec(memory_space=pltpu.SMEM)] + [whole(array) for array in arrays],
        out_specs=(
            pl.BlockSpec((1, PHASES, PADDED, PHASES * width), lambda i: (i, 0, 0, 0)),
            pl.BlockSpec((9, 4 * width, 2 * width), lambda i: (0, 0, 0)),
        ),
        scratch_shapes=[
            pltpu.VMEM((2, side, 16, width), jnp.float32),
            pltpu.VMEM((TILE_SIDE + 2, side + 16, width), jnp.float32),
            pltpu.VMEM((TILE_SIDE + 2, 4 * ACROSS * side, width), jnp.float32),
        ],
        compiler_params=pltpu.CompilerParams(vmem_limit_bytes=28 * MIB),
        cost_estimate=pl.CostEstimate(flops=10**10, bytes_accessed=16 * MIB, transcendentals=0),
        name="windows",
    )(inside, *arrays)


def convolve_kernel(first_ref, second_ref, third_ref, taps_ref, bias_ref, out_ref):
    width = FINE_WIDTH
    bias = bias_ref[...]

    def convolve(at_y, carry):
        total = jnp.zeros((2 * PADDED, 2 * width), jnp.float32)
        for step_x, windows_ref in enumerate((first_ref, second_ref, third_ref)):
            for step_y in range(3):
                taken = [
                    windows_ref[0, at_y + step_y, :, pair * 2 * width : (pair * 2 + 4) * width]
                    for pair in range(2)
                ]
                total += jnp.dot(
                    jnp.concatenate(taken, axis=0),
                    taps_ref[step_x * 3 + step_y],
                    preferred_element_type=jnp.float32,
                )
        total = total + bias
        hidden = (total / (1.0 + jnp.exp(-total))).astype(jnp.bfloat16)
        for pair in range(2):
            out_ref[at_y * 2 + pair] = hidden[pair * PADDED : (pair + 1) * PADDED]
        return carry

    lax.fori_loop(0, STRIDE, convolve, 0)


def convolve(windows, taps, bias, start, count):
    width = FINE_WIDTH
    each = STRIDE * STRIDE // 2
    block = (1, PHASES, PADDED, PHASES * width)
    return pl.pallas_call(
        convolve_kernel,
        out_shape=jax.ShapeDtypeStruct((count * each, PADDED, 2 * width), jnp.bfloat16),
        grid=(count,),
        in_specs=[
            pl.BlockSpec(block, lambda i, step=step: (i + start + step, 0, 0, 0)) for step in range(3)
        ]
        + [
            pl.BlockSpec(taps.shape, lambda i: (0, 0, 0)),
            pl.BlockSpec(bias.shape, lambda i: (0, 0)),
        ],
        out_specs=pl.BlockSpec((each, PADDED, 2 * width), lambda i: (i, 0, 0)),
        compiler_params=pltpu.CompilerParams(vmem_limit_bytes=28 * MIB),
        cost_estimate=pl.CostEstimate(
            flops=2 * count * each * PADDED * 36 * width * 2 * width,
            bytes_accessed=16 * MIB,
            transcendentals=count * each * PADDED * 2 * width,
        ),
        name="convolve",
    )(windows, windows, windows, taps, bias)


def project_kernel(split, place_ref, early_ref, late_ref, *refs):
    weight_refs, bias_ref, out_ref, total = refs[:-3], refs[-3], refs[-2], refs[-1]
    step = pl.program_id(0)
    width = out_ref.shape[1]

    def product(hidden_ref, number):
        used = weight_refs[:-2] + (weight_refs[len(weight_refs) - 2 + number],) if split else weight_refs
        acc = jnp.zeros(total.shape, jnp.float32)
        for pair in range(hidden_ref.shape[0]):
            weight = jnp.concatenate(
                [ref[2 * pair + item] for item in range(2) for ref in used], axis=0
            )
            acc += jnp.dot(hidden_ref[pair], weight, preferred_element_type=jnp.float32)
        return acc

    @pl.when(step == 0)
    def _():
        total[...] = product(early_ref, 0)

    @pl.when(step == 1)
    def _():
        start = pl.multiple_of(place_ref[0] * width, width)
        out_ref[...] = (total[...] + product(late_ref, 1) + bias_ref[:, pl.ds(start, width)]).astype(
            jnp.bfloat16
        )


def project(place, early, late, weights, split, bias):
    pairs, rows, depth = early.shape
    width = weights[0].shape[2]
    return pl.pallas_call(
        functools.partial(project_kernel, split),
        out_shape=jax.ShapeDtypeStruct((rows, width), jnp.bfloat16),
        grid=(2,),
        in_specs=[
            pl.BlockSpec(memory_space=pltpu.SMEM),
            pl.BlockSpec(early.shape, lambda i: (0, 0, 0)),
            pl.BlockSpec(late.shape, lambda i: (0, 0, 0)),
        ]
        + [
            pl.BlockSpec(
                (OFFSETS // 2,) + weight.shape[1:],
                (lambda i: (i, 0, 0)) if weight.shape[0] == OFFSETS else (lambda i: (0, 0, 0)),
            )
            for weight in weights
        ]
        + [pl.BlockSpec(bias.shape, lambda i: (0, 0))],
        out_specs=pl.BlockSpec((rows, width), lambda i: (0, 0)),
        scratch_shapes=[pltpu.VMEM((rows, width), jnp.float32)],
        compiler_params=pltpu.CompilerParams(vmem_limit_bytes=24 * MIB),
        cost_estimate=pl.CostEstimate(
            flops=4 * pairs * rows * depth * width, bytes_accessed=8 * MIB, transcendentals=0
        ),
        name="project",
    )(place, early, late, *weights, bias)


def bottle_kernel(place_ref, field_ref, weight_ref, own_ref, *refs):
    other_refs, total, packed, dense = refs[:-3], refs[-3], refs[-2], refs[-1]
    step_y = pl.program_id(0)
    width = field_ref.shape[4]
    share = own_ref.shape[1]
    frame = ACROSS + 2
    rows = CELLS * 2 * ACROSS * frame
    chunk = weight_ref.shape[4]

    @pl.when(jnp.logical_and(step_y == 0, pl.program_id(1) == 0))
    def _():
        for step_x in range(3):
            for step_z in range(3):
                place = step_x * 3 + step_z
                packed[:, place * width : (place + 1) * width] = (
                    field_ref[step_z : step_z + CELLS, :, step_x : step_x + ACROSS]
                    .astype(jnp.float32)
                    .reshape(rows, width)
                    .astype(jnp.bfloat16)
                )

    start = pl.multiple_of(pl.program_id(1) * chunk, chunk)
    total[step_y, :, pl.ds(start, chunk)] = jnp.dot(
        packed[...],
        weight_ref[...].reshape(9 * width, chunk),
        preferred_element_type=jnp.float32,
    )

    @pl.when(jnp.logical_and(step_y == 2, pl.program_id(1) == pl.num_programs(1) - 1))
    def _():
        for distance, out_ref in enumerate((own_ref,) + other_refs):
            start = pl.multiple_of((place_ref[0] ^ distance) * share, share)
            for group in range(rows // frame):
                at = group * frame
                dense[group * ACROSS : (group + 1) * ACROSS, :] = sum(
                    total[item, at + item : at + item + ACROSS, pl.ds(start, share)]
                    for item in range(3)
                )
            out_ref[...] = dense[...].astype(out_ref.dtype)


def bottle_terms(place, field, weight, owners):
    frame = ACROSS + 2
    rows = CELLS * 2 * ACROSS * frame
    width = weight.shape[3]
    share = COARSE_WIDTH // owners
    chunk = 256
    return pl.pallas_call(
        bottle_kernel,
        out_shape=[
            jax.ShapeDtypeStruct((ROWS, share), jnp.bfloat16 if distance else jnp.float32)
            for distance in range(owners)
        ],
        grid=(3, COARSE_WIDTH // chunk),
        in_specs=[
            pl.BlockSpec(memory_space=pltpu.SMEM),
            pl.BlockSpec(field.shape, lambda i, j: (0, 0, 0, 0, 0)),
            pl.BlockSpec((3, 1, 3, width, chunk), lambda i, j: (0, i, 0, 0, j)),
        ],
        out_specs=[pl.BlockSpec((ROWS, share), lambda i, j: (0, 0))] * owners,
        scratch_shapes=[
            pltpu.VMEM((3, rows, COARSE_WIDTH), jnp.float32),
            pltpu.VMEM((rows, 9 * width), jnp.bfloat16),
            pltpu.VMEM((ROWS, share), jnp.float32),
        ],
        compiler_params=pltpu.CompilerParams(vmem_limit_bytes=52 * MIB),
        cost_estimate=pl.CostEstimate(
            flops=2 * rows * 27 * width * COARSE_WIDTH, bytes_accessed=16 * MIB, transcendentals=0
        ),
        name="bottle_terms",
    )(place, field, weight)


def finish_kernel(place_ref, guide_ref, own_ref, *refs):
    other_refs, bias_ref, out_ref, spread = refs[:-3], refs[-3], refs[-2], refs[-1]
    share = own_ref.shape[1]
    start = pl.multiple_of(place_ref[0] * share, share)
    value = own_ref[...] + bias_ref[:, pl.ds(start, share)]
    for other_ref in other_refs:
        value = value + other_ref[...].astype(jnp.float32)
    value = value / (1.0 + jnp.exp(-value))
    half = PLANE // 2
    for cell in range(CELLS):
        plain = value[cell * PLANE : cell * PLANE + half]
        guided = value[cell * PLANE + half : (cell + 1) * PLANE]
        mixed = plain + guide_ref[0] * (guided - plain)
        for lane in range(spread.shape[0]):
            spread[lane, pl.ds(cell, half, stride=SPREAD), :] = mixed[:, lane * LANES : (lane + 1) * LANES]
    for lane in range(spread.shape[0]):
        for cell in range(half):
            out_ref[cell, :, lane * LANES : (lane + 1) * LANES] = spread[
                lane, cell * SPREAD : cell * SPREAD + CELLS, :
            ].astype(jnp.bfloat16)


def finish(place, guide, terms, bias):
    share = terms[0].shape[1]
    return pl.pallas_call(
        finish_kernel,
        out_shape=jax.ShapeDtypeStruct((PLANE // 2, CELLS, share), jnp.bfloat16),
        in_specs=[pl.BlockSpec(memory_space=pltpu.SMEM)] * 2 + vmem(len(terms) + 1),
        out_specs=vmem(1)[0],
        scratch_shapes=[pltpu.VMEM((share // LANES, PLANE // 2 * SPREAD, LANES), jnp.float32)],
        compiler_params=pltpu.CompilerParams(vmem_limit_bytes=8 * MIB),
        name="finish",
    )(place, guide, *terms, bias)


def passed(value, steps):
    count = lax.axis_size("region")
    return lax.ppermute(
        value, "region", [(at, at + steps) for at in range(max(0, -steps), min(count, count - steps))]
    )


def across_z(value):
    count = lax.axis_size("region")
    return lax.ppermute(value, "region", [(at, at ^ 1) for at in range(count)])


def along_y(value, steps):
    count = lax.axis_size("region")
    pairs = [
        (at, at + steps * REGIONS_Z)
        for at in range(count)
        if 0 <= at // REGIONS_Z % REGIONS_Y + steps < REGIONS_Y
    ]
    return lax.ppermute(value, "region", pairs)


def with_halos(value, dim_x, dim_y, dim_z):
    value = jnp.concatenate(z_ends(z_layer(value, dim_z), value, dim_z), axis=dim_z)
    value = jnp.concatenate(
        [along_y(edge(value, dim_y, True), 1), value, along_y(edge(value, dim_y, False), -1)],
        axis=dim_y,
    )
    low, high = x_layers(edge(value, dim_x, False), edge(value, dim_x, True))
    return jnp.concatenate([low, value, high], axis=dim_x)


def edge(array, dim, last):
    size = array.shape[dim]
    return lax.slice_in_dim(array, size - 1 if last else 0, size if last else 1, axis=dim)


def is_upper():
    return lax.axis_index("region") % REGIONS_Z == 1


def z_layer(value, dim):
    return across_z(jnp.where(is_upper(), edge(value, dim, False), edge(value, dim, True)))


def z_ends(layer, value, dim):
    zero = jnp.zeros_like(layer)
    return [jnp.where(is_upper(), layer, zero), value, jnp.where(is_upper(), zero, layer)]


def x_layers(first, last):
    count = lax.axis_size("region") // (REGIONS_Y * REGIONS_Z)
    if count == 1:
        return jnp.zeros_like(last), jnp.zeros_like(first)
    return passed(last, REGIONS_Y * REGIONS_Z), passed(first, -REGIONS_Y * REGIONS_Z)


def exchange(piece_at):
    chans = lax.axis_size("chan")
    return [piece_at(0)] + [
        lax.ppermute(piece_at(distance), "chan", [(at, at ^ distance) for at in range(chans)])
        for distance in range(1, chans)
    ]


def ring_of(count):
    return list(range(0, count, 2)) + list(range(1, count, 2))[::-1]


def hop(value, ahead):
    ring = ring_of(lax.axis_size("region"))
    following = ring[1:] + ring[:1]
    return lax.ppermute(value, "region", list(zip(ring, following) if ahead else zip(following, ring)))


def after(value, other):
    return lax.optimization_barrier((value, other))[0]


def piece_channels(each):
    chans, regions = lax.axis_size("chan"), lax.axis_size("region")
    ring = ring_of(regions)
    shifts = [0]
    for step in range(1, regions // 2 + 1):
        shifts += [-step] + [step] * (step < regions // 2)
    origin = np.array(
        [[ring[(ring.index(region) + shift) % regions] for shift in shifts] for region in range(regions)]
    )
    table = np.zeros((chans, regions, regions, chans, each), np.int32)
    for chan in range(chans):
        for distance in range(chans):
            first = (chan ^ distance) * regions + origin
            table[chan, :, :, distance] = first[:, :, None] * each + np.arange(each)
    table = jnp.asarray(table.reshape(chans * regions, FINE_WIDTH))
    device = lax.axis_index("chan") * regions + lax.axis_index("region")
    return lax.dynamic_index_in_dim(table, device, 0, keepdims=True)


def ring_pieces(piece, milestones):
    regions = lax.axis_size("region")
    forward = backward = piece
    held = [piece]
    for step in range(1, regions // 2 + 1):
        if step > 1 and step - 2 < len(milestones):
            forward, backward = (after(value, milestones[step - 2]) for value in (forward, backward))
        if step == regions // 2:
            held += [hop(forward[: OFFSETS // 2], True), hop(backward[OFFSETS // 2 :], False)]
        else:
            forward, backward = hop(forward, True), hop(backward, False)
            held += [forward, backward]
    return held


def whole_columns(proj_weight):
    chans, held = lax.axis_size("chan"), proj_weight.shape[0]
    width = COARSE_WIDTH // chans
    mine = lax.all_to_all(proj_weight, "chan", split_axis=1, concat_axis=0, tiled=True)
    whole = lax.all_gather(mine.reshape(chans, held, width), "region", axis=1, tiled=True)
    return whole.reshape(FINE_WIDTH, OFFSETS, width).transpose(1, 0, 2)


def shards(
    latent,
    cond_scale,
    cond_shift,
    fine_weight,
    fine_bias,
    proj_weight,
    proj_bias,
    bottle_weight,
    bottle_bias,
    guide,
):
    chans = lax.axis_size("chan")
    chan_place = lax.axis_index("chan")
    region = lax.axis_index("region")
    width = COARSE_WIDTH // chans
    side = 2 * TILE_SIDE
    count_x = lax.axis_size("region") // (REGIONS_Y * REGIONS_Z)
    steps = (REGIONS_Y * REGIONS_Z, REGIONS_Z, 1)
    counts = (count_x, REGIONS_Y, REGIONS_Z)
    places = [region // step % count for step, count in zip(steps, counts)]
    inside = jnp.stack(
        [
            flag
            for place, count in zip(places, counts)
            for flag in ((place > 0).astype(jnp.float32), (place < count - 1).astype(jnp.float32))
        ]
    )

    place = chan_place[None]
    each, rest = divmod(proj_weight.shape[0], OFFSETS)
    by_ring = rest == 0 and chans * each % 16 == 0
    if by_ring:
        mine = split_columns(place, proj_weight, chans)
        piece = regroup(exchange(lambda distance: mine[distance]))
        channel = piece_channels(each)
    else:
        channel = jnp.arange(FINE_WIDTH, dtype=jnp.int32)[None]
    order = lax.broadcasted_iota(jnp.int32, (FINE_WIDTH, FINE_WIDTH), 0) == channel

    block = latent[0].transpose(0, 2, 1, 3)
    face, first, last = faces(is_upper().astype(jnp.int32)[None], block)
    layer = across_z(face)
    corner = lax.broadcasted_iota(jnp.int32, first.shape, 1) == TILE_SIDE
    below = along_y(jnp.where(corner, layer[:, -1:], last), 1)
    above = along_y(jnp.where(corner, layer[:, :1], first), -1)
    ends = []
    for at in (0, -1):
        plane = jnp.concatenate(z_ends(layer[at][None], block[at], 0), axis=0)
        low, high = [
            jnp.concatenate(
                z_ends(part[at, TILE_SIDE : TILE_SIDE + 1], part[at, :TILE_SIDE], 0), axis=0
            )[:, None]
            for part in (below, above)
        ]
        spare = jnp.zeros((TILE_SIDE + 2, 6, FINE_WIDTH), plane.dtype)
        ends.append(jnp.concatenate([plane, high, spare, low], axis=1))
    outer = jnp.stack(x_layers(*ends))

    bias = jnp.sum(jnp.where(order, fine_bias[:, None], 0.0), axis=0)
    windows, taps = make_windows(
        inside,
        block,
        layer,
        below,
        above,
        outer,
        cond_scale[None],
        cond_shift[None],
        fine_weight.reshape(27, FINE_WIDTH, FINE_WIDTH),
        order.astype(jnp.bfloat16),
    )
    bias = jnp.concatenate([bias, bias])[None]
    half = STRIDE // 2
    early = convolve(windows, taps, bias, 0, half)
    late = convolve(windows, taps, bias, half, half)
    columns = ring_pieces(piece, [taps, early, late]) if by_ring else [whole_columns(proj_weight)]
    coarse = project(place, early, late, columns, by_ring, proj_bias[None])

    grid = coarse[:ROWS].reshape(CELLS, 2, ACROSS, ACROSS, width)
    field = with_halos(grid, 2, 3, 0)
    terms = bottle_terms(place, field, bottle_weight.reshape(3, 3, 3, width, COARSE_WIDTH), chans)
    terms = exchange(lambda distance: terms[distance])
    guided = finish(place, guide, terms, bottle_bias[None])
    return guided.reshape(1, ACROSS, ACROSS, CELLS, width)


def solution(mesh):
    placed = (
        P("region", None, None, None, None),
        P(),
        P(),
        P(),
        P(),
        P(("chan", "region"), None),
        P(),
        P(None, "chan", None),
        P(),
        P(),
    )
    return jax.shard_map(
        shards,
        mesh=mesh,
        in_specs=placed,
        out_specs=P("region", None, None, None, "chan"),
        check_vma=False,
    )
```

```python
import functools

import numpy as np

import jax
import jax.numpy as jnp
from jax import lax
from jax.experimental import pallas as pl
from jax.experimental.pallas import tpu as pltpu
from jax.sharding import PartitionSpec as P

FINE_WIDTH = 128
COARSE_WIDTH = 1024
TILE_SIDE = 12
STRIDE = 4
REGIONS_Y = 4
REGIONS_Z = 2

CELLS = TILE_SIDE // STRIDE
ACROSS = 2 * CELLS
PLANE = 2 * ACROSS * ACROSS
ROWS = CELLS * PLANE
PADDED = -(-ROWS // 16) * 16
PHASES = STRIDE + 2
OFFSETS = STRIDE**3
LANES = 128
SPREAD = 8
MIB = 2**20


def vmem(count):
    return [pl.BlockSpec(memory_space=pltpu.VMEM) for _ in range(count)]


def regroup_kernel(*refs):
    rows_refs, out_ref, wide = refs[:-2], refs[-2], refs[-1]
    held = rows_refs[0].shape[0]
    groups = out_ref.shape[1]
    for lane in range(wide.shape[0]):
        columns = slice(lane * LANES, (lane + 1) * LANES)
        for number, rows_ref in enumerate(rows_refs):
            wide[lane, number * held : (number + 1) * held, :] = rows_ref[:, columns].astype(jnp.float32)
        for offset in range(OFFSETS):
            out_ref[offset, :, columns] = wide[
                lane, pl.ds(offset, groups, stride=OFFSETS), :
            ].astype(jnp.bfloat16)


def regroup(pieces):
    held, width = pieces[0].shape
    total = len(pieces) * held
    return pl.pallas_call(
        regroup_kernel,
        out_shape=jax.ShapeDtypeStruct((OFFSETS, total // OFFSETS, width), jnp.bfloat16),
        in_specs=vmem(len(pieces)),
        out_specs=vmem(1)[0],
        scratch_shapes=[pltpu.VMEM((width // LANES, total, LANES), jnp.float32)],
        compiler_params=pltpu.CompilerParams(vmem_limit_bytes=8 * MIB),
        name="regroup",
    )(*pieces)


def split_kernel(place_ref, rows_ref, *out_refs):
    width = out_refs[0].shape[1]
    for distance, out_ref in enumerate(out_refs):
        start = pl.multiple_of((place_ref[0] ^ distance) * width, width)
        out_ref[...] = rows_ref[:, pl.ds(start, width)]


def split_columns(place, rows, owners):
    held, width = rows.shape[0], rows.shape[1] // owners
    return pl.pallas_call(
        split_kernel,
        out_shape=[jax.ShapeDtypeStruct((held, width), rows.dtype)] * owners,
        in_specs=[pl.BlockSpec(memory_space=pltpu.SMEM)] + vmem(1),
        out_specs=vmem(owners),
        compiler_params=pltpu.CompilerParams(vmem_limit_bytes=4 * MIB),
        name="split_columns",
    )(place, rows)


def faces_kernel(upper_ref, layer_ref, first_ref, last_ref, face_ref, low_ref, high_ref, wide):
    face_ref[...] = layer_ref[:, 0]

    def take(at_x, carry):
        for rows_ref, row, out_ref in ((first_ref, 0, low_ref), (last_ref, 7, high_ref)):
            for at_z in range(TILE_SIDE):
                wide[at_z : at_z + 1, :] = rows_ref[at_x, at_z].astype(jnp.float32)[row : row + 1]
            out_ref[at_x] = wide[...].astype(jnp.bfloat16)
        return carry

    wide[...] = jnp.zeros_like(wide)
    lax.fori_loop(0, layer_ref.shape[0], take, 0)


def faces(upper, block):
    side_x, depth, side_y, width = block.shape
    return pl.pallas_call(
        faces_kernel,
        out_shape=(
            jax.ShapeDtypeStruct((side_x, side_y, width), block.dtype),
            jax.ShapeDtypeStruct((side_x, 16, width), block.dtype),
            jax.ShapeDtypeStruct((side_x, 16, width), block.dtype),
        ),
        grid_spec=pltpu.PrefetchScalarGridSpec(
            num_scalar_prefetch=1,
            grid=(1,),
            in_specs=[
                pl.BlockSpec(
                    (side_x, 1, side_y, width), lambda i, upper: (0, (1 - upper[0]) * (depth - 1), 0, 0)
                ),
                pl.BlockSpec((side_x, depth, 8, width), lambda i, upper: (0, 0, 0, 0)),
                pl.BlockSpec((side_x, depth, 8, width), lambda i, upper: (0, 0, side_y // 8 - 1, 0)),
            ],
            out_specs=(
                pl.BlockSpec((side_x, side_y, width), lambda i, upper: (0, 0, 0)),
                pl.BlockSpec((side_x, 16, width), lambda i, upper: (0, 0, 0)),
                pl.BlockSpec((side_x, 16, width), lambda i, upper: (0, 0, 0)),
            ),
            scratch_shapes=[pltpu.VMEM((16, width), jnp.float32)],
        ),
        compiler_params=pltpu.CompilerParams(vmem_limit_bytes=54 * MIB),
        name="faces",
    )(upper, block, block, block)


def window_kernel(
    inside_ref, block_ref, layer_ref, below_ref, above_ref, outer_ref, scale_ref, shift_ref,
    weight_ref, order_ref, windows_ref, taps_ref, rows, line, layers,
):
    phase_x = pl.program_id(0)
    side, depth, width = 2 * TILE_SIDE, TILE_SIDE, FINE_WIDTH
    half = 2 * ACROSS * side

    @pl.when(phase_x == 0)
    def _():
        zero = jnp.zeros((width, width), jnp.bfloat16)
        for place in range(9):
            taps_ref[place, 3 * width :, :width] = zero
            taps_ref[place, :width, width:] = zero
            for step in range(3):
                block = jnp.dot(
                    weight_ref[place * 3 + step], order_ref[...], preferred_element_type=jnp.float32
                ).astype(jnp.bfloat16)
                taps_ref[place, step * width : (step + 1) * width, :width] = block
                taps_ref[place, (step + 1) * width : (step + 2) * width, width:] = block

        def widen(at_x, carry):
            rows[0, at_x] = below_ref[at_x].astype(jnp.float32)
            rows[1, at_x] = above_ref[at_x].astype(jnp.float32)
            return carry

        lax.fori_loop(0, side, widen, 0)

    scale = jnp.broadcast_to(scale_ref[...], (8, width))
    shift = jnp.broadcast_to(shift_ref[...], (8, width))
    row = lax.broadcasted_iota(jnp.int32, (8, width), 0)
    first = jnp.where(row == 0, shift * inside_ref[2], shift)
    last = jnp.where(row == side + 1 - 20, shift * inside_ref[3], shift)
    chunks = [(0, first), (8, shift), (16, shift), (4, shift), (12, shift), (20, last)]

    def split(cell_x, carry):
        at_x = phase_x + STRIDE * cell_x
        outside = jnp.logical_or(at_x == 0, at_x == side + 1)

        @pl.when(jnp.logical_not(outside))
        def _():
            at = at_x - 1
            for at_z in range(depth + 2):
                if at_z == 0:
                    flag, value, place = inside_ref[4], layer_ref[at], depth
                elif at_z == depth + 1:
                    flag, value, place = inside_ref[5], layer_ref[at], depth
                else:
                    flag, value, place = None, block_ref[at, at_z - 1], at_z - 1
                value = value.astype(jnp.float32)
                low, high = rows[0, at, place : place + 1, :], rows[1, at, place : place + 1, :]
                if flag is not None:
                    value, low, high = value * flag, low * flag, high * flag
                line[at_z, 7:8, :] = low
                line[at_z, 8 : side + 8, :] = value
                line[at_z, side + 8 : side + 9, :] = high

        @pl.when(outside)
        def _():
            end = jnp.where(at_x == 0, 0, 1)
            for at_z in range(depth + 2):
                value = outer_ref[end, at_z].astype(jnp.float32)
                line[at_z, 0:8, :] = value[side : side + 8]
                line[at_z, 8 : side + 8, :] = value[:side]
                line[at_z, side + 8 : side + 16, :] = value[side : side + 8]

        within = jnp.where(at_x == 0, inside_ref[0], 1.0)
        within = jnp.where(at_x == side + 1, inside_ref[1], within)
        for at_z in range(depth + 2):
            if at_z == 0:
                factor = within * inside_ref[4]
            elif at_z == depth + 1:
                factor = within * inside_ref[5]
            else:
                factor = within
            for number, (start, added) in enumerate(chunks):
                value = line[at_z, pl.ds(start + 7, 8), :]
                base = number // 3 * half + number % 3 * 8
                base = pl.multiple_of(base + cell_x * side, 8)
                layers[at_z, pl.ds(base, 8), :] = value
                layers[at_z, pl.ds(base + half // 2, 8), :] = value * scale + added * factor
        return carry

    lax.fori_loop(0, ACROSS, split, 0)
    for phase_y in range(PHASES):
        start = phase_y if phase_y < STRIDE else half + phase_y - STRIDE
        for phase_z in range(PHASES):
            parts = [
                layers[phase_z + STRIDE * cell, pl.ds(start, PLANE, stride=STRIDE), :]
                for cell in range(CELLS)
            ]
            parts.append(jnp.zeros((PADDED - ROWS, width), jnp.float32))
            windows_ref[0, phase_y, :, phase_z * width : (phase_z + 1) * width] = jnp.concatenate(
                parts, axis=0
            ).astype(jnp.bfloat16)


def make_windows(inside, *arrays):
    width, side = FINE_WIDTH, 2 * TILE_SIDE

    def whole(array):
        return pl.BlockSpec(array.shape, lambda i: (0,) * array.ndim)

    return pl.pallas_call(
        window_kernel,
        out_shape=(
            jax.ShapeDtypeStruct((PHASES, PHASES, PADDED, PHASES * width), jnp.bfloat16),
            jax.ShapeDtypeStruct((9, 4 * width, 2 * width), jnp.bfloat16),
        ),
        grid=(PHASES,),
        in_specs=[pl.BlockSpec(memory_space=pltpu.SMEM)] + [whole(array) for array in arrays],
        out_specs=(
            pl.BlockSpec((1, PHASES, PADDED, PHASES * width), lambda i: (i, 0, 0, 0)),
            pl.BlockSpec((9, 4 * width, 2 * width), lambda i: (0, 0, 0)),
        ),
        scratch_shapes=[
            pltpu.VMEM((2, side, 16, width), jnp.float32),
            pltpu.VMEM((TILE_SIDE + 2, side + 16, width), jnp.float32),
            pltpu.VMEM((TILE_SIDE + 2, 4 * ACROSS * side, width), jnp.float32),
        ],
        compiler_params=pltpu.CompilerParams(vmem_limit_bytes=28 * MIB),
        cost_estimate=pl.CostEstimate(flops=10**8, bytes_accessed=MIB, transcendentals=0),
        name="windows",
    )(inside, *arrays)


def convolve_kernel(first_ref, second_ref, third_ref, taps_ref, bias_ref, out_ref):
    width = FINE_WIDTH
    bias = bias_ref[...]

    def convolve(at_y, carry):
        total = jnp.zeros((2 * PADDED, 2 * width), jnp.float32)
        for step_x, windows_ref in enumerate((first_ref, second_ref, third_ref)):
            for step_y in range(3):
                taken = [
                    windows_ref[0, at_y + step_y, :, pair * 2 * width : (pair * 2 + 4) * width]
                    for pair in range(2)
                ]
                total += jnp.dot(
                    jnp.concatenate(taken, axis=0),
                    taps_ref[step_x * 3 + step_y],
                    preferred_element_type=jnp.float32,
                )
        total = total + bias
        hidden = (total / (1.0 + jnp.exp(-total))).astype(jnp.bfloat16)
        for pair in range(2):
            out_ref[at_y * 2 + pair] = hidden[pair * PADDED : (pair + 1) * PADDED]
        return carry

    lax.fori_loop(0, STRIDE, convolve, 0)


def convolve(windows, taps, bias, start, count):
    width = FINE_WIDTH
    each = STRIDE * STRIDE // 2
    block = (1, PHASES, PADDED, PHASES * width)
    return pl.pallas_call(
        convolve_kernel,
        out_shape=jax.ShapeDtypeStruct((count * each, PADDED, 2 * width), jnp.bfloat16),
        grid=(count,),
        in_specs=[
            pl.BlockSpec(block, lambda i, step=step: (i + start + step, 0, 0, 0)) for step in range(3)
        ]
        + [
            pl.BlockSpec(taps.shape, lambda i: (0, 0, 0)),
            pl.BlockSpec(bias.shape, lambda i: (0, 0)),
        ],
        out_specs=pl.BlockSpec((each, PADDED, 2 * width), lambda i: (i, 0, 0)),
        compiler_params=pltpu.CompilerParams(vmem_limit_bytes=28 * MIB),
        cost_estimate=pl.CostEstimate(
            flops=2 * count * each * PADDED * 36 * width * 2 * width,
            bytes_accessed=16 * MIB,
            transcendentals=count * each * PADDED * 2 * width,
        ),
        name="convolve",
    )(windows, windows, windows, taps, bias)


def project_kernel(split, place_ref, early_ref, late_ref, *refs):
    weight_refs, bias_ref, out_ref, total = refs[:-3], refs[-3], refs[-2], refs[-1]
    step = pl.program_id(0)
    width = out_ref.shape[1]

    def product(hidden_ref, number):
        used = weight_refs[:-2] + (weight_refs[len(weight_refs) - 2 + number],) if split else weight_refs
        acc = jnp.zeros(total.shape, jnp.float32)
        for pair in range(hidden_ref.shape[0]):
            weight = jnp.concatenate(
                [ref[2 * pair + item] for item in range(2) for ref in used], axis=0
            )
            acc += jnp.dot(hidden_ref[pair], weight, preferred_element_type=jnp.float32)
        return acc

    @pl.when(step == 0)
    def _():
        total[...] = product(early_ref, 0)

    @pl.when(step == 1)
    def _():
        start = pl.multiple_of(place_ref[0] * width, width)
        out_ref[...] = (total[...] + product(late_ref, 1) + bias_ref[:, pl.ds(start, width)]).astype(
            jnp.bfloat16
        )


def project(place, early, late, weights, split, bias):
    pairs, rows, depth = early.shape
    width = weights[0].shape[2]
    return pl.pallas_call(
        functools.partial(project_kernel, split),
        out_shape=jax.ShapeDtypeStruct((rows, width), jnp.bfloat16),
        grid=(2,),
        in_specs=[
            pl.BlockSpec(memory_space=pltpu.SMEM),
            pl.BlockSpec(early.shape, lambda i: (0, 0, 0)),
            pl.BlockSpec(late.shape, lambda i: (0, 0, 0)),
        ]
        + [
            pl.BlockSpec(
                (OFFSETS // 2,) + weight.shape[1:],
                (lambda i: (i, 0, 0)) if weight.shape[0] == OFFSETS else (lambda i: (0, 0, 0)),
            )
            for weight in weights
        ]
        + [pl.BlockSpec(bias.shape, lambda i: (0, 0))],
        out_specs=pl.BlockSpec((rows, width), lambda i: (0, 0)),
        scratch_shapes=[pltpu.VMEM((rows, width), jnp.float32)],
        compiler_params=pltpu.CompilerParams(vmem_limit_bytes=24 * MIB),
        cost_estimate=pl.CostEstimate(
            flops=4 * pairs * rows * depth * width, bytes_accessed=8 * MIB, transcendentals=0
        ),
        name="project",
    )(place, early, late, *weights, bias)


def bottle_kernel(place_ref, field_ref, weight_ref, own_ref, *refs):
    other_refs, total, packed, dense = refs[:-3], refs[-3], refs[-2], refs[-1]
    step = pl.program_id(0)
    step_x, step_y = step // 3, step % 3
    width = field_ref.shape[4]
    share = own_ref.shape[1]
    frame = ACROSS + 2
    rows = CELLS * 2 * ACROSS * frame

    @pl.when(step_y == 0)
    def _():
        for step_z in range(3):
            packed[:, step_z * width : (step_z + 1) * width] = (
                field_ref[step_z : step_z + CELLS, :, pl.ds(step_x, ACROSS)]
                .astype(jnp.float32)
                .reshape(rows, width)
                .astype(jnp.bfloat16)
            )

    terms = jnp.dot(
        packed[...],
        weight_ref[...].reshape(3 * width, COARSE_WIDTH),
        preferred_element_type=jnp.float32,
    )

    @pl.when(step_x == 0)
    def _():
        total[step_y] = terms

    @pl.when(step_x > 0)
    def _():
        total[step_y] += terms

    @pl.when(step == 8)
    def _():
        for distance, out_ref in enumerate((own_ref,) + other_refs):
            start = pl.multiple_of((place_ref[0] ^ distance) * share, share)
            for group in range(rows // frame):
                at = group * frame
                dense[group * ACROSS : (group + 1) * ACROSS, :] = sum(
                    total[item, at + item : at + item + ACROSS, pl.ds(start, share)]
                    for item in range(3)
                )
            out_ref[...] = dense[...].astype(out_ref.dtype)


def bottle_terms(place, field, weight, owners):
    frame = ACROSS + 2
    rows = CELLS * 2 * ACROSS * frame
    width = weight.shape[2]
    share = COARSE_WIDTH // owners
    return pl.pallas_call(
        bottle_kernel,
        out_shape=[
            jax.ShapeDtypeStruct((ROWS, share), jnp.bfloat16 if distance else jnp.float32)
            for distance in range(owners)
        ],
        grid=(9,),
        in_specs=[
            pl.BlockSpec(memory_space=pltpu.SMEM),
            pl.BlockSpec(field.shape, lambda i: (0, 0, 0, 0, 0)),
            pl.BlockSpec((1, 3, width, COARSE_WIDTH), lambda i: (i, 0, 0, 0)),
        ],
        out_specs=[pl.BlockSpec((ROWS, share), lambda i: (0, 0))] * owners,
        scratch_shapes=[
            pltpu.VMEM((3, rows, COARSE_WIDTH), jnp.float32),
            pltpu.VMEM((rows, 3 * width), jnp.bfloat16),
            pltpu.VMEM((ROWS, share), jnp.float32),
        ],
        compiler_params=pltpu.CompilerParams(vmem_limit_bytes=52 * MIB),
        cost_estimate=pl.CostEstimate(
            flops=2 * rows * 27 * width * COARSE_WIDTH, bytes_accessed=16 * MIB, transcendentals=0
        ),
        name="bottle_terms",
    )(place, field, weight)


def finish_kernel(place_ref, guide_ref, own_ref, *refs):
    other_refs, bias_ref, out_ref, spread = refs[:-3], refs[-3], refs[-2], refs[-1]
    share = own_ref.shape[1]
    start = pl.multiple_of(place_ref[0] * share, share)
    value = own_ref[...] + bias_ref[:, pl.ds(start, share)]
    for other_ref in other_refs:
        value = value + other_ref[...].astype(jnp.float32)
    value = value / (1.0 + jnp.exp(-value))
    half = PLANE // 2
    for cell in range(CELLS):
        plain = value[cell * PLANE : cell * PLANE + half]
        guided = value[cell * PLANE + half : (cell + 1) * PLANE]
        mixed = plain + guide_ref[0] * (guided - plain)
        for lane in range(spread.shape[0]):
            spread[lane, pl.ds(cell, half, stride=SPREAD), :] = mixed[:, lane * LANES : (lane + 1) * LANES]
    for lane in range(spread.shape[0]):
        for cell in range(half):
            out_ref[cell, :, lane * LANES : (lane + 1) * LANES] = spread[
                lane, cell * SPREAD : cell * SPREAD + CELLS, :
            ].astype(jnp.bfloat16)


def finish(place, guide, terms, bias):
    share = terms[0].shape[1]
    return pl.pallas_call(
        finish_kernel,
        out_shape=jax.ShapeDtypeStruct((PLANE // 2, CELLS, share), jnp.bfloat16),
        in_specs=[pl.BlockSpec(memory_space=pltpu.SMEM)] * 2 + vmem(len(terms) + 1),
        out_specs=vmem(1)[0],
        scratch_shapes=[pltpu.VMEM((share // LANES, PLANE // 2 * SPREAD, LANES), jnp.float32)],
        compiler_params=pltpu.CompilerParams(vmem_limit_bytes=8 * MIB),
        name="finish",
    )(place, guide, *terms, bias)


def passed(value, steps):
    count = lax.axis_size("region")
    return lax.ppermute(
        value, "region", [(at, at + steps) for at in range(max(0, -steps), min(count, count - steps))]
    )


def across_z(value):
    count = lax.axis_size("region")
    return lax.ppermute(value, "region", [(at, at ^ 1) for at in range(count)])


def along_y(value, steps):
    count = lax.axis_size("region")
    pairs = [
        (at, at + steps * REGIONS_Z)
        for at in range(count)
        if 0 <= at // REGIONS_Z % REGIONS_Y + steps < REGIONS_Y
    ]
    return lax.ppermute(value, "region", pairs)


def with_halos(value, dim_x, dim_y, dim_z):
    value = jnp.concatenate(z_ends(z_layer(value, dim_z), value, dim_z), axis=dim_z)
    value = jnp.concatenate(
        [along_y(edge(value, dim_y, True), 1), value, along_y(edge(value, dim_y, False), -1)],
        axis=dim_y,
    )
    low, high = x_layers(edge(value, dim_x, False), edge(value, dim_x, True))
    return jnp.concatenate([low, value, high], axis=dim_x)


def edge(array, dim, last):
    size = array.shape[dim]
    return lax.slice_in_dim(array, size - 1 if last else 0, size if last else 1, axis=dim)


def is_upper():
    return lax.axis_index("region") % REGIONS_Z == 1


def z_layer(value, dim):
    return across_z(jnp.where(is_upper(), edge(value, dim, False), edge(value, dim, True)))


def z_ends(layer, value, dim):
    zero = jnp.zeros_like(layer)
    return [jnp.where(is_upper(), layer, zero), value, jnp.where(is_upper(), zero, layer)]


def x_layers(first, last):
    count = lax.axis_size("region") // (REGIONS_Y * REGIONS_Z)
    if count == 1:
        return jnp.zeros_like(last), jnp.zeros_like(first)
    return passed(last, REGIONS_Y * REGIONS_Z), passed(first, -REGIONS_Y * REGIONS_Z)


def exchange(piece_at):
    chans = lax.axis_size("chan")
    return [piece_at(0)] + [
        lax.ppermute(piece_at(distance), "chan", [(at, at ^ distance) for at in range(chans)])
        for distance in range(1, chans)
    ]


def ring_of(count):
    return list(range(0, count, 2)) + list(range(1, count, 2))[::-1]


def hop(value, ahead):
    ring = ring_of(lax.axis_size("region"))
    following = ring[1:] + ring[:1]
    return lax.ppermute(value, "region", list(zip(ring, following) if ahead else zip(following, ring)))


def after(value, other):
    return lax.optimization_barrier((value, other))[0]


def piece_channels(each):
    chans, regions = lax.axis_size("chan"), lax.axis_size("region")
    ring = ring_of(regions)
    shifts = [0]
    for step in range(1, regions // 2 + 1):
        shifts += [-step] + [step] * (step < regions // 2)
    origin = np.array(
        [[ring[(ring.index(region) + shift) % regions] for shift in shifts] for region in range(regions)]
    )
    table = np.zeros((chans, regions, regions, chans, each), np.int32)
    for chan in range(chans):
        for distance in range(chans):
            first = (chan ^ distance) * regions + origin
            table[chan, :, :, distance] = first[:, :, None] * each + np.arange(each)
    table = jnp.asarray(table.reshape(chans * regions, FINE_WIDTH))
    device = lax.axis_index("chan") * regions + lax.axis_index("region")
    return lax.dynamic_index_in_dim(table, device, 0, keepdims=True)


def ring_pieces(piece, milestones):
    regions = lax.axis_size("region")
    forward = backward = piece
    held = [piece]
    for step in range(1, regions // 2 + 1):
        if step > 1 and step - 2 < len(milestones):
            forward, backward = (after(value, milestones[step - 2]) for value in (forward, backward))
        if step == regions // 2:
            held += [hop(forward[: OFFSETS // 2], True), hop(backward[OFFSETS // 2 :], False)]
        else:
            forward, backward = hop(forward, True), hop(backward, False)
            held += [forward, backward]
    return held


def whole_columns(proj_weight):
    chans, held = lax.axis_size("chan"), proj_weight.shape[0]
    width = COARSE_WIDTH // chans
    mine = lax.all_to_all(proj_weight, "chan", split_axis=1, concat_axis=0, tiled=True)
    whole = lax.all_gather(mine.reshape(chans, held, width), "region", axis=1, tiled=True)
    return whole.reshape(FINE_WIDTH, OFFSETS, width).transpose(1, 0, 2)


def shards(
    latent,
    cond_scale,
    cond_shift,
    fine_weight,
    fine_bias,
    proj_weight,
    proj_bias,
    bottle_weight,
    bottle_bias,
    guide,
):
    chans = lax.axis_size("chan")
    chan_place = lax.axis_index("chan")
    region = lax.axis_index("region")
    width = COARSE_WIDTH // chans
    side = 2 * TILE_SIDE
    count_x = lax.axis_size("region") // (REGIONS_Y * REGIONS_Z)
    steps = (REGIONS_Y * REGIONS_Z, REGIONS_Z, 1)
    counts = (count_x, REGIONS_Y, REGIONS_Z)
    places = [region // step % count for step, count in zip(steps, counts)]
    inside = jnp.stack(
        [
            flag
            for place, count in zip(places, counts)
            for flag in ((place > 0).astype(jnp.float32), (place < count - 1).astype(jnp.float32))
        ]
    )

    place = chan_place[None]
    each, rest = divmod(proj_weight.shape[0], OFFSETS)
    by_ring = rest == 0 and chans * each % 16 == 0
    if by_ring:
        split = split_columns(place, proj_weight, chans)
        mine = exchange(lambda distance: split[distance])
        piece = regroup(mine)
        channel = piece_channels(each)
    else:
        channel = jnp.arange(FINE_WIDTH, dtype=jnp.int32)[None]
    order = lax.broadcasted_iota(jnp.int32, (FINE_WIDTH, FINE_WIDTH), 0) == channel

    block = latent[0].transpose(0, 2, 1, 3)
    upper = is_upper().astype(jnp.int32)[None]
    if by_ring:
        upper = after(upper, mine[1])
    face, first, last = faces(upper, block)
    layer = across_z(face)
    if by_ring:
        first, last = after(first, piece), after(last, piece)
    corner = lax.broadcasted_iota(jnp.int32, first.shape, 1) == TILE_SIDE
    below = along_y(jnp.where(corner, layer[:, -1:], last), 1)
    above = along_y(jnp.where(corner, layer[:, :1], first), -1)
    ends = []
    for at in (0, -1):
        plane = jnp.concatenate(z_ends(layer[at][None], block[at], 0), axis=0)
        low, high = [
            jnp.concatenate(
                z_ends(part[at, TILE_SIDE : TILE_SIDE + 1], part[at, :TILE_SIDE], 0), axis=0
            )[:, None]
            for part in (below, above)
        ]
        spare = jnp.zeros((TILE_SIDE + 2, 6, FINE_WIDTH), plane.dtype)
        ends.append(jnp.concatenate([plane, high, spare, low], axis=1))
    outer = jnp.stack(x_layers(*ends))

    bias = jnp.sum(jnp.where(order, fine_bias[:, None], 0.0), axis=0)
    windows, taps = make_windows(
        inside,
        block,
        layer,
        below,
        above,
        outer,
        cond_scale[None],
        cond_shift[None],
        fine_weight.reshape(27, FINE_WIDTH, FINE_WIDTH),
        order.astype(jnp.bfloat16),
    )
    bias = jnp.concatenate([bias, bias])[None]
    half = STRIDE // 2
    early = convolve(windows, taps, bias, 0, half)
    late = convolve(windows, taps, bias, half, half)
    columns = ring_pieces(piece, [taps, early, late]) if by_ring else [whole_columns(proj_weight)]
    coarse = project(place, early, late, columns, by_ring, proj_bias[None])

    grid = coarse[:ROWS].reshape(CELLS, 2, ACROSS, ACROSS, width)
    field = with_halos(grid, 2, 3, 0)
    terms = bottle_terms(place, field, bottle_weight.reshape(9, 3, width, COARSE_WIDTH), chans)
    terms = exchange(lambda distance: terms[distance])
    guided = finish(place, guide, terms, bottle_bias[None])
    return guided.reshape(1, ACROSS, ACROSS, CELLS, width)


def solution(mesh):
    placed = (
        P("region", None, None, None, None),
        P(),
        P(),
        P(),
        P(),
        P(("chan", "region"), None),
        P(),
        P(None, "chan", None),
        P(),
        P(),
    )
    return jax.shard_map(
        shards,
        mesh=mesh,
        in_specs=placed,
        out_specs=P("region", None, None, None, "chan"),
        check_vma=False,
    )
```

```python
import functools

import numpy as np

import jax
import jax.numpy as jnp
from jax import lax
from jax.experimental import pallas as pl
from jax.experimental.pallas import tpu as pltpu
from jax.sharding import PartitionSpec as P

FINE_WIDTH = 128
COARSE_WIDTH = 1024
TILE_SIDE = 12
STRIDE = 4
REGIONS_Y = 4
REGIONS_Z = 2

CELLS = TILE_SIDE // STRIDE
ACROSS = 2 * CELLS
PLANE = 2 * ACROSS * ACROSS
ROWS = CELLS * PLANE
PADDED = -(-ROWS // 16) * 16
PHASES = STRIDE + 2
OFFSETS = STRIDE**3
LANES = 128
SPREAD = 8
MIB = 2**20


def vmem(count):
    return [pl.BlockSpec(memory_space=pltpu.VMEM) for _ in range(count)]


def regroup_kernel(*refs):
    rows_refs, out_ref, wide = refs[:-2], refs[-2], refs[-1]
    held = rows_refs[0].shape[0]
    groups = out_ref.shape[1]
    for lane in range(wide.shape[0]):
        columns = slice(lane * LANES, (lane + 1) * LANES)
        for number, rows_ref in enumerate(rows_refs):
            wide[lane, number * held : (number + 1) * held, :] = rows_ref[:, columns].astype(jnp.float32)
        for offset in range(OFFSETS):
            out_ref[offset, :, columns] = wide[
                lane, pl.ds(offset, groups, stride=OFFSETS), :
            ].astype(jnp.bfloat16)


def regroup(pieces):
    held, width = pieces[0].shape
    total = len(pieces) * held
    return pl.pallas_call(
        regroup_kernel,
        out_shape=jax.ShapeDtypeStruct((OFFSETS, total // OFFSETS, width), jnp.bfloat16),
        in_specs=vmem(len(pieces)),
        out_specs=vmem(1)[0],
        scratch_shapes=[pltpu.VMEM((width // LANES, total, LANES), jnp.float32)],
        compiler_params=pltpu.CompilerParams(vmem_limit_bytes=8 * MIB),
        name="regroup",
    )(*pieces)


def split_kernel(place_ref, rows_ref, *out_refs):
    width = out_refs[0].shape[1]
    for distance, out_ref in enumerate(out_refs):
        start = pl.multiple_of((place_ref[0] ^ distance) * width, width)
        out_ref[...] = rows_ref[:, pl.ds(start, width)]


def split_columns(place, rows, owners):
    held, width = rows.shape[0], rows.shape[1] // owners
    return pl.pallas_call(
        split_kernel,
        out_shape=[jax.ShapeDtypeStruct((held, width), rows.dtype)] * owners,
        in_specs=[pl.BlockSpec(memory_space=pltpu.SMEM)] + vmem(1),
        out_specs=vmem(owners),
        compiler_params=pltpu.CompilerParams(vmem_limit_bytes=4 * MIB),
        name="split_columns",
    )(place, rows)


def faces_kernel(upper_ref, layer_ref, first_ref, last_ref, face_ref, low_ref, high_ref, wide):
    face_ref[...] = layer_ref[:, 0]

    def take(at_x, carry):
        for rows_ref, row, out_ref in ((first_ref, 0, low_ref), (last_ref, 7, high_ref)):
            for at_z in range(TILE_SIDE):
                wide[at_z : at_z + 1, :] = rows_ref[at_x, at_z].astype(jnp.float32)[row : row + 1]
            out_ref[at_x] = wide[...].astype(jnp.bfloat16)
        return carry

    wide[...] = jnp.zeros_like(wide)
    lax.fori_loop(0, layer_ref.shape[0], take, 0)


def faces(upper, block):
    side_x, depth, side_y, width = block.shape
    return pl.pallas_call(
        faces_kernel,
        out_shape=(
            jax.ShapeDtypeStruct((side_x, side_y, width), block.dtype),
            jax.ShapeDtypeStruct((side_x, 16, width), block.dtype),
            jax.ShapeDtypeStruct((side_x, 16, width), block.dtype),
        ),
        grid_spec=pltpu.PrefetchScalarGridSpec(
            num_scalar_prefetch=1,
            grid=(1,),
            in_specs=[
                pl.BlockSpec(
                    (side_x, 1, side_y, width), lambda i, upper: (0, (1 - upper[0]) * (depth - 1), 0, 0)
                ),
                pl.BlockSpec((side_x, depth, 8, width), lambda i, upper: (0, 0, 0, 0)),
                pl.BlockSpec((side_x, depth, 8, width), lambda i, upper: (0, 0, side_y // 8 - 1, 0)),
            ],
            out_specs=(
                pl.BlockSpec((side_x, side_y, width), lambda i, upper: (0, 0, 0)),
                pl.BlockSpec((side_x, 16, width), lambda i, upper: (0, 0, 0)),
                pl.BlockSpec((side_x, 16, width), lambda i, upper: (0, 0, 0)),
            ),
            scratch_shapes=[pltpu.VMEM((16, width), jnp.float32)],
        ),
        compiler_params=pltpu.CompilerParams(vmem_limit_bytes=12 * MIB),
        name="faces",
    )(upper, block, block, block)


def window_kernel(
    inside_ref, block_ref, layer_ref, below_ref, above_ref, outer_ref, scale_ref, shift_ref,
    weight_ref, order_ref, windows_ref, taps_ref, rows, line, layers,
):
    phase_x = pl.program_id(0)
    side, depth, width = 2 * TILE_SIDE, TILE_SIDE, FINE_WIDTH
    half = 2 * ACROSS * side

    @pl.when(phase_x == 0)
    def _():
        zero = jnp.zeros((width, width), jnp.bfloat16)
        for place in range(9):
            taps_ref[place, 3 * width :, :width] = zero
            taps_ref[place, :width, width:] = zero
            for step in range(3):
                block = jnp.dot(
                    weight_ref[place * 3 + step], order_ref[...], preferred_element_type=jnp.float32
                ).astype(jnp.bfloat16)
                taps_ref[place, step * width : (step + 1) * width, :width] = block
                taps_ref[place, (step + 1) * width : (step + 2) * width, width:] = block

        def widen(at_x, carry):
            rows[0, at_x] = below_ref[at_x].astype(jnp.float32)
            rows[1, at_x] = above_ref[at_x].astype(jnp.float32)
            return carry

        lax.fori_loop(0, side, widen, 0)

    scale = jnp.broadcast_to(scale_ref[...], (8, width))
    shift = jnp.broadcast_to(shift_ref[...], (8, width))
    row = lax.broadcasted_iota(jnp.int32, (8, width), 0)
    first = jnp.where(row == 0, shift * inside_ref[2], shift)
    last = jnp.where(row == side + 1 - 20, shift * inside_ref[3], shift)
    chunks = [(0, first), (8, shift), (16, shift), (4, shift), (12, shift), (20, last)]

    def split(cell_x, carry):
        at_x = phase_x + STRIDE * cell_x
        outside = jnp.logical_or(at_x == 0, at_x == side + 1)

        @pl.when(jnp.logical_not(outside))
        def _():
            at = at_x - 1
            for at_z in range(depth + 2):
                if at_z == 0:
                    flag, value, place = inside_ref[4], layer_ref[at], depth
                elif at_z == depth + 1:
                    flag, value, place = inside_ref[5], layer_ref[at], depth
                else:
                    flag, value, place = None, block_ref[at, at_z - 1], at_z - 1
                value = value.astype(jnp.float32)
                low, high = rows[0, at, place : place + 1, :], rows[1, at, place : place + 1, :]
                if flag is not None:
                    value, low, high = value * flag, low * flag, high * flag
                line[at_z, 7:8, :] = low
                line[at_z, 8 : side + 8, :] = value
                line[at_z, side + 8 : side + 9, :] = high

        @pl.when(outside)
        def _():
            end = jnp.where(at_x == 0, 0, 1)
            for at_z in range(depth + 2):
                value = outer_ref[end, at_z].astype(jnp.float32)
                line[at_z, 0:8, :] = value[side : side + 8]
                line[at_z, 8 : side + 8, :] = value[:side]
                line[at_z, side + 8 : side + 16, :] = value[side : side + 8]

        within = jnp.where(at_x == 0, inside_ref[0], 1.0)
        within = jnp.where(at_x == side + 1, inside_ref[1], within)
        for at_z in range(depth + 2):
            if at_z == 0:
                factor = within * inside_ref[4]
            elif at_z == depth + 1:
                factor = within * inside_ref[5]
            else:
                factor = within
            for number, (start, added) in enumerate(chunks):
                value = line[at_z, pl.ds(start + 7, 8), :]
                base = number // 3 * half + number % 3 * 8
                base = pl.multiple_of(base + cell_x * side, 8)
                layers[at_z, pl.ds(base, 8), :] = value
                layers[at_z, pl.ds(base + half // 2, 8), :] = value * scale + added * factor
        return carry

    lax.fori_loop(0, ACROSS, split, 0)
    for phase_y in range(PHASES):
        start = phase_y if phase_y < STRIDE else half + phase_y - STRIDE
        for phase_z in range(PHASES):
            parts = [
                layers[phase_z + STRIDE * cell, pl.ds(start, PLANE, stride=STRIDE), :]
                for cell in range(CELLS)
            ]
            parts.append(jnp.zeros((PADDED - ROWS, width), jnp.float32))
            windows_ref[0, phase_y, :, phase_z * width : (phase_z + 1) * width] = jnp.concatenate(
                parts, axis=0
            ).astype(jnp.bfloat16)


def make_windows(inside, *arrays):
    width, side = FINE_WIDTH, 2 * TILE_SIDE

    def whole(array):
        return pl.BlockSpec(array.shape, lambda i: (0,) * array.ndim)

    return pl.pallas_call(
        window_kernel,
        out_shape=(
            jax.ShapeDtypeStruct((PHASES, PHASES, PADDED, PHASES * width), jnp.bfloat16),
            jax.ShapeDtypeStruct((9, 4 * width, 2 * width), jnp.bfloat16),
        ),
        grid=(PHASES,),
        in_specs=[pl.BlockSpec(memory_space=pltpu.SMEM)] + [whole(array) for array in arrays],
        out_specs=(
            pl.BlockSpec((1, PHASES, PADDED, PHASES * width), lambda i: (i, 0, 0, 0)),
            pl.BlockSpec((9, 4 * width, 2 * width), lambda i: (0, 0, 0)),
        ),
        scratch_shapes=[
            pltpu.VMEM((2, side, 16, width), jnp.float32),
            pltpu.VMEM((TILE_SIDE + 2, side + 16, width), jnp.float32),
            pltpu.VMEM((TILE_SIDE + 2, 4 * ACROSS * side, width), jnp.float32),
        ],
        compiler_params=pltpu.CompilerParams(vmem_limit_bytes=28 * MIB),
        cost_estimate=pl.CostEstimate(flops=10**10, bytes_accessed=16 * MIB, transcendentals=0),
        name="windows",
    )(inside, *arrays)


def convolve_kernel(first_ref, second_ref, third_ref, taps_ref, bias_ref, out_ref):
    width = FINE_WIDTH
    bias = bias_ref[...]

    def convolve(at_y, carry):
        total = jnp.zeros((2 * PADDED, 2 * width), jnp.float32)
        for step_x, windows_ref in enumerate((first_ref, second_ref, third_ref)):
            for step_y in range(3):
                taken = [
                    windows_ref[0, at_y + step_y, :, pair * 2 * width : (pair * 2 + 4) * width]
                    for pair in range(2)
                ]
                total += jnp.dot(
                    jnp.concatenate(taken, axis=0),
                    taps_ref[step_x * 3 + step_y],
                    preferred_element_type=jnp.float32,
                )
        total = total + bias
        hidden = (total / (1.0 + jnp.exp(-total))).astype(jnp.bfloat16)
        for pair in range(2):
            out_ref[at_y * 2 + pair] = hidden[pair * PADDED : (pair + 1) * PADDED]
        return carry

    lax.fori_loop(0, STRIDE, convolve, 0)


def convolve(windows, taps, bias, start, count):
    width = FINE_WIDTH
    each = STRIDE * STRIDE // 2
    block = (1, PHASES, PADDED, PHASES * width)
    return pl.pallas_call(
        convolve_kernel,
        out_shape=jax.ShapeDtypeStruct((count * each, PADDED, 2 * width), jnp.bfloat16),
        grid=(count,),
        in_specs=[
            pl.BlockSpec(block, lambda i, step=step: (i + start + step, 0, 0, 0)) for step in range(3)
        ]
        + [
            pl.BlockSpec(taps.shape, lambda i: (0, 0, 0)),
            pl.BlockSpec(bias.shape, lambda i: (0, 0)),
        ],
        out_specs=pl.BlockSpec((each, PADDED, 2 * width), lambda i: (i, 0, 0)),
        compiler_params=pltpu.CompilerParams(vmem_limit_bytes=28 * MIB),
        cost_estimate=pl.CostEstimate(
            flops=2 * count * each * PADDED * 36 * width * 2 * width,
            bytes_accessed=16 * MIB,
            transcendentals=count * each * PADDED * 2 * width,
        ),
        name="convolve",
    )(windows, windows, windows, taps, bias)


def project_kernel(split, place_ref, early_ref, late_ref, *refs):
    weight_refs, bias_ref, out_ref, total = refs[:-3], refs[-3], refs[-2], refs[-1]
    step = pl.program_id(0)
    width = out_ref.shape[1]

    def product(hidden_ref, number):
        used = weight_refs[:-2] + (weight_refs[len(weight_refs) - 2 + number],) if split else weight_refs
        acc = jnp.zeros(total.shape, jnp.float32)
        for pair in range(hidden_ref.shape[0]):
            weight = jnp.concatenate(
                [ref[2 * pair + item] for item in range(2) for ref in used], axis=0
            )
            acc += jnp.dot(hidden_ref[pair], weight, preferred_element_type=jnp.float32)
        return acc

    @pl.when(step == 0)
    def _():
        total[...] = product(early_ref, 0)

    @pl.when(step == 1)
    def _():
        start = pl.multiple_of(place_ref[0] * width, width)
        out_ref[...] = (total[...] + product(late_ref, 1) + bias_ref[:, pl.ds(start, width)]).astype(
            jnp.bfloat16
        )


def project(place, early, late, weights, split, bias):
    pairs, rows, depth = early.shape
    width = weights[0].shape[2]
    return pl.pallas_call(
        functools.partial(project_kernel, split),
        out_shape=jax.ShapeDtypeStruct((rows, width), jnp.bfloat16),
        grid=(2,),
        in_specs=[
            pl.BlockSpec(memory_space=pltpu.SMEM),
            pl.BlockSpec(early.shape, lambda i: (0, 0, 0)),
            pl.BlockSpec(late.shape, lambda i: (0, 0, 0)),
        ]
        + [
            pl.BlockSpec(
                (OFFSETS // 2,) + weight.shape[1:],
                (lambda i: (i, 0, 0)) if weight.shape[0] == OFFSETS else (lambda i: (0, 0, 0)),
            )
            for weight in weights
        ]
        + [pl.BlockSpec(bias.shape, lambda i: (0, 0))],
        out_specs=pl.BlockSpec((rows, width), lambda i: (0, 0)),
        scratch_shapes=[pltpu.VMEM((rows, width), jnp.float32)],
        compiler_params=pltpu.CompilerParams(vmem_limit_bytes=24 * MIB),
        cost_estimate=pl.CostEstimate(
            flops=4 * pairs * rows * depth * width, bytes_accessed=8 * MIB, transcendentals=0
        ),
        name="project",
    )(place, early, late, *weights, bias)


def bottle_kernel(place_ref, field_ref, weight_ref, own_ref, *refs):
    other_refs, held, total, packed, dense, sems = refs[:-5], *refs[-5:]
    width = field_ref.shape[4]
    share = own_ref.shape[1]
    frame = ACROSS + 2
    rows = CELLS * 2 * ACROSS * frame
    chunk = 256

    def copy_of(step_y, place):
        tap = (place // 3 * 3 + step_y) * 3 + place % 3
        return pltpu.make_async_copy(
            weight_ref.at[tap],
            held.at[step_y, pl.ds(place * width, width)],
            sems.at[step_y, place],
        )

    for step_y in range(3):
        for place in range(9):
            copy_of(step_y, place).start()

    for step_x in range(3):
        for step_z in range(3):
            place = step_x * 3 + step_z
            packed[:, place * width : (place + 1) * width] = (
                field_ref[step_z : step_z + CELLS, :, step_x : step_x + ACROSS]
                .astype(jnp.float32)
                .reshape(rows, width)
                .astype(jnp.bfloat16)
            )

    for step_x in range(3):
        for step_z in range(3):
            copy_of(0, step_x * 3 + step_z).wait()
        depth = slice(step_x * 3 * width, (step_x + 1) * 3 * width)
        for start in range(0, COARSE_WIDTH, chunk):
            columns = slice(start, start + chunk)
            terms = jnp.dot(
                packed[:, depth], held[0, depth, columns], preferred_element_type=jnp.float32
            )
            total[0, :, columns] = terms if step_x == 0 else total[0, :, columns] + terms

    def rest(step_y, carry):
        for place in range(9):
            copy_of(step_y, place).wait()
        for start in range(0, COARSE_WIDTH, chunk):
            columns = slice(start, start + chunk)
            total[step_y, :, columns] = jnp.dot(
                packed[...], held[step_y, :, columns], preferred_element_type=jnp.float32
            )
        return carry

    lax.fori_loop(1, 3, rest, 0)

    for distance, out_ref in enumerate((own_ref,) + other_refs):
        start = pl.multiple_of((place_ref[0] ^ distance) * share, share)
        for group in range(rows // frame):
            at = group * frame
            dense[group * ACROSS : (group + 1) * ACROSS, :] = sum(
                total[item, at + item : at + item + ACROSS, pl.ds(start, share)]
                for item in range(3)
            )
        out_ref[...] = dense[...].astype(out_ref.dtype)


def bottle_terms(place, field, weight, owners):
    frame = ACROSS + 2
    rows = CELLS * 2 * ACROSS * frame
    width = weight.shape[1]
    share = COARSE_WIDTH // owners
    return pl.pallas_call(
        bottle_kernel,
        out_shape=[
            jax.ShapeDtypeStruct((ROWS, share), jnp.bfloat16 if distance else jnp.float32)
            for distance in range(owners)
        ],
        in_specs=[
            pl.BlockSpec(memory_space=pltpu.SMEM),
            pl.BlockSpec(memory_space=pltpu.VMEM),
            pl.BlockSpec(memory_space=pltpu.HBM),
        ],
        out_specs=vmem(owners),
        scratch_shapes=[
            pltpu.VMEM((3, 9 * width, COARSE_WIDTH), jnp.bfloat16),
            pltpu.VMEM((3, rows, COARSE_WIDTH), jnp.float32),
            pltpu.VMEM((rows, 9 * width), jnp.bfloat16),
            pltpu.VMEM((ROWS, share), jnp.float32),
            pltpu.SemaphoreType.DMA((3, 9)),
        ],
        compiler_params=pltpu.CompilerParams(vmem_limit_bytes=54 * MIB),
        cost_estimate=pl.CostEstimate(
            flops=2 * rows * 27 * width * COARSE_WIDTH, bytes_accessed=16 * MIB, transcendentals=0
        ),
        name="bottle_terms",
    )(place, field, weight)


def finish_kernel(place_ref, guide_ref, own_ref, *refs):
    other_refs, bias_ref, out_ref, spread = refs[:-3], refs[-3], refs[-2], refs[-1]
    share = own_ref.shape[1]
    start = pl.multiple_of(place_ref[0] * share, share)
    value = own_ref[...] + bias_ref[:, pl.ds(start, share)]
    for other_ref in other_refs:
        value = value + other_ref[...].astype(jnp.float32)
    value = value / (1.0 + jnp.exp(-value))
    half = PLANE // 2
    for cell in range(CELLS):
        plain = value[cell * PLANE : cell * PLANE + half]
        guided = value[cell * PLANE + half : (cell + 1) * PLANE]
        mixed = plain + guide_ref[0] * (guided - plain)
        for lane in range(spread.shape[0]):
            spread[lane, pl.ds(cell, half, stride=SPREAD), :] = mixed[:, lane * LANES : (lane + 1) * LANES]
    for lane in range(spread.shape[0]):
        for cell in range(half):
            out_ref[cell, :, lane * LANES : (lane + 1) * LANES] = spread[
                lane, cell * SPREAD : cell * SPREAD + CELLS, :
            ].astype(jnp.bfloat16)


def finish(place, guide, terms, bias):
    share = terms[0].shape[1]
    return pl.pallas_call(
        finish_kernel,
        out_shape=jax.ShapeDtypeStruct((PLANE // 2, CELLS, share), jnp.bfloat16),
        in_specs=[pl.BlockSpec(memory_space=pltpu.SMEM)] * 2 + vmem(len(terms) + 1),
        out_specs=vmem(1)[0],
        scratch_shapes=[pltpu.VMEM((share // LANES, PLANE // 2 * SPREAD, LANES), jnp.float32)],
        compiler_params=pltpu.CompilerParams(vmem_limit_bytes=8 * MIB),
        name="finish",
    )(place, guide, *terms, bias)


def passed(value, steps):
    count = lax.axis_size("region")
    return lax.ppermute(
        value, "region", [(at, at + steps) for at in range(max(0, -steps), min(count, count - steps))]
    )


def across_z(value):
    count = lax.axis_size("region")
    return lax.ppermute(value, "region", [(at, at ^ 1) for at in range(count)])


def along_y(value, steps):
    count = lax.axis_size("region")
    pairs = [
        (at, at + steps * REGIONS_Z)
        for at in range(count)
        if 0 <= at // REGIONS_Z % REGIONS_Y + steps < REGIONS_Y
    ]
    return lax.ppermute(value, "region", pairs)


def with_halos(value, dim_x, dim_y, dim_z):
    value = jnp.concatenate(z_ends(z_layer(value, dim_z), value, dim_z), axis=dim_z)
    value = jnp.concatenate(
        [along_y(edge(value, dim_y, True), 1), value, along_y(edge(value, dim_y, False), -1)],
        axis=dim_y,
    )
    low, high = x_layers(edge(value, dim_x, False), edge(value, dim_x, True))
    return jnp.concatenate([low, value, high], axis=dim_x)


def edge(array, dim, last):
    size = array.shape[dim]
    return lax.slice_in_dim(array, size - 1 if last else 0, size if last else 1, axis=dim)


def is_upper():
    return lax.axis_index("region") % REGIONS_Z == 1


def z_layer(value, dim):
    return across_z(jnp.where(is_upper(), edge(value, dim, False), edge(value, dim, True)))


def z_ends(layer, value, dim):
    zero = jnp.zeros_like(layer)
    return [jnp.where(is_upper(), layer, zero), value, jnp.where(is_upper(), zero, layer)]


def x_layers(first, last):
    count = lax.axis_size("region") // (REGIONS_Y * REGIONS_Z)
    if count == 1:
        return jnp.zeros_like(last), jnp.zeros_like(first)
    return passed(last, REGIONS_Y * REGIONS_Z), passed(first, -REGIONS_Y * REGIONS_Z)


def exchange(piece_at):
    chans = lax.axis_size("chan")
    return [piece_at(0)] + [
        lax.ppermute(piece_at(distance), "chan", [(at, at ^ distance) for at in range(chans)])
        for distance in range(1, chans)
    ]


def ring_of(count):
    return list(range(0, count, 2)) + list(range(1, count, 2))[::-1]


def hop(value, ahead):
    ring = ring_of(lax.axis_size("region"))
    following = ring[1:] + ring[:1]
    return lax.ppermute(value, "region", list(zip(ring, following) if ahead else zip(following, ring)))


def after(value, other):
    return lax.optimization_barrier((value, other))[0]


def piece_channels(each):
    chans, regions = lax.axis_size("chan"), lax.axis_size("region")
    ring = ring_of(regions)
    shifts = [0]
    for step in range(1, regions // 2 + 1):
        shifts += [-step] + [step] * (step < regions // 2)
    origin = np.array(
        [[ring[(ring.index(region) + shift) % regions] for shift in shifts] for region in range(regions)]
    )
    table = np.zeros((chans, regions, regions, chans, each), np.int32)
    for chan in range(chans):
        for distance in range(chans):
            first = (chan ^ distance) * regions + origin
            table[chan, :, :, distance] = first[:, :, None] * each + np.arange(each)
    table = jnp.asarray(table.reshape(chans * regions, FINE_WIDTH))
    device = lax.axis_index("chan") * regions + lax.axis_index("region")
    return lax.dynamic_index_in_dim(table, device, 0, keepdims=True)


def ring_pieces(piece, milestones):
    regions = lax.axis_size("region")
    forward = backward = piece
    held = [piece]
    for step in range(1, regions // 2 + 1):
        if step > 1 and step - 2 < len(milestones):
            forward, backward = (after(value, milestones[step - 2]) for value in (forward, backward))
        if step == regions // 2:
            held += [hop(forward[: OFFSETS // 2], True), hop(backward[OFFSETS // 2 :], False)]
        else:
            forward, backward = hop(forward, True), hop(backward, False)
            held += [forward, backward]
    return held


def whole_columns(proj_weight):
    chans, held = lax.axis_size("chan"), proj_weight.shape[0]
    width = COARSE_WIDTH // chans
    mine = lax.all_to_all(proj_weight, "chan", split_axis=1, concat_axis=0, tiled=True)
    whole = lax.all_gather(mine.reshape(chans, held, width), "region", axis=1, tiled=True)
    return whole.reshape(FINE_WIDTH, OFFSETS, width).transpose(1, 0, 2)


def shards(
    latent,
    cond_scale,
    cond_shift,
    fine_weight,
    fine_bias,
    proj_weight,
    proj_bias,
    bottle_weight,
    bottle_bias,
    guide,
):
    chans = lax.axis_size("chan")
    chan_place = lax.axis_index("chan")
    region = lax.axis_index("region")
    width = COARSE_WIDTH // chans
    side = 2 * TILE_SIDE
    count_x = lax.axis_size("region") // (REGIONS_Y * REGIONS_Z)
    steps = (REGIONS_Y * REGIONS_Z, REGIONS_Z, 1)
    counts = (count_x, REGIONS_Y, REGIONS_Z)
    places = [region // step % count for step, count in zip(steps, counts)]
    inside = jnp.stack(
        [
            flag
            for place, count in zip(places, counts)
            for flag in ((place > 0).astype(jnp.float32), (place < count - 1).astype(jnp.float32))
        ]
    )

    place = chan_place[None]
    each, rest = divmod(proj_weight.shape[0], OFFSETS)
    by_ring = rest == 0 and chans * each % 16 == 0
    if by_ring:
        split = split_columns(place, proj_weight, chans)
        mine = exchange(lambda distance: split[distance])
        piece = regroup(mine)
        channel = piece_channels(each)
    else:
        channel = jnp.arange(FINE_WIDTH, dtype=jnp.int32)[None]
    order = lax.broadcasted_iota(jnp.int32, (FINE_WIDTH, FINE_WIDTH), 0) == channel

    block = latent[0].transpose(0, 2, 1, 3)
    upper = is_upper().astype(jnp.int32)[None]
    face, first, last = faces(upper, block)
    layer = across_z(face)
    corner = lax.broadcasted_iota(jnp.int32, first.shape, 1) == TILE_SIDE
    below = along_y(jnp.where(corner, layer[:, -1:], last), 1)
    above = along_y(jnp.where(corner, layer[:, :1], first), -1)
    ends = []
    for at in (0, -1):
        plane = jnp.concatenate(z_ends(layer[at][None], block[at], 0), axis=0)
        low, high = [
            jnp.concatenate(
                z_ends(part[at, TILE_SIDE : TILE_SIDE + 1], part[at, :TILE_SIDE], 0), axis=0
            )[:, None]
            for part in (below, above)
        ]
        spare = jnp.zeros((TILE_SIDE + 2, 6, FINE_WIDTH), plane.dtype)
        ends.append(jnp.concatenate([plane, high, spare, low], axis=1))
    outer = jnp.stack(x_layers(*ends))

    bias = jnp.sum(jnp.where(order, fine_bias[:, None], 0.0), axis=0)
    windows, taps = make_windows(
        inside,
        block,
        layer,
        below,
        above,
        outer,
        cond_scale[None],
        cond_shift[None],
        fine_weight.reshape(27, FINE_WIDTH, FINE_WIDTH),
        order.astype(jnp.bfloat16),
    )
    bias = jnp.concatenate([bias, bias])[None]
    half = STRIDE // 2
    early = convolve(windows, taps, bias, 0, half)
    late = convolve(windows, taps, bias, half, half)
    columns = ring_pieces(piece, [taps, early, late]) if by_ring else [whole_columns(proj_weight)]
    coarse = project(place, early, late, columns, by_ring, proj_bias[None])

    grid = coarse[:ROWS].reshape(CELLS, 2, ACROSS, ACROSS, width)
    field = with_halos(grid, 2, 3, 0)
    terms = bottle_terms(place, field, bottle_weight, chans)
    terms = exchange(lambda distance: terms[distance])
    guided = finish(place, guide, terms, bottle_bias[None])
    return guided.reshape(1, ACROSS, ACROSS, CELLS, width)


def solution(mesh):
    placed = (
        P("region", None, None, None, None),
        P(),
        P(),
        P(),
        P(),
        P(("chan", "region"), None),
        P(),
        P(None, "chan", None),
        P(),
        P(),
    )
    return jax.shard_map(
        shards,
        mesh=mesh,
        in_specs=placed,
        out_specs=P("region", None, None, None, "chan"),
        check_vma=False,
    )
```

```python
import functools

import numpy as np

import jax
import jax.numpy as jnp
from jax import lax
from jax.experimental import pallas as pl
from jax.experimental.pallas import tpu as pltpu
from jax.sharding import PartitionSpec as P

FINE_WIDTH = 128
COARSE_WIDTH = 1024
TILE_SIDE = 12
STRIDE = 4
REGIONS_Y = 4
REGIONS_Z = 2

CELLS = TILE_SIDE // STRIDE
ACROSS = 2 * CELLS
PLANE = 2 * ACROSS * ACROSS
ROWS = CELLS * PLANE
PADDED = -(-ROWS // 16) * 16
PHASES = STRIDE + 2
OFFSETS = STRIDE**3
LANES = 128
SPREAD = 8
MIB = 2**20


def vmem(count):
    return [pl.BlockSpec(memory_space=pltpu.VMEM) for _ in range(count)]


def regroup_kernel(*refs):
    rows_refs, out_ref, wide = refs[:-2], refs[-2], refs[-1]
    held = rows_refs[0].shape[0]
    groups = out_ref.shape[1]
    for lane in range(wide.shape[0]):
        columns = slice(lane * LANES, (lane + 1) * LANES)
        for number, rows_ref in enumerate(rows_refs):
            wide[lane, number * held : (number + 1) * held, :] = rows_ref[:, columns].astype(jnp.float32)
        for offset in range(OFFSETS):
            out_ref[offset, :, columns] = wide[
                lane, pl.ds(offset, groups, stride=OFFSETS), :
            ].astype(jnp.bfloat16)


def regroup(pieces):
    held, width = pieces[0].shape
    total = len(pieces) * held
    return pl.pallas_call(
        regroup_kernel,
        out_shape=jax.ShapeDtypeStruct((OFFSETS, total // OFFSETS, width), jnp.bfloat16),
        in_specs=vmem(len(pieces)),
        out_specs=vmem(1)[0],
        scratch_shapes=[pltpu.VMEM((width // LANES, total, LANES), jnp.float32)],
        compiler_params=pltpu.CompilerParams(vmem_limit_bytes=8 * MIB),
        name="regroup",
    )(*pieces)


def split_kernel(place_ref, rows_ref, *out_refs):
    width = out_refs[0].shape[1]
    for distance, out_ref in enumerate(out_refs):
        start = pl.multiple_of((place_ref[0] ^ distance) * width, width)
        out_ref[...] = rows_ref[:, pl.ds(start, width)]


def split_columns(place, rows, owners):
    held, width = rows.shape[0], rows.shape[1] // owners
    return pl.pallas_call(
        split_kernel,
        out_shape=[jax.ShapeDtypeStruct((held, width), rows.dtype)] * owners,
        in_specs=[pl.BlockSpec(memory_space=pltpu.SMEM)] + vmem(1),
        out_specs=vmem(owners),
        compiler_params=pltpu.CompilerParams(vmem_limit_bytes=4 * MIB),
        name="split_columns",
    )(place, rows)


def faces_kernel(upper_ref, layer_ref, first_ref, last_ref, face_ref, low_ref, high_ref, wide):
    face_ref[...] = layer_ref[:, 0]

    def take(at_x, carry):
        for rows_ref, row, out_ref in ((first_ref, 0, low_ref), (last_ref, 7, high_ref)):
            for at_z in range(TILE_SIDE):
                wide[at_z : at_z + 1, :] = rows_ref[at_x, at_z].astype(jnp.float32)[row : row + 1]
            out_ref[at_x] = wide[...].astype(jnp.bfloat16)
        return carry

    wide[...] = jnp.zeros_like(wide)
    lax.fori_loop(0, layer_ref.shape[0], take, 0)


def faces(upper, block):
    side_x, depth, side_y, width = block.shape
    return pl.pallas_call(
        faces_kernel,
        out_shape=(
            jax.ShapeDtypeStruct((side_x, side_y, width), block.dtype),
            jax.ShapeDtypeStruct((side_x, 16, width), block.dtype),
            jax.ShapeDtypeStruct((side_x, 16, width), block.dtype),
        ),
        grid_spec=pltpu.PrefetchScalarGridSpec(
            num_scalar_prefetch=1,
            grid=(1,),
            in_specs=[
                pl.BlockSpec(
                    (side_x, 1, side_y, width), lambda i, upper: (0, (1 - upper[0]) * (depth - 1), 0, 0)
                ),
                pl.BlockSpec((side_x, depth, 8, width), lambda i, upper: (0, 0, 0, 0)),
                pl.BlockSpec((side_x, depth, 8, width), lambda i, upper: (0, 0, side_y // 8 - 1, 0)),
            ],
            out_specs=(
                pl.BlockSpec((side_x, side_y, width), lambda i, upper: (0, 0, 0)),
                pl.BlockSpec((side_x, 16, width), lambda i, upper: (0, 0, 0)),
                pl.BlockSpec((side_x, 16, width), lambda i, upper: (0, 0, 0)),
            ),
            scratch_shapes=[pltpu.VMEM((16, width), jnp.float32)],
        ),
        compiler_params=pltpu.CompilerParams(vmem_limit_bytes=12 * MIB),
        name="faces",
    )(upper, block, block, block)


def window_kernel(
    inside_ref, block_ref, layer_ref, below_ref, above_ref, corner_ref, outer_ref, scale_ref, shift_ref,
    weight_ref, order_ref, windows_ref, taps_ref, rows, line, layers,
):
    phase_x = pl.program_id(0)
    side, depth, width = 2 * TILE_SIDE, TILE_SIDE, FINE_WIDTH
    half = 2 * ACROSS * side

    @pl.when(phase_x == 0)
    def _():
        zero = jnp.zeros((width, width), jnp.bfloat16)
        for place in range(9):
            taps_ref[place, 3 * width :, :width] = zero
            taps_ref[place, :width, width:] = zero
            for step in range(3):
                block = jnp.dot(
                    weight_ref[place * 3 + step], order_ref[...], preferred_element_type=jnp.float32
                ).astype(jnp.bfloat16)
                taps_ref[place, step * width : (step + 1) * width, :width] = block
                taps_ref[place, (step + 1) * width : (step + 2) * width, width:] = block

        def widen(at_x, carry):
            rows[0, at_x] = below_ref[at_x].astype(jnp.float32)
            rows[1, at_x] = above_ref[at_x].astype(jnp.float32)
            return carry

        lax.fori_loop(0, side, widen, 0)
        for end in range(2):
            corners = corner_ref[end].astype(jnp.float32)
            for at_x in range(side):
                rows[end, at_x, depth : depth + 1, :] = corners[at_x : at_x + 1]

    scale = jnp.broadcast_to(scale_ref[...], (8, width))
    shift = jnp.broadcast_to(shift_ref[...], (8, width))
    row = lax.broadcasted_iota(jnp.int32, (8, width), 0)
    first = jnp.where(row == 0, shift * inside_ref[2], shift)
    last = jnp.where(row == side + 1 - 20, shift * inside_ref[3], shift)
    chunks = [(0, first), (8, shift), (16, shift), (4, shift), (12, shift), (20, last)]

    def split(cell_x, carry):
        at_x = phase_x + STRIDE * cell_x
        outside = jnp.logical_or(at_x == 0, at_x == side + 1)

        @pl.when(jnp.logical_not(outside))
        def _():
            at = at_x - 1
            for at_z in range(depth + 2):
                if at_z == 0:
                    flag, value, place = inside_ref[4], layer_ref[at], depth
                elif at_z == depth + 1:
                    flag, value, place = inside_ref[5], layer_ref[at], depth
                else:
                    flag, value, place = None, block_ref[at, at_z - 1], at_z - 1
                value = value.astype(jnp.float32)
                low, high = rows[0, at, place : place + 1, :], rows[1, at, place : place + 1, :]
                if flag is not None:
                    value, low, high = value * flag, low * flag, high * flag
                line[at_z, 7:8, :] = low
                line[at_z, 8 : side + 8, :] = value
                line[at_z, side + 8 : side + 9, :] = high

        @pl.when(outside)
        def _():
            end = jnp.where(at_x == 0, 0, 1)
            for at_z in range(depth + 2):
                value = outer_ref[end, at_z].astype(jnp.float32)
                line[at_z, 0:8, :] = value[side : side + 8]
                line[at_z, 8 : side + 8, :] = value[:side]
                line[at_z, side + 8 : side + 16, :] = value[side : side + 8]

        within = jnp.where(at_x == 0, inside_ref[0], 1.0)
        within = jnp.where(at_x == side + 1, inside_ref[1], within)
        for at_z in range(depth + 2):
            if at_z == 0:
                factor = within * inside_ref[4]
            elif at_z == depth + 1:
                factor = within * inside_ref[5]
            else:
                factor = within
            for number, (start, added) in enumerate(chunks):
                value = line[at_z, pl.ds(start + 7, 8), :]
                base = number // 3 * half + number % 3 * 8
                base = pl.multiple_of(base + cell_x * side, 8)
                layers[at_z, pl.ds(base, 8), :] = value
                layers[at_z, pl.ds(base + half // 2, 8), :] = value * scale + added * factor
        return carry

    lax.fori_loop(0, ACROSS, split, 0)
    for phase_y in range(PHASES):
        start = phase_y if phase_y < STRIDE else half + phase_y - STRIDE
        for phase_z in range(PHASES):
            parts = [
                layers[phase_z + STRIDE * cell, pl.ds(start, PLANE, stride=STRIDE), :]
                for cell in range(CELLS)
            ]
            parts.append(jnp.zeros((PADDED - ROWS, width), jnp.float32))
            windows_ref[0, phase_y, :, phase_z * width : (phase_z + 1) * width] = jnp.concatenate(
                parts, axis=0
            ).astype(jnp.bfloat16)


def make_windows(inside, *arrays):
    width, side = FINE_WIDTH, 2 * TILE_SIDE

    def whole(array):
        return pl.BlockSpec(array.shape, lambda i: (0,) * array.ndim)

    return pl.pallas_call(
        window_kernel,
        out_shape=(
            jax.ShapeDtypeStruct((PHASES, PHASES, PADDED, PHASES * width), jnp.bfloat16),
            jax.ShapeDtypeStruct((9, 4 * width, 2 * width), jnp.bfloat16),
        ),
        grid=(PHASES,),
        in_specs=[pl.BlockSpec(memory_space=pltpu.SMEM)] + [whole(array) for array in arrays],
        out_specs=(
            pl.BlockSpec((1, PHASES, PADDED, PHASES * width), lambda i: (i, 0, 0, 0)),
            pl.BlockSpec((9, 4 * width, 2 * width), lambda i: (0, 0, 0)),
        ),
        scratch_shapes=[
            pltpu.VMEM((2, side, 16, width), jnp.float32),
            pltpu.VMEM((TILE_SIDE + 2, side + 16, width), jnp.float32),
            pltpu.VMEM((TILE_SIDE + 2, 4 * ACROSS * side, width), jnp.float32),
        ],
        compiler_params=pltpu.CompilerParams(vmem_limit_bytes=28 * MIB),
        cost_estimate=pl.CostEstimate(flops=10**10, bytes_accessed=16 * MIB, transcendentals=0),
        name="windows",
    )(inside, *arrays)


def convolve_kernel(first_ref, second_ref, third_ref, taps_ref, bias_ref, out_ref):
    width = FINE_WIDTH
    bias = bias_ref[...]

    def convolve(at_y, carry):
        total = jnp.zeros((2 * PADDED, 2 * width), jnp.float32)
        for step_x, windows_ref in enumerate((first_ref, second_ref, third_ref)):
            for step_y in range(3):
                taken = [
                    windows_ref[0, at_y + step_y, :, pair * 2 * width : (pair * 2 + 4) * width]
                    for pair in range(2)
                ]
                total += jnp.dot(
                    jnp.concatenate(taken, axis=0),
                    taps_ref[step_x * 3 + step_y],
                    preferred_element_type=jnp.float32,
                )
        total = total + bias
        hidden = (total / (1.0 + jnp.exp(-total))).astype(jnp.bfloat16)
        for pair in range(2):
            out_ref[at_y * 2 + pair] = hidden[pair * PADDED : (pair + 1) * PADDED]
        return carry

    lax.fori_loop(0, STRIDE, convolve, 0)


def convolve(windows, taps, bias, start, count):
    width = FINE_WIDTH
    each = STRIDE * STRIDE // 2
    block = (1, PHASES, PADDED, PHASES * width)
    return pl.pallas_call(
        convolve_kernel,
        out_shape=jax.ShapeDtypeStruct((count * each, PADDED, 2 * width), jnp.bfloat16),
        grid=(count,),
        in_specs=[
            pl.BlockSpec(block, lambda i, step=step: (i + start + step, 0, 0, 0)) for step in range(3)
        ]
        + [
            pl.BlockSpec(taps.shape, lambda i: (0, 0, 0)),
            pl.BlockSpec(bias.shape, lambda i: (0, 0)),
        ],
        out_specs=pl.BlockSpec((each, PADDED, 2 * width), lambda i: (i, 0, 0)),
        compiler_params=pltpu.CompilerParams(vmem_limit_bytes=28 * MIB),
        cost_estimate=pl.CostEstimate(
            flops=2 * count * each * PADDED * 36 * width * 2 * width,
            bytes_accessed=16 * MIB,
            transcendentals=count * each * PADDED * 2 * width,
        ),
        name="convolve",
    )(windows, windows, windows, taps, bias)


def project_kernel(split, place_ref, early_ref, late_ref, *refs):
    weight_refs, bias_ref, out_ref, total = refs[:-3], refs[-3], refs[-2], refs[-1]
    step = pl.program_id(0)
    width = out_ref.shape[1]

    def product(hidden_ref, number):
        used = weight_refs[:-2] + (weight_refs[len(weight_refs) - 2 + number],) if split else weight_refs
        acc = jnp.zeros(total.shape, jnp.float32)
        for pair in range(hidden_ref.shape[0]):
            weight = jnp.concatenate(
                [ref[2 * pair + item] for item in range(2) for ref in used], axis=0
            )
            acc += jnp.dot(hidden_ref[pair], weight, preferred_element_type=jnp.float32)
        return acc

    @pl.when(step == 0)
    def _():
        total[...] = product(early_ref, 0)

    @pl.when(step == 1)
    def _():
        start = pl.multiple_of(place_ref[0] * width, width)
        out_ref[...] = (total[...] + product(late_ref, 1) + bias_ref[:, pl.ds(start, width)]).astype(
            jnp.bfloat16
        )


def project(place, early, late, weights, split, bias):
    pairs, rows, depth = early.shape
    width = weights[0].shape[2]
    return pl.pallas_call(
        functools.partial(project_kernel, split),
        out_shape=jax.ShapeDtypeStruct((rows, width), jnp.bfloat16),
        grid=(2,),
        in_specs=[
            pl.BlockSpec(memory_space=pltpu.SMEM),
            pl.BlockSpec(early.shape, lambda i: (0, 0, 0)),
            pl.BlockSpec(late.shape, lambda i: (0, 0, 0)),
        ]
        + [
            pl.BlockSpec(
                (OFFSETS // 2,) + weight.shape[1:],
                (lambda i: (i, 0, 0)) if weight.shape[0] == OFFSETS else (lambda i: (0, 0, 0)),
            )
            for weight in weights
        ]
        + [pl.BlockSpec(bias.shape, lambda i: (0, 0))],
        out_specs=pl.BlockSpec((rows, width), lambda i: (0, 0)),
        scratch_shapes=[pltpu.VMEM((rows, width), jnp.float32)],
        compiler_params=pltpu.CompilerParams(vmem_limit_bytes=24 * MIB),
        cost_estimate=pl.CostEstimate(
            flops=4 * pairs * rows * depth * width, bytes_accessed=8 * MIB, transcendentals=0
        ),
        name="project",
    )(place, early, late, *weights, bias)


WITHOUT_CORNERS = ((0, (1,)), (2, (1,)), (1, (0, 1, 2)))
WITH_CORNERS = ((0, (0, 2)), (2, (0, 2)))


def bottle_sums(groups, field_ref, weight_ref, held, packed, sems, add):
    width = field_ref.shape[4]
    chunk = 256
    copies = []
    for step_y, steps_z in groups:
        copies.append([])
        for step_z in steps_z:
            for step_x in range(3):
                slot = sum(len(some) for some in copies)
                copies[-1].append(
                    pltpu.make_async_copy(
                        weight_ref.at[(step_x * 3 + step_y) * 3 + step_z],
                        held.at[pl.ds(slot * width, width)],
                        sems.at[slot],
                    )
                )
    for copy in sum(copies, []):
        copy.start()

    order_z = sorted({step_z for _, steps_z in groups for step_z in steps_z})
    rows = packed.shape[0]
    for number, step_z in enumerate(order_z):
        for step_x in range(3):
            slot = number * 3 + step_x
            packed[:, slot * width : (slot + 1) * width] = (
                field_ref[step_z : step_z + CELLS, :, step_x : step_x + ACROSS]
                .astype(jnp.float32)
                .reshape(rows, width)
                .astype(jnp.bfloat16)
            )

    row = 0
    for (step_y, steps_z), some in zip(groups, copies):
        for copy in some:
            copy.wait()
        depth = len(some) * width
        lane = order_z.index(steps_z[0]) * 3 * width
        for start in range(0, COARSE_WIDTH, chunk):
            columns = slice(start, start + chunk)
            add(
                step_y,
                columns,
                jnp.dot(
                    packed[:, lane : lane + depth],
                    held[row : row + depth, columns],
                    preferred_element_type=jnp.float32,
                ),
            )
        row += depth


def bottle_first_kernel(field_ref, weight_ref, total_ref, held, packed, sems):
    def add(step_y, columns, terms):
        total_ref[step_y, :, columns] = terms

    bottle_sums(WITHOUT_CORNERS, field_ref, weight_ref, held, packed, sems, add)


def bottle_last_kernel(place_ref, field_ref, first_ref, weight_ref, own_ref, *refs):
    other_refs, total, dense, held, packed, sems = refs[:-5], *refs[-5:]
    share = own_ref.shape[1]
    frame = ACROSS + 2

    def add(step_y, columns, terms):
        total[step_y // 2, :, columns] = first_ref[step_y, :, columns] + terms

    bottle_sums(WITH_CORNERS, field_ref, weight_ref, held, packed, sems, add)

    for distance, out_ref in enumerate((own_ref,) + other_refs):
        start = pl.multiple_of((place_ref[0] ^ distance) * share, share)
        columns = pl.ds(start, share)
        for group in range(packed.shape[0] // frame):
            at = group * frame
            dense[group * ACROSS : (group + 1) * ACROSS, :] = (
                total[0, at : at + ACROSS, columns]
                + first_ref[1, at + 1 : at + 1 + ACROSS, columns]
                + total[1, at + 2 : at + 2 + ACROSS, columns]
            )
        out_ref[...] = dense[...].astype(out_ref.dtype)


def bottle_call(kernel, groups, operands, in_specs, out_shape, scratch, name):
    width = operands[-1].shape[1]
    rows = CELLS * 2 * ACROSS * (ACROSS + 2)
    taps = 3 * sum(len(steps_z) for _, steps_z in groups)
    steps = {step_z for _, steps_z in groups for step_z in steps_z}
    return pl.pallas_call(
        kernel,
        out_shape=out_shape,
        in_specs=in_specs + [pl.BlockSpec(memory_space=pltpu.HBM)],
        out_specs=[pl.BlockSpec(memory_space=pltpu.VMEM) for _ in out_shape],
        scratch_shapes=scratch
        + [
            pltpu.VMEM((taps * width, COARSE_WIDTH), jnp.bfloat16),
            pltpu.VMEM((rows, len(steps) * 3 * width), jnp.bfloat16),
            pltpu.SemaphoreType.DMA((taps,)),
        ],
        compiler_params=pltpu.CompilerParams(vmem_limit_bytes=51 * MIB),
        cost_estimate=pl.CostEstimate(
            flops=2 * rows * taps * width * COARSE_WIDTH,
            bytes_accessed=2 * taps * width * COARSE_WIDTH,
            transcendentals=0,
        ),
        name=name,
    )(*operands)


def bottle_first(field, weight):
    rows = CELLS * 2 * ACROSS * (ACROSS + 2)
    shape = jax.ShapeDtypeStruct((3, rows, COARSE_WIDTH), jnp.float32)
    (total,) = bottle_call(
        bottle_first_kernel, WITHOUT_CORNERS, [field, weight], vmem(1), [shape], [], "bottle_first"
    )
    return total


def bottle_last(place, field, first, weight, owners):
    rows = CELLS * 2 * ACROSS * (ACROSS + 2)
    share = COARSE_WIDTH // owners
    return bottle_call(
        bottle_last_kernel,
        WITH_CORNERS,
        [place, field, first, weight],
        [pl.BlockSpec(memory_space=pltpu.SMEM)] + vmem(2),
        [
            jax.ShapeDtypeStruct((ROWS, share), jnp.bfloat16 if distance else jnp.float32)
            for distance in range(owners)
        ],
        [
            pltpu.VMEM((2, rows, COARSE_WIDTH), jnp.float32),
            pltpu.VMEM((ROWS, share), jnp.float32),
        ],
        "bottle_last",
    )


def finish_kernel(place_ref, guide_ref, own_ref, *refs):
    other_refs, bias_ref, out_ref, spread = refs[:-3], refs[-3], refs[-2], refs[-1]
    share = own_ref.shape[1]
    start = pl.multiple_of(place_ref[0] * share, share)
    value = own_ref[...] + bias_ref[:, pl.ds(start, share)]
    for other_ref in other_refs:
        value = value + other_ref[...].astype(jnp.float32)
    value = value / (1.0 + jnp.exp(-value))
    half = PLANE // 2
    for cell in range(CELLS):
        plain = value[cell * PLANE : cell * PLANE + half]
        guided = value[cell * PLANE + half : (cell + 1) * PLANE]
        mixed = plain + guide_ref[0] * (guided - plain)
        for lane in range(spread.shape[0]):
            spread[lane, pl.ds(cell, half, stride=SPREAD), :] = mixed[:, lane * LANES : (lane + 1) * LANES]
    for lane in range(spread.shape[0]):
        for cell in range(half):
            out_ref[cell, :, lane * LANES : (lane + 1) * LANES] = spread[
                lane, cell * SPREAD : cell * SPREAD + CELLS, :
            ].astype(jnp.bfloat16)


def finish(place, guide, terms, bias):
    share = terms[0].shape[1]
    return pl.pallas_call(
        finish_kernel,
        out_shape=jax.ShapeDtypeStruct((PLANE // 2, CELLS, share), jnp.bfloat16),
        in_specs=[pl.BlockSpec(memory_space=pltpu.SMEM)] * 2 + vmem(len(terms) + 1),
        out_specs=vmem(1)[0],
        scratch_shapes=[pltpu.VMEM((share // LANES, PLANE // 2 * SPREAD, LANES), jnp.float32)],
        compiler_params=pltpu.CompilerParams(vmem_limit_bytes=8 * MIB),
        name="finish",
    )(place, guide, *terms, bias)


def passed(value, steps):
    count = lax.axis_size("region")
    return lax.ppermute(
        value, "region", [(at, at + steps) for at in range(max(0, -steps), min(count, count - steps))]
    )


def across_z(value):
    count = lax.axis_size("region")
    return lax.ppermute(value, "region", [(at, at ^ 1) for at in range(count)])


def along_y(value, steps):
    count = lax.axis_size("region")
    pairs = [
        (at, at + steps * REGIONS_Z)
        for at in range(count)
        if 0 <= at // REGIONS_Z % REGIONS_Y + steps < REGIONS_Y
    ]
    return lax.ppermute(value, "region", pairs)


def coarse_halos(value, use):
    layer = z_layer(value, 0)
    below, above = along_y(edge(value, 3, True), 1), along_y(edge(value, 3, False), -1)
    corner = across_z(z_side(jnp.concatenate([below, above], axis=3), 0))
    body = jnp.concatenate([below, value, above], axis=3)

    def framed(low, high):
        outer = jnp.concatenate([low, layer, high], axis=3)
        field = jnp.concatenate(z_ends(outer, body, 0), axis=0)
        low, high = x_layers(edge(field, 2, False), edge(field, 2, True))
        return jnp.concatenate([low, field, high], axis=2)

    if lax.axis_size("region") > REGIONS_Y * REGIONS_Z:
        field = framed(corner[:, :, :, :1], corner[:, :, :, 1:])
        return field, use(field)
    zero = jnp.zeros_like(corner[:, :, :, :1])
    used = use(framed(zero, zero))
    corner = after(corner, used)
    return framed(corner[:, :, :, :1], corner[:, :, :, 1:]), used


def edge(array, dim, last):
    size = array.shape[dim]
    return lax.slice_in_dim(array, size - 1 if last else 0, size if last else 1, axis=dim)


def is_upper():
    return lax.axis_index("region") % REGIONS_Z == 1


def z_side(value, dim):
    return jnp.where(is_upper(), edge(value, dim, False), edge(value, dim, True))


def z_layer(value, dim):
    return across_z(z_side(value, dim))


def z_ends(layer, value, dim):
    zero = jnp.zeros_like(layer)
    return [jnp.where(is_upper(), layer, zero), value, jnp.where(is_upper(), zero, layer)]


def x_layers(first, last):
    count = lax.axis_size("region") // (REGIONS_Y * REGIONS_Z)
    if count == 1:
        return jnp.zeros_like(last), jnp.zeros_like(first)
    return passed(last, REGIONS_Y * REGIONS_Z), passed(first, -REGIONS_Y * REGIONS_Z)


def exchange(piece_at):
    chans = lax.axis_size("chan")
    return [piece_at(0)] + [
        lax.ppermute(piece_at(distance), "chan", [(at, at ^ distance) for at in range(chans)])
        for distance in range(1, chans)
    ]


def ring_of(count):
    return list(range(0, count, 2)) + list(range(1, count, 2))[::-1]


def hop(value, ahead):
    ring = ring_of(lax.axis_size("region"))
    following = ring[1:] + ring[:1]
    return lax.ppermute(value, "region", list(zip(ring, following) if ahead else zip(following, ring)))


def after(value, other):
    return lax.optimization_barrier((value, other))[0]


def piece_channels(each):
    chans, regions = lax.axis_size("chan"), lax.axis_size("region")
    ring = ring_of(regions)
    shifts = [0]
    for step in range(1, regions // 2 + 1):
        shifts += [-step] + [step] * (step < regions // 2)
    origin = np.array(
        [[ring[(ring.index(region) + shift) % regions] for shift in shifts] for region in range(regions)]
    )
    table = np.zeros((chans, regions, regions, chans, each), np.int32)
    for chan in range(chans):
        for distance in range(chans):
            first = (chan ^ distance) * regions + origin
            table[chan, :, :, distance] = first[:, :, None] * each + np.arange(each)
    table = jnp.asarray(table.reshape(chans * regions, FINE_WIDTH))
    device = lax.axis_index("chan") * regions + lax.axis_index("region")
    return lax.dynamic_index_in_dim(table, device, 0, keepdims=True)


def ring_pieces(piece, milestones):
    regions = lax.axis_size("region")
    forward = backward = piece
    held = [piece]
    for step in range(1, regions // 2 + 1):
        if step > 1 and step - 2 < len(milestones):
            forward, backward = (after(value, milestones[step - 2]) for value in (forward, backward))
        if step == regions // 2:
            held += [hop(forward[: OFFSETS // 2], True), hop(backward[OFFSETS // 2 :], False)]
        else:
            forward, backward = hop(forward, True), hop(backward, False)
            held += [forward, backward]
    return held


def whole_columns(proj_weight):
    chans, held = lax.axis_size("chan"), proj_weight.shape[0]
    width = COARSE_WIDTH // chans
    mine = lax.all_to_all(proj_weight, "chan", split_axis=1, concat_axis=0, tiled=True)
    whole = lax.all_gather(mine.reshape(chans, held, width), "region", axis=1, tiled=True)
    return whole.reshape(FINE_WIDTH, OFFSETS, width).transpose(1, 0, 2)


def shards(
    latent,
    cond_scale,
    cond_shift,
    fine_weight,
    fine_bias,
    proj_weight,
    proj_bias,
    bottle_weight,
    bottle_bias,
    guide,
):
    chans = lax.axis_size("chan")
    chan_place = lax.axis_index("chan")
    region = lax.axis_index("region")
    width = COARSE_WIDTH // chans
    side = 2 * TILE_SIDE
    count_x = lax.axis_size("region") // (REGIONS_Y * REGIONS_Z)
    steps = (REGIONS_Y * REGIONS_Z, REGIONS_Z, 1)
    counts = (count_x, REGIONS_Y, REGIONS_Z)
    places = [region // step % count for step, count in zip(steps, counts)]
    inside = jnp.stack(
        [
            flag
            for place, count in zip(places, counts)
            for flag in ((place > 0).astype(jnp.float32), (place < count - 1).astype(jnp.float32))
        ]
    )

    place = chan_place[None]
    each, rest = divmod(proj_weight.shape[0], OFFSETS)
    by_ring = rest == 0 and chans * each % 16 == 0
    if by_ring:
        split = split_columns(place, proj_weight, chans)
        mine = exchange(lambda distance: split[distance])
        piece = regroup(mine)
        channel = piece_channels(each)
    else:
        channel = jnp.arange(FINE_WIDTH, dtype=jnp.int32)[None]
    order = lax.broadcasted_iota(jnp.int32, (FINE_WIDTH, FINE_WIDTH), 0) == channel

    block = latent[0].transpose(0, 2, 1, 3)
    face, first, last = faces(is_upper().astype(jnp.int32)[None], block)
    layer = across_z(face)
    below, above = along_y(last, 1), along_y(first, -1)
    depth = lax.broadcasted_iota(jnp.int32, below.shape, 1)
    chosen = depth == jnp.where(is_upper(), 0, TILE_SIDE - 1)
    corner = across_z(
        jnp.stack([jnp.sum(jnp.where(chosen, part, 0), axis=1) for part in (below, above)])
    )
    ends = []
    for at in (0, -1):
        plane = jnp.concatenate(z_ends(layer[at][None], block[at], 0), axis=0)
        low, high = [
            jnp.concatenate(z_ends(corner[number, at][None], part[at, :TILE_SIDE], 0), axis=0)[:, None]
            for number, part in enumerate((below, above))
        ]
        spare = jnp.zeros((TILE_SIDE + 2, 6, FINE_WIDTH), plane.dtype)
        ends.append(jnp.concatenate([plane, high, spare, low], axis=1))
    outer = jnp.stack(x_layers(*ends))

    bias = jnp.sum(jnp.where(order, fine_bias[:, None], 0.0), axis=0)
    windows, taps = make_windows(
        inside,
        block,
        layer,
        below,
        above,
        corner,
        outer,
        cond_scale[None],
        cond_shift[None],
        fine_weight.reshape(27, FINE_WIDTH, FINE_WIDTH),
        order.astype(jnp.bfloat16),
    )
    bias = jnp.concatenate([bias, bias])[None]
    half = STRIDE // 2
    early = convolve(windows, taps, bias, 0, half)
    late = convolve(windows, taps, bias, half, half)
    columns = ring_pieces(piece, [taps, early, late]) if by_ring else [whole_columns(proj_weight)]
    coarse = project(place, early, late, columns, by_ring, proj_bias[None])

    grid = coarse[:ROWS].reshape(CELLS, 2, ACROSS, ACROSS, width)
    field, sums = coarse_halos(grid, lambda field: bottle_first(field, bottle_weight))
    terms = bottle_last(place, field, sums, bottle_weight, chans)
    terms = exchange(lambda distance: terms[distance])
    guided = finish(place, guide, terms, bottle_bias[None])
    return guided.reshape(1, ACROSS, ACROSS, CELLS, width)


def solution(mesh):
    placed = (
        P("region", None, None, None, None),
        P(),
        P(),
        P(),
        P(),
        P(("chan", "region"), None),
        P(),
        P(None, "chan", None),
        P(),
        P(),
    )
    return jax.shard_map(
        shards,
        mesh=mesh,
        in_specs=placed,
        out_specs=P("region", None, None, None, "chan"),
        check_vma=False,
    )
```

```python
import functools

import numpy as np

import jax
import jax.numpy as jnp
from jax import lax
from jax.experimental import pallas as pl
from jax.experimental.pallas import tpu as pltpu
from jax.sharding import PartitionSpec as P

FINE_WIDTH = 128
COARSE_WIDTH = 1024
TILE_SIDE = 12
STRIDE = 4
REGIONS_Y = 4
REGIONS_Z = 2

CELLS = TILE_SIDE // STRIDE
ACROSS = 2 * CELLS
PLANE = 2 * ACROSS * ACROSS
ROWS = CELLS * PLANE
PADDED = -(-ROWS // 16) * 16
PHASES = STRIDE + 2
OFFSETS = STRIDE**3
LANES = 128
SPREAD = 8
MIB = 2**20


def vmem(count):
    return [pl.BlockSpec(memory_space=pltpu.VMEM) for _ in range(count)]


def regroup_kernel(*refs):
    rows_refs, out_ref, wide = refs[:-2], refs[-2], refs[-1]
    held = rows_refs[0].shape[0]
    groups = out_ref.shape[1]
    for lane in range(wide.shape[0]):
        columns = slice(lane * LANES, (lane + 1) * LANES)
        for number, rows_ref in enumerate(rows_refs):
            wide[lane, number * held : (number + 1) * held, :] = rows_ref[:, columns].astype(jnp.float32)
        for offset in range(OFFSETS):
            out_ref[offset, :, columns] = wide[
                lane, pl.ds(offset, groups, stride=OFFSETS), :
            ].astype(jnp.bfloat16)


def regroup(pieces):
    held, width = pieces[0].shape
    total = len(pieces) * held
    return pl.pallas_call(
        regroup_kernel,
        out_shape=jax.ShapeDtypeStruct((OFFSETS, total // OFFSETS, width), jnp.bfloat16),
        in_specs=vmem(len(pieces)),
        out_specs=vmem(1)[0],
        scratch_shapes=[pltpu.VMEM((width // LANES, total, LANES), jnp.float32)],
        compiler_params=pltpu.CompilerParams(vmem_limit_bytes=8 * MIB),
        name="regroup",
    )(*pieces)


def split_kernel(place_ref, rows_ref, *out_refs):
    width = out_refs[0].shape[1]
    for distance, out_ref in enumerate(out_refs):
        start = pl.multiple_of((place_ref[0] ^ distance) * width, width)
        out_ref[...] = rows_ref[:, pl.ds(start, width)]


def split_columns(place, rows, owners):
    held, width = rows.shape[0], rows.shape[1] // owners
    return pl.pallas_call(
        split_kernel,
        out_shape=[jax.ShapeDtypeStruct((held, width), rows.dtype)] * owners,
        in_specs=[pl.BlockSpec(memory_space=pltpu.SMEM)] + vmem(1),
        out_specs=vmem(owners),
        compiler_params=pltpu.CompilerParams(vmem_limit_bytes=4 * MIB),
        name="split_columns",
    )(place, rows)


def faces_kernel(upper_ref, layer_ref, first_ref, last_ref, face_ref, low_ref, high_ref, wide):
    face_ref[...] = layer_ref[:, 0]

    def take(at_x, carry):
        for rows_ref, row, out_ref in ((first_ref, 0, low_ref), (last_ref, 7, high_ref)):
            for at_z in range(TILE_SIDE):
                wide[at_z : at_z + 1, :] = rows_ref[at_x, at_z].astype(jnp.float32)[row : row + 1]
            out_ref[at_x] = wide[...].astype(jnp.bfloat16)
        return carry

    wide[...] = jnp.zeros_like(wide)
    lax.fori_loop(0, layer_ref.shape[0], take, 0)


def faces(upper, block):
    side_x, depth, side_y, width = block.shape
    return pl.pallas_call(
        faces_kernel,
        out_shape=(
            jax.ShapeDtypeStruct((side_x, side_y, width), block.dtype),
            jax.ShapeDtypeStruct((side_x, 16, width), block.dtype),
            jax.ShapeDtypeStruct((side_x, 16, width), block.dtype),
        ),
        grid_spec=pltpu.PrefetchScalarGridSpec(
            num_scalar_prefetch=1,
            grid=(1,),
            in_specs=[
                pl.BlockSpec(
                    (side_x, 1, side_y, width), lambda i, upper: (0, (1 - upper[0]) * (depth - 1), 0, 0)
                ),
                pl.BlockSpec((side_x, depth, 8, width), lambda i, upper: (0, 0, 0, 0)),
                pl.BlockSpec((side_x, depth, 8, width), lambda i, upper: (0, 0, side_y // 8 - 1, 0)),
            ],
            out_specs=(
                pl.BlockSpec((side_x, side_y, width), lambda i, upper: (0, 0, 0)),
                pl.BlockSpec((side_x, 16, width), lambda i, upper: (0, 0, 0)),
                pl.BlockSpec((side_x, 16, width), lambda i, upper: (0, 0, 0)),
            ),
            scratch_shapes=[pltpu.VMEM((16, width), jnp.float32)],
        ),
        compiler_params=pltpu.CompilerParams(vmem_limit_bytes=12 * MIB),
        name="faces",
    )(upper, block, block, block)


def window_kernel(
    inside_ref, block_ref, layer_ref, below_ref, above_ref, outer_ref, scale_ref, shift_ref,
    weight_ref, order_ref, windows_ref, taps_ref, rows, line, layers,
):
    phase_x = pl.program_id(0)
    side, depth, width = 2 * TILE_SIDE, TILE_SIDE, FINE_WIDTH
    half = 2 * ACROSS * side

    @pl.when(phase_x == 0)
    def _():
        zero = jnp.zeros((width, width), jnp.bfloat16)
        for place in range(9):
            taps_ref[place, 3 * width :, :width] = zero
            taps_ref[place, :width, width:] = zero
            for step in range(3):
                block = jnp.dot(
                    weight_ref[place * 3 + step], order_ref[...], preferred_element_type=jnp.float32
                ).astype(jnp.bfloat16)
                taps_ref[place, step * width : (step + 1) * width, :width] = block
                taps_ref[place, (step + 1) * width : (step + 2) * width, width:] = block

        def widen(at_x, carry):
            rows[0, at_x] = below_ref[at_x].astype(jnp.float32)
            rows[1, at_x] = above_ref[at_x].astype(jnp.float32)
            return carry

        lax.fori_loop(0, side, widen, 0)

    scale = jnp.broadcast_to(scale_ref[...], (8, width))
    shift = jnp.broadcast_to(shift_ref[...], (8, width))
    row = lax.broadcasted_iota(jnp.int32, (8, width), 0)
    first = jnp.where(row == 0, shift * inside_ref[2], shift)
    last = jnp.where(row == side + 1 - 20, shift * inside_ref[3], shift)
    chunks = [(0, first), (8, shift), (16, shift), (4, shift), (12, shift), (20, last)]

    def split(cell_x, carry):
        at_x = phase_x + STRIDE * cell_x
        outside = jnp.logical_or(at_x == 0, at_x == side + 1)

        @pl.when(jnp.logical_not(outside))
        def _():
            at = at_x - 1
            for at_z in range(depth + 2):
                if at_z == 0:
                    flag, value, place = inside_ref[4], layer_ref[at], depth
                elif at_z == depth + 1:
                    flag, value, place = inside_ref[5], layer_ref[at], depth
                else:
                    flag, value, place = None, block_ref[at, at_z - 1], at_z - 1
                value = value.astype(jnp.float32)
                low, high = rows[0, at, place : place + 1, :], rows[1, at, place : place + 1, :]
                if flag is not None:
                    value, low, high = value * flag, low * flag, high * flag
                line[at_z, 7:8, :] = low
                line[at_z, 8 : side + 8, :] = value
                line[at_z, side + 8 : side + 9, :] = high

        @pl.when(outside)
        def _():
            end = jnp.where(at_x == 0, 0, 1)
            for at_z in range(depth + 2):
                value = outer_ref[end, at_z].astype(jnp.float32)
                line[at_z, 0:8, :] = value[side : side + 8]
                line[at_z, 8 : side + 8, :] = value[:side]
                line[at_z, side + 8 : side + 16, :] = value[side : side + 8]

        within = jnp.where(at_x == 0, inside_ref[0], 1.0)
        within = jnp.where(at_x == side + 1, inside_ref[1], within)
        for at_z in range(depth + 2):
            if at_z == 0:
                factor = within * inside_ref[4]
            elif at_z == depth + 1:
                factor = within * inside_ref[5]
            else:
                factor = within
            for number, (start, added) in enumerate(chunks):
                value = line[at_z, pl.ds(start + 7, 8), :]
                base = number // 3 * half + number % 3 * 8
                base = pl.multiple_of(base + cell_x * side, 8)
                layers[at_z, pl.ds(base, 8), :] = value
                layers[at_z, pl.ds(base + half // 2, 8), :] = value * scale + added * factor
        return carry

    lax.fori_loop(0, ACROSS, split, 0)
    for phase_y in range(PHASES):
        start = phase_y if phase_y < STRIDE else half + phase_y - STRIDE
        for phase_z in range(PHASES):
            parts = [
                layers[phase_z + STRIDE * cell, pl.ds(start, PLANE, stride=STRIDE), :]
                for cell in range(CELLS)
            ]
            parts.append(jnp.zeros((PADDED - ROWS, width), jnp.float32))
            windows_ref[0, phase_y, :, phase_z * width : (phase_z + 1) * width] = jnp.concatenate(
                parts, axis=0
            ).astype(jnp.bfloat16)


def make_windows(inside, *arrays):
    width, side = FINE_WIDTH, 2 * TILE_SIDE

    def whole(array):
        return pl.BlockSpec(array.shape, lambda i: (0,) * array.ndim)

    return pl.pallas_call(
        window_kernel,
        out_shape=(
            jax.ShapeDtypeStruct((PHASES, PHASES, PADDED, PHASES * width), jnp.bfloat16),
            jax.ShapeDtypeStruct((9, 4 * width, 2 * width), jnp.bfloat16),
        ),
        grid=(PHASES,),
        in_specs=[pl.BlockSpec(memory_space=pltpu.SMEM)] + [whole(array) for array in arrays],
        out_specs=(
            pl.BlockSpec((1, PHASES, PADDED, PHASES * width), lambda i: (i, 0, 0, 0)),
            pl.BlockSpec((9, 4 * width, 2 * width), lambda i: (0, 0, 0)),
        ),
        scratch_shapes=[
            pltpu.VMEM((2, side, 16, width), jnp.float32),
            pltpu.VMEM((TILE_SIDE + 2, side + 16, width), jnp.float32),
            pltpu.VMEM((TILE_SIDE + 2, 4 * ACROSS * side, width), jnp.float32),
        ],
        compiler_params=pltpu.CompilerParams(vmem_limit_bytes=28 * MIB),
        cost_estimate=pl.CostEstimate(flops=10**10, bytes_accessed=16 * MIB, transcendentals=0),
        name="windows",
    )(inside, *arrays)


def convolve_kernel(first_ref, second_ref, third_ref, taps_ref, bias_ref, out_ref):
    width = FINE_WIDTH
    bias = bias_ref[...]

    def convolve(at_y, carry):
        total = jnp.zeros((2 * PADDED, 2 * width), jnp.float32)
        for step_x, windows_ref in enumerate((first_ref, second_ref, third_ref)):
            for step_y in range(3):
                taken = [
                    windows_ref[0, at_y + step_y, :, pair * 2 * width : (pair * 2 + 4) * width]
                    for pair in range(2)
                ]
                total += jnp.dot(
                    jnp.concatenate(taken, axis=0),
                    taps_ref[step_x * 3 + step_y],
                    preferred_element_type=jnp.float32,
                )
        total = total + bias
        hidden = (total / (1.0 + jnp.exp(-total))).astype(jnp.bfloat16)
        for pair in range(2):
            out_ref[at_y * 2 + pair] = hidden[pair * PADDED : (pair + 1) * PADDED]
        return carry

    lax.fori_loop(0, STRIDE, convolve, 0)


def convolve(windows, taps, bias, start, count):
    width = FINE_WIDTH
    each = STRIDE * STRIDE // 2
    block = (1, PHASES, PADDED, PHASES * width)
    return pl.pallas_call(
        convolve_kernel,
        out_shape=jax.ShapeDtypeStruct((count * each, PADDED, 2 * width), jnp.bfloat16),
        grid=(count,),
        in_specs=[
            pl.BlockSpec(block, lambda i, step=step: (i + start + step, 0, 0, 0)) for step in range(3)
        ]
        + [
            pl.BlockSpec(taps.shape, lambda i: (0, 0, 0)),
            pl.BlockSpec(bias.shape, lambda i: (0, 0)),
        ],
        out_specs=pl.BlockSpec((each, PADDED, 2 * width), lambda i: (i, 0, 0)),
        compiler_params=pltpu.CompilerParams(vmem_limit_bytes=28 * MIB),
        cost_estimate=pl.CostEstimate(
            flops=2 * count * each * PADDED * 36 * width * 2 * width,
            bytes_accessed=16 * MIB,
            transcendentals=count * each * PADDED * 2 * width,
        ),
        name="convolve",
    )(windows, windows, windows, taps, bias)


def project_kernel(split, place_ref, early_ref, late_ref, *refs):
    weight_refs, bias_ref, out_ref, total = refs[:-3], refs[-3], refs[-2], refs[-1]
    step = pl.program_id(0)
    width = out_ref.shape[1]

    def product(hidden_ref, number):
        used = weight_refs[:-2] + (weight_refs[len(weight_refs) - 2 + number],) if split else weight_refs
        acc = jnp.zeros(total.shape, jnp.float32)
        for pair in range(hidden_ref.shape[0]):
            weight = jnp.concatenate(
                [ref[2 * pair + item] for item in range(2) for ref in used], axis=0
            )
            acc += jnp.dot(hidden_ref[pair], weight, preferred_element_type=jnp.float32)
        return acc

    @pl.when(step == 0)
    def _():
        total[...] = product(early_ref, 0)

    @pl.when(step == 1)
    def _():
        start = pl.multiple_of(place_ref[0] * width, width)
        out_ref[...] = (total[...] + product(late_ref, 1) + bias_ref[:, pl.ds(start, width)]).astype(
            jnp.bfloat16
        )


def project(place, early, late, weights, split, bias):
    pairs, rows, depth = early.shape
    width = weights[0].shape[2]
    return pl.pallas_call(
        functools.partial(project_kernel, split),
        out_shape=jax.ShapeDtypeStruct((rows, width), jnp.bfloat16),
        grid=(2,),
        in_specs=[
            pl.BlockSpec(memory_space=pltpu.SMEM),
            pl.BlockSpec(early.shape, lambda i: (0, 0, 0)),
            pl.BlockSpec(late.shape, lambda i: (0, 0, 0)),
        ]
        + [
            pl.BlockSpec(
                (OFFSETS // 2,) + weight.shape[1:],
                (lambda i: (i, 0, 0)) if weight.shape[0] == OFFSETS else (lambda i: (0, 0, 0)),
            )
            for weight in weights
        ]
        + [pl.BlockSpec(bias.shape, lambda i: (0, 0))],
        out_specs=pl.BlockSpec((rows, width), lambda i: (0, 0)),
        scratch_shapes=[pltpu.VMEM((rows, width), jnp.float32)],
        compiler_params=pltpu.CompilerParams(vmem_limit_bytes=24 * MIB),
        cost_estimate=pl.CostEstimate(
            flops=4 * pairs * rows * depth * width, bytes_accessed=8 * MIB, transcendentals=0
        ),
        name="project",
    )(place, early, late, *weights, bias)


def bottle_kernel(place_ref, field_ref, weight_ref, own_ref, *refs):
    other_refs, held, total, packed, dense, sems = refs[:-5], *refs[-5:]
    width = field_ref.shape[4]
    share = own_ref.shape[1]
    frame = ACROSS + 2
    rows = CELLS * 2 * ACROSS * frame
    chunk = 256

    def copy_of(step_y, place):
        tap = (place // 3 * 3 + step_y) * 3 + place % 3
        return pltpu.make_async_copy(
            weight_ref.at[tap],
            held.at[step_y, pl.ds(place * width, width)],
            sems.at[step_y, place],
        )

    for step_y in range(3):
        for place in range(9):
            copy_of(step_y, place).start()

    for step_x in range(3):
        for step_z in range(3):
            place = step_x * 3 + step_z
            packed[:, place * width : (place + 1) * width] = (
                field_ref[step_z : step_z + CELLS, :, step_x : step_x + ACROSS]
                .astype(jnp.float32)
                .reshape(rows, width)
                .astype(jnp.bfloat16)
            )

    for step_x in range(3):
        for step_z in range(3):
            copy_of(0, step_x * 3 + step_z).wait()
        depth = slice(step_x * 3 * width, (step_x + 1) * 3 * width)
        for start in range(0, COARSE_WIDTH, chunk):
            columns = slice(start, start + chunk)
            terms = jnp.dot(
                packed[:, depth], held[0, depth, columns], preferred_element_type=jnp.float32
            )
            total[0, :, columns] = terms if step_x == 0 else total[0, :, columns] + terms

    def rest(step_y, carry):
        for place in range(9):
            copy_of(step_y, place).wait()
        for start in range(0, COARSE_WIDTH, chunk):
            columns = slice(start, start + chunk)
            total[step_y, :, columns] = jnp.dot(
                packed[...], held[step_y, :, columns], preferred_element_type=jnp.float32
            )
        return carry

    lax.fori_loop(1, 3, rest, 0)

    for distance, out_ref in enumerate((own_ref,) + other_refs):
        start = pl.multiple_of((place_ref[0] ^ distance) * share, share)
        for group in range(rows // frame):
            at = group * frame
            dense[group * ACROSS : (group + 1) * ACROSS, :] = sum(
                total[item, at + item : at + item + ACROSS, pl.ds(start, share)]
                for item in range(3)
            )
        out_ref[...] = dense[...].astype(out_ref.dtype)


def bottle_terms(place, field, weight, owners):
    frame = ACROSS + 2
    rows = CELLS * 2 * ACROSS * frame
    width = weight.shape[1]
    share = COARSE_WIDTH // owners
    return pl.pallas_call(
        bottle_kernel,
        out_shape=[
            jax.ShapeDtypeStruct((ROWS, share), jnp.bfloat16 if distance else jnp.float32)
            for distance in range(owners)
        ],
        in_specs=[
            pl.BlockSpec(memory_space=pltpu.SMEM),
            pl.BlockSpec(memory_space=pltpu.VMEM),
            pl.BlockSpec(memory_space=pltpu.HBM),
        ],
        out_specs=vmem(owners),
        scratch_shapes=[
            pltpu.VMEM((3, 9 * width, COARSE_WIDTH), jnp.bfloat16),
            pltpu.VMEM((3, rows, COARSE_WIDTH), jnp.float32),
            pltpu.VMEM((rows, 9 * width), jnp.bfloat16),
            pltpu.VMEM((ROWS, share), jnp.float32),
            pltpu.SemaphoreType.DMA((3, 9)),
        ],
        compiler_params=pltpu.CompilerParams(vmem_limit_bytes=51 * MIB),
        cost_estimate=pl.CostEstimate(
            flops=2 * rows * 27 * width * COARSE_WIDTH, bytes_accessed=16 * MIB, transcendentals=0
        ),
        name="bottle_terms",
    )(place, field, weight)


def finish_kernel(place_ref, guide_ref, own_ref, *refs):
    other_refs, bias_ref, out_ref, spread = refs[:-3], refs[-3], refs[-2], refs[-1]
    share = own_ref.shape[1]
    start = pl.multiple_of(place_ref[0] * share, share)
    value = own_ref[...] + bias_ref[:, pl.ds(start, share)]
    for other_ref in other_refs:
        value = value + other_ref[...].astype(jnp.float32)
    value = value / (1.0 + jnp.exp(-value))
    half = PLANE // 2
    for cell in range(CELLS):
        plain = value[cell * PLANE : cell * PLANE + half]
        guided = value[cell * PLANE + half : (cell + 1) * PLANE]
        mixed = plain + guide_ref[0] * (guided - plain)
        for lane in range(spread.shape[0]):
            spread[lane, pl.ds(cell, half, stride=SPREAD), :] = mixed[:, lane * LANES : (lane + 1) * LANES]
    for lane in range(spread.shape[0]):
        for cell in range(half):
            out_ref[cell, :, lane * LANES : (lane + 1) * LANES] = spread[
                lane, cell * SPREAD : cell * SPREAD + CELLS, :
            ].astype(jnp.bfloat16)


def finish(place, guide, terms, bias):
    share = terms[0].shape[1]
    return pl.pallas_call(
        finish_kernel,
        out_shape=jax.ShapeDtypeStruct((PLANE // 2, CELLS, share), jnp.bfloat16),
        in_specs=[pl.BlockSpec(memory_space=pltpu.SMEM)] * 2 + vmem(len(terms) + 1),
        out_specs=vmem(1)[0],
        scratch_shapes=[pltpu.VMEM((share // LANES, PLANE // 2 * SPREAD, LANES), jnp.float32)],
        compiler_params=pltpu.CompilerParams(vmem_limit_bytes=8 * MIB),
        name="finish",
    )(place, guide, *terms, bias)


def passed(value, steps):
    count = lax.axis_size("region")
    return lax.ppermute(
        value, "region", [(at, at + steps) for at in range(max(0, -steps), min(count, count - steps))]
    )


def across_z(value):
    count = lax.axis_size("region")
    return lax.ppermute(value, "region", [(at, at ^ 1) for at in range(count)])


def is_even_y():
    return lax.axis_index("region") // REGIONS_Z % 2 == 0


def y_pairs(first, last):
    count = lax.axis_size("region")
    even = is_even_y()
    arrived = []
    for parity, payload in ((0, jnp.where(even, last, first)), (1, jnp.where(even, first, last))):
        pairs = []
        for at in range(count):
            place = at // REGIONS_Z % REGIONS_Y
            step = 1 if place % 2 == parity else -1
            if 0 <= place + step < REGIONS_Y:
                pairs.append((at, at + step * REGIONS_Z))
        arrived.append(lax.ppermute(payload, "region", pairs))
    return arrived


def y_halos(first, last):
    near, far = y_pairs(first, last)
    even = is_even_y()
    return jnp.where(even, far, near), jnp.where(even, near, far)


def with_halos(value, dim_x, dim_y, dim_z):
    value = jnp.concatenate(z_ends(z_layer(value, dim_z), value, dim_z), axis=dim_z)
    below, above = y_halos(edge(value, dim_y, False), edge(value, dim_y, True))
    value = jnp.concatenate([below, value, above], axis=dim_y)
    low, high = x_layers(edge(value, dim_x, False), edge(value, dim_x, True))
    return jnp.concatenate([low, value, high], axis=dim_x)


def edge(array, dim, last):
    size = array.shape[dim]
    return lax.slice_in_dim(array, size - 1 if last else 0, size if last else 1, axis=dim)


def is_upper():
    return lax.axis_index("region") % REGIONS_Z == 1


def z_layer(value, dim):
    return across_z(jnp.where(is_upper(), edge(value, dim, False), edge(value, dim, True)))


def z_ends(layer, value, dim):
    zero = jnp.zeros_like(layer)
    return [jnp.where(is_upper(), layer, zero), value, jnp.where(is_upper(), zero, layer)]


def x_layers(first, last):
    count = lax.axis_size("region") // (REGIONS_Y * REGIONS_Z)
    if count == 1:
        return jnp.zeros_like(last), jnp.zeros_like(first)
    return passed(last, REGIONS_Y * REGIONS_Z), passed(first, -REGIONS_Y * REGIONS_Z)


def exchange(piece_at):
    chans = lax.axis_size("chan")
    return [piece_at(0)] + [
        lax.ppermute(piece_at(distance), "chan", [(at, at ^ distance) for at in range(chans)])
        for distance in range(1, chans)
    ]


def ring_of(count):
    return list(range(0, count, 2)) + list(range(1, count, 2))[::-1]


def hop(value, ahead):
    ring = ring_of(lax.axis_size("region"))
    following = ring[1:] + ring[:1]
    return lax.ppermute(value, "region", list(zip(ring, following) if ahead else zip(following, ring)))


def after(value, other):
    return lax.optimization_barrier((value, other))[0]


def piece_channels(each):
    chans, regions = lax.axis_size("chan"), lax.axis_size("region")
    ring = ring_of(regions)
    shifts = [0]
    for step in range(1, regions // 2 + 1):
        shifts += [-step] + [step] * (step < regions // 2)
    origin = np.array(
        [[ring[(ring.index(region) + shift) % regions] for shift in shifts] for region in range(regions)]
    )
    table = np.zeros((chans, regions, regions, chans, each), np.int32)
    for chan in range(chans):
        for distance in range(chans):
            first = (chan ^ distance) * regions + origin
            table[chan, :, :, distance] = first[:, :, None] * each + np.arange(each)
    table = jnp.asarray(table.reshape(chans * regions, FINE_WIDTH))
    device = lax.axis_index("chan") * regions + lax.axis_index("region")
    return lax.dynamic_index_in_dim(table, device, 0, keepdims=True)


def ring_pieces(piece, milestones):
    regions = lax.axis_size("region")
    forward = backward = piece
    held = [piece]
    for step in range(1, regions // 2 + 1):
        if step > 1 and step - 2 < len(milestones):
            forward, backward = (after(value, milestones[step - 2]) for value in (forward, backward))
        if step == regions // 2:
            held += [hop(forward[: OFFSETS // 2], True), hop(backward[OFFSETS // 2 :], False)]
        else:
            forward, backward = hop(forward, True), hop(backward, False)
            held += [forward, backward]
    return held


def whole_columns(proj_weight):
    chans, held = lax.axis_size("chan"), proj_weight.shape[0]
    width = COARSE_WIDTH // chans
    mine = lax.all_to_all(proj_weight, "chan", split_axis=1, concat_axis=0, tiled=True)
    whole = lax.all_gather(mine.reshape(chans, held, width), "region", axis=1, tiled=True)
    return whole.reshape(FINE_WIDTH, OFFSETS, width).transpose(1, 0, 2)


def shards(
    latent,
    cond_scale,
    cond_shift,
    fine_weight,
    fine_bias,
    proj_weight,
    proj_bias,
    bottle_weight,
    bottle_bias,
    guide,
):
    chans = lax.axis_size("chan")
    chan_place = lax.axis_index("chan")
    region = lax.axis_index("region")
    width = COARSE_WIDTH // chans
    side = 2 * TILE_SIDE
    count_x = lax.axis_size("region") // (REGIONS_Y * REGIONS_Z)
    steps = (REGIONS_Y * REGIONS_Z, REGIONS_Z, 1)
    counts = (count_x, REGIONS_Y, REGIONS_Z)
    places = [region // step % count for step, count in zip(steps, counts)]
    inside = jnp.stack(
        [
            flag
            for place, count in zip(places, counts)
            for flag in ((place > 0).astype(jnp.float32), (place < count - 1).astype(jnp.float32))
        ]
    )

    place = chan_place[None]
    each, rest = divmod(proj_weight.shape[0], OFFSETS)
    by_ring = rest == 0 and chans * each % 16 == 0
    if by_ring:
        split = split_columns(place, proj_weight, chans)
        mine = exchange(lambda distance: split[distance])
        piece = regroup(mine)
        channel = piece_channels(each)
    else:
        channel = jnp.arange(FINE_WIDTH, dtype=jnp.int32)[None]
    order = lax.broadcasted_iota(jnp.int32, (FINE_WIDTH, FINE_WIDTH), 0) == channel

    block = latent[0].transpose(0, 2, 1, 3)
    upper = is_upper().astype(jnp.int32)[None]
    face, first, last = faces(upper, block)
    layer = across_z(face)
    corner = lax.broadcasted_iota(jnp.int32, first.shape, 1) == TILE_SIDE
    below, above = y_halos(
        jnp.where(corner, layer[:, :1], first), jnp.where(corner, layer[:, -1:], last)
    )
    ends = []
    for at in (0, -1):
        plane = jnp.concatenate(z_ends(layer[at][None], block[at], 0), axis=0)
        low, high = [
            jnp.concatenate(
                z_ends(part[at, TILE_SIDE : TILE_SIDE + 1], part[at, :TILE_SIDE], 0), axis=0
            )[:, None]
            for part in (below, above)
        ]
        spare = jnp.zeros((TILE_SIDE + 2, 6, FINE_WIDTH), plane.dtype)
        ends.append(jnp.concatenate([plane, high, spare, low], axis=1))
    outer = jnp.stack(x_layers(*ends))

    bias = jnp.sum(jnp.where(order, fine_bias[:, None], 0.0), axis=0)
    windows, taps = make_windows(
        inside,
        block,
        layer,
        below,
        above,
        outer,
        cond_scale[None],
        cond_shift[None],
        fine_weight.reshape(27, FINE_WIDTH, FINE_WIDTH),
        order.astype(jnp.bfloat16),
    )
    bias = jnp.concatenate([bias, bias])[None]
    half = STRIDE // 2
    early = convolve(windows, taps, bias, 0, half)
    late = convolve(windows, taps, bias, half, half)
    columns = ring_pieces(piece, [taps, early, late]) if by_ring else [whole_columns(proj_weight)]
    coarse = project(place, early, late, columns, by_ring, proj_bias[None])

    grid = coarse[:ROWS].reshape(CELLS, 2, ACROSS, ACROSS, width)
    field = with_halos(grid, 2, 3, 0)
    terms = bottle_terms(place, field, bottle_weight, chans)
    terms = exchange(lambda distance: terms[distance])
    guided = finish(place, guide, terms, bottle_bias[None])
    return guided.reshape(1, ACROSS, ACROSS, CELLS, width)


def solution(mesh):
    placed = (
        P("region", None, None, None, None),
        P(),
        P(),
        P(),
        P(),
        P(("chan", "region"), None),
        P(),
        P(None, "chan", None),
        P(),
        P(),
    )
    return jax.shard_map(
        shards,
        mesh=mesh,
        in_specs=placed,
        out_specs=P("region", None, None, None, "chan"),
        check_vma=False,
    )
```

```python
import functools

import numpy as np

import jax
import jax.numpy as jnp
from jax import lax
from jax.experimental import pallas as pl
from jax.experimental.pallas import tpu as pltpu
from jax.sharding import PartitionSpec as P

FINE_WIDTH = 128
COARSE_WIDTH = 1024
TILE_SIDE = 12
STRIDE = 4
REGIONS_Y = 4
REGIONS_Z = 2

CELLS = TILE_SIDE // STRIDE
ACROSS = 2 * CELLS
PLANE = 2 * ACROSS * ACROSS
ROWS = CELLS * PLANE
PADDED = -(-ROWS // 16) * 16
PHASES = STRIDE + 2
OFFSETS = STRIDE**3
LANES = 128
SPREAD = 8
MIB = 2**20


def vmem(count):
    return [pl.BlockSpec(memory_space=pltpu.VMEM) for _ in range(count)]


def regroup_kernel(*refs):
    rows_refs, out_ref, wide = refs[:-2], refs[-2], refs[-1]
    held = rows_refs[0].shape[0]
    members = wide.shape[1] // OFFSETS
    for lane in range(wide.shape[0]):
        columns = slice(lane * LANES, (lane + 1) * LANES)
        for number, rows_ref in enumerate(rows_refs):
            wide[lane, number * held : (number + 1) * held, :] = rows_ref[:, columns].astype(jnp.float32)
        for pair in range(OFFSETS // 2):
            out_ref[pair, :, columns] = jnp.concatenate(
                [
                    wide[lane, pl.ds(2 * pair + cell, members, stride=OFFSETS), :]
                    for cell in range(2)
                ],
                axis=0,
            ).astype(jnp.bfloat16)


def regroup(pieces):
    held, width = pieces[0].shape
    total = len(pieces) * held
    return pl.pallas_call(
        regroup_kernel,
        out_shape=jax.ShapeDtypeStruct((OFFSETS // 2, 2 * total // OFFSETS, width), jnp.bfloat16),
        in_specs=vmem(len(pieces)),
        out_specs=vmem(1)[0],
        scratch_shapes=[pltpu.VMEM((width // LANES, total, LANES), jnp.float32)],
        compiler_params=pltpu.CompilerParams(vmem_limit_bytes=8 * MIB),
        name="regroup",
    )(*pieces)


def taps_kernel(weight_ref, order_ref, out_ref):
    width = FINE_WIDTH
    for place in range(9):
        both = jnp.dot(
            weight_ref[place * 3 * width : (place + 1) * 3 * width, :],
            order_ref[...],
            preferred_element_type=jnp.float32,
        )
        lower, upper = both[:, : 2 * width], both[:, 2 * width :]
        out_ref[place, :width, :] = lower[:width].astype(jnp.bfloat16)
        out_ref[place, width : 3 * width, :] = (lower[width:] + upper[: 2 * width]).astype(jnp.bfloat16)
        out_ref[place, 3 * width :, :] = upper[2 * width :].astype(jnp.bfloat16)


def make_taps(weight, order):
    width = FINE_WIDTH
    return pl.pallas_call(
        taps_kernel,
        out_shape=jax.ShapeDtypeStruct((9, 4 * width, 2 * width), jnp.bfloat16),
        in_specs=vmem(2),
        out_specs=vmem(1)[0],
        compiler_params=pltpu.CompilerParams(vmem_limit_bytes=12 * MIB),
        name="taps",
    )(weight, order)


def split_kernel(place_ref, rows_ref, *out_refs):
    width = out_refs[0].shape[1]
    for distance, out_ref in enumerate(out_refs):
        start = pl.multiple_of((place_ref[0] ^ distance) * width, width)
        out_ref[...] = rows_ref[:, pl.ds(start, width)]


def split_columns(place, rows, owners):
    held, width = rows.shape[0], rows.shape[1] // owners
    return pl.pallas_call(
        split_kernel,
        out_shape=[jax.ShapeDtypeStruct((held, width), rows.dtype)] * owners,
        in_specs=[pl.BlockSpec(memory_space=pltpu.SMEM)] + vmem(1),
        out_specs=vmem(owners),
        compiler_params=pltpu.CompilerParams(vmem_limit_bytes=4 * MIB),
        name="split_columns",
    )(place, rows)


def faces_kernel(upper_ref, layer_ref, first_ref, last_ref, face_ref, low_ref, high_ref, wide):
    face_ref[...] = layer_ref[:, 0]

    def take(at_x, carry):
        for rows_ref, row, out_ref in ((first_ref, 0, low_ref), (last_ref, 7, high_ref)):
            for at_z in range(TILE_SIDE):
                wide[at_z : at_z + 1, :] = rows_ref[at_x, at_z].astype(jnp.float32)[row : row + 1]
            out_ref[at_x] = wide[...].astype(jnp.bfloat16)
        return carry

    wide[...] = jnp.zeros_like(wide)
    lax.fori_loop(0, layer_ref.shape[0], take, 0)


def faces(upper, block):
    side_x, depth, side_y, width = block.shape
    return pl.pallas_call(
        faces_kernel,
        out_shape=(
            jax.ShapeDtypeStruct((side_x, side_y, width), block.dtype),
            jax.ShapeDtypeStruct((side_x, 16, width), block.dtype),
            jax.ShapeDtypeStruct((side_x, 16, width), block.dtype),
        ),
        grid_spec=pltpu.PrefetchScalarGridSpec(
            num_scalar_prefetch=1,
            grid=(1,),
            in_specs=[
                pl.BlockSpec(
                    (side_x, 1, side_y, width), lambda i, upper: (0, (1 - upper[0]) * (depth - 1), 0, 0)
                ),
                pl.BlockSpec((side_x, depth, 8, width), lambda i, upper: (0, 0, 0, 0)),
                pl.BlockSpec((side_x, depth, 8, width), lambda i, upper: (0, 0, side_y // 8 - 1, 0)),
            ],
            out_specs=(
                pl.BlockSpec((side_x, side_y, width), lambda i, upper: (0, 0, 0)),
                pl.BlockSpec((side_x, 16, width), lambda i, upper: (0, 0, 0)),
                pl.BlockSpec((side_x, 16, width), lambda i, upper: (0, 0, 0)),
            ),
            scratch_shapes=[pltpu.VMEM((16, width), jnp.float32)],
        ),
        compiler_params=pltpu.CompilerParams(vmem_limit_bytes=12 * MIB),
        name="faces",
    )(upper, block, block, block)


def window_kernel(
    inside_ref, block_ref, layer_ref, below_ref, above_ref, outer_ref, scale_ref, shift_ref,
    windows_ref, rows, line, layers,
):
    phase_x = pl.program_id(0)
    side, depth, width = 2 * TILE_SIDE, TILE_SIDE, FINE_WIDTH
    half = 2 * ACROSS * side

    @pl.when(phase_x == 0)
    def _():
        def widen(at_x, carry):
            rows[0, at_x] = below_ref[at_x].astype(jnp.float32)
            rows[1, at_x] = above_ref[at_x].astype(jnp.float32)
            return carry

        lax.fori_loop(0, side, widen, 0)

    scale = jnp.broadcast_to(scale_ref[...], (8, width))
    shift = jnp.broadcast_to(shift_ref[...], (8, width))
    row = lax.broadcasted_iota(jnp.int32, (8, width), 0)
    first = jnp.where(row == 0, shift * inside_ref[2], shift)
    last = jnp.where(row == side + 1 - 20, shift * inside_ref[3], shift)
    chunks = [(0, first), (8, shift), (16, shift), (4, shift), (12, shift), (20, last)]

    def split(cell_x, carry):
        at_x = phase_x + STRIDE * cell_x
        outside = jnp.logical_or(at_x == 0, at_x == side + 1)

        @pl.when(jnp.logical_not(outside))
        def _():
            at = at_x - 1
            for at_z in range(depth + 2):
                if at_z == 0:
                    flag, value, place = inside_ref[4], layer_ref[at], depth
                elif at_z == depth + 1:
                    flag, value, place = inside_ref[5], layer_ref[at], depth
                else:
                    flag, value, place = None, block_ref[at, at_z - 1], at_z - 1
                value = value.astype(jnp.float32)
                low, high = rows[0, at, place : place + 1, :], rows[1, at, place : place + 1, :]
                if flag is not None:
                    value, low, high = value * flag, low * flag, high * flag
                line[at_z, 7:8, :] = low
                line[at_z, 8 : side + 8, :] = value
                line[at_z, side + 8 : side + 9, :] = high

        @pl.when(outside)
        def _():
            end = jnp.where(at_x == 0, 0, 1)
            for at_z in range(depth + 2):
                value = outer_ref[end, at_z].astype(jnp.float32)
                line[at_z, 0:8, :] = value[side : side + 8]
                line[at_z, 8 : side + 8, :] = value[:side]
                line[at_z, side + 8 : side + 16, :] = value[side : side + 8]

        within = jnp.where(at_x == 0, inside_ref[0], 1.0)
        within = jnp.where(at_x == side + 1, inside_ref[1], within)
        for at_z in range(depth + 2):
            if at_z == 0:
                factor = within * inside_ref[4]
            elif at_z == depth + 1:
                factor = within * inside_ref[5]
            else:
                factor = within
            for number, (start, added) in enumerate(chunks):
                value = line[at_z, pl.ds(start + 7, 8), :]
                base = number // 3 * half + number % 3 * 8
                base = pl.multiple_of(base + cell_x * side, 8)
                layers[at_z, pl.ds(base, 8), :] = value
                layers[at_z, pl.ds(base + half // 2, 8), :] = value * scale + added * factor
        return carry

    lax.fori_loop(0, ACROSS, split, 0)
    for phase_y in range(PHASES):
        start = phase_y if phase_y < STRIDE else half + phase_y - STRIDE
        for phase_z in range(PHASES):
            parts = [
                layers[phase_z + STRIDE * cell, pl.ds(start, PLANE, stride=STRIDE), :]
                for cell in range(CELLS)
            ]
            parts.append(jnp.zeros((PADDED - ROWS, width), jnp.float32))
            windows_ref[0, phase_y, :, phase_z * width : (phase_z + 1) * width] = jnp.concatenate(
                parts, axis=0
            ).astype(jnp.bfloat16)


def make_windows(inside, *arrays):
    width, side = FINE_WIDTH, 2 * TILE_SIDE

    def whole(array):
        return pl.BlockSpec(array.shape, lambda i: (0,) * array.ndim)

    return pl.pallas_call(
        window_kernel,
        out_shape=jax.ShapeDtypeStruct((PHASES, PHASES, PADDED, PHASES * width), jnp.bfloat16),
        grid=(PHASES,),
        in_specs=[pl.BlockSpec(memory_space=pltpu.SMEM)] + [whole(array) for array in arrays],
        out_specs=pl.BlockSpec((1, PHASES, PADDED, PHASES * width), lambda i: (i, 0, 0, 0)),
        scratch_shapes=[
            pltpu.VMEM((2, side, 16, width), jnp.float32),
            pltpu.VMEM((TILE_SIDE + 2, side + 16, width), jnp.float32),
            pltpu.VMEM((TILE_SIDE + 2, 4 * ACROSS * side, width), jnp.float32),
        ],
        compiler_params=pltpu.CompilerParams(vmem_limit_bytes=28 * MIB),
        cost_estimate=pl.CostEstimate(flops=10**10, bytes_accessed=16 * MIB, transcendentals=0),
        name="windows",
    )(inside, *arrays)


def convolve_kernel(first_ref, second_ref, third_ref, taps_ref, bias_ref, out_ref):
    width = FINE_WIDTH
    bias = bias_ref[...]

    def convolve(at_y, carry):
        total = jnp.zeros((2 * PADDED, 2 * width), jnp.float32)
        for step_x, windows_ref in enumerate((first_ref, second_ref, third_ref)):
            for step_y in range(3):
                taken = [
                    windows_ref[0, at_y + step_y, :, pair * 2 * width : (pair * 2 + 4) * width]
                    for pair in range(2)
                ]
                total += jnp.dot(
                    jnp.concatenate(taken, axis=0),
                    taps_ref[step_x * 3 + step_y],
                    preferred_element_type=jnp.float32,
                )
        total = total + bias
        hidden = (total / (1.0 + jnp.exp(-total))).astype(jnp.bfloat16)
        for pair in range(2):
            out_ref[at_y * 2 + pair] = hidden[pair * PADDED : (pair + 1) * PADDED]
        return carry

    lax.fori_loop(0, STRIDE, convolve, 0)


def convolve(windows, taps, bias, start, count):
    width = FINE_WIDTH
    each = STRIDE * STRIDE // 2
    block = (1, PHASES, PADDED, PHASES * width)
    return pl.pallas_call(
        convolve_kernel,
        out_shape=jax.ShapeDtypeStruct((count * each, PADDED, 2 * width), jnp.bfloat16),
        grid=(count,),
        in_specs=[
            pl.BlockSpec(block, lambda i, step=step: (i + start + step, 0, 0, 0)) for step in range(3)
        ]
        + [
            pl.BlockSpec(taps.shape, lambda i: (0, 0, 0)),
            pl.BlockSpec(bias.shape, lambda i: (0, 0)),
        ],
        out_specs=pl.BlockSpec((each, PADDED, 2 * width), lambda i: (i, 0, 0)),
        compiler_params=pltpu.CompilerParams(vmem_limit_bytes=28 * MIB),
        cost_estimate=pl.CostEstimate(
            flops=2 * count * each * PADDED * 36 * width * 2 * width,
            bytes_accessed=16 * MIB,
            transcendentals=count * each * PADDED * 2 * width,
        ),
        name="convolve",
    )(windows, windows, windows, taps, bias)


def project_kernel(place_ref, early_ref, late_ref, *refs):
    weight_refs, bias_ref, out_ref, total = refs[:-3], refs[-3], refs[-2], refs[-1]
    step = pl.program_id(0)
    width = out_ref.shape[1]

    def product(hidden_ref):
        acc = jnp.zeros(total.shape, jnp.float32)
        for pair in range(hidden_ref.shape[0]):
            weight = jnp.concatenate([ref[pair] for ref in weight_refs], axis=0)
            acc += jnp.dot(hidden_ref[pair], weight, preferred_element_type=jnp.float32)
        return acc

    @pl.when(step == 0)
    def _():
        total[...] = product(early_ref)

    @pl.when(step == 1)
    def _():
        start = pl.multiple_of(place_ref[0] * width, width)
        out_ref[...] = (total[...] + product(late_ref) + bias_ref[:, pl.ds(start, width)]).astype(
            jnp.bfloat16
        )


def project(place, early, late, weights, bias):
    pairs, rows, depth = early.shape
    width = weights[0].shape[2]
    return pl.pallas_call(
        project_kernel,
        out_shape=jax.ShapeDtypeStruct((rows, width), jnp.bfloat16),
        grid=(2,),
        in_specs=[
            pl.BlockSpec(memory_space=pltpu.SMEM),
            pl.BlockSpec(early.shape, lambda i: (0, 0, 0)),
            pl.BlockSpec(late.shape, lambda i: (0, 0, 0)),
        ]
        + [pl.BlockSpec((pairs,) + weight.shape[1:], lambda i: (i, 0, 0)) for weight in weights]
        + [pl.BlockSpec(bias.shape, lambda i: (0, 0))],
        out_specs=pl.BlockSpec((rows, width), lambda i: (0, 0)),
        scratch_shapes=[pltpu.VMEM((rows, width), jnp.float32)],
        compiler_params=pltpu.CompilerParams(vmem_limit_bytes=24 * MIB),
        cost_estimate=pl.CostEstimate(
            flops=4 * pairs * rows * depth * width, bytes_accessed=8 * MIB, transcendentals=0
        ),
        name="project",
    )(place, early, late, *weights, bias)


def bottle_kernel(place_ref, field_ref, weight_ref, own_ref, *refs):
    other_refs, held, total, packed, dense, sems = refs[:-5], *refs[-5:]
    width = field_ref.shape[4]
    share = own_ref.shape[1]
    frame = ACROSS + 2
    rows = CELLS * 2 * ACROSS * frame
    chunk = 256

    def copy_of(step_y, place):
        tap = (place // 3 * 3 + step_y) * 3 + place % 3
        return pltpu.make_async_copy(
            weight_ref.at[tap],
            held.at[step_y, pl.ds(place * width, width)],
            sems.at[step_y, place],
        )

    for step_y in range(3):
        for place in range(9):
            copy_of(step_y, place).start()

    for step_x in range(3):
        for step_z in range(3):
            place = step_x * 3 + step_z
            packed[:, place * width : (place + 1) * width] = (
                field_ref[step_z : step_z + CELLS, :, step_x : step_x + ACROSS]
                .astype(jnp.float32)
                .reshape(rows, width)
                .astype(jnp.bfloat16)
            )

    for step_x in range(3):
        for step_z in range(3):
            copy_of(0, step_x * 3 + step_z).wait()
        depth = slice(step_x * 3 * width, (step_x + 1) * 3 * width)
        for start in range(0, COARSE_WIDTH, chunk):
            columns = slice(start, start + chunk)
            terms = jnp.dot(
                packed[:, depth], held[0, depth, columns], preferred_element_type=jnp.float32
            )
            total[0, :, columns] = terms if step_x == 0 else total[0, :, columns] + terms

    def rest(step_y, carry):
        for place in range(9):
            copy_of(step_y, place).wait()
        for start in range(0, COARSE_WIDTH, chunk):
            columns = slice(start, start + chunk)
            total[step_y, :, columns] = jnp.dot(
                packed[...], held[step_y, :, columns], preferred_element_type=jnp.float32
            )
        return carry

    lax.fori_loop(1, 3, rest, 0)

    for distance, out_ref in enumerate((own_ref,) + other_refs):
        start = pl.multiple_of((place_ref[0] ^ distance) * share, share)
        for group in range(rows // frame):
            at = group * frame
            dense[group * ACROSS : (group + 1) * ACROSS, :] = sum(
                total[item, at + item : at + item + ACROSS, pl.ds(start, share)]
                for item in range(3)
            )
        out_ref[...] = dense[...].astype(out_ref.dtype)


def bottle_terms(place, field, weight, owners):
    frame = ACROSS + 2
    rows = CELLS * 2 * ACROSS * frame
    width = weight.shape[1]
    share = COARSE_WIDTH // owners
    return pl.pallas_call(
        bottle_kernel,
        out_shape=[
            jax.ShapeDtypeStruct((ROWS, share), jnp.bfloat16 if distance else jnp.float32)
            for distance in range(owners)
        ],
        in_specs=[
            pl.BlockSpec(memory_space=pltpu.SMEM),
            pl.BlockSpec(memory_space=pltpu.VMEM),
            pl.BlockSpec(memory_space=pltpu.HBM),
        ],
        out_specs=vmem(owners),
        scratch_shapes=[
            pltpu.VMEM((3, 9 * width, COARSE_WIDTH), jnp.bfloat16),
            pltpu.VMEM((3, rows, COARSE_WIDTH), jnp.float32),
            pltpu.VMEM((rows, 9 * width), jnp.bfloat16),
            pltpu.VMEM((ROWS, share), jnp.float32),
            pltpu.SemaphoreType.DMA((3, 9)),
        ],
        compiler_params=pltpu.CompilerParams(vmem_limit_bytes=51 * MIB),
        cost_estimate=pl.CostEstimate(
            flops=2 * rows * 27 * width * COARSE_WIDTH, bytes_accessed=16 * MIB, transcendentals=0
        ),
        name="bottle_terms",
    )(place, field, weight)


def finish_kernel(place_ref, guide_ref, own_ref, *refs):
    other_refs, bias_ref, out_ref, spread = refs[:-3], refs[-3], refs[-2], refs[-1]
    share = own_ref.shape[1]
    start = pl.multiple_of(place_ref[0] * share, share)
    value = own_ref[...] + bias_ref[:, pl.ds(start, share)]
    for other_ref in other_refs:
        value = value + other_ref[...].astype(jnp.float32)
    value = value / (1.0 + jnp.exp(-value))
    half = PLANE // 2
    for cell in range(CELLS):
        plain = value[cell * PLANE : cell * PLANE + half]
        guided = value[cell * PLANE + half : (cell + 1) * PLANE]
        mixed = plain + guide_ref[0] * (guided - plain)
        for lane in range(spread.shape[0]):
            spread[lane, pl.ds(cell, half, stride=SPREAD), :] = mixed[:, lane * LANES : (lane + 1) * LANES]
    for lane in range(spread.shape[0]):
        for cell in range(half):
            out_ref[cell, :, lane * LANES : (lane + 1) * LANES] = spread[
                lane, cell * SPREAD : cell * SPREAD + CELLS, :
            ].astype(jnp.bfloat16)


def finish(place, guide, terms, bias):
    share = terms[0].shape[1]
    return pl.pallas_call(
        finish_kernel,
        out_shape=jax.ShapeDtypeStruct((PLANE // 2, CELLS, share), jnp.bfloat16),
        in_specs=[pl.BlockSpec(memory_space=pltpu.SMEM)] * 2 + vmem(len(terms) + 1),
        out_specs=vmem(1)[0],
        scratch_shapes=[pltpu.VMEM((share // LANES, PLANE // 2 * SPREAD, LANES), jnp.float32)],
        compiler_params=pltpu.CompilerParams(vmem_limit_bytes=8 * MIB),
        name="finish",
    )(place, guide, *terms, bias)


def passed(value, steps):
    count = lax.axis_size("region")
    return lax.ppermute(
        value, "region", [(at, at + steps) for at in range(max(0, -steps), min(count, count - steps))]
    )


def across_z(value):
    count = lax.axis_size("region")
    return lax.ppermute(value, "region", [(at, at ^ 1) for at in range(count)])


def is_even_y():
    return lax.axis_index("region") // REGIONS_Z % 2 == 0


def y_pairs(first, last):
    count = lax.axis_size("region")
    even = is_even_y()
    arrived = []
    for parity, payload in ((0, jnp.where(even, last, first)), (1, jnp.where(even, first, last))):
        pairs = []
        for at in range(count):
            place = at // REGIONS_Z % REGIONS_Y
            step = 1 if place % 2 == parity else -1
            if 0 <= place + step < REGIONS_Y:
                pairs.append((at, at + step * REGIONS_Z))
        arrived.append(lax.ppermute(payload, "region", pairs))
    return arrived


def y_halos(first, last):
    near, far = y_pairs(first, last)
    even = is_even_y()
    return jnp.where(even, far, near), jnp.where(even, near, far)


def with_halos(value, dim_x, dim_y, dim_z):
    value = jnp.concatenate(z_ends(z_layer(value, dim_z), value, dim_z), axis=dim_z)
    below, above = y_halos(edge(value, dim_y, False), edge(value, dim_y, True))
    value = jnp.concatenate([below, value, above], axis=dim_y)
    low, high = x_layers(edge(value, dim_x, False), edge(value, dim_x, True))
    return jnp.concatenate([low, value, high], axis=dim_x)


def edge(array, dim, last):
    size = array.shape[dim]
    return lax.slice_in_dim(array, size - 1 if last else 0, size if last else 1, axis=dim)


def is_upper():
    return lax.axis_index("region") % REGIONS_Z == 1


def z_layer(value, dim):
    return across_z(jnp.where(is_upper(), edge(value, dim, False), edge(value, dim, True)))


def z_ends(layer, value, dim):
    zero = jnp.zeros_like(layer)
    return [jnp.where(is_upper(), layer, zero), value, jnp.where(is_upper(), zero, layer)]


def x_layers(first, last):
    count = lax.axis_size("region") // (REGIONS_Y * REGIONS_Z)
    if count == 1:
        return jnp.zeros_like(last), jnp.zeros_like(first)
    return passed(last, REGIONS_Y * REGIONS_Z), passed(first, -REGIONS_Y * REGIONS_Z)


def exchange(piece_at):
    chans = lax.axis_size("chan")
    return [piece_at(0)] + [
        lax.ppermute(piece_at(distance), "chan", [(at, at ^ distance) for at in range(chans)])
        for distance in range(1, chans)
    ]


def ring_of(count):
    return list(range(0, count, 2)) + list(range(1, count, 2))[::-1]


def hop(value, ahead):
    ring = ring_of(lax.axis_size("region"))
    following = ring[1:] + ring[:1]
    return lax.ppermute(value, "region", list(zip(ring, following) if ahead else zip(following, ring)))


def after(value, other):
    return lax.optimization_barrier((value, other))[0]


def piece_lanes(each):
    chans, regions = lax.axis_size("chan"), lax.axis_size("region")
    ring = ring_of(regions)
    shifts = [0]
    for step in range(1, regions // 2 + 1):
        shifts += [-step] + [step] * (step < regions // 2)
    origin = np.array(
        [[ring[(ring.index(region) + shift) % regions] for shift in shifts] for region in range(regions)]
    )
    table = np.zeros((chans, regions, regions, 2, 2, chans // 2, each), np.int32)
    cells = np.zeros(table.shape[2:], np.int32)
    cells[:, :, 1] = 1
    for chan in range(chans):
        for distance in range(chans):
            half, member = divmod(distance, chans // 2)
            first = (chan ^ distance) * regions + origin
            table[chan, :, :, half, :, member] = (first[:, :, None] * each + np.arange(each))[:, :, None]
    table = jnp.asarray(table.reshape(chans * regions, 2 * FINE_WIDTH))
    device = lax.axis_index("chan") * regions + lax.axis_index("region")
    return lax.dynamic_index_in_dim(table, device, 0, keepdims=True), jnp.asarray(cells.reshape(1, -1))


def relay(values, *others):
    ahead, back = (after(value, others) if others else value for value in values)
    return hop(ahead, True), hop(back, False)


def whole_columns(proj_weight):
    chans, held = lax.axis_size("chan"), proj_weight.shape[0]
    width = COARSE_WIDTH // chans
    mine = lax.all_to_all(proj_weight, "chan", split_axis=1, concat_axis=0, tiled=True)
    whole = lax.all_gather(mine.reshape(chans, held, width), "region", axis=1, tiled=True)
    whole = whole.reshape(FINE_WIDTH, OFFSETS, width).transpose(1, 0, 2)
    return whole.reshape(OFFSETS // 2, 2 * FINE_WIDTH, width)


def shards(
    latent,
    cond_scale,
    cond_shift,
    fine_weight,
    fine_bias,
    proj_weight,
    proj_bias,
    bottle_weight,
    bottle_bias,
    guide,
):
    chans = lax.axis_size("chan")
    chan_place = lax.axis_index("chan")
    region = lax.axis_index("region")
    width = COARSE_WIDTH // chans
    side = 2 * TILE_SIDE
    count_x = lax.axis_size("region") // (REGIONS_Y * REGIONS_Z)
    steps = (REGIONS_Y * REGIONS_Z, REGIONS_Z, 1)
    counts = (count_x, REGIONS_Y, REGIONS_Z)
    places = [region // step % count for step, count in zip(steps, counts)]
    inside = jnp.stack(
        [
            flag
            for place, count in zip(places, counts)
            for flag in ((place > 0).astype(jnp.float32), (place < count - 1).astype(jnp.float32))
        ]
    )

    place = chan_place[None]
    each, rest = divmod(proj_weight.shape[0], OFFSETS)
    by_ring = rest == 0 and chans * each % 16 == 0 and lax.axis_size("region") >= 8
    if by_ring:
        split = split_columns(place, proj_weight, chans)
        mine = exchange(lambda distance: split[distance])
        halves = [regroup(mine[: chans // 2])]
        one = relay((halves[0], halves[0]))
        halves.append(regroup([after(value, one) for value in mine[chans // 2 :]]))
        two = relay((halves[1], halves[1]))
        channel, cell = piece_lanes(each)
    else:
        lanes = jnp.arange(2 * FINE_WIDTH, dtype=jnp.int32)[None]
        channel, cell = lanes % FINE_WIDTH, lanes // FINE_WIDTH
    order = lax.broadcasted_iota(jnp.int32, (FINE_WIDTH, 2 * FINE_WIDTH), 0) == channel
    taps = make_taps(
        fine_weight.reshape(27 * FINE_WIDTH, FINE_WIDTH),
        jnp.concatenate([order & (cell == 0), order & (cell == 1)], axis=1).astype(jnp.bfloat16),
    )
    bias = jnp.sum(jnp.where(order, fine_bias[:, None], 0.0), axis=0)[None]

    block = latent[0].transpose(0, 2, 1, 3)
    upper = is_upper().astype(jnp.int32)[None]
    face, first, last = faces(upper, block)
    layer = across_z(face)
    corner = lax.broadcasted_iota(jnp.int32, first.shape, 1) == TILE_SIDE
    below, above = y_halos(
        jnp.where(corner, layer[:, :1], first), jnp.where(corner, layer[:, -1:], last)
    )
    ends = []
    for at in (0, -1):
        plane = jnp.concatenate(z_ends(layer[at][None], block[at], 0), axis=0)
        low, high = [
            jnp.concatenate(
                z_ends(part[at, TILE_SIDE : TILE_SIDE + 1], part[at, :TILE_SIDE], 0), axis=0
            )[:, None]
            for part in (below, above)
        ]
        spare = jnp.zeros((TILE_SIDE + 2, 6, FINE_WIDTH), plane.dtype)
        ends.append(jnp.concatenate([plane, high, spare, low], axis=1))
    outer = jnp.stack(x_layers(*ends))

    half = STRIDE // 2
    arrays = [block, layer, below, above, outer, cond_scale[None], cond_shift[None]]
    if by_ring:
        columns = list(halves)
        windows = make_windows(inside, *arrays)
        early = late = None
        for step in range(1, lax.axis_size("region") // 2):
            columns += [one[0], two[0], one[1], two[1]]
            if step == 1:
                held = one + two
                one, two = relay(one, windows), relay(two, windows)
                early = convolve(windows, taps, after(bias, held), 0, half)
            elif step == 2:
                held = one + two
                one, two = relay(one, early), relay(two, early)
                late = convolve(windows, taps, after(bias, held), half, half)
            elif step < lax.axis_size("region") // 2 - 1:
                one, two = relay(one), relay(two)
        last = after(one[0], (late, one, two)), after(two[1], (late, one, two))
        columns += [hop(last[0], True), hop(last[1], False)]
    else:
        windows = make_windows(inside, *arrays)
        early = convolve(windows, taps, bias, 0, half)
        late = convolve(windows, taps, bias, half, half)
        columns = [whole_columns(proj_weight)]
    coarse = project(place, early, late, columns, proj_bias[None])

    grid = coarse[:ROWS].reshape(CELLS, 2, ACROSS, ACROSS, width)
    field = with_halos(grid, 2, 3, 0)
    terms = bottle_terms(place, field, bottle_weight, chans)
    terms = exchange(lambda distance: terms[distance])
    guided = finish(place, guide, terms, bottle_bias[None])
    return guided.reshape(1, ACROSS, ACROSS, CELLS, width)


def solution(mesh):
    placed = (
        P("region", None, None, None, None),
        P(),
        P(),
        P(),
        P(),
        P(("chan", "region"), None),
        P(),
        P(None, "chan", None),
        P(),
        P(),
    )
    return jax.shard_map(
        shards,
        mesh=mesh,
        in_specs=placed,
        out_specs=P("region", None, None, None, "chan"),
        check_vma=False,
    )
```

```python
import functools

import numpy as np

import jax
import jax.numpy as jnp
from jax import lax
from jax.experimental import pallas as pl
from jax.experimental.pallas import tpu as pltpu
from jax.sharding import PartitionSpec as P

FINE_WIDTH = 128
COARSE_WIDTH = 1024
TILE_SIDE = 12
STRIDE = 4
REGIONS_Y = 4
REGIONS_Z = 2

CELLS = TILE_SIDE // STRIDE
ACROSS = 2 * CELLS
PLANE = 2 * ACROSS * ACROSS
ROWS = CELLS * PLANE
PADDED = -(-ROWS // 16) * 16
PHASES = STRIDE + 2
OFFSETS = STRIDE**3
LANES = 128
SPREAD = 8
MIB = 2**20


def vmem(count):
    return [pl.BlockSpec(memory_space=pltpu.VMEM) for _ in range(count)]


def regroup_kernel(*refs):
    rows_refs, out_ref, wide = refs[:-2], refs[-2], refs[-1]
    held = rows_refs[0].shape[0]
    groups = out_ref.shape[1]
    for lane in range(wide.shape[0]):
        columns = slice(lane * LANES, (lane + 1) * LANES)
        for number, rows_ref in enumerate(rows_refs):
            wide[lane, number * held : (number + 1) * held, :] = rows_ref[:, columns].astype(jnp.float32)
        for offset in range(OFFSETS):
            out_ref[offset, :, columns] = wide[
                lane, pl.ds(offset, groups, stride=OFFSETS), :
            ].astype(jnp.bfloat16)


def regroup(pieces):
    held, width = pieces[0].shape
    total = len(pieces) * held
    return pl.pallas_call(
        regroup_kernel,
        out_shape=jax.ShapeDtypeStruct((OFFSETS, total // OFFSETS, width), jnp.bfloat16),
        in_specs=vmem(len(pieces)),
        out_specs=vmem(1)[0],
        scratch_shapes=[pltpu.VMEM((width // LANES, total, LANES), jnp.float32)],
        compiler_params=pltpu.CompilerParams(vmem_limit_bytes=8 * MIB),
        name="regroup",
    )(*pieces)


def split_kernel(place_ref, rows_ref, *out_refs):
    width = out_refs[0].shape[1]
    for distance, out_ref in enumerate(out_refs):
        start = pl.multiple_of((place_ref[0] ^ distance) * width, width)
        out_ref[...] = rows_ref[:, pl.ds(start, width)]


def split_columns(place, rows, owners):
    held, width = rows.shape[0], rows.shape[1] // owners
    return pl.pallas_call(
        split_kernel,
        out_shape=[jax.ShapeDtypeStruct((held, width), rows.dtype)] * owners,
        in_specs=[pl.BlockSpec(memory_space=pltpu.SMEM)] + vmem(1),
        out_specs=vmem(owners),
        compiler_params=pltpu.CompilerParams(vmem_limit_bytes=4 * MIB),
        name="split_columns",
    )(place, rows)


def face_kernel(upper_ref, layer_ref, face_ref):
    face_ref[...] = layer_ref[:, 0]


def z_face(upper, block):
    side_x, depth, side_y, width = block.shape
    return pl.pallas_call(
        face_kernel,
        out_shape=jax.ShapeDtypeStruct((side_x, side_y, width), block.dtype),
        grid_spec=pltpu.PrefetchScalarGridSpec(
            num_scalar_prefetch=1,
            grid=(1,),
            in_specs=[
                pl.BlockSpec(
                    (side_x, 1, side_y, width), lambda i, upper: (0, (1 - upper[0]) * (depth - 1), 0, 0)
                )
            ],
            out_specs=pl.BlockSpec((side_x, side_y, width), lambda i, upper: (0, 0, 0)),
        ),
        compiler_params=pltpu.CompilerParams(vmem_limit_bytes=60 * MIB),
        name="z_face",
    )(upper, block)


def rows_kernel(first_ref, last_ref, low_ref, high_ref, wide):
    def take(at_x, carry):
        for rows_ref, row, out_ref in ((first_ref, 0, low_ref), (last_ref, 7, high_ref)):
            for at_z in range(TILE_SIDE):
                wide[at_z : at_z + 1, :] = rows_ref[at_x, at_z].astype(jnp.float32)[row : row + 1]
            out_ref[at_x] = wide[...].astype(jnp.bfloat16)
        return carry

    wide[...] = jnp.zeros_like(wide)
    lax.fori_loop(0, first_ref.shape[0], take, 0)


def y_rows(block):
    side_x, depth, side_y, width = block.shape
    return pl.pallas_call(
        rows_kernel,
        out_shape=(
            jax.ShapeDtypeStruct((side_x, 16, width), block.dtype),
            jax.ShapeDtypeStruct((side_x, 16, width), block.dtype),
        ),
        grid=(1,),
        in_specs=[
            pl.BlockSpec((side_x, depth, 8, width), lambda i: (0, 0, 0, 0)),
            pl.BlockSpec((side_x, depth, 8, width), lambda i: (0, 0, side_y // 8 - 1, 0)),
        ],
        out_specs=(
            pl.BlockSpec((side_x, 16, width), lambda i: (0, 0, 0)),
            pl.BlockSpec((side_x, 16, width), lambda i: (0, 0, 0)),
        ),
        scratch_shapes=[pltpu.VMEM((16, width), jnp.float32)],
        compiler_params=pltpu.CompilerParams(vmem_limit_bytes=12 * MIB),
        name="y_rows",
    )(block, block)


def window_kernel(
    inside_ref, block_ref, layer_ref, below_ref, above_ref, outer_ref, scale_ref, shift_ref,
    weight_ref, order_ref, windows_ref, taps_ref, rows, line, layers,
):
    phase_x = pl.program_id(0)
    side, depth, width = 2 * TILE_SIDE, TILE_SIDE, FINE_WIDTH
    half = 2 * ACROSS * side

    @pl.when(phase_x == 0)
    def _():
        zero = jnp.zeros((width, width), jnp.bfloat16)
        for place in range(9):
            taps_ref[place, 3 * width :, :width] = zero
            taps_ref[place, :width, width:] = zero
            for step in range(3):
                block = jnp.dot(
                    weight_ref[place * 3 + step], order_ref[...], preferred_element_type=jnp.float32
                ).astype(jnp.bfloat16)
                taps_ref[place, step * width : (step + 1) * width, :width] = block
                taps_ref[place, (step + 1) * width : (step + 2) * width, width:] = block

        def widen(at_x, carry):
            rows[0, at_x] = below_ref[at_x].astype(jnp.float32)
            rows[1, at_x] = above_ref[at_x].astype(jnp.float32)
            return carry

        lax.fori_loop(0, side, widen, 0)

    scale = jnp.broadcast_to(scale_ref[...], (8, width))
    shift = jnp.broadcast_to(shift_ref[...], (8, width))
    row = lax.broadcasted_iota(jnp.int32, (8, width), 0)
    first = jnp.where(row == 0, shift * inside_ref[2], shift)
    last = jnp.where(row == side + 1 - 20, shift * inside_ref[3], shift)
    chunks = [(0, first), (8, shift), (16, shift), (4, shift), (12, shift), (20, last)]

    def split(cell_x, carry):
        at_x = phase_x + STRIDE * cell_x
        outside = jnp.logical_or(at_x == 0, at_x == side + 1)

        @pl.when(jnp.logical_not(outside))
        def _():
            at = at_x - 1
            for at_z in range(depth + 2):
                if at_z == 0:
                    flag, value, place = inside_ref[4], layer_ref[at], depth
                elif at_z == depth + 1:
                    flag, value, place = inside_ref[5], layer_ref[at], depth
                else:
                    flag, value, place = None, block_ref[at, at_z - 1], at_z - 1
                value = value.astype(jnp.float32)
                low, high = rows[0, at, place : place + 1, :], rows[1, at, place : place + 1, :]
                if flag is not None:
                    value, low, high = value * flag, low * flag, high * flag
                line[at_z, 7:8, :] = low
                line[at_z, 8 : side + 8, :] = value
                line[at_z, side + 8 : side + 9, :] = high

        @pl.when(outside)
        def _():
            end = jnp.where(at_x == 0, 0, 1)
            for at_z in range(depth + 2):
                value = outer_ref[end, at_z].astype(jnp.float32)
                line[at_z, 0:8, :] = value[side : side + 8]
                line[at_z, 8 : side + 8, :] = value[:side]
                line[at_z, side + 8 : side + 16, :] = value[side : side + 8]

        within = jnp.where(at_x == 0, inside_ref[0], 1.0)
        within = jnp.where(at_x == side + 1, inside_ref[1], within)
        for at_z in range(depth + 2):
            if at_z == 0:
                factor = within * inside_ref[4]
            elif at_z == depth + 1:
                factor = within * inside_ref[5]
            else:
                factor = within
            for number, (start, added) in enumerate(chunks):
                value = line[at_z, pl.ds(start + 7, 8), :]
                base = number // 3 * half + number % 3 * 8
                base = pl.multiple_of(base + cell_x * side, 8)
                layers[at_z, pl.ds(base, 8), :] = value
                layers[at_z, pl.ds(base + half // 2, 8), :] = value * scale + added * factor
        return carry

    lax.fori_loop(0, ACROSS, split, 0)
    for phase_y in range(PHASES):
        start = phase_y if phase_y < STRIDE else half + phase_y - STRIDE
        for phase_z in range(PHASES):
            parts = [
                layers[phase_z + STRIDE * cell, pl.ds(start, PLANE, stride=STRIDE), :]
                for cell in range(CELLS)
            ]
            parts.append(jnp.zeros((PADDED - ROWS, width), jnp.float32))
            windows_ref[0, phase_y, :, phase_z * width : (phase_z + 1) * width] = jnp.concatenate(
                parts, axis=0
            ).astype(jnp.bfloat16)


def make_windows(inside, *arrays):
    width, side = FINE_WIDTH, 2 * TILE_SIDE

    def whole(array):
        return pl.BlockSpec(array.shape, lambda i: (0,) * array.ndim)

    return pl.pallas_call(
        window_kernel,
        out_shape=(
            jax.ShapeDtypeStruct((PHASES, PHASES, PADDED, PHASES * width), jnp.bfloat16),
            jax.ShapeDtypeStruct((9, 4 * width, 2 * width), jnp.bfloat16),
        ),
        grid=(PHASES,),
        in_specs=[pl.BlockSpec(memory_space=pltpu.SMEM)] + [whole(array) for array in arrays],
        out_specs=(
            pl.BlockSpec((1, PHASES, PADDED, PHASES * width), lambda i: (i, 0, 0, 0)),
            pl.BlockSpec((9, 4 * width, 2 * width), lambda i: (0, 0, 0)),
        ),
        scratch_shapes=[
            pltpu.VMEM((2, side, 16, width), jnp.float32),
            pltpu.VMEM((TILE_SIDE + 2, side + 16, width), jnp.float32),
            pltpu.VMEM((TILE_SIDE + 2, 4 * ACROSS * side, width), jnp.float32),
        ],
        compiler_params=pltpu.CompilerParams(vmem_limit_bytes=28 * MIB),
        cost_estimate=pl.CostEstimate(flops=10**10, bytes_accessed=16 * MIB, transcendentals=0),
        name="windows",
    )(inside, *arrays)


def convolve_kernel(first_ref, second_ref, third_ref, taps_ref, bias_ref, out_ref):
    width = FINE_WIDTH
    bias = bias_ref[...]

    def convolve(at_y, carry):
        total = jnp.zeros((2 * PADDED, 2 * width), jnp.float32)
        for step_x, windows_ref in enumerate((first_ref, second_ref, third_ref)):
            for step_y in range(3):
                taken = [
                    windows_ref[0, at_y + step_y, :, pair * 2 * width : (pair * 2 + 4) * width]
                    for pair in range(2)
                ]
                total += jnp.dot(
                    jnp.concatenate(taken, axis=0),
                    taps_ref[step_x * 3 + step_y],
                    preferred_element_type=jnp.float32,
                )
        total = total + bias
        hidden = (total / (1.0 + jnp.exp(-total))).astype(jnp.bfloat16)
        for pair in range(2):
            out_ref[at_y * 2 + pair] = hidden[pair * PADDED : (pair + 1) * PADDED]
        return carry

    lax.fori_loop(0, STRIDE, convolve, 0)


def convolve(windows, taps, bias, start, count):
    width = FINE_WIDTH
    each = STRIDE * STRIDE // 2
    block = (1, PHASES, PADDED, PHASES * width)
    return pl.pallas_call(
        convolve_kernel,
        out_shape=jax.ShapeDtypeStruct((count * each, PADDED, 2 * width), jnp.bfloat16),
        grid=(count,),
        in_specs=[
            pl.BlockSpec(block, lambda i, step=step: (i + start + step, 0, 0, 0)) for step in range(3)
        ]
        + [
            pl.BlockSpec(taps.shape, lambda i: (0, 0, 0)),
            pl.BlockSpec(bias.shape, lambda i: (0, 0)),
        ],
        out_specs=pl.BlockSpec((each, PADDED, 2 * width), lambda i: (i, 0, 0)),
        compiler_params=pltpu.CompilerParams(vmem_limit_bytes=28 * MIB),
        cost_estimate=pl.CostEstimate(
            flops=2 * count * each * PADDED * 36 * width * 2 * width,
            bytes_accessed=16 * MIB,
            transcendentals=count * each * PADDED * 2 * width,
        ),
        name="convolve",
    )(windows, windows, windows, taps, bias)


def project_kernel(split, place_ref, early_ref, late_ref, *refs):
    weight_refs, bias_ref, out_ref, total = refs[:-3], refs[-3], refs[-2], refs[-1]
    step = pl.program_id(0)
    width = out_ref.shape[1]

    def product(hidden_ref, number):
        used = weight_refs[:-2] + (weight_refs[len(weight_refs) - 2 + number],) if split else weight_refs
        acc = jnp.zeros(total.shape, jnp.float32)
        for pair in range(hidden_ref.shape[0]):
            weight = jnp.concatenate(
                [ref[2 * pair + item] for item in range(2) for ref in used], axis=0
            )
            acc += jnp.dot(hidden_ref[pair], weight, preferred_element_type=jnp.float32)
        return acc

    @pl.when(step == 0)
    def _():
        total[...] = product(early_ref, 0)

    @pl.when(step == 1)
    def _():
        start = pl.multiple_of(place_ref[0] * width, width)
        out_ref[...] = (total[...] + product(late_ref, 1) + bias_ref[:, pl.ds(start, width)]).astype(
            jnp.bfloat16
        )


def project(place, early, late, weights, split, bias):
    pairs, rows, depth = early.shape
    width = weights[0].shape[2]
    return pl.pallas_call(
        functools.partial(project_kernel, split),
        out_shape=jax.ShapeDtypeStruct((rows, width), jnp.bfloat16),
        grid=(2,),
        in_specs=[
            pl.BlockSpec(memory_space=pltpu.SMEM),
            pl.BlockSpec(early.shape, lambda i: (0, 0, 0)),
            pl.BlockSpec(late.shape, lambda i: (0, 0, 0)),
        ]
        + [
            pl.BlockSpec(
                (OFFSETS // 2,) + weight.shape[1:],
                (lambda i: (i, 0, 0)) if weight.shape[0] == OFFSETS else (lambda i: (0, 0, 0)),
            )
            for weight in weights
        ]
        + [pl.BlockSpec(bias.shape, lambda i: (0, 0))],
        out_specs=pl.BlockSpec((rows, width), lambda i: (0, 0)),
        scratch_shapes=[pltpu.VMEM((rows, width), jnp.float32)],
        compiler_params=pltpu.CompilerParams(vmem_limit_bytes=24 * MIB),
        cost_estimate=pl.CostEstimate(
            flops=4 * pairs * rows * depth * width, bytes_accessed=8 * MIB, transcendentals=0
        ),
        name="project",
    )(place, early, late, *weights, bias)


def bottle_kernel(far, place_ref, field_ref, weight_ref, *refs):
    out_refs, (held, total, packed, dense, sems) = refs[:-5], refs[-5:]
    width = field_ref.shape[4]
    share = out_refs[0].shape[1]
    span = held.shape[2]
    frame = ACROSS + 2
    rows = CELLS * 2 * ACROSS * frame
    chunk = 256
    owners = 2 * len(out_refs)
    first = pl.multiple_of((place_ref[0] // len(out_refs) ^ far) * span, span)

    def copy_of(step_y, place):
        tap = (place // 3 * 3 + step_y) * 3 + place % 3
        return pltpu.make_async_copy(
            weight_ref.at[tap, :, pl.ds(first, span)],
            held.at[step_y, pl.ds(place * width, width)],
            sems.at[step_y, place],
        )

    for step_y in range(3):
        for place in range(9):
            copy_of(step_y, place).start()

    for step_x in range(3):
        for step_z in range(3):
            place = step_x * 3 + step_z
            packed[:, place * width : (place + 1) * width] = (
                field_ref[step_z : step_z + CELLS, :, step_x : step_x + ACROSS]
                .astype(jnp.float32)
                .reshape(rows, width)
                .astype(jnp.bfloat16)
            )

    for step_x in range(3):
        for step_z in range(3):
            copy_of(0, step_x * 3 + step_z).wait()
        depth = slice(step_x * 3 * width, (step_x + 1) * 3 * width)
        for start in range(0, span, chunk):
            columns = slice(start, start + chunk)
            terms = jnp.dot(
                packed[:, depth], held[0, depth, columns], preferred_element_type=jnp.float32
            )
            total[0, :, columns] = terms if step_x == 0 else total[0, :, columns] + terms

    def rest(step_y, carry):
        for place in range(9):
            copy_of(step_y, place).wait()
        for start in range(0, span, chunk):
            columns = slice(start, start + chunk)
            total[step_y, :, columns] = jnp.dot(
                packed[...], held[step_y, :, columns], preferred_element_type=jnp.float32
            )
        return carry

    lax.fori_loop(1, 3, rest, 0)

    for number, out_ref in enumerate(out_refs):
        distance = number + far * owners // 2
        start = pl.multiple_of((place_ref[0] ^ distance) % len(out_refs) * share, share)
        for group in range(rows // frame):
            at = group * frame
            dense[group * ACROSS : (group + 1) * ACROSS, :] = sum(
                total[item, at + item : at + item + ACROSS, pl.ds(start, share)]
                for item in range(3)
            )
        out_ref[...] = dense[...].astype(out_ref.dtype)


def bottle_terms(place, field, weight, owners, far):
    frame = ACROSS + 2
    rows = CELLS * 2 * ACROSS * frame
    width = weight.shape[1]
    share = COARSE_WIDTH // owners
    span = COARSE_WIDTH // 2
    return pl.pallas_call(
        functools.partial(bottle_kernel, int(far)),
        out_shape=[
            jax.ShapeDtypeStruct((ROWS, share), jnp.bfloat16 if far or number else jnp.float32)
            for number in range(owners // 2)
        ],
        in_specs=[
            pl.BlockSpec(memory_space=pltpu.SMEM),
            pl.BlockSpec(memory_space=pltpu.VMEM),
            pl.BlockSpec(memory_space=pltpu.HBM),
        ],
        out_specs=vmem(owners // 2),
        scratch_shapes=[
            pltpu.VMEM((3, 9 * width, span), jnp.bfloat16),
            pltpu.VMEM((3, rows, span), jnp.float32),
            pltpu.VMEM((rows, 9 * width), jnp.bfloat16),
            pltpu.VMEM((ROWS, share), jnp.float32),
            pltpu.SemaphoreType.DMA((3, 9)),
        ],
        compiler_params=pltpu.CompilerParams(vmem_limit_bytes=51 * MIB),
        cost_estimate=pl.CostEstimate(
            flops=2 * rows * 27 * width * span, bytes_accessed=8 * MIB, transcendentals=0
        ),
        name="bottle_far" if far else "bottle_near",
    )(place, field, weight)


def finish_kernel(place_ref, guide_ref, own_ref, *refs):
    other_refs, bias_ref, out_ref, spread = refs[:-3], refs[-3], refs[-2], refs[-1]
    share = own_ref.shape[1]
    start = pl.multiple_of(place_ref[0] * share, share)
    value = own_ref[...] + bias_ref[:, pl.ds(start, share)]
    for other_ref in other_refs:
        value = value + other_ref[...].astype(jnp.float32)
    value = value / (1.0 + jnp.exp(-value))
    half = PLANE // 2
    for cell in range(CELLS):
        plain = value[cell * PLANE : cell * PLANE + half]
        guided = value[cell * PLANE + half : (cell + 1) * PLANE]
        mixed = plain + guide_ref[0] * (guided - plain)
        for lane in range(spread.shape[0]):
            spread[lane, pl.ds(cell, half, stride=SPREAD), :] = mixed[:, lane * LANES : (lane + 1) * LANES]
    for lane in range(spread.shape[0]):
        for cell in range(half):
            out_ref[cell, :, lane * LANES : (lane + 1) * LANES] = spread[
                lane, cell * SPREAD : cell * SPREAD + CELLS, :
            ].astype(jnp.bfloat16)


def finish(place, guide, terms, bias):
    share = terms[0].shape[1]
    return pl.pallas_call(
        finish_kernel,
        out_shape=jax.ShapeDtypeStruct((PLANE // 2, CELLS, share), jnp.bfloat16),
        in_specs=[pl.BlockSpec(memory_space=pltpu.SMEM)] * 2 + vmem(len(terms) + 1),
        out_specs=vmem(1)[0],
        scratch_shapes=[pltpu.VMEM((share // LANES, PLANE // 2 * SPREAD, LANES), jnp.float32)],
        compiler_params=pltpu.CompilerParams(vmem_limit_bytes=8 * MIB),
        name="finish",
    )(place, guide, *terms, bias)


def passed(value, steps):
    count = lax.axis_size("region")
    return lax.ppermute(
        value, "region", [(at, at + steps) for at in range(max(0, -steps), min(count, count - steps))]
    )


def across_z(value):
    count = lax.axis_size("region")
    return lax.ppermute(value, "region", [(at, at ^ 1) for at in range(count)])


def is_even_y():
    return lax.axis_index("region") // REGIONS_Z % 2 == 0


def y_pairs(first, last):
    count = lax.axis_size("region")
    even = is_even_y()
    arrived = []
    for parity, payload in ((0, jnp.where(even, last, first)), (1, jnp.where(even, first, last))):
        pairs = []
        for at in range(count):
            place = at // REGIONS_Z % REGIONS_Y
            step = 1 if place % 2 == parity else -1
            if 0 <= place + step < REGIONS_Y:
                pairs.append((at, at + step * REGIONS_Z))
        arrived.append(lax.ppermute(payload, "region", pairs))
    return arrived


def y_halos(first, last):
    near, far = y_pairs(first, last)
    even = is_even_y()
    return jnp.where(even, far, near), jnp.where(even, near, far)


def with_halos(value, dim_x, dim_y, dim_z):
    value = jnp.concatenate(z_ends(z_layer(value, dim_z), value, dim_z), axis=dim_z)
    below, above = y_halos(edge(value, dim_y, False), edge(value, dim_y, True))
    value = jnp.concatenate([below, value, above], axis=dim_y)
    low, high = x_layers(edge(value, dim_x, False), edge(value, dim_x, True))
    return jnp.concatenate([low, value, high], axis=dim_x)


def edge(array, dim, last):
    size = array.shape[dim]
    return lax.slice_in_dim(array, size - 1 if last else 0, size if last else 1, axis=dim)


def is_upper():
    return lax.axis_index("region") % REGIONS_Z == 1


def z_layer(value, dim):
    return across_z(jnp.where(is_upper(), edge(value, dim, False), edge(value, dim, True)))


def z_ends(layer, value, dim):
    zero = jnp.zeros_like(layer)
    return [jnp.where(is_upper(), layer, zero), value, jnp.where(is_upper(), zero, layer)]


def x_layers(first, last):
    count = lax.axis_size("region") // (REGIONS_Y * REGIONS_Z)
    if count == 1:
        return jnp.zeros_like(last), jnp.zeros_like(first)
    return passed(last, REGIONS_Y * REGIONS_Z), passed(first, -REGIONS_Y * REGIONS_Z)


def chan_swap(value, distance):
    return lax.ppermute(value, "chan", [(at, at ^ distance) for at in range(lax.axis_size("chan"))])


def exchange(piece_at):
    chans = lax.axis_size("chan")
    return [piece_at(0)] + [chan_swap(piece_at(distance), distance) for distance in range(1, chans)]


def ring_of(count):
    return list(range(0, count, 2)) + list(range(1, count, 2))[::-1]


def hop(value, ahead):
    ring = ring_of(lax.axis_size("region"))
    following = ring[1:] + ring[:1]
    return lax.ppermute(value, "region", list(zip(ring, following) if ahead else zip(following, ring)))


def after(value, other):
    return lax.optimization_barrier((value, other))[0]


def piece_channels(each):
    chans, regions = lax.axis_size("chan"), lax.axis_size("region")
    ring = ring_of(regions)
    shifts = [0]
    for step in range(1, regions // 2 + 1):
        shifts += [-step] + [step] * (step < regions // 2)
    origin = np.array(
        [[ring[(ring.index(region) + shift) % regions] for shift in shifts] for region in range(regions)]
    )
    table = np.zeros((chans, regions, regions, chans, each), np.int32)
    for chan in range(chans):
        for distance in range(chans):
            first = (chan ^ distance) * regions + origin
            table[chan, :, :, distance] = first[:, :, None] * each + np.arange(each)
    table = jnp.asarray(table.reshape(chans * regions, FINE_WIDTH))
    device = lax.axis_index("chan") * regions + lax.axis_index("region")
    return lax.dynamic_index_in_dim(table, device, 0, keepdims=True)


def ring_pieces(piece, milestones):
    regions = lax.axis_size("region")
    forward = backward = piece
    held = [piece]
    for step in range(1, regions // 2 + 1):
        if step > 1 and step - 2 < len(milestones):
            forward, backward = (after(value, milestones[step - 2]) for value in (forward, backward))
        if step == regions // 2:
            held += [hop(forward[: OFFSETS // 2], True), hop(backward[OFFSETS // 2 :], False)]
        else:
            forward, backward = hop(forward, True), hop(backward, False)
            held += [forward, backward]
    return held


def whole_columns(proj_weight):
    chans, held = lax.axis_size("chan"), proj_weight.shape[0]
    width = COARSE_WIDTH // chans
    mine = lax.all_to_all(proj_weight, "chan", split_axis=1, concat_axis=0, tiled=True)
    whole = lax.all_gather(mine.reshape(chans, held, width), "region", axis=1, tiled=True)
    return whole.reshape(FINE_WIDTH, OFFSETS, width).transpose(1, 0, 2)


def shards(
    latent,
    cond_scale,
    cond_shift,
    fine_weight,
    fine_bias,
    proj_weight,
    proj_bias,
    bottle_weight,
    bottle_bias,
    guide,
):
    chans = lax.axis_size("chan")
    chan_place = lax.axis_index("chan")
    region = lax.axis_index("region")
    width = COARSE_WIDTH // chans
    side = 2 * TILE_SIDE
    count_x = lax.axis_size("region") // (REGIONS_Y * REGIONS_Z)
    steps = (REGIONS_Y * REGIONS_Z, REGIONS_Z, 1)
    counts = (count_x, REGIONS_Y, REGIONS_Z)
    places = [region // step % count for step, count in zip(steps, counts)]
    inside = jnp.stack(
        [
            flag
            for place, count in zip(places, counts)
            for flag in ((place > 0).astype(jnp.float32), (place < count - 1).astype(jnp.float32))
        ]
    )

    place = chan_place[None]
    each, rest = divmod(proj_weight.shape[0], OFFSETS)
    by_ring = rest == 0 and chans * each % 16 == 0
    if by_ring:
        split = split_columns(place, proj_weight, chans)
        mine = exchange(lambda distance: split[distance])
        piece = regroup(mine)
        channel = piece_channels(each)
    else:
        channel = jnp.arange(FINE_WIDTH, dtype=jnp.int32)[None]
    order = lax.broadcasted_iota(jnp.int32, (FINE_WIDTH, FINE_WIDTH), 0) == channel

    block = latent[0].transpose(0, 2, 1, 3)
    face = z_face(is_upper().astype(jnp.int32)[None], block)
    first, last = y_rows(block)
    layer = across_z(face)
    corner = lax.broadcasted_iota(jnp.int32, first.shape, 1) == TILE_SIDE
    below, above = y_halos(
        jnp.where(corner, layer[:, :1], first), jnp.where(corner, layer[:, -1:], last)
    )
    ends = []
    for at in (0, -1):
        plane = jnp.concatenate(z_ends(layer[at][None], block[at], 0), axis=0)
        low, high = [
            jnp.concatenate(
                z_ends(part[at, TILE_SIDE : TILE_SIDE + 1], part[at, :TILE_SIDE], 0), axis=0
            )[:, None]
            for part in (below, above)
        ]
        spare = jnp.zeros((TILE_SIDE + 2, 6, FINE_WIDTH), plane.dtype)
        ends.append(jnp.concatenate([plane, high, spare, low], axis=1))
    outer = jnp.stack(x_layers(*ends))

    bias = jnp.sum(jnp.where(order, fine_bias[:, None], 0.0), axis=0)
    windows, taps = make_windows(
        inside,
        block,
        layer,
        below,
        above,
        outer,
        cond_scale[None],
        cond_shift[None],
        fine_weight.reshape(27, FINE_WIDTH, FINE_WIDTH),
        order.astype(jnp.bfloat16),
    )
    bias = jnp.concatenate([bias, bias])[None]
    half = STRIDE // 2
    early = convolve(windows, taps, bias, 0, half)
    late = convolve(windows, taps, bias, half, half)
    columns = ring_pieces(piece, [taps, early, late]) if by_ring else [whole_columns(proj_weight)]
    coarse = project(place, early, late, columns, by_ring, proj_bias[None])

    grid = coarse[:ROWS].reshape(CELLS, 2, ACROSS, ACROSS, width)
    field = with_halos(grid, 2, 3, 0)
    far_sums = bottle_terms(place, field, bottle_weight, chans, True)
    far = [chan_swap(value, chans // 2 + number) for number, value in enumerate(far_sums)]
    own, *near = bottle_terms(after(place, far_sums), field, bottle_weight, chans, False)
    near = [chan_swap(value, 1 + number) for number, value in enumerate(near)]
    terms = [own] + near + far
    guided = finish(place, guide, terms, bottle_bias[None])
    return guided.reshape(1, ACROSS, ACROSS, CELLS, width)


def solution(mesh):
    placed = (
        P("region", None, None, None, None),
        P(),
        P(),
        P(),
        P(),
        P(("chan", "region"), None),
        P(),
        P(None, "chan", None),
        P(),
        P(),
    )
    return jax.shard_map(
        shards,
        mesh=mesh,
        in_specs=placed,
        out_specs=P("region", None, None, None, "chan"),
        check_vma=False,
    )
```

```python
import functools

import numpy as np

import jax
import jax.numpy as jnp
from jax import lax
from jax.experimental import pallas as pl
from jax.experimental.pallas import tpu as pltpu
from jax.sharding import PartitionSpec as P

FINE_WIDTH = 128
COARSE_WIDTH = 1024
TILE_SIDE = 12
STRIDE = 4
REGIONS_Y = 4
REGIONS_Z = 2

CELLS = TILE_SIDE // STRIDE
ACROSS = 2 * CELLS
PLANE = 2 * ACROSS * ACROSS
ROWS = CELLS * PLANE
PADDED = -(-ROWS // 16) * 16
PHASES = STRIDE + 2
OFFSETS = STRIDE**3
LANES = 128
SPREAD = 8
MIB = 2**20


def vmem(count):
    return [pl.BlockSpec(memory_space=pltpu.VMEM) for _ in range(count)]


def regroup_kernel(*refs):
    rows_refs, out_ref, wide = refs[:-2], refs[-2], refs[-1]
    held = rows_refs[0].shape[0]
    groups = out_ref.shape[1]
    for lane in range(wide.shape[0]):
        columns = slice(lane * LANES, (lane + 1) * LANES)
        for number, rows_ref in enumerate(rows_refs):
            wide[lane, number * held : (number + 1) * held, :] = rows_ref[:, columns].astype(jnp.float32)
        for offset in range(OFFSETS):
            out_ref[offset, :, columns] = wide[
                lane, pl.ds(offset, groups, stride=OFFSETS), :
            ].astype(jnp.bfloat16)


def regroup(pieces):
    held, width = pieces[0].shape
    total = len(pieces) * held
    return pl.pallas_call(
        regroup_kernel,
        out_shape=jax.ShapeDtypeStruct((OFFSETS, total // OFFSETS, width), jnp.bfloat16),
        in_specs=vmem(len(pieces)),
        out_specs=vmem(1)[0],
        scratch_shapes=[pltpu.VMEM((width // LANES, total, LANES), jnp.float32)],
        compiler_params=pltpu.CompilerParams(vmem_limit_bytes=8 * MIB),
        name="regroup",
    )(*pieces)


def split_kernel(place_ref, rows_ref, *out_refs):
    width = out_refs[0].shape[1]
    for distance, out_ref in enumerate(out_refs):
        start = pl.multiple_of((place_ref[0] ^ distance) * width, width)
        out_ref[...] = rows_ref[:, pl.ds(start, width)]


def split_columns(place, rows, owners):
    held, width = rows.shape[0], rows.shape[1] // owners
    return pl.pallas_call(
        split_kernel,
        out_shape=[jax.ShapeDtypeStruct((held, width), rows.dtype)] * owners,
        in_specs=[pl.BlockSpec(memory_space=pltpu.SMEM)] + vmem(1),
        out_specs=vmem(owners),
        compiler_params=pltpu.CompilerParams(vmem_limit_bytes=4 * MIB),
        name="split_columns",
    )(place, rows)


def faces_kernel(upper_ref, layer_ref, first_ref, last_ref, face_ref, low_ref, high_ref, wide):
    face_ref[...] = layer_ref[:, 0]

    def take(at_x, carry):
        for rows_ref, row, out_ref in ((first_ref, 0, low_ref), (last_ref, 7, high_ref)):
            for at_z in range(TILE_SIDE):
                wide[at_z : at_z + 1, :] = rows_ref[at_x, at_z].astype(jnp.float32)[row : row + 1]
            out_ref[at_x] = wide[...].astype(jnp.bfloat16)
        return carry

    wide[...] = jnp.zeros_like(wide)
    lax.fori_loop(0, layer_ref.shape[0], take, 0)


def faces(upper, block):
    side_x, depth, side_y, width = block.shape
    return pl.pallas_call(
        faces_kernel,
        out_shape=(
            jax.ShapeDtypeStruct((side_x, side_y, width), block.dtype),
            jax.ShapeDtypeStruct((side_x, 16, width), block.dtype),
            jax.ShapeDtypeStruct((side_x, 16, width), block.dtype),
        ),
        grid_spec=pltpu.PrefetchScalarGridSpec(
            num_scalar_prefetch=1,
            grid=(1,),
            in_specs=[
                pl.BlockSpec(
                    (side_x, 1, side_y, width), lambda i, upper: (0, (1 - upper[0]) * (depth - 1), 0, 0)
                ),
                pl.BlockSpec((side_x, depth, 8, width), lambda i, upper: (0, 0, 0, 0)),
                pl.BlockSpec((side_x, depth, 8, width), lambda i, upper: (0, 0, side_y // 8 - 1, 0)),
            ],
            out_specs=(
                pl.BlockSpec((side_x, side_y, width), lambda i, upper: (0, 0, 0)),
                pl.BlockSpec((side_x, 16, width), lambda i, upper: (0, 0, 0)),
                pl.BlockSpec((side_x, 16, width), lambda i, upper: (0, 0, 0)),
            ),
            scratch_shapes=[pltpu.VMEM((16, width), jnp.float32)],
        ),
        compiler_params=pltpu.CompilerParams(vmem_limit_bytes=12 * MIB),
        name="faces",
    )(upper, block, block, block)


def window_kernel(
    inside_ref, block_ref, layer_ref, below_ref, above_ref, outer_ref, scale_ref, shift_ref,
    weight_ref, order_ref, windows_ref, taps_ref, rows, line, layers,
):
    phase_x = pl.program_id(0)
    side, depth, width = 2 * TILE_SIDE, TILE_SIDE, FINE_WIDTH
    half = 2 * ACROSS * side

    @pl.when(phase_x == 0)
    def _():
        zero = jnp.zeros((width, width), jnp.bfloat16)
        for place in range(9):
            taps_ref[place, 3 * width :, :width] = zero
            taps_ref[place, :width, width:] = zero
            for step in range(3):
                block = jnp.dot(
                    weight_ref[place * 3 + step], order_ref[...], preferred_element_type=jnp.float32
                ).astype(jnp.bfloat16)
                taps_ref[place, step * width : (step + 1) * width, :width] = block
                taps_ref[place, (step + 1) * width : (step + 2) * width, width:] = block

        def widen(at_x, carry):
            rows[0, at_x] = below_ref[at_x].astype(jnp.float32)
            rows[1, at_x] = above_ref[at_x].astype(jnp.float32)
            return carry

        lax.fori_loop(0, side, widen, 0)

    scale = jnp.broadcast_to(scale_ref[...], (8, width))
    shift = jnp.broadcast_to(shift_ref[...], (8, width))
    row = lax.broadcasted_iota(jnp.int32, (8, width), 0)
    first = jnp.where(row == 0, shift * inside_ref[2], shift)
    last = jnp.where(row == side + 1 - 20, shift * inside_ref[3], shift)
    chunks = [(0, first), (8, shift), (16, shift), (4, shift), (12, shift), (20, last)]

    def split(cell_x, carry):
        at_x = phase_x + STRIDE * cell_x
        outside = jnp.logical_or(at_x == 0, at_x == side + 1)

        @pl.when(jnp.logical_not(outside))
        def _():
            at = at_x - 1
            for at_z in range(depth + 2):
                if at_z == 0:
                    flag, value, place = inside_ref[4], layer_ref[at], depth
                elif at_z == depth + 1:
                    flag, value, place = inside_ref[5], layer_ref[at], depth
                else:
                    flag, value, place = None, block_ref[at, at_z - 1], at_z - 1
                value = value.astype(jnp.float32)
                low, high = rows[0, at, place : place + 1, :], rows[1, at, place : place + 1, :]
                if flag is not None:
                    value, low, high = value * flag, low * flag, high * flag
                line[at_z, 7:8, :] = low
                line[at_z, 8 : side + 8, :] = value
                line[at_z, side + 8 : side + 9, :] = high

        @pl.when(outside)
        def _():
            end = jnp.where(at_x == 0, 0, 1)
            for at_z in range(depth + 2):
                value = outer_ref[end, at_z].astype(jnp.float32)
                line[at_z, 0:8, :] = value[side : side + 8]
                line[at_z, 8 : side + 8, :] = value[:side]
                line[at_z, side + 8 : side + 16, :] = value[side : side + 8]

        within = jnp.where(at_x == 0, inside_ref[0], 1.0)
        within = jnp.where(at_x == side + 1, inside_ref[1], within)
        for at_z in range(depth + 2):
            if at_z == 0:
                factor = within * inside_ref[4]
            elif at_z == depth + 1:
                factor = within * inside_ref[5]
            else:
                factor = within
            for number, (start, added) in enumerate(chunks):
                value = line[at_z, pl.ds(start + 7, 8), :]
                base = number // 3 * half + number % 3 * 8
                base = pl.multiple_of(base + cell_x * side, 8)
                layers[at_z, pl.ds(base, 8), :] = value
                layers[at_z, pl.ds(base + half // 2, 8), :] = value * scale + added * factor
        return carry

    lax.fori_loop(0, ACROSS, split, 0)
    for phase_y in range(PHASES):
        start = phase_y if phase_y < STRIDE else half + phase_y - STRIDE
        for phase_z in range(PHASES):
            parts = [
                layers[phase_z + STRIDE * cell, pl.ds(start, PLANE, stride=STRIDE), :]
                for cell in range(CELLS)
            ]
            parts.append(jnp.zeros((PADDED - ROWS, width), jnp.float32))
            windows_ref[0, phase_y, :, phase_z * width : (phase_z + 1) * width] = jnp.concatenate(
                parts, axis=0
            ).astype(jnp.bfloat16)


def make_windows(inside, *arrays):
    width, side = FINE_WIDTH, 2 * TILE_SIDE

    def whole(array):
        return pl.BlockSpec(array.shape, lambda i: (0,) * array.ndim)

    return pl.pallas_call(
        window_kernel,
        out_shape=(
            jax.ShapeDtypeStruct((PHASES, PHASES, PADDED, PHASES * width), jnp.bfloat16),
            jax.ShapeDtypeStruct((9, 4 * width, 2 * width), jnp.bfloat16),
        ),
        grid=(PHASES,),
        in_specs=[pl.BlockSpec(memory_space=pltpu.SMEM)] + [whole(array) for array in arrays],
        out_specs=(
            pl.BlockSpec((1, PHASES, PADDED, PHASES * width), lambda i: (i, 0, 0, 0)),
            pl.BlockSpec((9, 4 * width, 2 * width), lambda i: (0, 0, 0)),
        ),
        scratch_shapes=[
            pltpu.VMEM((2, side, 16, width), jnp.float32),
            pltpu.VMEM((TILE_SIDE + 2, side + 16, width), jnp.float32),
            pltpu.VMEM((TILE_SIDE + 2, 4 * ACROSS * side, width), jnp.float32),
        ],
        compiler_params=pltpu.CompilerParams(vmem_limit_bytes=28 * MIB),
        cost_estimate=pl.CostEstimate(flops=10**10, bytes_accessed=16 * MIB, transcendentals=0),
        name="windows",
    )(inside, *arrays)


def convolve_kernel(first_ref, second_ref, third_ref, taps_ref, bias_ref, out_ref):
    width = FINE_WIDTH
    bias = bias_ref[...]

    def convolve(at_y, carry):
        total = jnp.zeros((2 * PADDED, 2 * width), jnp.float32)
        for step_x, windows_ref in enumerate((first_ref, second_ref, third_ref)):
            for step_y in range(3):
                taken = [
                    windows_ref[0, at_y + step_y, :, pair * 2 * width : (pair * 2 + 4) * width]
                    for pair in range(2)
                ]
                total += jnp.dot(
                    jnp.concatenate(taken, axis=0),
                    taps_ref[step_x * 3 + step_y],
                    preferred_element_type=jnp.float32,
                )
        total = total + bias
        hidden = (total / (1.0 + jnp.exp(-total))).astype(jnp.bfloat16)
        for pair in range(2):
            out_ref[at_y * 2 + pair] = hidden[pair * PADDED : (pair + 1) * PADDED]
        return carry

    lax.fori_loop(0, STRIDE, convolve, 0)


def convolve(windows, taps, bias, start, count):
    width = FINE_WIDTH
    each = STRIDE * STRIDE // 2
    block = (1, PHASES, PADDED, PHASES * width)
    return pl.pallas_call(
        convolve_kernel,
        out_shape=jax.ShapeDtypeStruct((count * each, PADDED, 2 * width), jnp.bfloat16),
        grid=(count,),
        in_specs=[
            pl.BlockSpec(block, lambda i, step=step: (i + start + step, 0, 0, 0)) for step in range(3)
        ]
        + [
            pl.BlockSpec(taps.shape, lambda i: (0, 0, 0)),
            pl.BlockSpec(bias.shape, lambda i: (0, 0)),
        ],
        out_specs=pl.BlockSpec((each, PADDED, 2 * width), lambda i: (i, 0, 0)),
        compiler_params=pltpu.CompilerParams(vmem_limit_bytes=28 * MIB),
        cost_estimate=pl.CostEstimate(
            flops=2 * count * each * PADDED * 36 * width * 2 * width,
            bytes_accessed=16 * MIB,
            transcendentals=count * each * PADDED * 2 * width,
        ),
        name="convolve",
    )(windows, windows, windows, taps, bias)


def project_kernel(split, place_ref, early_ref, late_ref, *refs):
    weight_refs, bias_ref, out_ref, total = refs[:-3], refs[-3], refs[-2], refs[-1]
    step = pl.program_id(0)
    width = out_ref.shape[1]

    def product(hidden_ref, number):
        used = weight_refs[:-2] + (weight_refs[len(weight_refs) - 2 + number],) if split else weight_refs
        acc = jnp.zeros(total.shape, jnp.float32)
        for pair in range(hidden_ref.shape[0]):
            weight = jnp.concatenate(
                [ref[2 * pair + item] for item in range(2) for ref in used], axis=0
            )
            acc += jnp.dot(hidden_ref[pair], weight, preferred_element_type=jnp.float32)
        return acc

    @pl.when(step == 0)
    def _():
        total[...] = product(early_ref, 0)

    @pl.when(step == 1)
    def _():
        start = pl.multiple_of(place_ref[0] * width, width)
        out_ref[...] = (total[...] + product(late_ref, 1) + bias_ref[:, pl.ds(start, width)]).astype(
            jnp.bfloat16
        )


def project(place, early, late, weights, split, bias):
    pairs, rows, depth = early.shape
    width = weights[0].shape[2]
    return pl.pallas_call(
        functools.partial(project_kernel, split),
        out_shape=jax.ShapeDtypeStruct((rows, width), jnp.bfloat16),
        grid=(2,),
        in_specs=[
            pl.BlockSpec(memory_space=pltpu.SMEM),
            pl.BlockSpec(early.shape, lambda i: (0, 0, 0)),
            pl.BlockSpec(late.shape, lambda i: (0, 0, 0)),
        ]
        + [
            pl.BlockSpec(
                (OFFSETS // 2,) + weight.shape[1:],
                (lambda i: (i, 0, 0)) if weight.shape[0] == OFFSETS else (lambda i: (0, 0, 0)),
            )
            for weight in weights
        ]
        + [pl.BlockSpec(bias.shape, lambda i: (0, 0))],
        out_specs=pl.BlockSpec((rows, width), lambda i: (0, 0)),
        scratch_shapes=[pltpu.VMEM((rows, width), jnp.float32)],
        compiler_params=pltpu.CompilerParams(vmem_limit_bytes=24 * MIB),
        cost_estimate=pl.CostEstimate(
            flops=4 * pairs * rows * depth * width, bytes_accessed=8 * MIB, transcendentals=0
        ),
        name="project",
    )(place, early, late, *weights, bias)


def bottle_kernel(far, place_ref, field_ref, weight_ref, *refs):
    out_refs, (held, total, packed, dense, sems) = refs[:-5], refs[-5:]
    width = field_ref.shape[4]
    share = out_refs[0].shape[1]
    span = held.shape[2]
    frame = ACROSS + 2
    rows = CELLS * 2 * ACROSS * frame
    chunk = 256
    owners = 2 * len(out_refs)
    first = pl.multiple_of((place_ref[0] // len(out_refs) ^ far) * span, span)

    def copy_of(step_y, place):
        tap = (place // 3 * 3 + step_y) * 3 + place % 3
        return pltpu.make_async_copy(
            weight_ref.at[tap, :, pl.ds(first, span)],
            held.at[step_y, pl.ds(place * width, width)],
            sems.at[step_y, place],
        )

    for step_y in range(3):
        for place in range(9):
            copy_of(step_y, place).start()

    for step_x in range(3):
        for step_z in range(3):
            place = step_x * 3 + step_z
            packed[:, place * width : (place + 1) * width] = (
                field_ref[step_z : step_z + CELLS, :, step_x : step_x + ACROSS]
                .astype(jnp.float32)
                .reshape(rows, width)
                .astype(jnp.bfloat16)
            )

    for step_x in range(3):
        for step_z in range(3):
            copy_of(0, step_x * 3 + step_z).wait()
        depth = slice(step_x * 3 * width, (step_x + 1) * 3 * width)
        for start in range(0, span, chunk):
            columns = slice(start, start + chunk)
            terms = jnp.dot(
                packed[:, depth], held[0, depth, columns], preferred_element_type=jnp.float32
            )
            total[0, :, columns] = terms if step_x == 0 else total[0, :, columns] + terms

    def rest(step_y, carry):
        for place in range(9):
            copy_of(step_y, place).wait()
        for start in range(0, span, chunk):
            columns = slice(start, start + chunk)
            total[step_y, :, columns] = jnp.dot(
                packed[...], held[step_y, :, columns], preferred_element_type=jnp.float32
            )
        return carry

    lax.fori_loop(1, 3, rest, 0)

    for number, out_ref in enumerate(out_refs):
        distance = number + far * owners // 2
        start = pl.multiple_of((place_ref[0] ^ distance) % len(out_refs) * share, share)
        for group in range(rows // frame):
            at = group * frame
            dense[group * ACROSS : (group + 1) * ACROSS, :] = sum(
                total[item, at + item : at + item + ACROSS, pl.ds(start, share)]
                for item in range(3)
            )
        out_ref[...] = dense[...].astype(out_ref.dtype)


def bottle_terms(place, field, weight, owners, far):
    frame = ACROSS + 2
    rows = CELLS * 2 * ACROSS * frame
    width = weight.shape[1]
    share = COARSE_WIDTH // owners
    span = COARSE_WIDTH // 2
    return pl.pallas_call(
        functools.partial(bottle_kernel, int(far)),
        out_shape=[
            jax.ShapeDtypeStruct((ROWS, share), jnp.bfloat16 if far or number else jnp.float32)
            for number in range(owners // 2)
        ],
        in_specs=[
            pl.BlockSpec(memory_space=pltpu.SMEM),
            pl.BlockSpec(memory_space=pltpu.VMEM),
            pl.BlockSpec(memory_space=pltpu.HBM),
        ],
        out_specs=vmem(owners // 2),
        scratch_shapes=[
            pltpu.VMEM((3, 9 * width, span), jnp.bfloat16),
            pltpu.VMEM((3, rows, span), jnp.float32),
            pltpu.VMEM((rows, 9 * width), jnp.bfloat16),
            pltpu.VMEM((ROWS, share), jnp.float32),
            pltpu.SemaphoreType.DMA((3, 9)),
        ],
        compiler_params=pltpu.CompilerParams(vmem_limit_bytes=51 * MIB),
        cost_estimate=pl.CostEstimate(
            flops=2 * rows * 27 * width * span, bytes_accessed=8 * MIB, transcendentals=0
        ),
        name="bottle_far" if far else "bottle_near",
    )(place, field, weight)


def finish_kernel(place_ref, guide_ref, own_ref, *refs):
    other_refs, bias_ref, out_ref, spread = refs[:-3], refs[-3], refs[-2], refs[-1]
    share = own_ref.shape[1]
    start = pl.multiple_of(place_ref[0] * share, share)
    value = own_ref[...] + bias_ref[:, pl.ds(start, share)]
    for other_ref in other_refs:
        value = value + other_ref[...].astype(jnp.float32)
    value = value / (1.0 + jnp.exp(-value))
    half = PLANE // 2
    for cell in range(CELLS):
        plain = value[cell * PLANE : cell * PLANE + half]
        guided = value[cell * PLANE + half : (cell + 1) * PLANE]
        mixed = plain + guide_ref[0] * (guided - plain)
        for lane in range(spread.shape[0]):
            spread[lane, pl.ds(cell, half, stride=SPREAD), :] = mixed[:, lane * LANES : (lane + 1) * LANES]
    for lane in range(spread.shape[0]):
        for cell in range(half):
            out_ref[cell, :, lane * LANES : (lane + 1) * LANES] = spread[
                lane, cell * SPREAD : cell * SPREAD + CELLS, :
            ].astype(jnp.bfloat16)


def finish(place, guide, terms, bias):
    share = terms[0].shape[1]
    return pl.pallas_call(
        finish_kernel,
        out_shape=jax.ShapeDtypeStruct((PLANE // 2, CELLS, share), jnp.bfloat16),
        in_specs=[pl.BlockSpec(memory_space=pltpu.SMEM)] * 2 + vmem(len(terms) + 1),
        out_specs=vmem(1)[0],
        scratch_shapes=[pltpu.VMEM((share // LANES, PLANE // 2 * SPREAD, LANES), jnp.float32)],
        compiler_params=pltpu.CompilerParams(vmem_limit_bytes=8 * MIB),
        name="finish",
    )(place, guide, *terms, bias)


def passed(value, steps):
    count = lax.axis_size("region")
    return lax.ppermute(
        value, "region", [(at, at + steps) for at in range(max(0, -steps), min(count, count - steps))]
    )


def across_z(value):
    count = lax.axis_size("region")
    return lax.ppermute(value, "region", [(at, at ^ 1) for at in range(count)])


def is_even_y():
    return lax.axis_index("region") // REGIONS_Z % 2 == 0


def y_pairs(first, last):
    count = lax.axis_size("region")
    even = is_even_y()
    arrived = []
    for parity, payload in ((0, jnp.where(even, last, first)), (1, jnp.where(even, first, last))):
        pairs = []
        for at in range(count):
            place = at // REGIONS_Z % REGIONS_Y
            step = 1 if place % 2 == parity else -1
            if 0 <= place + step < REGIONS_Y:
                pairs.append((at, at + step * REGIONS_Z))
        arrived.append(lax.ppermute(payload, "region", pairs))
    return arrived


def y_halos(first, last):
    near, far = y_pairs(first, last)
    even = is_even_y()
    return jnp.where(even, far, near), jnp.where(even, near, far)


def with_halos(value, dim_x, dim_y, dim_z):
    value = jnp.concatenate(z_ends(z_layer(value, dim_z), value, dim_z), axis=dim_z)
    below, above = y_halos(edge(value, dim_y, False), edge(value, dim_y, True))
    value = jnp.concatenate([below, value, above], axis=dim_y)
    low, high = x_layers(edge(value, dim_x, False), edge(value, dim_x, True))
    return jnp.concatenate([low, value, high], axis=dim_x)


def edge(array, dim, last):
    size = array.shape[dim]
    return lax.slice_in_dim(array, size - 1 if last else 0, size if last else 1, axis=dim)


def is_upper():
    return lax.axis_index("region") % REGIONS_Z == 1


def z_layer(value, dim):
    return across_z(jnp.where(is_upper(), edge(value, dim, False), edge(value, dim, True)))


def z_ends(layer, value, dim):
    zero = jnp.zeros_like(layer)
    return [jnp.where(is_upper(), layer, zero), value, jnp.where(is_upper(), zero, layer)]


def x_layers(first, last):
    count = lax.axis_size("region") // (REGIONS_Y * REGIONS_Z)
    if count == 1:
        return jnp.zeros_like(last), jnp.zeros_like(first)
    return passed(last, REGIONS_Y * REGIONS_Z), passed(first, -REGIONS_Y * REGIONS_Z)


def chan_swap(value, distance):
    return lax.ppermute(value, "chan", [(at, at ^ distance) for at in range(lax.axis_size("chan"))])


def exchange(piece_at):
    chans = lax.axis_size("chan")
    return [piece_at(0)] + [chan_swap(piece_at(distance), distance) for distance in range(1, chans)]


def ring_of(count):
    return list(range(0, count, 2)) + list(range(1, count, 2))[::-1]


def hop(value, ahead):
    ring = ring_of(lax.axis_size("region"))
    following = ring[1:] + ring[:1]
    return lax.ppermute(value, "region", list(zip(ring, following) if ahead else zip(following, ring)))


def after(value, other):
    return lax.optimization_barrier((value, other))[0]


def piece_channels(each):
    chans, regions = lax.axis_size("chan"), lax.axis_size("region")
    ring = ring_of(regions)
    shifts = [0]
    for step in range(1, regions // 2 + 1):
        shifts += [-step] + [step] * (step < regions // 2)
    origin = np.array(
        [[ring[(ring.index(region) + shift) % regions] for shift in shifts] for region in range(regions)]
    )
    table = np.zeros((chans, regions, regions, chans, each), np.int32)
    for chan in range(chans):
        for distance in range(chans):
            first = (chan ^ distance) * regions + origin
            table[chan, :, :, distance] = first[:, :, None] * each + np.arange(each)
    table = jnp.asarray(table.reshape(chans * regions, FINE_WIDTH))
    device = lax.axis_index("chan") * regions + lax.axis_index("region")
    return lax.dynamic_index_in_dim(table, device, 0, keepdims=True)


def ring_pieces(piece, milestones):
    regions = lax.axis_size("region")
    forward = backward = piece
    held = [piece]
    for step in range(1, regions // 2 + 1):
        if step > 1 and step - 2 < len(milestones):
            forward, backward = (after(value, milestones[step - 2]) for value in (forward, backward))
        if step == regions // 2:
            held += [hop(forward[: OFFSETS // 2], True), hop(backward[OFFSETS // 2 :], False)]
        else:
            forward, backward = hop(forward, True), hop(backward, False)
            held += [forward, backward]
    return held


def whole_columns(proj_weight):
    chans, held = lax.axis_size("chan"), proj_weight.shape[0]
    width = COARSE_WIDTH // chans
    mine = lax.all_to_all(proj_weight, "chan", split_axis=1, concat_axis=0, tiled=True)
    whole = lax.all_gather(mine.reshape(chans, held, width), "region", axis=1, tiled=True)
    return whole.reshape(FINE_WIDTH, OFFSETS, width).transpose(1, 0, 2)


def shards(
    latent,
    cond_scale,
    cond_shift,
    fine_weight,
    fine_bias,
    proj_weight,
    proj_bias,
    bottle_weight,
    bottle_bias,
    guide,
):
    chans = lax.axis_size("chan")
    chan_place = lax.axis_index("chan")
    region = lax.axis_index("region")
    width = COARSE_WIDTH // chans
    side = 2 * TILE_SIDE
    count_x = lax.axis_size("region") // (REGIONS_Y * REGIONS_Z)
    steps = (REGIONS_Y * REGIONS_Z, REGIONS_Z, 1)
    counts = (count_x, REGIONS_Y, REGIONS_Z)
    places = [region // step % count for step, count in zip(steps, counts)]
    inside = jnp.stack(
        [
            flag
            for place, count in zip(places, counts)
            for flag in ((place > 0).astype(jnp.float32), (place < count - 1).astype(jnp.float32))
        ]
    )

    place = chan_place[None]
    each, rest = divmod(proj_weight.shape[0], OFFSETS)
    by_ring = rest == 0 and chans * each % 16 == 0
    if by_ring:
        split = split_columns(place, proj_weight, chans)
        mine = exchange(lambda distance: split[distance])
        piece = regroup(mine)
        channel = piece_channels(each)
    else:
        channel = jnp.arange(FINE_WIDTH, dtype=jnp.int32)[None]
    order = lax.broadcasted_iota(jnp.int32, (FINE_WIDTH, FINE_WIDTH), 0) == channel

    block = latent[0].transpose(0, 2, 1, 3)
    upper = is_upper().astype(jnp.int32)[None]
    face, first, last = faces(upper, block)
    layer = across_z(face)
    corner = lax.broadcasted_iota(jnp.int32, first.shape, 1) == TILE_SIDE
    below, above = y_halos(
        jnp.where(corner, layer[:, :1], first), jnp.where(corner, layer[:, -1:], last)
    )
    ends = []
    for at in (0, -1):
        plane = jnp.concatenate(z_ends(layer[at][None], block[at], 0), axis=0)
        low, high = [
            jnp.concatenate(
                z_ends(part[at, TILE_SIDE : TILE_SIDE + 1], part[at, :TILE_SIDE], 0), axis=0
            )[:, None]
            for part in (below, above)
        ]
        spare = jnp.zeros((TILE_SIDE + 2, 6, FINE_WIDTH), plane.dtype)
        ends.append(jnp.concatenate([plane, high, spare, low], axis=1))
    outer = jnp.stack(x_layers(*ends))

    bias = jnp.sum(jnp.where(order, fine_bias[:, None], 0.0), axis=0)
    windows, taps = make_windows(
        inside,
        block,
        layer,
        below,
        above,
        outer,
        cond_scale[None],
        cond_shift[None],
        fine_weight.reshape(27, FINE_WIDTH, FINE_WIDTH),
        order.astype(jnp.bfloat16),
    )
    bias = jnp.concatenate([bias, bias])[None]
    half = STRIDE // 2
    early = convolve(windows, taps, bias, 0, half)
    late = convolve(windows, taps, bias, half, half)
    columns = ring_pieces(piece, [taps, early, late]) if by_ring else [whole_columns(proj_weight)]
    coarse = project(place, early, late, columns, by_ring, proj_bias[None])

    grid = coarse[:ROWS].reshape(CELLS, 2, ACROSS, ACROSS, width)
    field = with_halos(grid, 2, 3, 0)
    far = bottle_terms(place, field, bottle_weight, chans, True)
    swapped = [chan_swap(value, chans // 2 + number) for number, value in enumerate(far)]
    own, *near = bottle_terms(after(place, far), field, bottle_weight, chans, False)
    near = [chan_swap(value, 1 + number) for number, value in enumerate(near)]
    terms = [own, sum(value.astype(jnp.float32) for value in swapped)] + near
    guided = finish(place, guide, terms, bottle_bias[None])
    return guided.reshape(1, ACROSS, ACROSS, CELLS, width)


def solution(mesh):
    placed = (
        P("region", None, None, None, None),
        P(),
        P(),
        P(),
        P(),
        P(("chan", "region"), None),
        P(),
        P(None, "chan", None),
        P(),
        P(),
    )
    return jax.shard_map(
        shards,
        mesh=mesh,
        in_specs=placed,
        out_specs=P("region", None, None, None, "chan"),
        check_vma=False,
    )
```

```python
import functools

import numpy as np

import jax
import jax.numpy as jnp
from jax import lax
from jax.experimental import pallas as pl
from jax.experimental.pallas import tpu as pltpu
from jax.sharding import PartitionSpec as P

FINE_WIDTH = 128
COARSE_WIDTH = 1024
TILE_SIDE = 12
STRIDE = 4
REGIONS_Y = 4
REGIONS_Z = 2

CELLS = TILE_SIDE // STRIDE
ACROSS = 2 * CELLS
PLANE = 2 * ACROSS * ACROSS
ROWS = CELLS * PLANE
PADDED = -(-ROWS // 16) * 16
PHASES = STRIDE + 2
OFFSETS = STRIDE**3
LANES = 128
SPREAD = 8
MIB = 2**20


def vmem(count):
    return [pl.BlockSpec(memory_space=pltpu.VMEM) for _ in range(count)]


def regroup_kernel(*refs):
    rows_refs, out_ref, wide = refs[:-2], refs[-2], refs[-1]
    held = rows_refs[0].shape[0]
    groups = out_ref.shape[1]
    for lane in range(wide.shape[0]):
        columns = slice(lane * LANES, (lane + 1) * LANES)
        for number, rows_ref in enumerate(rows_refs):
            wide[lane, number * held : (number + 1) * held, :] = rows_ref[:, columns].astype(jnp.float32)
        for offset in range(OFFSETS):
            out_ref[offset, :, columns] = wide[
                lane, pl.ds(offset, groups, stride=OFFSETS), :
            ].astype(jnp.bfloat16)


def regroup(pieces):
    held, width = pieces[0].shape
    total = len(pieces) * held
    return pl.pallas_call(
        regroup_kernel,
        out_shape=jax.ShapeDtypeStruct((OFFSETS, total // OFFSETS, width), jnp.bfloat16),
        in_specs=vmem(len(pieces)),
        out_specs=vmem(1)[0],
        scratch_shapes=[pltpu.VMEM((width // LANES, total, LANES), jnp.float32)],
        compiler_params=pltpu.CompilerParams(vmem_limit_bytes=8 * MIB),
        name="regroup",
    )(*pieces)


def split_kernel(place_ref, rows_ref, *out_refs):
    width = out_refs[0].shape[1]
    for distance, out_ref in enumerate(out_refs):
        start = pl.multiple_of((place_ref[0] ^ distance) * width, width)
        out_ref[...] = rows_ref[:, pl.ds(start, width)]


def split_columns(place, rows, owners):
    held, width = rows.shape[0], rows.shape[1] // owners
    return pl.pallas_call(
        split_kernel,
        out_shape=[jax.ShapeDtypeStruct((held, width), rows.dtype)] * owners,
        in_specs=[pl.BlockSpec(memory_space=pltpu.SMEM)] + vmem(1),
        out_specs=vmem(owners),
        compiler_params=pltpu.CompilerParams(vmem_limit_bytes=4 * MIB),
        name="split_columns",
    )(place, rows)


def faces_kernel(upper_ref, layer_ref, first_ref, last_ref, face_ref, low_ref, high_ref, wide):
    face_ref[...] = layer_ref[:, 0]

    def take(at_x, carry):
        for rows_ref, row, out_ref in ((first_ref, 0, low_ref), (last_ref, 7, high_ref)):
            for at_z in range(TILE_SIDE):
                wide[at_z : at_z + 1, :] = rows_ref[at_x, at_z].astype(jnp.float32)[row : row + 1]
            out_ref[at_x] = wide[...].astype(jnp.bfloat16)
        return carry

    wide[...] = jnp.zeros_like(wide)
    lax.fori_loop(0, layer_ref.shape[0], take, 0)


def faces(upper, block):
    side_x, depth, side_y, width = block.shape
    return pl.pallas_call(
        faces_kernel,
        out_shape=(
            jax.ShapeDtypeStruct((side_x, side_y, width), block.dtype),
            jax.ShapeDtypeStruct((side_x, 16, width), block.dtype),
            jax.ShapeDtypeStruct((side_x, 16, width), block.dtype),
        ),
        grid_spec=pltpu.PrefetchScalarGridSpec(
            num_scalar_prefetch=1,
            grid=(1,),
            in_specs=[
                pl.BlockSpec(
                    (side_x, 1, side_y, width), lambda i, upper: (0, (1 - upper[0]) * (depth - 1), 0, 0)
                ),
                pl.BlockSpec((side_x, depth, 8, width), lambda i, upper: (0, 0, 0, 0)),
                pl.BlockSpec((side_x, depth, 8, width), lambda i, upper: (0, 0, side_y // 8 - 1, 0)),
            ],
            out_specs=(
                pl.BlockSpec((side_x, side_y, width), lambda i, upper: (0, 0, 0)),
                pl.BlockSpec((side_x, 16, width), lambda i, upper: (0, 0, 0)),
                pl.BlockSpec((side_x, 16, width), lambda i, upper: (0, 0, 0)),
            ),
            scratch_shapes=[pltpu.VMEM((16, width), jnp.float32)],
        ),
        compiler_params=pltpu.CompilerParams(vmem_limit_bytes=12 * MIB),
        name="faces",
    )(upper, block, block, block)


def window_kernel(
    inside_ref, block_ref, layer_ref, below_ref, above_ref, outer_ref, scale_ref, shift_ref,
    weight_ref, order_ref, windows_ref, taps_ref, rows, line, layers,
):
    phase_x = pl.program_id(0)
    side, depth, width = 2 * TILE_SIDE, TILE_SIDE, FINE_WIDTH
    half = 2 * ACROSS * side

    @pl.when(phase_x == 0)
    def _():
        zero = jnp.zeros((width, width), jnp.bfloat16)
        for place in range(9):
            taps_ref[place, 3 * width :, :width] = zero
            taps_ref[place, :width, width:] = zero
            for step in range(3):
                block = jnp.dot(
                    weight_ref[place * 3 + step], order_ref[...], preferred_element_type=jnp.float32
                ).astype(jnp.bfloat16)
                taps_ref[place, step * width : (step + 1) * width, :width] = block
                taps_ref[place, (step + 1) * width : (step + 2) * width, width:] = block

        def widen(at_x, carry):
            rows[0, at_x] = below_ref[at_x].astype(jnp.float32)
            rows[1, at_x] = above_ref[at_x].astype(jnp.float32)
            return carry

        lax.fori_loop(0, side, widen, 0)

    scale = jnp.broadcast_to(scale_ref[...], (8, width))
    shift = jnp.broadcast_to(shift_ref[...], (8, width))
    row = lax.broadcasted_iota(jnp.int32, (8, width), 0)
    first = jnp.where(row == 0, shift * inside_ref[2], shift)
    last = jnp.where(row == side + 1 - 20, shift * inside_ref[3], shift)
    chunks = [(0, first), (8, shift), (16, shift), (4, shift), (12, shift), (20, last)]

    def split(cell_x, carry):
        at_x = phase_x + STRIDE * cell_x
        outside = jnp.logical_or(at_x == 0, at_x == side + 1)

        @pl.when(jnp.logical_not(outside))
        def _():
            at = at_x - 1
            for at_z in range(depth + 2):
                if at_z == 0:
                    flag, value, place = inside_ref[4], layer_ref[at], depth
                elif at_z == depth + 1:
                    flag, value, place = inside_ref[5], layer_ref[at], depth
                else:
                    flag, value, place = None, block_ref[at, at_z - 1], at_z - 1
                value = value.astype(jnp.float32)
                low, high = rows[0, at, place : place + 1, :], rows[1, at, place : place + 1, :]
                if flag is not None:
                    value, low, high = value * flag, low * flag, high * flag
                line[at_z, 7:8, :] = low
                line[at_z, 8 : side + 8, :] = value
                line[at_z, side + 8 : side + 9, :] = high

        @pl.when(outside)
        def _():
            end = jnp.where(at_x == 0, 0, 1)
            for at_z in range(depth + 2):
                value = outer_ref[end, at_z].astype(jnp.float32)
                line[at_z, 0:8, :] = value[side : side + 8]
                line[at_z, 8 : side + 8, :] = value[:side]
                line[at_z, side + 8 : side + 16, :] = value[side : side + 8]

        within = jnp.where(at_x == 0, inside_ref[0], 1.0)
        within = jnp.where(at_x == side + 1, inside_ref[1], within)
        for at_z in range(depth + 2):
            if at_z == 0:
                factor = within * inside_ref[4]
            elif at_z == depth + 1:
                factor = within * inside_ref[5]
            else:
                factor = within
            for number, (start, added) in enumerate(chunks):
                value = line[at_z, pl.ds(start + 7, 8), :]
                base = number // 3 * half + number % 3 * 8
                base = pl.multiple_of(base + cell_x * side, 8)
                layers[at_z, pl.ds(base, 8), :] = value
                layers[at_z, pl.ds(base + half // 2, 8), :] = value * scale + added * factor
        return carry

    lax.fori_loop(0, ACROSS, split, 0)
    for phase_y in range(PHASES):
        start = phase_y if phase_y < STRIDE else half + phase_y - STRIDE
        for phase_z in range(PHASES):
            parts = [
                layers[phase_z + STRIDE * cell, pl.ds(start, PLANE, stride=STRIDE), :]
                for cell in range(CELLS)
            ]
            parts.append(jnp.zeros((PADDED - ROWS, width), jnp.float32))
            windows_ref[0, phase_y, :, phase_z * width : (phase_z + 1) * width] = jnp.concatenate(
                parts, axis=0
            ).astype(jnp.bfloat16)


def make_windows(inside, *arrays):
    width, side = FINE_WIDTH, 2 * TILE_SIDE

    def whole(array):
        return pl.BlockSpec(array.shape, lambda i: (0,) * array.ndim)

    return pl.pallas_call(
        window_kernel,
        out_shape=(
            jax.ShapeDtypeStruct((PHASES, PHASES, PADDED, PHASES * width), jnp.bfloat16),
            jax.ShapeDtypeStruct((9, 4 * width, 2 * width), jnp.bfloat16),
        ),
        grid=(PHASES,),
        in_specs=[pl.BlockSpec(memory_space=pltpu.SMEM)] + [whole(array) for array in arrays],
        out_specs=(
            pl.BlockSpec((1, PHASES, PADDED, PHASES * width), lambda i: (i, 0, 0, 0)),
            pl.BlockSpec((9, 4 * width, 2 * width), lambda i: (0, 0, 0)),
        ),
        scratch_shapes=[
            pltpu.VMEM((2, side, 16, width), jnp.float32),
            pltpu.VMEM((TILE_SIDE + 2, side + 16, width), jnp.float32),
            pltpu.VMEM((TILE_SIDE + 2, 4 * ACROSS * side, width), jnp.float32),
        ],
        compiler_params=pltpu.CompilerParams(vmem_limit_bytes=28 * MIB),
        cost_estimate=pl.CostEstimate(flops=10**10, bytes_accessed=16 * MIB, transcendentals=0),
        name="windows",
    )(inside, *arrays)


def convolve_kernel(first_ref, second_ref, third_ref, taps_ref, bias_ref, out_ref):
    width = FINE_WIDTH
    bias = bias_ref[...]

    def convolve(at_y, carry):
        total = jnp.zeros((2 * PADDED, 2 * width), jnp.float32)
        for step_x, windows_ref in enumerate((first_ref, second_ref, third_ref)):
            for step_y in range(3):
                taken = [
                    windows_ref[0, at_y + step_y, :, pair * 2 * width : (pair * 2 + 4) * width]
                    for pair in range(2)
                ]
                total += jnp.dot(
                    jnp.concatenate(taken, axis=0),
                    taps_ref[step_x * 3 + step_y],
                    preferred_element_type=jnp.float32,
                )
        total = total + bias
        hidden = (total / (1.0 + jnp.exp(-total))).astype(jnp.bfloat16)
        for pair in range(2):
            out_ref[at_y * 2 + pair] = hidden[pair * PADDED : (pair + 1) * PADDED]
        return carry

    lax.fori_loop(0, STRIDE, convolve, 0)


def convolve(windows, taps, bias, start, count):
    width = FINE_WIDTH
    each = STRIDE * STRIDE // 2
    block = (1, PHASES, PADDED, PHASES * width)
    return pl.pallas_call(
        convolve_kernel,
        out_shape=jax.ShapeDtypeStruct((count * each, PADDED, 2 * width), jnp.bfloat16),
        grid=(count,),
        in_specs=[
            pl.BlockSpec(block, lambda i, step=step: (i + start + step, 0, 0, 0)) for step in range(3)
        ]
        + [
            pl.BlockSpec(taps.shape, lambda i: (0, 0, 0)),
            pl.BlockSpec(bias.shape, lambda i: (0, 0)),
        ],
        out_specs=pl.BlockSpec((each, PADDED, 2 * width), lambda i: (i, 0, 0)),
        compiler_params=pltpu.CompilerParams(vmem_limit_bytes=28 * MIB),
        cost_estimate=pl.CostEstimate(
            flops=2 * count * each * PADDED * 36 * width * 2 * width,
            bytes_accessed=16 * MIB,
            transcendentals=count * each * PADDED * 2 * width,
        ),
        name="convolve",
    )(windows, windows, windows, taps, bias)


def project_kernel(split, place_ref, early_ref, late_ref, *refs):
    weight_refs, bias_ref, out_ref, total = refs[:-3], refs[-3], refs[-2], refs[-1]
    step = pl.program_id(0)
    width = out_ref.shape[1]

    def product(hidden_ref, number):
        used = weight_refs[:-2] + (weight_refs[len(weight_refs) - 2 + number],) if split else weight_refs
        acc = jnp.zeros(total.shape, jnp.float32)
        for pair in range(hidden_ref.shape[0]):
            weight = jnp.concatenate(
                [ref[2 * pair + item] for item in range(2) for ref in used], axis=0
            )
            acc += jnp.dot(hidden_ref[pair], weight, preferred_element_type=jnp.float32)
        return acc

    @pl.when(step == 0)
    def _():
        total[...] = product(early_ref, 0)

    @pl.when(step == 1)
    def _():
        start = pl.multiple_of(place_ref[0] * width, width)
        out_ref[...] = (total[...] + product(late_ref, 1) + bias_ref[:, pl.ds(start, width)]).astype(
            jnp.bfloat16
        )


def project(place, early, late, weights, split, bias):
    pairs, rows, depth = early.shape
    width = weights[0].shape[2]
    return pl.pallas_call(
        functools.partial(project_kernel, split),
        out_shape=jax.ShapeDtypeStruct((rows, width), jnp.bfloat16),
        grid=(2,),
        in_specs=[
            pl.BlockSpec(memory_space=pltpu.SMEM),
            pl.BlockSpec(early.shape, lambda i: (0, 0, 0)),
            pl.BlockSpec(late.shape, lambda i: (0, 0, 0)),
        ]
        + [
            pl.BlockSpec(
                (OFFSETS // 2,) + weight.shape[1:],
                (lambda i: (i, 0, 0)) if weight.shape[0] == OFFSETS else (lambda i: (0, 0, 0)),
            )
            for weight in weights
        ]
        + [pl.BlockSpec(bias.shape, lambda i: (0, 0))],
        out_specs=pl.BlockSpec((rows, width), lambda i: (0, 0)),
        scratch_shapes=[pltpu.VMEM((rows, width), jnp.float32)],
        compiler_params=pltpu.CompilerParams(vmem_limit_bytes=24 * MIB),
        cost_estimate=pl.CostEstimate(
            flops=4 * pairs * rows * depth * width, bytes_accessed=8 * MIB, transcendentals=0
        ),
        name="project",
    )(place, early, late, *weights, bias)


def bottle_kernel(far, place_ref, field_ref, weight_ref, *refs):
    out_refs, (held, total, packed, dense, sems) = refs[:-5], refs[-5:]
    width = field_ref.shape[4]
    share = out_refs[0].shape[1]
    span = held.shape[2]
    frame = ACROSS + 2
    rows = CELLS * 2 * ACROSS * frame
    chunk = 256
    owners = 2 * len(out_refs)
    first = pl.multiple_of((place_ref[0] // len(out_refs) ^ far) * span, span)

    def copy_of(step_y, place):
        tap = (place // 3 * 3 + step_y) * 3 + place % 3
        return pltpu.make_async_copy(
            weight_ref.at[tap, :, pl.ds(first, span)],
            held.at[step_y, pl.ds(place * width, width)],
            sems.at[step_y, place],
        )

    for step_y in range(3):
        for place in range(9):
            copy_of(step_y, place).start()

    for step_x in range(3):
        for step_z in range(3):
            place = step_x * 3 + step_z
            packed[:, place * width : (place + 1) * width] = (
                field_ref[step_z : step_z + CELLS, :, step_x : step_x + ACROSS]
                .astype(jnp.float32)
                .reshape(rows, width)
                .astype(jnp.bfloat16)
            )

    for step_x in range(3):
        for step_z in range(3):
            copy_of(0, step_x * 3 + step_z).wait()
        depth = slice(step_x * 3 * width, (step_x + 1) * 3 * width)
        for start in range(0, span, chunk):
            columns = slice(start, start + chunk)
            terms = jnp.dot(
                packed[:, depth], held[0, depth, columns], preferred_element_type=jnp.float32
            )
            total[0, :, columns] = terms if step_x == 0 else total[0, :, columns] + terms

    def rest(step_y, carry):
        for place in range(9):
            copy_of(step_y, place).wait()
        for start in range(0, span, chunk):
            columns = slice(start, start + chunk)
            total[step_y, :, columns] = jnp.dot(
                packed[...], held[step_y, :, columns], preferred_element_type=jnp.float32
            )
        return carry

    lax.fori_loop(1, 3, rest, 0)

    for number, out_ref in enumerate(out_refs):
        distance = number + far * owners // 2
        start = pl.multiple_of((place_ref[0] ^ distance) % len(out_refs) * share, share)
        for group in range(rows // frame):
            at = group * frame
            dense[group * ACROSS : (group + 1) * ACROSS, :] = sum(
                total[item, at + item : at + item + ACROSS, pl.ds(start, share)]
                for item in range(3)
            )
        out_ref[...] = dense[...].astype(out_ref.dtype)


def bottle_terms(place, field, weight, owners, far):
    frame = ACROSS + 2
    rows = CELLS * 2 * ACROSS * frame
    width = weight.shape[1]
    share = COARSE_WIDTH // owners
    span = COARSE_WIDTH // 2
    return pl.pallas_call(
        functools.partial(bottle_kernel, int(far)),
        out_shape=[
            jax.ShapeDtypeStruct((ROWS, share), jnp.bfloat16 if far or number else jnp.float32)
            for number in range(owners // 2)
        ],
        in_specs=[
            pl.BlockSpec(memory_space=pltpu.SMEM),
            pl.BlockSpec(memory_space=pltpu.VMEM),
            pl.BlockSpec(memory_space=pltpu.HBM),
        ],
        out_specs=vmem(owners // 2),
        scratch_shapes=[
            pltpu.VMEM((3, 9 * width, span), jnp.bfloat16),
            pltpu.VMEM((3, rows, span), jnp.float32),
            pltpu.VMEM((rows, 9 * width), jnp.bfloat16),
            pltpu.VMEM((ROWS, share), jnp.float32),
            pltpu.SemaphoreType.DMA((3, 9)),
        ],
        compiler_params=pltpu.CompilerParams(vmem_limit_bytes=51 * MIB),
        cost_estimate=pl.CostEstimate(
            flops=2 * rows * 27 * width * span, bytes_accessed=8 * MIB, transcendentals=0
        ),
        name="bottle_far" if far else "bottle_near",
    )(place, field, weight)


def finish_kernel(place_ref, guide_ref, own_ref, *refs):
    other_refs, bias_ref, out_ref, spread = refs[:-3], refs[-3], refs[-2], refs[-1]
    share = own_ref.shape[1]
    start = pl.multiple_of(place_ref[0] * share, share)
    value = own_ref[...] + bias_ref[:, pl.ds(start, share)]
    for other_ref in other_refs:
        value = value + other_ref[...].astype(jnp.float32)
    value = value / (1.0 + jnp.exp(-value))
    half = PLANE // 2
    for cell in range(CELLS):
        plain = value[cell * PLANE : cell * PLANE + half]
        guided = value[cell * PLANE + half : (cell + 1) * PLANE]
        mixed = plain + guide_ref[0] * (guided - plain)
        for lane in range(spread.shape[0]):
            spread[lane, pl.ds(cell, half, stride=SPREAD), :] = mixed[:, lane * LANES : (lane + 1) * LANES]
    for lane in range(spread.shape[0]):
        for cell in range(half):
            out_ref[cell, :, lane * LANES : (lane + 1) * LANES] = spread[
                lane, cell * SPREAD : cell * SPREAD + CELLS, :
            ].astype(jnp.bfloat16)


def finish(place, guide, terms, bias):
    share = terms[0].shape[1]
    return pl.pallas_call(
        finish_kernel,
        out_shape=jax.ShapeDtypeStruct((PLANE // 2, CELLS, share), jnp.bfloat16),
        in_specs=[pl.BlockSpec(memory_space=pltpu.SMEM)] * 2 + vmem(len(terms) + 1),
        out_specs=vmem(1)[0],
        scratch_shapes=[pltpu.VMEM((share // LANES, PLANE // 2 * SPREAD, LANES), jnp.float32)],
        compiler_params=pltpu.CompilerParams(vmem_limit_bytes=8 * MIB),
        name="finish",
    )(place, guide, *terms, bias)


def passed(value, steps):
    count = lax.axis_size("region")
    return lax.ppermute(
        value, "region", [(at, at + steps) for at in range(max(0, -steps), min(count, count - steps))]
    )


def across_z(value):
    count = lax.axis_size("region")
    return lax.ppermute(value, "region", [(at, at ^ 1) for at in range(count)])


def y_halos(first, last):
    place = lax.axis_index("region") // REGIONS_Z % REGIONS_Y
    upper = is_upper()
    ahead = hop(jnp.where(upper, first, last), True)
    back = hop(jnp.where(upper, last, first), False)
    zero = jnp.zeros_like(ahead)
    below = jnp.where(place > 0, jnp.where(upper, back, ahead), zero)
    above = jnp.where(place < REGIONS_Y - 1, jnp.where(upper, ahead, back), zero)
    return below, above


def with_halos(value, dim_x, dim_y, dim_z):
    value = jnp.concatenate(z_ends(z_layer(value, dim_z), value, dim_z), axis=dim_z)
    below, above = y_halos(edge(value, dim_y, False), edge(value, dim_y, True))
    value = jnp.concatenate([below, value, above], axis=dim_y)
    low, high = x_layers(edge(value, dim_x, False), edge(value, dim_x, True))
    return jnp.concatenate([low, value, high], axis=dim_x)


def edge(array, dim, last):
    size = array.shape[dim]
    return lax.slice_in_dim(array, size - 1 if last else 0, size if last else 1, axis=dim)


def is_upper():
    return lax.axis_index("region") % REGIONS_Z == 1


def z_layer(value, dim):
    return across_z(jnp.where(is_upper(), edge(value, dim, False), edge(value, dim, True)))


def z_ends(layer, value, dim):
    zero = jnp.zeros_like(layer)
    return [jnp.where(is_upper(), layer, zero), value, jnp.where(is_upper(), zero, layer)]


def x_layers(first, last):
    count = lax.axis_size("region") // (REGIONS_Y * REGIONS_Z)
    if count == 1:
        return jnp.zeros_like(last), jnp.zeros_like(first)
    return passed(last, REGIONS_Y * REGIONS_Z), passed(first, -REGIONS_Y * REGIONS_Z)


def chan_swap(value, distance):
    return lax.ppermute(value, "chan", [(at, at ^ distance) for at in range(lax.axis_size("chan"))])


def exchange(piece_at):
    chans = lax.axis_size("chan")
    return [piece_at(0)] + [chan_swap(piece_at(distance), distance) for distance in range(1, chans)]


def ring_of(count):
    return list(range(0, count, 2)) + list(range(1, count, 2))[::-1]


def hop(value, ahead):
    ring = ring_of(lax.axis_size("region"))
    following = ring[1:] + ring[:1]
    return lax.ppermute(value, "region", list(zip(ring, following) if ahead else zip(following, ring)))


def after(value, other):
    return lax.optimization_barrier((value, other))[0]


def piece_channels(each):
    chans, regions = lax.axis_size("chan"), lax.axis_size("region")
    ring = ring_of(regions)
    shifts = [0]
    for step in range(1, regions // 2 + 1):
        shifts += [-step] + [step] * (step < regions // 2)
    origin = np.array(
        [[ring[(ring.index(region) + shift) % regions] for shift in shifts] for region in range(regions)]
    )
    table = np.zeros((chans, regions, regions, chans, each), np.int32)
    for chan in range(chans):
        for distance in range(chans):
            first = (chan ^ distance) * regions + origin
            table[chan, :, :, distance] = first[:, :, None] * each + np.arange(each)
    table = jnp.asarray(table.reshape(chans * regions, FINE_WIDTH))
    device = lax.axis_index("chan") * regions + lax.axis_index("region")
    return lax.dynamic_index_in_dim(table, device, 0, keepdims=True)


def ring_pieces(piece, milestones):
    regions = lax.axis_size("region")
    forward = backward = piece
    held = [piece]
    for step in range(1, regions // 2 + 1):
        if step > 1 and step - 2 < len(milestones):
            forward, backward = (after(value, milestones[step - 2]) for value in (forward, backward))
        if step == regions // 2:
            held += [hop(forward[: OFFSETS // 2], True), hop(backward[OFFSETS // 2 :], False)]
        else:
            forward, backward = hop(forward, True), hop(backward, False)
            held += [forward, backward]
    return held


def whole_columns(proj_weight):
    chans, held = lax.axis_size("chan"), proj_weight.shape[0]
    width = COARSE_WIDTH // chans
    mine = lax.all_to_all(proj_weight, "chan", split_axis=1, concat_axis=0, tiled=True)
    whole = lax.all_gather(mine.reshape(chans, held, width), "region", axis=1, tiled=True)
    return whole.reshape(FINE_WIDTH, OFFSETS, width).transpose(1, 0, 2)


def shards(
    latent,
    cond_scale,
    cond_shift,
    fine_weight,
    fine_bias,
    proj_weight,
    proj_bias,
    bottle_weight,
    bottle_bias,
    guide,
):
    chans = lax.axis_size("chan")
    chan_place = lax.axis_index("chan")
    region = lax.axis_index("region")
    width = COARSE_WIDTH // chans
    side = 2 * TILE_SIDE
    count_x = lax.axis_size("region") // (REGIONS_Y * REGIONS_Z)
    steps = (REGIONS_Y * REGIONS_Z, REGIONS_Z, 1)
    counts = (count_x, REGIONS_Y, REGIONS_Z)
    places = [region // step % count for step, count in zip(steps, counts)]
    inside = jnp.stack(
        [
            flag
            for place, count in zip(places, counts)
            for flag in ((place > 0).astype(jnp.float32), (place < count - 1).astype(jnp.float32))
        ]
    )

    place = chan_place[None]
    each, rest = divmod(proj_weight.shape[0], OFFSETS)
    by_ring = rest == 0 and chans * each % 16 == 0
    if by_ring:
        split = split_columns(place, proj_weight, chans)
        mine = exchange(lambda distance: split[distance])
        piece = regroup(mine)
        channel = piece_channels(each)
    else:
        channel = jnp.arange(FINE_WIDTH, dtype=jnp.int32)[None]
    order = lax.broadcasted_iota(jnp.int32, (FINE_WIDTH, FINE_WIDTH), 0) == channel

    block = latent[0].transpose(0, 2, 1, 3)
    upper = is_upper().astype(jnp.int32)[None]
    face, first, last = faces(upper, block)
    layer = across_z(face)
    corner = lax.broadcasted_iota(jnp.int32, first.shape, 1) == TILE_SIDE
    below, above = y_halos(
        jnp.where(corner, layer[:, :1], first), jnp.where(corner, layer[:, -1:], last)
    )
    ends = []
    for at in (0, -1):
        plane = jnp.concatenate(z_ends(layer[at][None], block[at], 0), axis=0)
        low, high = [
            jnp.concatenate(
                z_ends(part[at, TILE_SIDE : TILE_SIDE + 1], part[at, :TILE_SIDE], 0), axis=0
            )[:, None]
            for part in (below, above)
        ]
        spare = jnp.zeros((TILE_SIDE + 2, 6, FINE_WIDTH), plane.dtype)
        ends.append(jnp.concatenate([plane, high, spare, low], axis=1))
    outer = jnp.stack(x_layers(*ends))

    bias = jnp.sum(jnp.where(order, fine_bias[:, None], 0.0), axis=0)
    windows, taps = make_windows(
        inside,
        block,
        layer,
        below,
        above,
        outer,
        cond_scale[None],
        cond_shift[None],
        fine_weight.reshape(27, FINE_WIDTH, FINE_WIDTH),
        order.astype(jnp.bfloat16),
    )
    bias = jnp.concatenate([bias, bias])[None]
    half = STRIDE // 2
    early = convolve(windows, taps, bias, 0, half)
    late = convolve(windows, taps, bias, half, half)
    columns = ring_pieces(piece, [taps, early, late]) if by_ring else [whole_columns(proj_weight)]
    coarse = project(place, early, late, columns, by_ring, proj_bias[None])

    grid = coarse[:ROWS].reshape(CELLS, 2, ACROSS, ACROSS, width)
    field = with_halos(grid, 2, 3, 0)
    far = bottle_terms(place, field, bottle_weight, chans, True)
    swapped = [chan_swap(value, chans // 2 + number) for number, value in enumerate(far)]
    own, *near = bottle_terms(after(place, far), field, bottle_weight, chans, False)
    near = [chan_swap(value, 1 + number) for number, value in enumerate(near)]
    terms = [own, sum(value.astype(jnp.float32) for value in swapped)] + near
    guided = finish(place, guide, terms, bottle_bias[None])
    return guided.reshape(1, ACROSS, ACROSS, CELLS, width)


def solution(mesh):
    placed = (
        P("region", None, None, None, None),
        P(),
        P(),
        P(),
        P(),
        P(("chan", "region"), None),
        P(),
        P(None, "chan", None),
        P(),
        P(),
    )
    return jax.shard_map(
        shards,
        mesh=mesh,
        in_specs=placed,
        out_specs=P("region", None, None, None, "chan"),
        check_vma=False,
    )
```

```python
import functools

import numpy as np

import jax
import jax.numpy as jnp
from jax import lax
from jax.experimental import pallas as pl
from jax.experimental.pallas import tpu as pltpu
from jax.sharding import PartitionSpec as P

FINE_WIDTH = 128
COARSE_WIDTH = 1024
TILE_SIDE = 12
STRIDE = 4
REGIONS_Y = 4
REGIONS_Z = 2

CELLS = TILE_SIDE // STRIDE
ACROSS = 2 * CELLS
PLANE = 2 * ACROSS * ACROSS
ROWS = CELLS * PLANE
PADDED = -(-ROWS // 16) * 16
PHASES = STRIDE + 2
OFFSETS = STRIDE**3
LANES = 128
SPREAD = 8
MIB = 2**20


def vmem(count):
    return [pl.BlockSpec(memory_space=pltpu.VMEM) for _ in range(count)]


def regroup_kernel(*refs):
    rows_refs, out_ref, wide = refs[:-2], refs[-2], refs[-1]
    held = rows_refs[0].shape[0]
    members = wide.shape[1] // OFFSETS
    for lane in range(wide.shape[0]):
        columns = slice(lane * LANES, (lane + 1) * LANES)
        for number, rows_ref in enumerate(rows_refs):
            wide[lane, number * held : (number + 1) * held, :] = rows_ref[:, columns].astype(jnp.float32)
        for pair in range(OFFSETS // 2):
            out_ref[pair, :, columns] = jnp.concatenate(
                [
                    wide[lane, pl.ds(2 * pair + cell, members, stride=OFFSETS), :]
                    for cell in range(2)
                ],
                axis=0,
            ).astype(jnp.bfloat16)


def regroup(pieces):
    held, width = pieces[0].shape
    total = len(pieces) * held
    return pl.pallas_call(
        regroup_kernel,
        out_shape=jax.ShapeDtypeStruct((OFFSETS // 2, 2 * total // OFFSETS, width), jnp.bfloat16),
        in_specs=vmem(len(pieces)),
        out_specs=vmem(1)[0],
        scratch_shapes=[pltpu.VMEM((width // LANES, total, LANES), jnp.float32)],
        compiler_params=pltpu.CompilerParams(vmem_limit_bytes=8 * MIB),
        name="regroup",
    )(*pieces)


def taps_kernel(weight_ref, order_ref, out_ref):
    width = FINE_WIDTH
    for place in range(9):
        both = jnp.dot(
            weight_ref[place * 3 * width : (place + 1) * 3 * width, :],
            order_ref[...],
            preferred_element_type=jnp.float32,
        )
        lower, upper = both[:, : 2 * width], both[:, 2 * width :]
        out_ref[place, :width, :] = lower[:width].astype(jnp.bfloat16)
        out_ref[place, width : 3 * width, :] = (lower[width:] + upper[: 2 * width]).astype(jnp.bfloat16)
        out_ref[place, 3 * width :, :] = upper[2 * width :].astype(jnp.bfloat16)


def make_taps(weight, order):
    width = FINE_WIDTH
    return pl.pallas_call(
        taps_kernel,
        out_shape=jax.ShapeDtypeStruct((9, 4 * width, 2 * width), jnp.bfloat16),
        in_specs=vmem(2),
        out_specs=vmem(1)[0],
        compiler_params=pltpu.CompilerParams(vmem_limit_bytes=12 * MIB),
        name="taps",
    )(weight, order)


def split_kernel(place_ref, rows_ref, *out_refs):
    width = out_refs[0].shape[1]
    for distance, out_ref in enumerate(out_refs):
        start = pl.multiple_of((place_ref[0] ^ distance) * width, width)
        out_ref[...] = rows_ref[:, pl.ds(start, width)]


def split_columns(place, rows, owners):
    held, width = rows.shape[0], rows.shape[1] // owners
    return pl.pallas_call(
        split_kernel,
        out_shape=[jax.ShapeDtypeStruct((held, width), rows.dtype)] * owners,
        in_specs=[pl.BlockSpec(memory_space=pltpu.SMEM)] + vmem(1),
        out_specs=vmem(owners),
        compiler_params=pltpu.CompilerParams(vmem_limit_bytes=4 * MIB),
        name="split_columns",
    )(place, rows)


def faces_kernel(upper_ref, layer_ref, first_ref, last_ref, face_ref, low_ref, high_ref, wide):
    face_ref[...] = layer_ref[:, 0]

    def take(at_x, carry):
        for rows_ref, row, out_ref in ((first_ref, 0, low_ref), (last_ref, 7, high_ref)):
            for at_z in range(TILE_SIDE):
                wide[at_z : at_z + 1, :] = rows_ref[at_x, at_z].astype(jnp.float32)[row : row + 1]
            out_ref[at_x] = wide[...].astype(jnp.bfloat16)
        return carry

    wide[...] = jnp.zeros_like(wide)
    lax.fori_loop(0, layer_ref.shape[0], take, 0)


def faces(upper, block):
    side_x, depth, side_y, width = block.shape
    return pl.pallas_call(
        faces_kernel,
        out_shape=(
            jax.ShapeDtypeStruct((side_x, side_y, width), block.dtype),
            jax.ShapeDtypeStruct((side_x, 16, width), block.dtype),
            jax.ShapeDtypeStruct((side_x, 16, width), block.dtype),
        ),
        grid_spec=pltpu.PrefetchScalarGridSpec(
            num_scalar_prefetch=1,
            grid=(1,),
            in_specs=[
                pl.BlockSpec(
                    (side_x, 1, side_y, width), lambda i, upper: (0, (1 - upper[0]) * (depth - 1), 0, 0)
                ),
                pl.BlockSpec((side_x, depth, 8, width), lambda i, upper: (0, 0, 0, 0)),
                pl.BlockSpec((side_x, depth, 8, width), lambda i, upper: (0, 0, side_y // 8 - 1, 0)),
            ],
            out_specs=(
                pl.BlockSpec((side_x, side_y, width), lambda i, upper: (0, 0, 0)),
                pl.BlockSpec((side_x, 16, width), lambda i, upper: (0, 0, 0)),
                pl.BlockSpec((side_x, 16, width), lambda i, upper: (0, 0, 0)),
            ),
            scratch_shapes=[pltpu.VMEM((16, width), jnp.float32)],
        ),
        compiler_params=pltpu.CompilerParams(vmem_limit_bytes=12 * MIB),
        name="faces",
    )(upper, block, block, block)


def window_kernel(
    inside_ref, block_ref, layer_ref, below_ref, above_ref, outer_ref, scale_ref, shift_ref,
    windows_ref, rows, line, layers,
):
    phase_x = pl.program_id(0)
    side, depth, width = 2 * TILE_SIDE, TILE_SIDE, FINE_WIDTH
    half = 2 * ACROSS * side

    @pl.when(phase_x == 0)
    def _():
        def widen(at_x, carry):
            rows[0, at_x] = below_ref[at_x].astype(jnp.float32)
            rows[1, at_x] = above_ref[at_x].astype(jnp.float32)
            return carry

        lax.fori_loop(0, side, widen, 0)

    scale = jnp.broadcast_to(scale_ref[...], (8, width))
    shift = jnp.broadcast_to(shift_ref[...], (8, width))
    row = lax.broadcasted_iota(jnp.int32, (8, width), 0)
    first = jnp.where(row == 0, shift * inside_ref[2], shift)
    last = jnp.where(row == side + 1 - 20, shift * inside_ref[3], shift)
    chunks = [(0, first), (8, shift), (16, shift), (4, shift), (12, shift), (20, last)]

    def split(cell_x, carry):
        at_x = phase_x + STRIDE * cell_x
        outside = jnp.logical_or(at_x == 0, at_x == side + 1)

        @pl.when(jnp.logical_not(outside))
        def _():
            at = at_x - 1
            for at_z in range(depth + 2):
                if at_z == 0:
                    flag, value, place = inside_ref[4], layer_ref[at], depth
                elif at_z == depth + 1:
                    flag, value, place = inside_ref[5], layer_ref[at], depth
                else:
                    flag, value, place = None, block_ref[at, at_z - 1], at_z - 1
                value = value.astype(jnp.float32)
                low, high = rows[0, at, place : place + 1, :], rows[1, at, place : place + 1, :]
                if flag is not None:
                    value, low, high = value * flag, low * flag, high * flag
                line[at_z, 7:8, :] = low
                line[at_z, 8 : side + 8, :] = value
                line[at_z, side + 8 : side + 9, :] = high

        @pl.when(outside)
        def _():
            end = jnp.where(at_x == 0, 0, 1)
            for at_z in range(depth + 2):
                value = outer_ref[end, at_z].astype(jnp.float32)
                line[at_z, 0:8, :] = value[side : side + 8]
                line[at_z, 8 : side + 8, :] = value[:side]
                line[at_z, side + 8 : side + 16, :] = value[side : side + 8]

        within = jnp.where(at_x == 0, inside_ref[0], 1.0)
        within = jnp.where(at_x == side + 1, inside_ref[1], within)
        for at_z in range(depth + 2):
            if at_z == 0:
                factor = within * inside_ref[4]
            elif at_z == depth + 1:
                factor = within * inside_ref[5]
            else:
                factor = within
            for number, (start, added) in enumerate(chunks):
                value = line[at_z, pl.ds(start + 7, 8), :]
                base = number // 3 * half + number % 3 * 8
                base = pl.multiple_of(base + cell_x * side, 8)
                layers[at_z, pl.ds(base, 8), :] = value
                layers[at_z, pl.ds(base + half // 2, 8), :] = value * scale + added * factor
        return carry

    lax.fori_loop(0, ACROSS, split, 0)
    for phase_y in range(PHASES):
        start = phase_y if phase_y < STRIDE else half + phase_y - STRIDE
        for phase_z in range(PHASES):
            parts = [
                layers[phase_z + STRIDE * cell, pl.ds(start, PLANE, stride=STRIDE), :]
                for cell in range(CELLS)
            ]
            parts.append(jnp.zeros((PADDED - ROWS, width), jnp.float32))
            windows_ref[0, phase_y, :, phase_z * width : (phase_z + 1) * width] = jnp.concatenate(
                parts, axis=0
            ).astype(jnp.bfloat16)


def make_windows(inside, *arrays):
    width, side = FINE_WIDTH, 2 * TILE_SIDE

    def whole(array):
        return pl.BlockSpec(array.shape, lambda i: (0,) * array.ndim)

    return pl.pallas_call(
        window_kernel,
        out_shape=jax.ShapeDtypeStruct((PHASES, PHASES, PADDED, PHASES * width), jnp.bfloat16),
        grid=(PHASES,),
        in_specs=[pl.BlockSpec(memory_space=pltpu.SMEM)] + [whole(array) for array in arrays],
        out_specs=pl.BlockSpec((1, PHASES, PADDED, PHASES * width), lambda i: (i, 0, 0, 0)),
        scratch_shapes=[
            pltpu.VMEM((2, side, 16, width), jnp.float32),
            pltpu.VMEM((TILE_SIDE + 2, side + 16, width), jnp.float32),
            pltpu.VMEM((TILE_SIDE + 2, 4 * ACROSS * side, width), jnp.float32),
        ],
        compiler_params=pltpu.CompilerParams(vmem_limit_bytes=28 * MIB),
        cost_estimate=pl.CostEstimate(flops=10**10, bytes_accessed=16 * MIB, transcendentals=0),
        name="windows",
    )(inside, *arrays)


def convolve_kernel(first_ref, second_ref, third_ref, taps_ref, bias_ref, out_ref):
    width = FINE_WIDTH
    bias = bias_ref[...]

    def convolve(at_y, carry):
        total = jnp.zeros((2 * PADDED, 2 * width), jnp.float32)
        for step_x, windows_ref in enumerate((first_ref, second_ref, third_ref)):
            for step_y in range(3):
                taken = [
                    windows_ref[0, at_y + step_y, :, pair * 2 * width : (pair * 2 + 4) * width]
                    for pair in range(2)
                ]
                total += jnp.dot(
                    jnp.concatenate(taken, axis=0),
                    taps_ref[step_x * 3 + step_y],
                    preferred_element_type=jnp.float32,
                )
        total = total + bias
        hidden = (total / (1.0 + jnp.exp(-total))).astype(jnp.bfloat16)
        for pair in range(2):
            out_ref[at_y * 2 + pair] = hidden[pair * PADDED : (pair + 1) * PADDED]
        return carry

    lax.fori_loop(0, STRIDE, convolve, 0)


def convolve(windows, taps, bias, start, count):
    width = FINE_WIDTH
    each = STRIDE * STRIDE // 2
    block = (1, PHASES, PADDED, PHASES * width)
    return pl.pallas_call(
        convolve_kernel,
        out_shape=jax.ShapeDtypeStruct((count * each, PADDED, 2 * width), jnp.bfloat16),
        grid=(count,),
        in_specs=[
            pl.BlockSpec(block, lambda i, step=step: (i + start + step, 0, 0, 0)) for step in range(3)
        ]
        + [
            pl.BlockSpec(taps.shape, lambda i: (0, 0, 0)),
            pl.BlockSpec(bias.shape, lambda i: (0, 0)),
        ],
        out_specs=pl.BlockSpec((each, PADDED, 2 * width), lambda i: (i, 0, 0)),
        compiler_params=pltpu.CompilerParams(vmem_limit_bytes=28 * MIB),
        cost_estimate=pl.CostEstimate(
            flops=2 * count * each * PADDED * 36 * width * 2 * width,
            bytes_accessed=16 * MIB,
            transcendentals=count * each * PADDED * 2 * width,
        ),
        name="convolve",
    )(windows, windows, windows, taps, bias)


def project_kernel(place_ref, early_ref, late_ref, *refs):
    weight_refs, bias_ref, out_ref = refs[:-2], refs[-2], refs[-1]
    width = out_ref.shape[1]
    start = pl.multiple_of(place_ref[0] * width, width)
    total = jnp.broadcast_to(bias_ref[:, pl.ds(start, width)], out_ref.shape)
    pairs = OFFSETS // 2
    for pair in range(pairs):
        weight = jnp.concatenate(
            [ref[at + pair] for ref in weight_refs for at in range(0, ref.shape[0], pairs)], axis=0
        )
        hidden_ref = early_ref if pair < pairs // 2 else late_ref
        total += jnp.dot(
            hidden_ref[pair % (pairs // 2)], weight, preferred_element_type=jnp.float32
        )
    out_ref[...] = total.astype(jnp.bfloat16)


def project(place, early, late, weights, bias):
    pairs, rows, depth = early.shape
    width = weights[0].shape[2]
    return pl.pallas_call(
        project_kernel,
        out_shape=jax.ShapeDtypeStruct((rows, width), jnp.bfloat16),
        in_specs=[pl.BlockSpec(memory_space=pltpu.SMEM)] + vmem(len(weights) + 3),
        out_specs=vmem(1)[0],
        compiler_params=pltpu.CompilerParams(vmem_limit_bytes=24 * MIB),
        cost_estimate=pl.CostEstimate(
            flops=4 * pairs * rows * depth * width, bytes_accessed=8 * MIB, transcendentals=0
        ),
        name="project",
    )(place, early, late, *weights, bias)


def bottle_kernel(far, place_ref, field_ref, weight_ref, *refs):
    out_refs, (held, total, packed, dense, sems) = refs[:-5], refs[-5:]
    width = field_ref.shape[4]
    share = out_refs[0].shape[1]
    span = held.shape[2]
    frame = ACROSS + 2
    rows = CELLS * 2 * ACROSS * frame
    chunk = 256
    owners = 2 * len(out_refs)
    first = pl.multiple_of((place_ref[0] // len(out_refs) ^ far) * span, span)

    def copy_of(step_y, place):
        tap = (place // 3 * 3 + step_y) * 3 + place % 3
        return pltpu.make_async_copy(
            weight_ref.at[tap, :, pl.ds(first, span)],
            held.at[step_y, pl.ds(place * width, width)],
            sems.at[step_y, place],
        )

    for step_y in range(3):
        for place in range(9):
            copy_of(step_y, place).start()

    for step_x in range(3):
        for step_z in range(3):
            place = step_x * 3 + step_z
            packed[:, place * width : (place + 1) * width] = (
                field_ref[step_z : step_z + CELLS, :, step_x : step_x + ACROSS]
                .astype(jnp.float32)
                .reshape(rows, width)
                .astype(jnp.bfloat16)
            )

    for step_x in range(3):
        for step_z in range(3):
            copy_of(0, step_x * 3 + step_z).wait()
        depth = slice(step_x * 3 * width, (step_x + 1) * 3 * width)
        for start in range(0, span, chunk):
            columns = slice(start, start + chunk)
            terms = jnp.dot(
                packed[:, depth], held[0, depth, columns], preferred_element_type=jnp.float32
            )
            total[0, :, columns] = terms if step_x == 0 else total[0, :, columns] + terms

    def rest(step_y, carry):
        for place in range(9):
            copy_of(step_y, place).wait()
        for start in range(0, span, chunk):
            columns = slice(start, start + chunk)
            total[step_y, :, columns] = jnp.dot(
                packed[...], held[step_y, :, columns], preferred_element_type=jnp.float32
            )
        return carry

    lax.fori_loop(1, 3, rest, 0)

    for number, out_ref in enumerate(out_refs):
        distance = number + far * owners // 2
        start = pl.multiple_of((place_ref[0] ^ distance) % len(out_refs) * share, share)
        for group in range(rows // frame):
            at = group * frame
            dense[group * ACROSS : (group + 1) * ACROSS, :] = sum(
                total[item, at + item : at + item + ACROSS, pl.ds(start, share)]
                for item in range(3)
            )
        out_ref[...] = dense[...].astype(out_ref.dtype)


def bottle_terms(place, field, weight, owners, far):
    frame = ACROSS + 2
    rows = CELLS * 2 * ACROSS * frame
    width = weight.shape[1]
    share = COARSE_WIDTH // owners
    span = COARSE_WIDTH // 2
    return pl.pallas_call(
        functools.partial(bottle_kernel, int(far)),
        out_shape=[
            jax.ShapeDtypeStruct((ROWS, share), jnp.bfloat16 if far or number else jnp.float32)
            for number in range(owners // 2)
        ],
        in_specs=[
            pl.BlockSpec(memory_space=pltpu.SMEM),
            pl.BlockSpec(memory_space=pltpu.VMEM),
            pl.BlockSpec(memory_space=pltpu.HBM),
        ],
        out_specs=vmem(owners // 2),
        scratch_shapes=[
            pltpu.VMEM((3, 9 * width, span), jnp.bfloat16),
            pltpu.VMEM((3, rows, span), jnp.float32),
            pltpu.VMEM((rows, 9 * width), jnp.bfloat16),
            pltpu.VMEM((ROWS, share), jnp.float32),
            pltpu.SemaphoreType.DMA((3, 9)),
        ],
        compiler_params=pltpu.CompilerParams(vmem_limit_bytes=51 * MIB),
        cost_estimate=pl.CostEstimate(
            flops=2 * rows * 27 * width * span, bytes_accessed=8 * MIB, transcendentals=0
        ),
        name="bottle_far" if far else "bottle_near",
    )(place, field, weight)


def finish_kernel(place_ref, guide_ref, own_ref, *refs):
    other_refs, bias_ref, out_ref, spread = refs[:-3], refs[-3], refs[-2], refs[-1]
    share = own_ref.shape[1]
    start = pl.multiple_of(place_ref[0] * share, share)
    value = own_ref[...] + bias_ref[:, pl.ds(start, share)]
    for other_ref in other_refs:
        value = value + other_ref[...].astype(jnp.float32)
    value = value / (1.0 + jnp.exp(-value))
    half = PLANE // 2
    for cell in range(CELLS):
        plain = value[cell * PLANE : cell * PLANE + half]
        guided = value[cell * PLANE + half : (cell + 1) * PLANE]
        mixed = plain + guide_ref[0] * (guided - plain)
        for lane in range(spread.shape[0]):
            spread[lane, pl.ds(cell, half, stride=SPREAD), :] = mixed[:, lane * LANES : (lane + 1) * LANES]
    for lane in range(spread.shape[0]):
        for cell in range(half):
            out_ref[cell, :, lane * LANES : (lane + 1) * LANES] = spread[
                lane, cell * SPREAD : cell * SPREAD + CELLS, :
            ].astype(jnp.bfloat16)


def finish(place, guide, terms, bias):
    share = terms[0].shape[1]
    return pl.pallas_call(
        finish_kernel,
        out_shape=jax.ShapeDtypeStruct((PLANE // 2, CELLS, share), jnp.bfloat16),
        in_specs=[pl.BlockSpec(memory_space=pltpu.SMEM)] * 2 + vmem(len(terms) + 1),
        out_specs=vmem(1)[0],
        scratch_shapes=[pltpu.VMEM((share // LANES, PLANE // 2 * SPREAD, LANES), jnp.float32)],
        compiler_params=pltpu.CompilerParams(vmem_limit_bytes=8 * MIB),
        name="finish",
    )(place, guide, *terms, bias)


def passed(value, steps):
    count = lax.axis_size("region")
    return lax.ppermute(
        value, "region", [(at, at + steps) for at in range(max(0, -steps), min(count, count - steps))]
    )


def across_z(value):
    count = lax.axis_size("region")
    return lax.ppermute(value, "region", [(at, at ^ 1) for at in range(count)])


def y_halos(first, last):
    place = lax.axis_index("region") // REGIONS_Z % REGIONS_Y
    upper = is_upper()
    ahead = hop(jnp.where(upper, first, last), True)
    back = hop(jnp.where(upper, last, first), False)
    zero = jnp.zeros_like(ahead)
    below = jnp.where(place > 0, jnp.where(upper, back, ahead), zero)
    above = jnp.where(place < REGIONS_Y - 1, jnp.where(upper, ahead, back), zero)
    return below, above


def with_halos(value, dim_x, dim_y, dim_z):
    value = jnp.concatenate(z_ends(z_layer(value, dim_z), value, dim_z), axis=dim_z)
    below, above = y_halos(edge(value, dim_y, False), edge(value, dim_y, True))
    value = jnp.concatenate([below, value, above], axis=dim_y)
    low, high = x_layers(edge(value, dim_x, False), edge(value, dim_x, True))
    return jnp.concatenate([low, value, high], axis=dim_x)


def edge(array, dim, last):
    size = array.shape[dim]
    return lax.slice_in_dim(array, size - 1 if last else 0, size if last else 1, axis=dim)


def is_upper():
    return lax.axis_index("region") % REGIONS_Z == 1


def z_layer(value, dim):
    return across_z(jnp.where(is_upper(), edge(value, dim, False), edge(value, dim, True)))


def z_ends(layer, value, dim):
    zero = jnp.zeros_like(layer)
    return [jnp.where(is_upper(), layer, zero), value, jnp.where(is_upper(), zero, layer)]


def x_layers(first, last):
    count = lax.axis_size("region") // (REGIONS_Y * REGIONS_Z)
    if count == 1:
        return jnp.zeros_like(last), jnp.zeros_like(first)
    return passed(last, REGIONS_Y * REGIONS_Z), passed(first, -REGIONS_Y * REGIONS_Z)


def chan_swap(value, distance):
    return lax.ppermute(value, "chan", [(at, at ^ distance) for at in range(lax.axis_size("chan"))])


def exchange(piece_at):
    chans = lax.axis_size("chan")
    return [piece_at(0)] + [chan_swap(piece_at(distance), distance) for distance in range(1, chans)]


def ring_of(count):
    return list(range(0, count, 2)) + list(range(1, count, 2))[::-1]


def hop(value, ahead):
    ring = ring_of(lax.axis_size("region"))
    following = ring[1:] + ring[:1]
    return lax.ppermute(value, "region", list(zip(ring, following) if ahead else zip(following, ring)))


def after(value, other):
    return lax.optimization_barrier((value, other))[0]


def piece_lanes(each):
    chans, regions = lax.axis_size("chan"), lax.axis_size("region")
    ring = ring_of(regions)
    shifts = [0]
    for step in range(1, regions // 2 + 1):
        shifts += [-step] + [step] * (step < regions // 2)
    origin = np.array(
        [[ring[(ring.index(region) + shift) % regions] for shift in shifts] for region in range(regions)]
    )
    table = np.zeros((chans, regions, regions, 2, 2, chans // 2, each), np.int32)
    cells = np.zeros(table.shape[2:], np.int32)
    cells[:, :, 1] = 1
    for chan in range(chans):
        for distance in range(chans):
            half, member = divmod(distance, chans // 2)
            first = (chan ^ distance) * regions + origin
            table[chan, :, :, half, :, member] = (first[:, :, None] * each + np.arange(each))[:, :, None]
    table = jnp.asarray(table.reshape(chans * regions, 2 * FINE_WIDTH))
    device = lax.axis_index("chan") * regions + lax.axis_index("region")
    return lax.dynamic_index_in_dim(table, device, 0, keepdims=True), jnp.asarray(cells.reshape(1, -1))


def relay(values, *others):
    ahead, back = (after(value, others) if others else value for value in values)
    return hop(ahead, True), hop(back, False)


def whole_columns(proj_weight):
    chans, held = lax.axis_size("chan"), proj_weight.shape[0]
    width = COARSE_WIDTH // chans
    mine = lax.all_to_all(proj_weight, "chan", split_axis=1, concat_axis=0, tiled=True)
    whole = lax.all_gather(mine.reshape(chans, held, width), "region", axis=1, tiled=True)
    whole = whole.reshape(FINE_WIDTH, OFFSETS, width).transpose(1, 0, 2)
    return whole.reshape(OFFSETS // 2, 2 * FINE_WIDTH, width)


def shards(
    latent,
    cond_scale,
    cond_shift,
    fine_weight,
    fine_bias,
    proj_weight,
    proj_bias,
    bottle_weight,
    bottle_bias,
    guide,
):
    chans = lax.axis_size("chan")
    chan_place = lax.axis_index("chan")
    region = lax.axis_index("region")
    width = COARSE_WIDTH // chans
    side = 2 * TILE_SIDE
    count_x = lax.axis_size("region") // (REGIONS_Y * REGIONS_Z)
    steps = (REGIONS_Y * REGIONS_Z, REGIONS_Z, 1)
    counts = (count_x, REGIONS_Y, REGIONS_Z)
    places = [region // step % count for step, count in zip(steps, counts)]
    inside = jnp.stack(
        [
            flag
            for place, count in zip(places, counts)
            for flag in ((place > 0).astype(jnp.float32), (place < count - 1).astype(jnp.float32))
        ]
    )

    place = chan_place[None]
    each, rest = divmod(proj_weight.shape[0], OFFSETS)
    by_ring = rest == 0 and chans * each % 16 == 0 and lax.axis_size("region") >= 8
    if by_ring:
        split = split_columns(place, proj_weight, chans)
        across = chan_swap(jnp.concatenate(split[chans // 2 :]), chans // 2)
        beside = [split[0]] + [chan_swap(split[number], number) for number in range(1, chans // 2)]
        halves = [regroup(beside)]
        one = relay((halves[0], halves[0]))
        across = after(across, one)
        size = across.shape[0] // (chans // 2)
        parts = [across[number * size : (number + 1) * size] for number in range(chans // 2)]
        parts = [parts[0]] + [chan_swap(parts[number], number) for number in range(1, chans // 2)]
        halves.append(regroup(parts))
        two = relay((halves[1], halves[1]))
        channel, cell = piece_lanes(each)
    else:
        lanes = jnp.arange(2 * FINE_WIDTH, dtype=jnp.int32)[None]
        channel, cell = lanes % FINE_WIDTH, lanes // FINE_WIDTH
    order = lax.broadcasted_iota(jnp.int32, (FINE_WIDTH, 2 * FINE_WIDTH), 0) == channel
    taps = make_taps(
        fine_weight.reshape(27 * FINE_WIDTH, FINE_WIDTH),
        jnp.concatenate([order & (cell == 0), order & (cell == 1)], axis=1).astype(jnp.bfloat16),
    )
    bias = jnp.sum(jnp.where(order, fine_bias[:, None], 0.0), axis=0)[None]

    block = latent[0].transpose(0, 2, 1, 3)
    upper = is_upper().astype(jnp.int32)[None]
    face, first, last = faces(upper, block)
    layer = across_z(face)
    corner = lax.broadcasted_iota(jnp.int32, first.shape, 1) == TILE_SIDE
    below, above = y_halos(
        jnp.where(corner, layer[:, :1], first), jnp.where(corner, layer[:, -1:], last)
    )
    ends = []
    for at in (0, -1):
        plane = jnp.concatenate(z_ends(layer[at][None], block[at], 0), axis=0)
        low, high = [
            jnp.concatenate(
                z_ends(part[at, TILE_SIDE : TILE_SIDE + 1], part[at, :TILE_SIDE], 0), axis=0
            )[:, None]
            for part in (below, above)
        ]
        spare = jnp.zeros((TILE_SIDE + 2, 6, FINE_WIDTH), plane.dtype)
        ends.append(jnp.concatenate([plane, high, spare, low], axis=1))
    outer = jnp.stack(x_layers(*ends))

    windows = make_windows(
        inside, block, layer, below, above, outer, cond_scale[None], cond_shift[None]
    )
    half = STRIDE // 2
    if by_ring:
        columns = halves + [one[0], two[0], one[1], two[1]]
        both = [jnp.concatenate(pair) for pair in zip(one, two)]
        rounds = lax.axis_size("region") // 2
        work = windows
        for step in range(2, rounds):
            both = relay(both, work)
            columns += both
            if step == 2:
                work = early = convolve(windows, taps, bias, 0, half)
            elif step == 3:
                work = late = convolve(windows, taps, bias, half, half)
        pairs = OFFSETS // 2
        ahead, back = after(both[0][:pairs], (late, both)), after(both[1][pairs:], (late, both))
        columns += [hop(ahead, True), hop(back, False)]
    else:
        early = convolve(windows, taps, bias, 0, half)
        late = convolve(windows, taps, bias, half, half)
        columns = [whole_columns(proj_weight)]
    coarse = project(place, early, late, columns, proj_bias[None])

    grid = coarse[:ROWS].reshape(CELLS, 2, ACROSS, ACROSS, width)
    field = with_halos(grid, 2, 3, 0)
    far = bottle_terms(place, field, bottle_weight, chans, True)
    swapped = [chan_swap(value, chans // 2 + number) for number, value in enumerate(far)]
    own, *near = bottle_terms(after(place, far), field, bottle_weight, chans, False)
    near = [chan_swap(value, 1 + number) for number, value in enumerate(near)]
    terms = [own, sum(value.astype(jnp.float32) for value in swapped)] + near
    guided = finish(place, guide, terms, bottle_bias[None])
    return guided.reshape(1, ACROSS, ACROSS, CELLS, width)


def solution(mesh):
    placed = (
        P("region", None, None, None, None),
        P(),
        P(),
        P(),
        P(),
        P(("chan", "region"), None),
        P(),
        P(None, "chan", None),
        P(),
        P(),
    )
    return jax.shard_map(
        shards,
        mesh=mesh,
        in_specs=placed,
        out_specs=P("region", None, None, None, "chan"),
        check_vma=False,
    )
```

```python
import functools

import numpy as np

import jax
import jax.numpy as jnp
from jax import lax
from jax.experimental import pallas as pl
from jax.experimental.pallas import tpu as pltpu
from jax.sharding import PartitionSpec as P

FINE_WIDTH = 128
COARSE_WIDTH = 1024
TILE_SIDE = 12
STRIDE = 4
REGIONS_Y = 4
REGIONS_Z = 2

CELLS = TILE_SIDE // STRIDE
ACROSS = 2 * CELLS
PLANE = 2 * ACROSS * ACROSS
ROWS = CELLS * PLANE
PADDED = -(-ROWS // 16) * 16
PHASES = STRIDE + 2
OFFSETS = STRIDE**3
LANES = 128
SPREAD = 8
MIB = 2**20


def vmem(count):
    return [pl.BlockSpec(memory_space=pltpu.VMEM) for _ in range(count)]


def regroup_kernel(*refs):
    rows_refs, out_ref, wide = refs[:-2], refs[-2], refs[-1]
    held = rows_refs[0].shape[0]
    groups = out_ref.shape[1]
    for lane in range(wide.shape[0]):
        columns = slice(lane * LANES, (lane + 1) * LANES)
        for number, rows_ref in enumerate(rows_refs):
            wide[lane, number * held : (number + 1) * held, :] = rows_ref[:, columns].astype(jnp.float32)
        for offset in range(OFFSETS):
            out_ref[offset, :, columns] = wide[
                lane, pl.ds(offset, groups, stride=OFFSETS), :
            ].astype(jnp.bfloat16)


def regroup(pieces):
    held, width = pieces[0].shape
    total = len(pieces) * held
    return pl.pallas_call(
        regroup_kernel,
        out_shape=jax.ShapeDtypeStruct((OFFSETS, total // OFFSETS, width), jnp.bfloat16),
        in_specs=vmem(len(pieces)),
        out_specs=vmem(1)[0],
        scratch_shapes=[pltpu.VMEM((width // LANES, total, LANES), jnp.float32)],
        compiler_params=pltpu.CompilerParams(vmem_limit_bytes=8 * MIB),
        name="regroup",
    )(*pieces)


def split_kernel(place_ref, rows_ref, *out_refs):
    width = out_refs[0].shape[1]
    for distance, out_ref in enumerate(out_refs):
        start = pl.multiple_of((place_ref[0] ^ distance) * width, width)
        out_ref[...] = rows_ref[:, pl.ds(start, width)]


def split_columns(place, rows, owners):
    held, width = rows.shape[0], rows.shape[1] // owners
    return pl.pallas_call(
        split_kernel,
        out_shape=[jax.ShapeDtypeStruct((held, width), rows.dtype)] * owners,
        in_specs=[pl.BlockSpec(memory_space=pltpu.SMEM)] + vmem(1),
        out_specs=vmem(owners),
        compiler_params=pltpu.CompilerParams(vmem_limit_bytes=4 * MIB),
        name="split_columns",
    )(place, rows)


def faces_kernel(upper_ref, layer_ref, first_ref, last_ref, face_ref, low_ref, high_ref, wide):
    face_ref[...] = layer_ref[:, 0]

    def take(at_x, carry):
        for rows_ref, row, out_ref in ((first_ref, 0, low_ref), (last_ref, 7, high_ref)):
            for at_z in range(TILE_SIDE):
                wide[at_z : at_z + 1, :] = rows_ref[at_x, at_z].astype(jnp.float32)[row : row + 1]
            out_ref[at_x] = wide[...].astype(jnp.bfloat16)
        return carry

    wide[...] = jnp.zeros_like(wide)
    lax.fori_loop(0, layer_ref.shape[0], take, 0)


def faces(upper, block):
    side_x, depth, side_y, width = block.shape
    return pl.pallas_call(
        faces_kernel,
        out_shape=(
            jax.ShapeDtypeStruct((side_x, side_y, width), block.dtype),
            jax.ShapeDtypeStruct((side_x, 16, width), block.dtype),
            jax.ShapeDtypeStruct((side_x, 16, width), block.dtype),
        ),
        grid_spec=pltpu.PrefetchScalarGridSpec(
            num_scalar_prefetch=1,
            grid=(1,),
            in_specs=[
                pl.BlockSpec(
                    (side_x, 1, side_y, width), lambda i, upper: (0, (1 - upper[0]) * (depth - 1), 0, 0)
                ),
                pl.BlockSpec((side_x, depth, 8, width), lambda i, upper: (0, 0, 0, 0)),
                pl.BlockSpec((side_x, depth, 8, width), lambda i, upper: (0, 0, side_y // 8 - 1, 0)),
            ],
            out_specs=(
                pl.BlockSpec((side_x, side_y, width), lambda i, upper: (0, 0, 0)),
                pl.BlockSpec((side_x, 16, width), lambda i, upper: (0, 0, 0)),
                pl.BlockSpec((side_x, 16, width), lambda i, upper: (0, 0, 0)),
            ),
            scratch_shapes=[pltpu.VMEM((16, width), jnp.float32)],
        ),
        compiler_params=pltpu.CompilerParams(vmem_limit_bytes=12 * MIB),
        name="faces",
    )(upper, block, block, block)


def window_kernel(
    inside_ref, block_ref, layer_ref, below_ref, above_ref, outer_ref, scale_ref, shift_ref,
    weight_ref, order_ref, windows_ref, taps_ref, rows, line, layers,
):
    phase_x = pl.program_id(0)
    side, depth, width = 2 * TILE_SIDE, TILE_SIDE, FINE_WIDTH
    half = 2 * ACROSS * side

    @pl.when(phase_x == 0)
    def _():
        zero = jnp.zeros((width, width), jnp.bfloat16)
        for place in range(9):
            taps_ref[place, 3 * width :, :width] = zero
            taps_ref[place, :width, width:] = zero
            for step in range(3):
                block = jnp.dot(
                    weight_ref[place * 3 + step], order_ref[...], preferred_element_type=jnp.float32
                ).astype(jnp.bfloat16)
                taps_ref[place, step * width : (step + 1) * width, :width] = block
                taps_ref[place, (step + 1) * width : (step + 2) * width, width:] = block

        def widen(at_x, carry):
            rows[0, at_x] = below_ref[at_x].astype(jnp.float32)
            rows[1, at_x] = above_ref[at_x].astype(jnp.float32)
            return carry

        lax.fori_loop(0, side, widen, 0)

    scale = jnp.broadcast_to(scale_ref[...], (8, width))
    shift = jnp.broadcast_to(shift_ref[...], (8, width))
    row = lax.broadcasted_iota(jnp.int32, (8, width), 0)
    first = jnp.where(row == 0, shift * inside_ref[2], shift)
    last = jnp.where(row == side + 1 - 20, shift * inside_ref[3], shift)
    chunks = [(0, first), (8, shift), (16, shift), (4, shift), (12, shift), (20, last)]

    def split(cell_x, carry):
        at_x = phase_x + STRIDE * cell_x
        outside = jnp.logical_or(at_x == 0, at_x == side + 1)

        @pl.when(jnp.logical_not(outside))
        def _():
            at = at_x - 1
            for at_z in range(depth + 2):
                if at_z == 0:
                    flag, value, place = inside_ref[4], layer_ref[at], depth
                elif at_z == depth + 1:
                    flag, value, place = inside_ref[5], layer_ref[at], depth
                else:
                    flag, value, place = None, block_ref[at, at_z - 1], at_z - 1
                value = value.astype(jnp.float32)
                low, high = rows[0, at, place : place + 1, :], rows[1, at, place : place + 1, :]
                if flag is not None:
                    value, low, high = value * flag, low * flag, high * flag
                line[at_z, 7:8, :] = low
                line[at_z, 8 : side + 8, :] = value
                line[at_z, side + 8 : side + 9, :] = high

        @pl.when(outside)
        def _():
            end = jnp.where(at_x == 0, 0, 1)
            for at_z in range(depth + 2):
                value = outer_ref[end, at_z].astype(jnp.float32)
                line[at_z, 0:8, :] = value[side : side + 8]
                line[at_z, 8 : side + 8, :] = value[:side]
                line[at_z, side + 8 : side + 16, :] = value[side : side + 8]

        within = jnp.where(at_x == 0, inside_ref[0], 1.0)
        within = jnp.where(at_x == side + 1, inside_ref[1], within)
        for at_z in range(depth + 2):
            if at_z == 0:
                factor = within * inside_ref[4]
            elif at_z == depth + 1:
                factor = within * inside_ref[5]
            else:
                factor = within
            for number, (start, added) in enumerate(chunks):
                value = line[at_z, pl.ds(start + 7, 8), :]
                base = number // 3 * half + number % 3 * 8
                base = pl.multiple_of(base + cell_x * side, 8)
                layers[at_z, pl.ds(base, 8), :] = value
                layers[at_z, pl.ds(base + half // 2, 8), :] = value * scale + added * factor
        return carry

    lax.fori_loop(0, ACROSS, split, 0)
    for phase_y in range(PHASES):
        start = phase_y if phase_y < STRIDE else half + phase_y - STRIDE
        for phase_z in range(PHASES):
            parts = [
                layers[phase_z + STRIDE * cell, pl.ds(start, PLANE, stride=STRIDE), :]
                for cell in range(CELLS)
            ]
            parts.append(jnp.zeros((PADDED - ROWS, width), jnp.float32))
            windows_ref[0, phase_y, :, phase_z * width : (phase_z + 1) * width] = jnp.concatenate(
                parts, axis=0
            ).astype(jnp.bfloat16)


def make_windows(inside, *arrays):
    width, side = FINE_WIDTH, 2 * TILE_SIDE

    def whole(array):
        return pl.BlockSpec(array.shape, lambda i: (0,) * array.ndim)

    return pl.pallas_call(
        window_kernel,
        out_shape=(
            jax.ShapeDtypeStruct((PHASES, PHASES, PADDED, PHASES * width), jnp.bfloat16),
            jax.ShapeDtypeStruct((9, 4 * width, 2 * width), jnp.bfloat16),
        ),
        grid=(PHASES,),
        in_specs=[pl.BlockSpec(memory_space=pltpu.SMEM)] + [whole(array) for array in arrays],
        out_specs=(
            pl.BlockSpec((1, PHASES, PADDED, PHASES * width), lambda i: (i, 0, 0, 0)),
            pl.BlockSpec((9, 4 * width, 2 * width), lambda i: (0, 0, 0)),
        ),
        scratch_shapes=[
            pltpu.VMEM((2, side, 16, width), jnp.float32),
            pltpu.VMEM((TILE_SIDE + 2, side + 16, width), jnp.float32),
            pltpu.VMEM((TILE_SIDE + 2, 4 * ACROSS * side, width), jnp.float32),
        ],
        compiler_params=pltpu.CompilerParams(vmem_limit_bytes=28 * MIB),
        cost_estimate=pl.CostEstimate(flops=10**10, bytes_accessed=16 * MIB, transcendentals=0),
        name="windows",
    )(inside, *arrays)


def convolve_kernel(first_ref, second_ref, third_ref, taps_ref, bias_ref, out_ref):
    width = FINE_WIDTH
    bias = bias_ref[...]

    def convolve(at_y, carry):
        total = jnp.zeros((2 * PADDED, 2 * width), jnp.float32)
        for step_x, windows_ref in enumerate((first_ref, second_ref, third_ref)):
            for step_y in range(3):
                taken = [
                    windows_ref[0, at_y + step_y, :, pair * 2 * width : (pair * 2 + 4) * width]
                    for pair in range(2)
                ]
                total += jnp.dot(
                    jnp.concatenate(taken, axis=0),
                    taps_ref[step_x * 3 + step_y],
                    preferred_element_type=jnp.float32,
                )
        total = total + bias
        hidden = (total / (1.0 + jnp.exp(-total))).astype(jnp.bfloat16)
        for pair in range(2):
            out_ref[at_y * 2 + pair] = hidden[pair * PADDED : (pair + 1) * PADDED]
        return carry

    lax.fori_loop(0, STRIDE, convolve, 0)


def convolve(windows, taps, bias, start, count):
    width = FINE_WIDTH
    each = STRIDE * STRIDE // 2
    block = (1, PHASES, PADDED, PHASES * width)
    return pl.pallas_call(
        convolve_kernel,
        out_shape=jax.ShapeDtypeStruct((count * each, PADDED, 2 * width), jnp.bfloat16),
        grid=(count,),
        in_specs=[
            pl.BlockSpec(block, lambda i, step=step: (i + start + step, 0, 0, 0)) for step in range(3)
        ]
        + [
            pl.BlockSpec(taps.shape, lambda i: (0, 0, 0)),
            pl.BlockSpec(bias.shape, lambda i: (0, 0)),
        ],
        out_specs=pl.BlockSpec((each, PADDED, 2 * width), lambda i: (i, 0, 0)),
        compiler_params=pltpu.CompilerParams(vmem_limit_bytes=28 * MIB),
        cost_estimate=pl.CostEstimate(
            flops=2 * count * each * PADDED * 36 * width * 2 * width,
            bytes_accessed=16 * MIB,
            transcendentals=count * each * PADDED * 2 * width,
        ),
        name="convolve",
    )(windows, windows, windows, taps, bias)


def project_kernel(split, place_ref, early_ref, late_ref, *refs):
    weight_refs, bias_ref, out_ref, total = refs[:-3], refs[-3], refs[-2], refs[-1]
    step = pl.program_id(0)
    width = out_ref.shape[1]

    def product(hidden_ref, number):
        used = weight_refs[:-2] + (weight_refs[len(weight_refs) - 2 + number],) if split else weight_refs
        acc = jnp.zeros(total.shape, jnp.float32)
        for pair in range(hidden_ref.shape[0]):
            weight = jnp.concatenate(
                [ref[2 * pair + item] for item in range(2) for ref in used], axis=0
            )
            acc += jnp.dot(hidden_ref[pair], weight, preferred_element_type=jnp.float32)
        return acc

    @pl.when(step == 0)
    def _():
        total[...] = product(early_ref, 0)

    @pl.when(step == 1)
    def _():
        start = pl.multiple_of(place_ref[0] * width, width)
        out_ref[...] = (total[...] + product(late_ref, 1) + bias_ref[:, pl.ds(start, width)]).astype(
            jnp.bfloat16
        )


def project(place, early, late, weights, split, bias):
    pairs, rows, depth = early.shape
    width = weights[0].shape[2]
    return pl.pallas_call(
        functools.partial(project_kernel, split),
        out_shape=jax.ShapeDtypeStruct((rows, width), jnp.bfloat16),
        grid=(2,),
        in_specs=[
            pl.BlockSpec(memory_space=pltpu.SMEM),
            pl.BlockSpec(early.shape, lambda i: (0, 0, 0)),
            pl.BlockSpec(late.shape, lambda i: (0, 0, 0)),
        ]
        + [
            pl.BlockSpec(
                (OFFSETS // 2,) + weight.shape[1:],
                (lambda i: (i, 0, 0)) if weight.shape[0] == OFFSETS else (lambda i: (0, 0, 0)),
            )
            for weight in weights
        ]
        + [pl.BlockSpec(bias.shape, lambda i: (0, 0))],
        out_specs=pl.BlockSpec((rows, width), lambda i: (0, 0)),
        scratch_shapes=[pltpu.VMEM((rows, width), jnp.float32)],
        compiler_params=pltpu.CompilerParams(vmem_limit_bytes=24 * MIB),
        cost_estimate=pl.CostEstimate(
            flops=4 * pairs * rows * depth * width, bytes_accessed=8 * MIB, transcendentals=0
        ),
        name="project",
    )(place, early, late, *weights, bias)


def tap_copies(far, place_ref, owners, weight_ref, held_ref, sems):
    width, span = weight_ref.shape[1], held_ref.shape[2]
    first = pl.multiple_of((place_ref[0] // (owners // 2) ^ far) * span, span)
    return [
        pltpu.make_async_copy(
            weight_ref.at[(place // 3 * 3 + step_y) * 3 + place % 3, :, pl.ds(first, span)],
            held_ref.at[step_y, pl.ds(place * width, width)],
            sems.at[step_y, place],
        )
        for step_y in range(3)
        for place in range(9)
    ]


def load_kernel(owners, place_ref, weight_ref, held_ref, sems):
    copies = tap_copies(1, place_ref, owners, weight_ref, held_ref, sems)
    for copy in copies:
        copy.start()
    for copy in copies:
        copy.wait()


def load_taps(place, weight, owners):
    width, span = weight.shape[1], COARSE_WIDTH // 2
    return pl.pallas_call(
        functools.partial(load_kernel, owners),
        out_shape=jax.ShapeDtypeStruct((3, 9 * width, span), jnp.bfloat16),
        in_specs=[pl.BlockSpec(memory_space=pltpu.SMEM), pl.BlockSpec(memory_space=pltpu.HBM)],
        out_specs=pl.BlockSpec(memory_space=pl.ANY),
        scratch_shapes=[pltpu.SemaphoreType.DMA((3, 9))],
        compiler_params=pltpu.CompilerParams(vmem_limit_bytes=44 * MIB),
        cost_estimate=pl.CostEstimate(
            flops=0, bytes_accessed=2 * 27 * width * span, transcendentals=0
        ),
        name="load_taps",
    )(place, weight)


def bottle_kernel(far, owners, place_ref, field_ref, held_ref, *refs):
    if far:
        weight_ref, *out_refs, next_ref, total, packed, dense, sems = refs
        copies = tap_copies(0, place_ref, owners, weight_ref, next_ref, sems)
    else:
        *out_refs, total, packed, dense = refs
        copies = []
    for copy in copies:
        copy.start()
    width = field_ref.shape[4]
    share = out_refs[0].shape[1]
    span = held_ref.shape[2]
    frame = ACROSS + 2
    rows = CELLS * 2 * ACROSS * frame
    chunk = 256

    for step_x in range(3):
        for step_z in range(3):
            place = step_x * 3 + step_z
            packed[:, place * width : (place + 1) * width] = (
                field_ref[step_z : step_z + CELLS, :, step_x : step_x + ACROSS]
                .astype(jnp.float32)
                .reshape(rows, width)
                .astype(jnp.bfloat16)
            )

    def multiply(step_y, carry):
        for start in range(0, span, chunk):
            columns = slice(start, start + chunk)
            total[step_y, :, columns] = jnp.dot(
                packed[...], held_ref[step_y, :, columns], preferred_element_type=jnp.float32
            )
        return carry

    lax.fori_loop(0, 3, multiply, 0)

    for number, out_ref in enumerate(out_refs):
        distance = number + far * owners // 2
        start = pl.multiple_of((place_ref[0] ^ distance) % len(out_refs) * share, share)
        for group in range(rows // frame):
            at = group * frame
            dense[group * ACROSS : (group + 1) * ACROSS, :] = sum(
                total[item, at + item : at + item + ACROSS, pl.ds(start, share)]
                for item in range(3)
            )
        out_ref[...] = dense[...].astype(out_ref.dtype)
    for copy in copies:
        copy.wait()


def bottle_terms(place, field, held, owners, weight=None):
    far = weight is not None
    frame = ACROSS + 2
    rows = CELLS * 2 * ACROSS * frame
    width = field.shape[4]
    share = COARSE_WIDTH // owners
    span = COARSE_WIDTH // 2
    out_shape = [
        jax.ShapeDtypeStruct((ROWS, share), jnp.bfloat16 if far or number else jnp.float32)
        for number in range(owners // 2)
    ]
    scratch = [
        pltpu.VMEM((3, rows, span), jnp.float32),
        pltpu.VMEM((rows, 9 * width), jnp.bfloat16),
        pltpu.VMEM((ROWS, share), jnp.float32),
    ]
    in_specs = [pl.BlockSpec(memory_space=pltpu.SMEM)] + vmem(2)
    out_specs = vmem(owners // 2)
    arrays = [place, field, held]
    if far:
        arrays.append(weight)
        in_specs.append(pl.BlockSpec(memory_space=pltpu.HBM))
        out_shape.append(jax.ShapeDtypeStruct(held.shape, held.dtype))
        out_specs.append(pl.BlockSpec(memory_space=pl.ANY))
        scratch.append(pltpu.SemaphoreType.DMA((3, 9)))
    return pl.pallas_call(
        functools.partial(bottle_kernel, int(far), owners),
        out_shape=out_shape,
        in_specs=in_specs,
        out_specs=out_specs,
        scratch_shapes=scratch,
        compiler_params=pltpu.CompilerParams(vmem_limit_bytes=(36 if far else 20) * MIB),
        cost_estimate=pl.CostEstimate(
            flops=2 * rows * 27 * width * span, bytes_accessed=8 * MIB, transcendentals=0
        ),
        name="bottle_far" if far else "bottle_near",
    )(*arrays)


def finish_kernel(place_ref, guide_ref, own_ref, *refs):
    other_refs, bias_ref, out_ref, spread = refs[:-3], refs[-3], refs[-2], refs[-1]
    share = own_ref.shape[1]
    start = pl.multiple_of(place_ref[0] * share, share)
    value = own_ref[...] + bias_ref[:, pl.ds(start, share)]
    for other_ref in other_refs:
        value = value + other_ref[...].astype(jnp.float32)
    value = value / (1.0 + jnp.exp(-value))
    half = PLANE // 2
    for cell in range(CELLS):
        plain = value[cell * PLANE : cell * PLANE + half]
        guided = value[cell * PLANE + half : (cell + 1) * PLANE]
        mixed = plain + guide_ref[0] * (guided - plain)
        for lane in range(spread.shape[0]):
            spread[lane, pl.ds(cell, half, stride=SPREAD), :] = mixed[:, lane * LANES : (lane + 1) * LANES]
    for lane in range(spread.shape[0]):
        for cell in range(half):
            out_ref[cell, :, lane * LANES : (lane + 1) * LANES] = spread[
                lane, cell * SPREAD : cell * SPREAD + CELLS, :
            ].astype(jnp.bfloat16)


def finish(place, guide, terms, bias):
    share = terms[0].shape[1]
    return pl.pallas_call(
        finish_kernel,
        out_shape=jax.ShapeDtypeStruct((PLANE // 2, CELLS, share), jnp.bfloat16),
        in_specs=[pl.BlockSpec(memory_space=pltpu.SMEM)] * 2 + vmem(len(terms) + 1),
        out_specs=vmem(1)[0],
        scratch_shapes=[pltpu.VMEM((share // LANES, PLANE // 2 * SPREAD, LANES), jnp.float32)],
        compiler_params=pltpu.CompilerParams(vmem_limit_bytes=8 * MIB),
        name="finish",
    )(place, guide, *terms, bias)


def passed(value, steps):
    count = lax.axis_size("region")
    return lax.ppermute(
        value, "region", [(at, at + steps) for at in range(max(0, -steps), min(count, count - steps))]
    )


def across_z(value):
    count = lax.axis_size("region")
    return lax.ppermute(value, "region", [(at, at ^ 1) for at in range(count)])


def y_halos(first, last):
    place = lax.axis_index("region") // REGIONS_Z % REGIONS_Y
    upper = is_upper()
    ahead = hop(jnp.where(upper, first, last), True)
    back = hop(jnp.where(upper, last, first), False)
    zero = jnp.zeros_like(ahead)
    below = jnp.where(place > 0, jnp.where(upper, back, ahead), zero)
    above = jnp.where(place < REGIONS_Y - 1, jnp.where(upper, ahead, back), zero)
    return below, above


def with_halos(value, dim_x, dim_y, dim_z, beside):
    value = jnp.concatenate(z_ends(z_layer(value, dim_z), value, dim_z), axis=dim_z)
    below, above = y_halos(*(after(edge(value, dim_y, last), beside) for last in (False, True)))
    value = jnp.concatenate([below, value, above], axis=dim_y)
    low, high = x_layers(edge(value, dim_x, False), edge(value, dim_x, True))
    return jnp.concatenate([low, value, high], axis=dim_x)


def edge(array, dim, last):
    size = array.shape[dim]
    return lax.slice_in_dim(array, size - 1 if last else 0, size if last else 1, axis=dim)


def is_upper():
    return lax.axis_index("region") % REGIONS_Z == 1


def z_layer(value, dim):
    return across_z(jnp.where(is_upper(), edge(value, dim, False), edge(value, dim, True)))


def z_ends(layer, value, dim):
    zero = jnp.zeros_like(layer)
    return [jnp.where(is_upper(), layer, zero), value, jnp.where(is_upper(), zero, layer)]


def x_layers(first, last):
    count = lax.axis_size("region") // (REGIONS_Y * REGIONS_Z)
    if count == 1:
        return jnp.zeros_like(last), jnp.zeros_like(first)
    return passed(last, REGIONS_Y * REGIONS_Z), passed(first, -REGIONS_Y * REGIONS_Z)


def chan_swap(value, distance):
    return lax.ppermute(value, "chan", [(at, at ^ distance) for at in range(lax.axis_size("chan"))])


def exchange(piece_at):
    chans = lax.axis_size("chan")
    return [piece_at(0)] + [chan_swap(piece_at(distance), distance) for distance in range(1, chans)]


def ring_of(count):
    return list(range(0, count, 2)) + list(range(1, count, 2))[::-1]


def hop(value, ahead):
    ring = ring_of(lax.axis_size("region"))
    following = ring[1:] + ring[:1]
    return lax.ppermute(value, "region", list(zip(ring, following) if ahead else zip(following, ring)))


def after(value, other):
    return lax.optimization_barrier((value, other))[0]


def piece_channels(each):
    chans, regions = lax.axis_size("chan"), lax.axis_size("region")
    ring = ring_of(regions)
    shifts = [0]
    for step in range(1, regions // 2 + 1):
        shifts += [-step] + [step] * (step < regions // 2)
    origin = np.array(
        [[ring[(ring.index(region) + shift) % regions] for shift in shifts] for region in range(regions)]
    )
    table = np.zeros((chans, regions, regions, chans, each), np.int32)
    for chan in range(chans):
        for distance in range(chans):
            first = (chan ^ distance) * regions + origin
            table[chan, :, :, distance] = first[:, :, None] * each + np.arange(each)
    table = jnp.asarray(table.reshape(chans * regions, FINE_WIDTH))
    device = lax.axis_index("chan") * regions + lax.axis_index("region")
    return lax.dynamic_index_in_dim(table, device, 0, keepdims=True)


def ring_pieces(piece, milestones):
    regions = lax.axis_size("region")
    forward = backward = piece
    held = [piece]
    for step in range(1, regions // 2 + 1):
        if step > 1 and step - 2 < len(milestones):
            forward, backward = (after(value, milestones[step - 2]) for value in (forward, backward))
        if step == regions // 2:
            held += [hop(forward[: OFFSETS // 2], True), hop(backward[OFFSETS // 2 :], False)]
        else:
            forward, backward = hop(forward, True), hop(backward, False)
            held += [forward, backward]
    return held


def whole_columns(proj_weight):
    chans, held = lax.axis_size("chan"), proj_weight.shape[0]
    width = COARSE_WIDTH // chans
    mine = lax.all_to_all(proj_weight, "chan", split_axis=1, concat_axis=0, tiled=True)
    whole = lax.all_gather(mine.reshape(chans, held, width), "region", axis=1, tiled=True)
    return whole.reshape(FINE_WIDTH, OFFSETS, width).transpose(1, 0, 2)


def shards(
    latent,
    cond_scale,
    cond_shift,
    fine_weight,
    fine_bias,
    proj_weight,
    proj_bias,
    bottle_weight,
    bottle_bias,
    guide,
):
    chans = lax.axis_size("chan")
    chan_place = lax.axis_index("chan")
    region = lax.axis_index("region")
    width = COARSE_WIDTH // chans
    side = 2 * TILE_SIDE
    count_x = lax.axis_size("region") // (REGIONS_Y * REGIONS_Z)
    steps = (REGIONS_Y * REGIONS_Z, REGIONS_Z, 1)
    counts = (count_x, REGIONS_Y, REGIONS_Z)
    places = [region // step % count for step, count in zip(steps, counts)]
    inside = jnp.stack(
        [
            flag
            for place, count in zip(places, counts)
            for flag in ((place > 0).astype(jnp.float32), (place < count - 1).astype(jnp.float32))
        ]
    )

    place = chan_place[None]
    each, rest = divmod(proj_weight.shape[0], OFFSETS)
    by_ring = rest == 0 and chans * each % 16 == 0
    if by_ring:
        split = split_columns(place, proj_weight, chans)
        mine = exchange(lambda distance: split[distance])
        piece = regroup(mine)
        channel = piece_channels(each)
    else:
        channel = jnp.arange(FINE_WIDTH, dtype=jnp.int32)[None]
    order = lax.broadcasted_iota(jnp.int32, (FINE_WIDTH, FINE_WIDTH), 0) == channel

    block = latent[0].transpose(0, 2, 1, 3)
    upper = is_upper().astype(jnp.int32)[None]
    face, first, last = faces(upper, block)
    layer = across_z(face)
    corner = lax.broadcasted_iota(jnp.int32, first.shape, 1) == TILE_SIDE
    below, above = y_halos(
        jnp.where(corner, layer[:, :1], first), jnp.where(corner, layer[:, -1:], last)
    )
    ends = []
    for at in (0, -1):
        plane = jnp.concatenate(z_ends(layer[at][None], block[at], 0), axis=0)
        low, high = [
            jnp.concatenate(
                z_ends(part[at, TILE_SIDE : TILE_SIDE + 1], part[at, :TILE_SIDE], 0), axis=0
            )[:, None]
            for part in (below, above)
        ]
        spare = jnp.zeros((TILE_SIDE + 2, 6, FINE_WIDTH), plane.dtype)
        ends.append(jnp.concatenate([plane, high, spare, low], axis=1))
    outer = jnp.stack(x_layers(*ends))

    bias = jnp.sum(jnp.where(order, fine_bias[:, None], 0.0), axis=0)
    windows, taps = make_windows(
        inside,
        block,
        layer,
        below,
        above,
        outer,
        cond_scale[None],
        cond_shift[None],
        fine_weight.reshape(27, FINE_WIDTH, FINE_WIDTH),
        order.astype(jnp.bfloat16),
    )
    bias = jnp.concatenate([bias, bias])[None]
    half = STRIDE // 2
    early = convolve(windows, taps, bias, 0, half)
    late = convolve(windows, taps, bias, half, half)
    columns = ring_pieces(piece, [taps, early, late]) if by_ring else [whole_columns(proj_weight)]
    coarse = project(place, early, late, columns, by_ring, proj_bias[None])

    grid = coarse[:ROWS].reshape(CELLS, 2, ACROSS, ACROSS, width)
    held = load_taps(after(place, coarse), bottle_weight, chans)
    field = with_halos(grid, 2, 3, 0, held)
    *far, held = bottle_terms(place, field, held, chans, bottle_weight)
    swapped = [chan_swap(value, chans // 2 + number) for number, value in enumerate(far)]
    own, *near = bottle_terms(place, field, held, chans)
    near = [chan_swap(value, 1 + number) for number, value in enumerate(near)]
    terms = [own, sum(value.astype(jnp.float32) for value in swapped)] + near
    guided = finish(place, guide, terms, bottle_bias[None])
    return guided.reshape(1, ACROSS, ACROSS, CELLS, width)


def solution(mesh):
    placed = (
        P("region", None, None, None, None),
        P(),
        P(),
        P(),
        P(),
        P(("chan", "region"), None),
        P(),
        P(None, "chan", None),
        P(),
        P(),
    )
    return jax.shard_map(
        shards,
        mesh=mesh,
        in_specs=placed,
        out_specs=P("region", None, None, None, "chan"),
        check_vma=False,
    )
```

```python
import functools

import numpy as np

import jax
import jax.numpy as jnp
from jax import lax
from jax.experimental import pallas as pl
from jax.experimental.pallas import tpu as pltpu
from jax.sharding import PartitionSpec as P

FINE_WIDTH = 128
COARSE_WIDTH = 1024
TILE_SIDE = 12
STRIDE = 4
REGIONS_Y = 4
REGIONS_Z = 2

CELLS = TILE_SIDE // STRIDE
ACROSS = 2 * CELLS
PLANE = 2 * ACROSS * ACROSS
ROWS = CELLS * PLANE
PADDED = -(-ROWS // 16) * 16
PHASES = STRIDE + 2
OFFSETS = STRIDE**3
LANES = 128
SPREAD = 8
MIB = 2**20


def vmem(count):
    return [pl.BlockSpec(memory_space=pltpu.VMEM) for _ in range(count)]


def regroup_kernel(*refs):
    rows_refs, out_ref, wide = refs[:-2], refs[-2], refs[-1]
    held = rows_refs[0].shape[0]
    groups = out_ref.shape[1]
    for lane in range(wide.shape[0]):
        columns = slice(lane * LANES, (lane + 1) * LANES)
        for number, rows_ref in enumerate(rows_refs):
            wide[lane, number * held : (number + 1) * held, :] = rows_ref[:, columns].astype(jnp.float32)
        for offset in range(OFFSETS):
            out_ref[offset, :, columns] = wide[
                lane, pl.ds(offset, groups, stride=OFFSETS), :
            ].astype(jnp.bfloat16)


def regroup(pieces):
    held, width = pieces[0].shape
    total = len(pieces) * held
    return pl.pallas_call(
        regroup_kernel,
        out_shape=jax.ShapeDtypeStruct((OFFSETS, total // OFFSETS, width), jnp.bfloat16),
        in_specs=vmem(len(pieces)),
        out_specs=vmem(1)[0],
        scratch_shapes=[pltpu.VMEM((width // LANES, total, LANES), jnp.float32)],
        compiler_params=pltpu.CompilerParams(vmem_limit_bytes=8 * MIB),
        name="regroup",
    )(*pieces)


def split_kernel(place_ref, rows_ref, *out_refs):
    width = out_refs[0].shape[1]
    for distance, out_ref in enumerate(out_refs):
        start = pl.multiple_of((place_ref[0] ^ distance) * width, width)
        out_ref[...] = rows_ref[:, pl.ds(start, width)]


def split_columns(place, rows, owners):
    held, width = rows.shape[0], rows.shape[1] // owners
    return pl.pallas_call(
        split_kernel,
        out_shape=[jax.ShapeDtypeStruct((held, width), rows.dtype)] * owners,
        in_specs=[pl.BlockSpec(memory_space=pltpu.SMEM)] + vmem(1),
        out_specs=vmem(owners),
        compiler_params=pltpu.CompilerParams(vmem_limit_bytes=4 * MIB),
        name="split_columns",
    )(place, rows)


def rows_kernel(first_ref, last_ref, low_ref, high_ref, wide):
    def take(at_x, carry):
        for rows_ref, row, out_ref in ((first_ref, 0, low_ref), (last_ref, 7, high_ref)):
            for at_z in range(TILE_SIDE):
                wide[at_z : at_z + 1, :] = rows_ref[at_x, at_z].astype(jnp.float32)[row : row + 1]
            out_ref[at_x] = wide[...].astype(jnp.bfloat16)
        return carry

    wide[...] = jnp.zeros_like(wide)
    lax.fori_loop(0, first_ref.shape[0], take, 0)


def y_rows(block):
    side_x, depth, side_y, width = block.shape
    return pl.pallas_call(
        rows_kernel,
        out_shape=(
            jax.ShapeDtypeStruct((side_x, 16, width), block.dtype),
            jax.ShapeDtypeStruct((side_x, 16, width), block.dtype),
        ),
        grid=(1,),
        in_specs=[
            pl.BlockSpec((side_x, depth, 8, width), lambda i: (0, 0, 0, 0)),
            pl.BlockSpec((side_x, depth, 8, width), lambda i: (0, 0, side_y // 8 - 1, 0)),
        ],
        out_specs=(
            pl.BlockSpec((side_x, 16, width), lambda i: (0, 0, 0)),
            pl.BlockSpec((side_x, 16, width), lambda i: (0, 0, 0)),
        ),
        scratch_shapes=[pltpu.VMEM((16, width), jnp.float32)],
        compiler_params=pltpu.CompilerParams(vmem_limit_bytes=12 * MIB),
        name="y_rows",
    )(block, block)


def window_kernel(
    inside_ref, block_ref, layer_ref, below_ref, above_ref, outer_ref, scale_ref, shift_ref,
    weight_ref, order_ref, windows_ref, taps_ref, rows, line, layers,
):
    phase_x = pl.program_id(0)
    side, depth, width = 2 * TILE_SIDE, TILE_SIDE, FINE_WIDTH
    half = 2 * ACROSS * side

    @pl.when(phase_x == 0)
    def _():
        zero = jnp.zeros((width, width), jnp.bfloat16)
        for place in range(9):
            taps_ref[place, 3 * width :, :width] = zero
            taps_ref[place, :width, width:] = zero
            for step in range(3):
                block = jnp.dot(
                    weight_ref[place * 3 + step], order_ref[...], preferred_element_type=jnp.float32
                ).astype(jnp.bfloat16)
                taps_ref[place, step * width : (step + 1) * width, :width] = block
                taps_ref[place, (step + 1) * width : (step + 2) * width, width:] = block

        def widen(at_x, carry):
            rows[0, at_x] = below_ref[at_x].astype(jnp.float32)
            rows[1, at_x] = above_ref[at_x].astype(jnp.float32)
            return carry

        lax.fori_loop(0, side, widen, 0)

    scale = jnp.broadcast_to(scale_ref[...], (8, width))
    shift = jnp.broadcast_to(shift_ref[...], (8, width))
    row = lax.broadcasted_iota(jnp.int32, (8, width), 0)
    first = jnp.where(row == 0, shift * inside_ref[2], shift)
    last = jnp.where(row == side + 1 - 20, shift * inside_ref[3], shift)
    chunks = [(0, first), (8, shift), (16, shift), (4, shift), (12, shift), (20, last)]

    def split(cell_x, carry):
        at_x = phase_x + STRIDE * cell_x
        outside = jnp.logical_or(at_x == 0, at_x == side + 1)

        @pl.when(jnp.logical_not(outside))
        def _():
            at = at_x - 1
            for at_z in range(depth + 2):
                if at_z == 0:
                    flag, value, place = inside_ref[4], layer_ref[at], depth
                elif at_z == depth + 1:
                    flag, value, place = inside_ref[5], layer_ref[at], depth
                else:
                    flag, value, place = None, block_ref[at, at_z - 1], at_z - 1
                value = value.astype(jnp.float32)
                low, high = rows[0, at, place : place + 1, :], rows[1, at, place : place + 1, :]
                if flag is not None:
                    value, low, high = value * flag, low * flag, high * flag
                line[at_z, 7:8, :] = low
                line[at_z, 8 : side + 8, :] = value
                line[at_z, side + 8 : side + 9, :] = high

        @pl.when(outside)
        def _():
            end = jnp.where(at_x == 0, 0, 1)
            for at_z in range(depth + 2):
                value = outer_ref[end, at_z].astype(jnp.float32)
                line[at_z, 0:8, :] = value[side : side + 8]
                line[at_z, 8 : side + 8, :] = value[:side]
                line[at_z, side + 8 : side + 16, :] = value[side : side + 8]

        within = jnp.where(at_x == 0, inside_ref[0], 1.0)
        within = jnp.where(at_x == side + 1, inside_ref[1], within)
        for at_z in range(depth + 2):
            if at_z == 0:
                factor = within * inside_ref[4]
            elif at_z == depth + 1:
                factor = within * inside_ref[5]
            else:
                factor = within
            for number, (start, added) in enumerate(chunks):
                value = line[at_z, pl.ds(start + 7, 8), :]
                base = number // 3 * half + number % 3 * 8
                base = pl.multiple_of(base + cell_x * side, 8)
                layers[at_z, pl.ds(base, 8), :] = value
                layers[at_z, pl.ds(base + half // 2, 8), :] = value * scale + added * factor
        return carry

    lax.fori_loop(0, ACROSS, split, 0)
    for phase_y in range(PHASES):
        start = phase_y if phase_y < STRIDE else half + phase_y - STRIDE
        for phase_z in range(PHASES):
            parts = [
                layers[phase_z + STRIDE * cell, pl.ds(start, PLANE, stride=STRIDE), :]
                for cell in range(CELLS)
            ]
            parts.append(jnp.zeros((PADDED - ROWS, width), jnp.float32))
            windows_ref[0, phase_y, :, phase_z * width : (phase_z + 1) * width] = jnp.concatenate(
                parts, axis=0
            ).astype(jnp.bfloat16)


def make_windows(inside, *arrays):
    width, side = FINE_WIDTH, 2 * TILE_SIDE

    def whole(array):
        return pl.BlockSpec(array.shape, lambda i: (0,) * array.ndim)

    return pl.pallas_call(
        window_kernel,
        out_shape=(
            jax.ShapeDtypeStruct((PHASES, PHASES, PADDED, PHASES * width), jnp.bfloat16),
            jax.ShapeDtypeStruct((9, 4 * width, 2 * width), jnp.bfloat16),
        ),
        grid=(PHASES,),
        in_specs=[pl.BlockSpec(memory_space=pltpu.SMEM)] + [whole(array) for array in arrays],
        out_specs=(
            pl.BlockSpec((1, PHASES, PADDED, PHASES * width), lambda i: (i, 0, 0, 0)),
            pl.BlockSpec((9, 4 * width, 2 * width), lambda i: (0, 0, 0)),
        ),
        scratch_shapes=[
            pltpu.VMEM((2, side, 16, width), jnp.float32),
            pltpu.VMEM((TILE_SIDE + 2, side + 16, width), jnp.float32),
            pltpu.VMEM((TILE_SIDE + 2, 4 * ACROSS * side, width), jnp.float32),
        ],
        compiler_params=pltpu.CompilerParams(vmem_limit_bytes=28 * MIB),
        cost_estimate=pl.CostEstimate(flops=10**10, bytes_accessed=16 * MIB, transcendentals=0),
        name="windows",
    )(inside, *arrays)


def convolve_kernel(first_ref, second_ref, third_ref, taps_ref, bias_ref, out_ref):
    width = FINE_WIDTH
    bias = bias_ref[...]

    def convolve(at_y, carry):
        total = jnp.zeros((2 * PADDED, 2 * width), jnp.float32)
        for step_x, windows_ref in enumerate((first_ref, second_ref, third_ref)):
            for step_y in range(3):
                taken = [
                    windows_ref[0, at_y + step_y, :, pair * 2 * width : (pair * 2 + 4) * width]
                    for pair in range(2)
                ]
                total += jnp.dot(
                    jnp.concatenate(taken, axis=0),
                    taps_ref[step_x * 3 + step_y],
                    preferred_element_type=jnp.float32,
                )
        total = total + bias
        hidden = (total / (1.0 + jnp.exp(-total))).astype(jnp.bfloat16)
        for pair in range(2):
            out_ref[at_y * 2 + pair] = hidden[pair * PADDED : (pair + 1) * PADDED]
        return carry

    lax.fori_loop(0, STRIDE, convolve, 0)


def convolve(windows, taps, bias, start, count):
    width = FINE_WIDTH
    each = STRIDE * STRIDE // 2
    block = (1, PHASES, PADDED, PHASES * width)
    return pl.pallas_call(
        convolve_kernel,
        out_shape=jax.ShapeDtypeStruct((count * each, PADDED, 2 * width), jnp.bfloat16),
        grid=(count,),
        in_specs=[
            pl.BlockSpec(block, lambda i, step=step: (i + start + step, 0, 0, 0)) for step in range(3)
        ]
        + [
            pl.BlockSpec(taps.shape, lambda i: (0, 0, 0)),
            pl.BlockSpec(bias.shape, lambda i: (0, 0)),
        ],
        out_specs=pl.BlockSpec((each, PADDED, 2 * width), lambda i: (i, 0, 0)),
        compiler_params=pltpu.CompilerParams(vmem_limit_bytes=28 * MIB),
        cost_estimate=pl.CostEstimate(
            flops=2 * count * each * PADDED * 36 * width * 2 * width,
            bytes_accessed=16 * MIB,
            transcendentals=count * each * PADDED * 2 * width,
        ),
        name="convolve",
    )(windows, windows, windows, taps, bias)


def project_kernel(split, place_ref, early_ref, late_ref, *refs):
    weight_refs, bias_ref, out_ref = refs[:-2], refs[-2], refs[-1]
    width = out_ref.shape[1]
    start = pl.multiple_of(place_ref[0] * width, width)
    total = jnp.broadcast_to(bias_ref[:, pl.ds(start, width)], out_ref.shape)
    pairs = early_ref.shape[0]
    for number, hidden_ref in enumerate((early_ref, late_ref)):
        used = weight_refs[:-2] + (weight_refs[len(weight_refs) - 2 + number],) if split else weight_refs
        for pair in range(pairs):
            weight = jnp.concatenate(
                [
                    ref[2 * pair + item + (number * 2 * pairs if ref.shape[0] == OFFSETS else 0)]
                    for item in range(2)
                    for ref in used
                ],
                axis=0,
            )
            total += jnp.dot(hidden_ref[pair], weight, preferred_element_type=jnp.float32)
    out_ref[...] = total.astype(jnp.bfloat16)


def project(place, early, late, weights, split, bias):
    pairs, rows, depth = early.shape
    width = weights[0].shape[2]
    return pl.pallas_call(
        functools.partial(project_kernel, split),
        out_shape=jax.ShapeDtypeStruct((rows, width), jnp.bfloat16),
        in_specs=[pl.BlockSpec(memory_space=pltpu.SMEM)] + vmem(len(weights) + 3),
        out_specs=vmem(1)[0],
        compiler_params=pltpu.CompilerParams(vmem_limit_bytes=24 * MIB),
        cost_estimate=pl.CostEstimate(
            flops=4 * pairs * rows * depth * width, bytes_accessed=8 * MIB, transcendentals=0
        ),
        name="project",
    )(place, early, late, *weights, bias)


def bottle_kernel(far, place_ref, field_ref, weight_ref, *refs):
    out_refs, (held, total, packed, dense, sems) = refs[:-5], refs[-5:]
    width = field_ref.shape[4]
    share = out_refs[0].shape[1]
    span = held.shape[2]
    frame = ACROSS + 2
    rows = CELLS * 2 * ACROSS * frame
    chunk = 256
    owners = 2 * len(out_refs)
    first = pl.multiple_of((place_ref[0] // len(out_refs) ^ far) * span, span)

    def copy_of(step_y, place):
        tap = (place // 3 * 3 + step_y) * 3 + place % 3
        return pltpu.make_async_copy(
            weight_ref.at[tap, :, pl.ds(first, span)],
            held.at[step_y, pl.ds(place * width, width)],
            sems.at[step_y, place],
        )

    for step_y in range(3):
        for place in range(9):
            copy_of(step_y, place).start()

    for step_x in range(3):
        for step_z in range(3):
            place = step_x * 3 + step_z
            packed[:, place * width : (place + 1) * width] = (
                field_ref[step_z : step_z + CELLS, :, step_x : step_x + ACROSS]
                .astype(jnp.float32)
                .reshape(rows, width)
                .astype(jnp.bfloat16)
            )

    for step_x in range(3):
        for step_z in range(3):
            copy_of(0, step_x * 3 + step_z).wait()
        depth = slice(step_x * 3 * width, (step_x + 1) * 3 * width)
        for start in range(0, span, chunk):
            columns = slice(start, start + chunk)
            terms = jnp.dot(
                packed[:, depth], held[0, depth, columns], preferred_element_type=jnp.float32
            )
            total[0, :, columns] = terms if step_x == 0 else total[0, :, columns] + terms

    def rest(step_y, carry):
        for place in range(9):
            copy_of(step_y, place).wait()
        for start in range(0, span, chunk):
            columns = slice(start, start + chunk)
            total[step_y, :, columns] = jnp.dot(
                packed[...], held[step_y, :, columns], preferred_element_type=jnp.float32
            )
        return carry

    lax.fori_loop(1, 3, rest, 0)

    for number, out_ref in enumerate(out_refs):
        distance = number + far * owners // 2
        start = pl.multiple_of((place_ref[0] ^ distance) % len(out_refs) * share, share)
        for group in range(rows // frame):
            at = group * frame
            dense[group * ACROSS : (group + 1) * ACROSS, :] = sum(
                total[item, at + item : at + item + ACROSS, pl.ds(start, share)]
                for item in range(3)
            )
        out_ref[...] = dense[...].astype(out_ref.dtype)


def bottle_terms(place, field, weight, owners, far):
    frame = ACROSS + 2
    rows = CELLS * 2 * ACROSS * frame
    width = weight.shape[1]
    share = COARSE_WIDTH // owners
    span = COARSE_WIDTH // 2
    return pl.pallas_call(
        functools.partial(bottle_kernel, int(far)),
        out_shape=[
            jax.ShapeDtypeStruct((ROWS, share), jnp.bfloat16 if far or number else jnp.float32)
            for number in range(owners // 2)
        ],
        in_specs=[
            pl.BlockSpec(memory_space=pltpu.SMEM),
            pl.BlockSpec(memory_space=pltpu.VMEM),
            pl.BlockSpec(memory_space=pltpu.HBM),
        ],
        out_specs=vmem(owners // 2),
        scratch_shapes=[
            pltpu.VMEM((3, 9 * width, span), jnp.bfloat16),
            pltpu.VMEM((3, rows, span), jnp.float32),
            pltpu.VMEM((rows, 9 * width), jnp.bfloat16),
            pltpu.VMEM((ROWS, share), jnp.float32),
            pltpu.SemaphoreType.DMA((3, 9)),
        ],
        compiler_params=pltpu.CompilerParams(vmem_limit_bytes=51 * MIB),
        cost_estimate=pl.CostEstimate(
            flops=2 * rows * 27 * width * span, bytes_accessed=8 * MIB, transcendentals=0
        ),
        name="bottle_far" if far else "bottle_near",
    )(place, field, weight)


def finish_kernel(place_ref, guide_ref, own_ref, *refs):
    other_refs, bias_ref, out_ref, spread = refs[:-3], refs[-3], refs[-2], refs[-1]
    share = own_ref.shape[1]
    start = pl.multiple_of(place_ref[0] * share, share)
    value = own_ref[...] + bias_ref[:, pl.ds(start, share)]
    for other_ref in other_refs:
        value = value + other_ref[...].astype(jnp.float32)
    value = value / (1.0 + jnp.exp(-value))
    half = PLANE // 2
    for cell in range(CELLS):
        plain = value[cell * PLANE : cell * PLANE + half]
        guided = value[cell * PLANE + half : (cell + 1) * PLANE]
        mixed = plain + guide_ref[0] * (guided - plain)
        for lane in range(spread.shape[0]):
            spread[lane, pl.ds(cell, half, stride=SPREAD), :] = mixed[:, lane * LANES : (lane + 1) * LANES]
    for lane in range(spread.shape[0]):
        for cell in range(half):
            out_ref[cell, :, lane * LANES : (lane + 1) * LANES] = spread[
                lane, cell * SPREAD : cell * SPREAD + CELLS, :
            ].astype(jnp.bfloat16)


def finish(place, guide, terms, bias):
    share = terms[0].shape[1]
    return pl.pallas_call(
        finish_kernel,
        out_shape=jax.ShapeDtypeStruct((PLANE // 2, CELLS, share), jnp.bfloat16),
        in_specs=[pl.BlockSpec(memory_space=pltpu.SMEM)] * 2 + vmem(len(terms) + 1),
        out_specs=vmem(1)[0],
        scratch_shapes=[pltpu.VMEM((share // LANES, PLANE // 2 * SPREAD, LANES), jnp.float32)],
        compiler_params=pltpu.CompilerParams(vmem_limit_bytes=8 * MIB),
        name="finish",
    )(place, guide, *terms, bias)


def passed(value, steps):
    count = lax.axis_size("region")
    return lax.ppermute(
        value, "region", [(at, at + steps) for at in range(max(0, -steps), min(count, count - steps))]
    )


def across_z(value):
    count = lax.axis_size("region")
    return lax.ppermute(value, "region", [(at, at ^ 1) for at in range(count)])


def y_halos(first, last):
    place = lax.axis_index("region") // REGIONS_Z % REGIONS_Y
    upper = is_upper()
    ahead = hop(jnp.where(upper, first, last), True)
    back = hop(jnp.where(upper, last, first), False)
    zero = jnp.zeros_like(ahead)
    below = jnp.where(place > 0, jnp.where(upper, back, ahead), zero)
    above = jnp.where(place < REGIONS_Y - 1, jnp.where(upper, ahead, back), zero)
    return below, above


def with_halos(value, dim_x, dim_y, dim_z):
    value = jnp.concatenate(z_ends(z_layer(value, dim_z), value, dim_z), axis=dim_z)
    below, above = y_halos(edge(value, dim_y, False), edge(value, dim_y, True))
    value = jnp.concatenate([below, value, above], axis=dim_y)
    low, high = x_layers(edge(value, dim_x, False), edge(value, dim_x, True))
    return jnp.concatenate([low, value, high], axis=dim_x)


def edge(array, dim, last):
    size = array.shape[dim]
    return lax.slice_in_dim(array, size - 1 if last else 0, size if last else 1, axis=dim)


def is_upper():
    return lax.axis_index("region") % REGIONS_Z == 1


def z_layer(value, dim):
    return across_z(jnp.where(is_upper(), edge(value, dim, False), edge(value, dim, True)))


def z_ends(layer, value, dim):
    zero = jnp.zeros_like(layer)
    return [jnp.where(is_upper(), layer, zero), value, jnp.where(is_upper(), zero, layer)]


def x_layers(first, last):
    count = lax.axis_size("region") // (REGIONS_Y * REGIONS_Z)
    if count == 1:
        return jnp.zeros_like(last), jnp.zeros_like(first)
    return passed(last, REGIONS_Y * REGIONS_Z), passed(first, -REGIONS_Y * REGIONS_Z)


def chan_swap(value, distance):
    return lax.ppermute(value, "chan", [(at, at ^ distance) for at in range(lax.axis_size("chan"))])


def exchange(piece_at):
    chans = lax.axis_size("chan")
    return [piece_at(0)] + [chan_swap(piece_at(distance), distance) for distance in range(1, chans)]


def ring_of(count):
    return list(range(0, count, 2)) + list(range(1, count, 2))[::-1]


def hop(value, ahead):
    ring = ring_of(lax.axis_size("region"))
    following = ring[1:] + ring[:1]
    return lax.ppermute(value, "region", list(zip(ring, following) if ahead else zip(following, ring)))


def after(value, other):
    return lax.optimization_barrier((value, other))[0]


def piece_channels(each):
    chans, regions = lax.axis_size("chan"), lax.axis_size("region")
    ring = ring_of(regions)
    shifts = [0]
    for step in range(1, regions // 2 + 1):
        shifts += [-step] + [step] * (step < regions // 2)
    origin = np.array(
        [[ring[(ring.index(region) + shift) % regions] for shift in shifts] for region in range(regions)]
    )
    table = np.zeros((chans, regions, regions, chans, each), np.int32)
    for chan in range(chans):
        for distance in range(chans):
            first = (chan ^ distance) * regions + origin
            table[chan, :, :, distance] = first[:, :, None] * each + np.arange(each)
    table = jnp.asarray(table.reshape(chans * regions, FINE_WIDTH))
    device = lax.axis_index("chan") * regions + lax.axis_index("region")
    return lax.dynamic_index_in_dim(table, device, 0, keepdims=True)


def ring_pieces(piece, milestones):
    regions = lax.axis_size("region")
    forward = backward = piece
    held = [piece]
    for step in range(1, regions // 2 + 1):
        if step > 1 and step - 2 < len(milestones):
            forward, backward = (after(value, milestones[step - 2]) for value in (forward, backward))
        if step == regions // 2:
            held += [hop(forward[: OFFSETS // 2], True), hop(backward[OFFSETS // 2 :], False)]
        else:
            forward, backward = hop(forward, True), hop(backward, False)
            held += [forward, backward]
    return held


def whole_columns(proj_weight):
    chans, held = lax.axis_size("chan"), proj_weight.shape[0]
    width = COARSE_WIDTH // chans
    mine = lax.all_to_all(proj_weight, "chan", split_axis=1, concat_axis=0, tiled=True)
    whole = lax.all_gather(mine.reshape(chans, held, width), "region", axis=1, tiled=True)
    return whole.reshape(FINE_WIDTH, OFFSETS, width).transpose(1, 0, 2)


def shards(
    latent,
    cond_scale,
    cond_shift,
    fine_weight,
    fine_bias,
    proj_weight,
    proj_bias,
    bottle_weight,
    bottle_bias,
    guide,
):
    chans = lax.axis_size("chan")
    chan_place = lax.axis_index("chan")
    region = lax.axis_index("region")
    width = COARSE_WIDTH // chans
    side = 2 * TILE_SIDE
    count_x = lax.axis_size("region") // (REGIONS_Y * REGIONS_Z)
    steps = (REGIONS_Y * REGIONS_Z, REGIONS_Z, 1)
    counts = (count_x, REGIONS_Y, REGIONS_Z)
    places = [region // step % count for step, count in zip(steps, counts)]
    inside = jnp.stack(
        [
            flag
            for place, count in zip(places, counts)
            for flag in ((place > 0).astype(jnp.float32), (place < count - 1).astype(jnp.float32))
        ]
    )

    place = chan_place[None]
    each, rest = divmod(proj_weight.shape[0], OFFSETS)
    by_ring = rest == 0 and chans * each % 16 == 0
    if by_ring:
        split = split_columns(place, proj_weight, chans)
        mine = exchange(lambda distance: split[distance])
        piece = regroup(mine)
        channel = piece_channels(each)
    else:
        channel = jnp.arange(FINE_WIDTH, dtype=jnp.int32)[None]
    order = lax.broadcasted_iota(jnp.int32, (FINE_WIDTH, FINE_WIDTH), 0) == channel

    block = latent[0].transpose(0, 2, 1, 3)
    face = lax.dynamic_index_in_dim(
        block, jnp.where(is_upper(), 0, TILE_SIDE - 1), axis=1, keepdims=False
    )
    first, last = y_rows(block)
    layer = across_z(face)
    corner = lax.broadcasted_iota(jnp.int32, first.shape, 1) == TILE_SIDE
    below, above = y_halos(
        jnp.where(corner, layer[:, :1], first), jnp.where(corner, layer[:, -1:], last)
    )
    ends = []
    for at in (0, -1):
        plane = jnp.concatenate(z_ends(layer[at][None], block[at], 0), axis=0)
        low, high = [
            jnp.concatenate(
                z_ends(part[at, TILE_SIDE : TILE_SIDE + 1], part[at, :TILE_SIDE], 0), axis=0
            )[:, None]
            for part in (below, above)
        ]
        spare = jnp.zeros((TILE_SIDE + 2, 6, FINE_WIDTH), plane.dtype)
        ends.append(jnp.concatenate([plane, high, spare, low], axis=1))
    outer = jnp.stack(x_layers(*ends))

    bias = jnp.sum(jnp.where(order, fine_bias[:, None], 0.0), axis=0)
    windows, taps = make_windows(
        inside,
        block,
        layer,
        below,
        above,
        outer,
        cond_scale[None],
        cond_shift[None],
        fine_weight.reshape(27, FINE_WIDTH, FINE_WIDTH),
        order.astype(jnp.bfloat16),
    )
    bias = jnp.concatenate([bias, bias])[None]
    half = STRIDE // 2
    early = convolve(windows, taps, bias, 0, half)
    late = convolve(windows, taps, bias, half, half)
    columns = ring_pieces(piece, [taps, early, late]) if by_ring else [whole_columns(proj_weight)]
    coarse = project(place, early, late, columns, by_ring, proj_bias[None])

    grid = coarse[:ROWS].reshape(CELLS, 2, ACROSS, ACROSS, width)
    field = with_halos(grid, 2, 3, 0)
    far = bottle_terms(place, field, bottle_weight, chans, True)
    swapped = [chan_swap(value, chans // 2 + number) for number, value in enumerate(far)]
    own, *near = bottle_terms(after(place, far), field, bottle_weight, chans, False)
    near = [chan_swap(value, 1 + number) for number, value in enumerate(near)]
    terms = [own, sum(value.astype(jnp.float32) for value in swapped)] + near
    guided = finish(place, guide, terms, bottle_bias[None])
    return guided.reshape(1, ACROSS, ACROSS, CELLS, width)


def solution(mesh):
    placed = (
        P("region", None, None, None, None),
        P(),
        P(),
        P(),
        P(),
        P(("chan", "region"), None),
        P(),
        P(None, "chan", None),
        P(),
        P(),
    )
    return jax.shard_map(
        shards,
        mesh=mesh,
        in_specs=placed,
        out_specs=P("region", None, None, None, "chan"),
        check_vma=False,
    )
```

```python
import functools

import numpy as np

import jax
import jax.numpy as jnp
from jax import lax
from jax.experimental import pallas as pl
from jax.experimental.pallas import tpu as pltpu
from jax.sharding import PartitionSpec as P

FINE_WIDTH = 128
COARSE_WIDTH = 1024
TILE_SIDE = 12
STRIDE = 4
REGIONS_Y = 4
REGIONS_Z = 2

CELLS = TILE_SIDE // STRIDE
ACROSS = 2 * CELLS
PLANE = 2 * ACROSS * ACROSS
ROWS = CELLS * PLANE
PADDED = -(-ROWS // 16) * 16
PHASES = STRIDE + 2
OFFSETS = STRIDE**3
LANES = 128
SPREAD = 8
MIB = 2**20


def vmem(count):
    return [pl.BlockSpec(memory_space=pltpu.VMEM) for _ in range(count)]


def regroup_kernel(*refs):
    rows_refs, out_ref, wide = refs[:-2], refs[-2], refs[-1]
    held = rows_refs[0].shape[0]
    groups = out_ref.shape[1]
    for lane in range(wide.shape[0]):
        columns = slice(lane * LANES, (lane + 1) * LANES)
        for number, rows_ref in enumerate(rows_refs):
            wide[lane, number * held : (number + 1) * held, :] = rows_ref[:, columns].astype(jnp.float32)
        for offset in range(OFFSETS):
            out_ref[offset, :, columns] = wide[
                lane, pl.ds(offset, groups, stride=OFFSETS), :
            ].astype(jnp.bfloat16)


def regroup(pieces):
    held, width = pieces[0].shape
    total = len(pieces) * held
    return pl.pallas_call(
        regroup_kernel,
        out_shape=jax.ShapeDtypeStruct((OFFSETS, total // OFFSETS, width), jnp.bfloat16),
        in_specs=vmem(len(pieces)),
        out_specs=vmem(1)[0],
        scratch_shapes=[pltpu.VMEM((width // LANES, total, LANES), jnp.float32)],
        compiler_params=pltpu.CompilerParams(vmem_limit_bytes=8 * MIB),
        name="regroup",
    )(*pieces)


def split_kernel(place_ref, rows_ref, *out_refs):
    width = out_refs[0].shape[1]
    for distance, out_ref in enumerate(out_refs):
        start = pl.multiple_of((place_ref[0] ^ distance) * width, width)
        out_ref[...] = rows_ref[:, pl.ds(start, width)]


def split_columns(place, rows, owners):
    held, width = rows.shape[0], rows.shape[1] // owners
    return pl.pallas_call(
        split_kernel,
        out_shape=[jax.ShapeDtypeStruct((held, width), rows.dtype)] * owners,
        in_specs=[pl.BlockSpec(memory_space=pltpu.SMEM)] + vmem(1),
        out_specs=vmem(owners),
        compiler_params=pltpu.CompilerParams(vmem_limit_bytes=4 * MIB),
        name="split_columns",
    )(place, rows)


def window_kernel(
    inside_ref, block_ref, layer_ref, below_ref, above_ref, outer_ref, scale_ref, shift_ref,
    weight_ref, order_ref, windows_ref, taps_ref, rows, line, layers,
):
    phase_x = pl.program_id(0)
    side, depth, width = 2 * TILE_SIDE, TILE_SIDE, FINE_WIDTH
    half = 2 * ACROSS * side

    @pl.when(phase_x == 0)
    def _():
        zero = jnp.zeros((width, width), jnp.bfloat16)
        for place in range(9):
            taps_ref[place, 3 * width :, :width] = zero
            taps_ref[place, :width, width:] = zero
            for step in range(3):
                block = jnp.dot(
                    weight_ref[place * 3 + step], order_ref[...], preferred_element_type=jnp.float32
                ).astype(jnp.bfloat16)
                taps_ref[place, step * width : (step + 1) * width, :width] = block
                taps_ref[place, (step + 1) * width : (step + 2) * width, width:] = block

        def widen(at_x, carry):
            rows[0, at_x] = below_ref[at_x].astype(jnp.float32)
            rows[1, at_x] = above_ref[at_x].astype(jnp.float32)
            return carry

        lax.fori_loop(0, side, widen, 0)

    scale = jnp.broadcast_to(scale_ref[...], (8, width))
    shift = jnp.broadcast_to(shift_ref[...], (8, width))
    row = lax.broadcasted_iota(jnp.int32, (8, width), 0)
    first = jnp.where(row == 0, shift * inside_ref[2], shift)
    last = jnp.where(row == side + 1 - 20, shift * inside_ref[3], shift)
    chunks = [(0, first), (8, shift), (16, shift), (4, shift), (12, shift), (20, last)]

    def split(cell_x, carry):
        at_x = phase_x + STRIDE * cell_x
        outside = jnp.logical_or(at_x == 0, at_x == side + 1)

        @pl.when(jnp.logical_not(outside))
        def _():
            at = at_x - 1
            for at_z in range(depth + 2):
                if at_z == 0:
                    flag, value, place = inside_ref[4], layer_ref[at], depth
                elif at_z == depth + 1:
                    flag, value, place = inside_ref[5], layer_ref[at], depth
                else:
                    flag, value, place = None, block_ref[at, at_z - 1], at_z - 1
                value = value.astype(jnp.float32)
                low, high = rows[0, at, place : place + 1, :], rows[1, at, place : place + 1, :]
                if flag is not None:
                    value, low, high = value * flag, low * flag, high * flag
                line[at_z, 7:8, :] = low
                line[at_z, 8 : side + 8, :] = value
                line[at_z, side + 8 : side + 9, :] = high

        @pl.when(outside)
        def _():
            end = jnp.where(at_x == 0, 0, 1)
            for at_z in range(depth + 2):
                value = outer_ref[end, at_z].astype(jnp.float32)
                line[at_z, 0:8, :] = value[side : side + 8]
                line[at_z, 8 : side + 8, :] = value[:side]
                line[at_z, side + 8 : side + 16, :] = value[side : side + 8]

        within = jnp.where(at_x == 0, inside_ref[0], 1.0)
        within = jnp.where(at_x == side + 1, inside_ref[1], within)
        for at_z in range(depth + 2):
            if at_z == 0:
                factor = within * inside_ref[4]
            elif at_z == depth + 1:
                factor = within * inside_ref[5]
            else:
                factor = within
            for number, (start, added) in enumerate(chunks):
                value = line[at_z, pl.ds(start + 7, 8), :]
                base = number // 3 * half + number % 3 * 8
                base = pl.multiple_of(base + cell_x * side, 8)
                layers[at_z, pl.ds(base, 8), :] = value
                layers[at_z, pl.ds(base + half // 2, 8), :] = value * scale + added * factor
        return carry

    lax.fori_loop(0, ACROSS, split, 0)
    for phase_y in range(PHASES):
        start = phase_y if phase_y < STRIDE else half + phase_y - STRIDE
        for phase_z in range(PHASES):
            parts = [
                layers[phase_z + STRIDE * cell, pl.ds(start, PLANE, stride=STRIDE), :]
                for cell in range(CELLS)
            ]
            parts.append(jnp.zeros((PADDED - ROWS, width), jnp.float32))
            windows_ref[0, phase_y, :, phase_z * width : (phase_z + 1) * width] = jnp.concatenate(
                parts, axis=0
            ).astype(jnp.bfloat16)


def make_windows(inside, *arrays):
    width, side = FINE_WIDTH, 2 * TILE_SIDE

    def whole(array):
        return pl.BlockSpec(array.shape, lambda i: (0,) * array.ndim)

    return pl.pallas_call(
        window_kernel,
        out_shape=(
            jax.ShapeDtypeStruct((PHASES, PHASES, PADDED, PHASES * width), jnp.bfloat16),
            jax.ShapeDtypeStruct((9, 4 * width, 2 * width), jnp.bfloat16),
        ),
        grid=(PHASES,),
        in_specs=[pl.BlockSpec(memory_space=pltpu.SMEM)] + [whole(array) for array in arrays],
        out_specs=(
            pl.BlockSpec((1, PHASES, PADDED, PHASES * width), lambda i: (i, 0, 0, 0)),
            pl.BlockSpec((9, 4 * width, 2 * width), lambda i: (0, 0, 0)),
        ),
        scratch_shapes=[
            pltpu.VMEM((2, side, 16, width), jnp.float32),
            pltpu.VMEM((TILE_SIDE + 2, side + 16, width), jnp.float32),
            pltpu.VMEM((TILE_SIDE + 2, 4 * ACROSS * side, width), jnp.float32),
        ],
        compiler_params=pltpu.CompilerParams(vmem_limit_bytes=28 * MIB),
        cost_estimate=pl.CostEstimate(flops=10**10, bytes_accessed=16 * MIB, transcendentals=0),
        name="windows",
    )(inside, *arrays)


def convolve_kernel(first_ref, second_ref, third_ref, taps_ref, bias_ref, out_ref):
    width = FINE_WIDTH
    bias = bias_ref[...]

    def convolve(at_y, carry):
        total = jnp.zeros((2 * PADDED, 2 * width), jnp.float32)
        for step_x, windows_ref in enumerate((first_ref, second_ref, third_ref)):
            for step_y in range(3):
                taken = [
                    windows_ref[0, at_y + step_y, :, pair * 2 * width : (pair * 2 + 4) * width]
                    for pair in range(2)
                ]
                total += jnp.dot(
                    jnp.concatenate(taken, axis=0),
                    taps_ref[step_x * 3 + step_y],
                    preferred_element_type=jnp.float32,
                )
        total = total + bias
        hidden = (total / (1.0 + jnp.exp(-total))).astype(jnp.bfloat16)
        for pair in range(2):
            out_ref[at_y * 2 + pair] = hidden[pair * PADDED : (pair + 1) * PADDED]
        return carry

    lax.fori_loop(0, STRIDE, convolve, 0)


def convolve(windows, taps, bias, start, count):
    width = FINE_WIDTH
    each = STRIDE * STRIDE // 2
    block = (1, PHASES, PADDED, PHASES * width)
    return pl.pallas_call(
        convolve_kernel,
        out_shape=jax.ShapeDtypeStruct((count * each, PADDED, 2 * width), jnp.bfloat16),
        grid=(count,),
        in_specs=[
            pl.BlockSpec(block, lambda i, step=step: (i + start + step, 0, 0, 0)) for step in range(3)
        ]
        + [
            pl.BlockSpec(taps.shape, lambda i: (0, 0, 0)),
            pl.BlockSpec(bias.shape, lambda i: (0, 0)),
        ],
        out_specs=pl.BlockSpec((each, PADDED, 2 * width), lambda i: (i, 0, 0)),
        compiler_params=pltpu.CompilerParams(vmem_limit_bytes=28 * MIB),
        cost_estimate=pl.CostEstimate(
            flops=2 * count * each * PADDED * 36 * width * 2 * width,
            bytes_accessed=16 * MIB,
            transcendentals=count * each * PADDED * 2 * width,
        ),
        name="convolve",
    )(windows, windows, windows, taps, bias)


def project_kernel(split, place_ref, early_ref, late_ref, *refs):
    weight_refs, bias_ref, out_ref = refs[:-2], refs[-2], refs[-1]
    width = out_ref.shape[1]
    start = pl.multiple_of(place_ref[0] * width, width)
    total = jnp.broadcast_to(bias_ref[:, pl.ds(start, width)], out_ref.shape)
    pairs = early_ref.shape[0]
    for number, hidden_ref in enumerate((early_ref, late_ref)):
        used = weight_refs[:-2] + (weight_refs[len(weight_refs) - 2 + number],) if split else weight_refs
        for pair in range(pairs):
            weight = jnp.concatenate(
                [
                    ref[2 * pair + item + (number * 2 * pairs if ref.shape[0] == OFFSETS else 0)]
                    for item in range(2)
                    for ref in used
                ],
                axis=0,
            )
            total += jnp.dot(hidden_ref[pair], weight, preferred_element_type=jnp.float32)
    out_ref[...] = total.astype(jnp.bfloat16)


def project(place, early, late, weights, split, bias):
    pairs, rows, depth = early.shape
    width = weights[0].shape[2]
    return pl.pallas_call(
        functools.partial(project_kernel, split),
        out_shape=jax.ShapeDtypeStruct((rows, width), jnp.bfloat16),
        in_specs=[pl.BlockSpec(memory_space=pltpu.SMEM)] + vmem(len(weights) + 3),
        out_specs=vmem(1)[0],
        compiler_params=pltpu.CompilerParams(vmem_limit_bytes=24 * MIB),
        cost_estimate=pl.CostEstimate(
            flops=4 * pairs * rows * depth * width, bytes_accessed=8 * MIB, transcendentals=0
        ),
        name="project",
    )(place, early, late, *weights, bias)


def bottle_kernel(far, place_ref, field_ref, weight_ref, *refs):
    out_refs, (held, total, packed, dense, sems) = refs[:-5], refs[-5:]
    width = field_ref.shape[4]
    share = out_refs[0].shape[1]
    span = held.shape[2]
    frame = ACROSS + 2
    rows = CELLS * 2 * ACROSS * frame
    chunk = 256
    owners = 2 * len(out_refs)
    first = pl.multiple_of((place_ref[0] // len(out_refs) ^ far) * span, span)

    def copy_of(step_y, place):
        tap = (place // 3 * 3 + step_y) * 3 + place % 3
        return pltpu.make_async_copy(
            weight_ref.at[tap, :, pl.ds(first, span)],
            held.at[step_y, pl.ds(place * width, width)],
            sems.at[step_y, place],
        )

    for step_y in range(3):
        for place in range(9):
            copy_of(step_y, place).start()

    for step_x in range(3):
        for step_z in range(3):
            place = step_x * 3 + step_z
            packed[:, place * width : (place + 1) * width] = (
                field_ref[step_z : step_z + CELLS, :, step_x : step_x + ACROSS]
                .astype(jnp.float32)
                .reshape(rows, width)
                .astype(jnp.bfloat16)
            )

    for step_x in range(3):
        for step_z in range(3):
            copy_of(0, step_x * 3 + step_z).wait()
        depth = slice(step_x * 3 * width, (step_x + 1) * 3 * width)
        for start in range(0, span, chunk):
            columns = slice(start, start + chunk)
            terms = jnp.dot(
                packed[:, depth], held[0, depth, columns], preferred_element_type=jnp.float32
            )
            total[0, :, columns] = terms if step_x == 0 else total[0, :, columns] + terms

    def rest(step_y, carry):
        for place in range(9):
            copy_of(step_y, place).wait()
        for start in range(0, span, chunk):
            columns = slice(start, start + chunk)
            total[step_y, :, columns] = jnp.dot(
                packed[...], held[step_y, :, columns], preferred_element_type=jnp.float32
            )
        return carry

    lax.fori_loop(1, 3, rest, 0)

    for number, out_ref in enumerate(out_refs):
        distance = number + far * owners // 2
        start = pl.multiple_of((place_ref[0] ^ distance) % len(out_refs) * share, share)
        for group in range(rows // frame):
            at = group * frame
            dense[group * ACROSS : (group + 1) * ACROSS, :] = sum(
                total[item, at + item : at + item + ACROSS, pl.ds(start, share)]
                for item in range(3)
            )
        out_ref[...] = dense[...].astype(out_ref.dtype)


def bottle_terms(place, field, weight, owners, far):
    frame = ACROSS + 2
    rows = CELLS * 2 * ACROSS * frame
    width = weight.shape[1]
    share = COARSE_WIDTH // owners
    span = COARSE_WIDTH // 2
    return pl.pallas_call(
        functools.partial(bottle_kernel, int(far)),
        out_shape=[
            jax.ShapeDtypeStruct((ROWS, share), jnp.bfloat16 if far or number else jnp.float32)
            for number in range(owners // 2)
        ],
        in_specs=[
            pl.BlockSpec(memory_space=pltpu.SMEM),
            pl.BlockSpec(memory_space=pltpu.VMEM),
            pl.BlockSpec(memory_space=pltpu.HBM),
        ],
        out_specs=vmem(owners // 2),
        scratch_shapes=[
            pltpu.VMEM((3, 9 * width, span), jnp.bfloat16),
            pltpu.VMEM((3, rows, span), jnp.float32),
            pltpu.VMEM((rows, 9 * width), jnp.bfloat16),
            pltpu.VMEM((ROWS, share), jnp.float32),
            pltpu.SemaphoreType.DMA((3, 9)),
        ],
        compiler_params=pltpu.CompilerParams(vmem_limit_bytes=51 * MIB),
        cost_estimate=pl.CostEstimate(
            flops=2 * rows * 27 * width * span, bytes_accessed=8 * MIB, transcendentals=0
        ),
        name="bottle_far" if far else "bottle_near",
    )(place, field, weight)


def finish_kernel(place_ref, guide_ref, own_ref, *refs):
    other_refs, bias_ref, out_ref, spread = refs[:-3], refs[-3], refs[-2], refs[-1]
    share = own_ref.shape[1]
    start = pl.multiple_of(place_ref[0] * share, share)
    value = own_ref[...] + bias_ref[:, pl.ds(start, share)]
    for other_ref in other_refs:
        value = value + other_ref[...].astype(jnp.float32)
    value = value / (1.0 + jnp.exp(-value))
    half = PLANE // 2
    for cell in range(CELLS):
        plain = value[cell * PLANE : cell * PLANE + half]
        guided = value[cell * PLANE + half : (cell + 1) * PLANE]
        mixed = plain + guide_ref[0] * (guided - plain)
        for lane in range(spread.shape[0]):
            spread[lane, pl.ds(cell, half, stride=SPREAD), :] = mixed[:, lane * LANES : (lane + 1) * LANES]
    for lane in range(spread.shape[0]):
        for cell in range(half):
            out_ref[cell, :, lane * LANES : (lane + 1) * LANES] = spread[
                lane, cell * SPREAD : cell * SPREAD + CELLS, :
            ].astype(jnp.bfloat16)


def finish(place, guide, terms, bias):
    share = terms[0].shape[1]
    return pl.pallas_call(
        finish_kernel,
        out_shape=jax.ShapeDtypeStruct((PLANE // 2, CELLS, share), jnp.bfloat16),
        in_specs=[pl.BlockSpec(memory_space=pltpu.SMEM)] * 2 + vmem(len(terms) + 1),
        out_specs=vmem(1)[0],
        scratch_shapes=[pltpu.VMEM((share // LANES, PLANE // 2 * SPREAD, LANES), jnp.float32)],
        compiler_params=pltpu.CompilerParams(vmem_limit_bytes=8 * MIB),
        name="finish",
    )(place, guide, *terms, bias)


def passed(value, steps):
    count = lax.axis_size("region")
    return lax.ppermute(
        value, "region", [(at, at + steps) for at in range(max(0, -steps), min(count, count - steps))]
    )


def across_z(value):
    count = lax.axis_size("region")
    return lax.ppermute(value, "region", [(at, at ^ 1) for at in range(count)])


def y_arrivals(ahead, back):
    place = lax.axis_index("region") // REGIONS_Z % REGIONS_Y
    upper = is_upper()
    ahead, back = hop(ahead, True), hop(back, False)
    zero = jnp.zeros_like(ahead)
    below = jnp.where(place > 0, jnp.where(upper, back, ahead), zero)
    above = jnp.where(place < REGIONS_Y - 1, jnp.where(upper, ahead, back), zero)
    return below, above


def y_halos(first, last):
    upper = is_upper()
    return y_arrivals(jnp.where(upper, first, last), jnp.where(upper, last, first))


def with_halos(value, dim_x, dim_y, dim_z):
    value = jnp.concatenate(z_ends(z_layer(value, dim_z), value, dim_z), axis=dim_z)
    below, above = y_halos(edge(value, dim_y, False), edge(value, dim_y, True))
    value = jnp.concatenate([below, value, above], axis=dim_y)
    low, high = x_layers(edge(value, dim_x, False), edge(value, dim_x, True))
    return jnp.concatenate([low, value, high], axis=dim_x)


def edge(array, dim, last):
    size = array.shape[dim]
    return lax.slice_in_dim(array, size - 1 if last else 0, size if last else 1, axis=dim)


def is_upper():
    return lax.axis_index("region") % REGIONS_Z == 1


def z_layer(value, dim):
    return across_z(jnp.where(is_upper(), edge(value, dim, False), edge(value, dim, True)))


def z_ends(layer, value, dim):
    zero = jnp.zeros_like(layer)
    return [jnp.where(is_upper(), layer, zero), value, jnp.where(is_upper(), zero, layer)]


def x_layers(first, last):
    count = lax.axis_size("region") // (REGIONS_Y * REGIONS_Z)
    if count == 1:
        return jnp.zeros_like(last), jnp.zeros_like(first)
    return passed(last, REGIONS_Y * REGIONS_Z), passed(first, -REGIONS_Y * REGIONS_Z)


def chan_swap(value, distance):
    return lax.ppermute(value, "chan", [(at, at ^ distance) for at in range(lax.axis_size("chan"))])


def exchange(piece_at):
    chans = lax.axis_size("chan")
    return [piece_at(0)] + [chan_swap(piece_at(distance), distance) for distance in range(1, chans)]


def ring_of(count):
    return list(range(0, count, 2)) + list(range(1, count, 2))[::-1]


def hop(value, ahead):
    ring = ring_of(lax.axis_size("region"))
    following = ring[1:] + ring[:1]
    return lax.ppermute(value, "region", list(zip(ring, following) if ahead else zip(following, ring)))


def after(value, other):
    return lax.optimization_barrier((value, other))[0]


def piece_channels(each):
    chans, regions = lax.axis_size("chan"), lax.axis_size("region")
    ring = ring_of(regions)
    shifts = [0]
    for step in range(1, regions // 2 + 1):
        shifts += [-step] + [step] * (step < regions // 2)
    origin = np.array(
        [[ring[(ring.index(region) + shift) % regions] for shift in shifts] for region in range(regions)]
    )
    table = np.zeros((chans, regions, regions, chans, each), np.int32)
    for chan in range(chans):
        for distance in range(chans):
            first = (chan ^ distance) * regions + origin
            table[chan, :, :, distance] = first[:, :, None] * each + np.arange(each)
    table = jnp.asarray(table.reshape(chans * regions, FINE_WIDTH))
    device = lax.axis_index("chan") * regions + lax.axis_index("region")
    return lax.dynamic_index_in_dim(table, device, 0, keepdims=True)


def ring_pieces(piece, milestones):
    regions = lax.axis_size("region")
    forward = backward = piece
    held = [piece]
    for step in range(1, regions // 2 + 1):
        if step > 1 and step - 2 < len(milestones):
            forward, backward = (after(value, milestones[step - 2]) for value in (forward, backward))
        if step == regions // 2:
            held += [hop(forward[: OFFSETS // 2], True), hop(backward[OFFSETS // 2 :], False)]
        else:
            forward, backward = hop(forward, True), hop(backward, False)
            held += [forward, backward]
    return held


def whole_columns(proj_weight):
    chans, held = lax.axis_size("chan"), proj_weight.shape[0]
    width = COARSE_WIDTH // chans
    mine = lax.all_to_all(proj_weight, "chan", split_axis=1, concat_axis=0, tiled=True)
    whole = lax.all_gather(mine.reshape(chans, held, width), "region", axis=1, tiled=True)
    return whole.reshape(FINE_WIDTH, OFFSETS, width).transpose(1, 0, 2)


def shards(
    latent,
    cond_scale,
    cond_shift,
    fine_weight,
    fine_bias,
    proj_weight,
    proj_bias,
    bottle_weight,
    bottle_bias,
    guide,
):
    chans = lax.axis_size("chan")
    chan_place = lax.axis_index("chan")
    region = lax.axis_index("region")
    width = COARSE_WIDTH // chans
    side = 2 * TILE_SIDE
    count_x = lax.axis_size("region") // (REGIONS_Y * REGIONS_Z)
    steps = (REGIONS_Y * REGIONS_Z, REGIONS_Z, 1)
    counts = (count_x, REGIONS_Y, REGIONS_Z)
    places = [region // step % count for step, count in zip(steps, counts)]
    inside = jnp.stack(
        [
            flag
            for place, count in zip(places, counts)
            for flag in ((place > 0).astype(jnp.float32), (place < count - 1).astype(jnp.float32))
        ]
    )

    place = chan_place[None]
    each, rest = divmod(proj_weight.shape[0], OFFSETS)
    by_ring = rest == 0 and chans * each % 16 == 0
    if by_ring:
        split = split_columns(place, proj_weight, chans)
        mine = exchange(lambda distance: split[distance])
        piece = regroup(mine)
        channel = piece_channels(each)
    else:
        channel = jnp.arange(FINE_WIDTH, dtype=jnp.int32)[None]
    order = lax.broadcasted_iota(jnp.int32, (FINE_WIDTH, FINE_WIDTH), 0) == channel

    block = latent[0].transpose(0, 2, 1, 3)
    face = lax.dynamic_index_in_dim(
        block, jnp.where(is_upper(), 0, TILE_SIDE - 1), axis=1, keepdims=False
    )
    layer = across_z(face)
    spare = jnp.zeros((block.shape[0], 16 - TILE_SIDE - 1, FINE_WIDTH), block.dtype)

    def rows_at(row):
        rows = lax.dynamic_index_in_dim(block, row, axis=2, keepdims=False)
        corner = lax.dynamic_slice_in_dim(layer, row, 1, axis=1)
        return jnp.concatenate([rows, corner, spare], axis=1)

    top = 2 * TILE_SIDE - 1
    below, above = y_arrivals(
        rows_at(jnp.where(is_upper(), 0, top)), rows_at(jnp.where(is_upper(), top, 0))
    )
    ends = []
    for at in (0, -1):
        plane = jnp.concatenate(z_ends(layer[at][None], block[at], 0), axis=0)
        low, high = [
            jnp.concatenate(
                z_ends(part[at, TILE_SIDE : TILE_SIDE + 1], part[at, :TILE_SIDE], 0), axis=0
            )[:, None]
            for part in (below, above)
        ]
        spare = jnp.zeros((TILE_SIDE + 2, 6, FINE_WIDTH), plane.dtype)
        ends.append(jnp.concatenate([plane, high, spare, low], axis=1))
    outer = jnp.stack(x_layers(*ends))

    bias = jnp.sum(jnp.where(order, fine_bias[:, None], 0.0), axis=0)
    windows, taps = make_windows(
        inside,
        block,
        layer,
        below,
        above,
        outer,
        cond_scale[None],
        cond_shift[None],
        fine_weight.reshape(27, FINE_WIDTH, FINE_WIDTH),
        order.astype(jnp.bfloat16),
    )
    bias = jnp.concatenate([bias, bias])[None]
    half = STRIDE // 2
    early = convolve(windows, taps, bias, 0, half)
    late = convolve(windows, taps, bias, half, half)
    columns = ring_pieces(piece, [taps, early, late]) if by_ring else [whole_columns(proj_weight)]
    coarse = project(place, early, late, columns, by_ring, proj_bias[None])

    grid = coarse[:ROWS].reshape(CELLS, 2, ACROSS, ACROSS, width)
    field = with_halos(grid, 2, 3, 0)
    far = bottle_terms(place, field, bottle_weight, chans, True)
    swapped = [chan_swap(value, chans // 2 + number) for number, value in enumerate(far)]
    own, *near = bottle_terms(after(place, far), field, bottle_weight, chans, False)
    near = [chan_swap(value, 1 + number) for number, value in enumerate(near)]
    terms = [own, sum(value.astype(jnp.float32) for value in swapped)] + near
    guided = finish(place, guide, terms, bottle_bias[None])
    return guided.reshape(1, ACROSS, ACROSS, CELLS, width)


def solution(mesh):
    placed = (
        P("region", None, None, None, None),
        P(),
        P(),
        P(),
        P(),
        P(("chan", "region"), None),
        P(),
        P(None, "chan", None),
        P(),
        P(),
    )
    return jax.shard_map(
        shards,
        mesh=mesh,
        in_specs=placed,
        out_specs=P("region", None, None, None, "chan"),
        check_vma=False,
    )
```

```python
import functools

import numpy as np

import jax
import jax.numpy as jnp
from jax import lax
from jax.experimental import pallas as pl
from jax.experimental.pallas import tpu as pltpu
from jax.sharding import PartitionSpec as P

FINE_WIDTH = 128
COARSE_WIDTH = 1024
TILE_SIDE = 12
STRIDE = 4
REGIONS_Y = 4
REGIONS_Z = 2

CELLS = TILE_SIDE // STRIDE
ACROSS = 2 * CELLS
PLANE = 2 * ACROSS * ACROSS
ROWS = CELLS * PLANE
PADDED = -(-ROWS // 16) * 16
PHASES = STRIDE + 2
OFFSETS = STRIDE**3
LANES = 128
SPREAD = 8
MIB = 2**20


def vmem(count):
    return [pl.BlockSpec(memory_space=pltpu.VMEM) for _ in range(count)]


def regroup_kernel(*refs):
    rows_refs, out_ref, wide = refs[:-2], refs[-2], refs[-1]
    held = rows_refs[0].shape[0]
    groups = out_ref.shape[1]
    for lane in range(wide.shape[0]):
        columns = slice(lane * LANES, (lane + 1) * LANES)
        for number, rows_ref in enumerate(rows_refs):
            wide[lane, number * held : (number + 1) * held, :] = rows_ref[:, columns].astype(jnp.float32)
        for offset in range(OFFSETS):
            out_ref[offset, :, columns] = wide[
                lane, pl.ds(offset, groups, stride=OFFSETS), :
            ].astype(jnp.bfloat16)


def regroup(pieces):
    held, width = pieces[0].shape
    total = len(pieces) * held
    return pl.pallas_call(
        regroup_kernel,
        out_shape=jax.ShapeDtypeStruct((OFFSETS, total // OFFSETS, width), jnp.bfloat16),
        in_specs=vmem(len(pieces)),
        out_specs=vmem(1)[0],
        scratch_shapes=[pltpu.VMEM((width // LANES, total, LANES), jnp.float32)],
        compiler_params=pltpu.CompilerParams(vmem_limit_bytes=8 * MIB),
        name="regroup",
    )(*pieces)


def split_kernel(place_ref, rows_ref, *out_refs):
    width = out_refs[0].shape[1]
    for distance, out_ref in enumerate(out_refs):
        start = pl.multiple_of((place_ref[0] ^ distance) * width, width)
        out_ref[...] = rows_ref[:, pl.ds(start, width)]


def split_columns(place, rows, owners):
    held, width = rows.shape[0], rows.shape[1] // owners
    return pl.pallas_call(
        split_kernel,
        out_shape=[jax.ShapeDtypeStruct((held, width), rows.dtype)] * owners,
        in_specs=[pl.BlockSpec(memory_space=pltpu.SMEM)] + vmem(1),
        out_specs=vmem(owners),
        compiler_params=pltpu.CompilerParams(vmem_limit_bytes=4 * MIB),
        name="split_columns",
    )(place, rows)


def rows_kernel(first_ref, last_ref, low_ref, high_ref, wide):
    def take(at_x, carry):
        for rows_ref, row, out_ref in ((first_ref, 0, low_ref), (last_ref, 7, high_ref)):
            for at_z in range(TILE_SIDE):
                wide[at_z : at_z + 1, :] = rows_ref[at_x, at_z].astype(jnp.float32)[row : row + 1]
            out_ref[at_x] = wide[...].astype(jnp.bfloat16)
        return carry

    wide[...] = jnp.zeros_like(wide)
    lax.fori_loop(0, first_ref.shape[0], take, 0)


def y_rows(block):
    side_x, depth, side_y, width = block.shape
    return pl.pallas_call(
        rows_kernel,
        out_shape=(
            jax.ShapeDtypeStruct((side_x, 16, width), block.dtype),
            jax.ShapeDtypeStruct((side_x, 16, width), block.dtype),
        ),
        grid=(1,),
        in_specs=[
            pl.BlockSpec((side_x, depth, 8, width), lambda i: (0, 0, 0, 0)),
            pl.BlockSpec((side_x, depth, 8, width), lambda i: (0, 0, side_y // 8 - 1, 0)),
        ],
        out_specs=(
            pl.BlockSpec((side_x, 16, width), lambda i: (0, 0, 0)),
            pl.BlockSpec((side_x, 16, width), lambda i: (0, 0, 0)),
        ),
        scratch_shapes=[pltpu.VMEM((16, width), jnp.float32)],
        compiler_params=pltpu.CompilerParams(vmem_limit_bytes=12 * MIB),
        name="y_rows",
    )(block, block)


def window_kernel(
    inside_ref, block_ref, layer_ref, below_ref, above_ref, outer_ref, scale_ref, shift_ref,
    weight_ref, order_ref, windows_ref, taps_ref, rows, line, layers,
):
    phase_x = pl.program_id(0)
    side, depth, width = 2 * TILE_SIDE, TILE_SIDE, FINE_WIDTH
    half = 2 * ACROSS * side

    @pl.when(phase_x == 0)
    def _():
        zero = jnp.zeros((width, width), jnp.bfloat16)
        for place in range(9):
            taps_ref[place, 3 * width :, :width] = zero
            taps_ref[place, :width, width:] = zero
            for step in range(3):
                block = jnp.dot(
                    weight_ref[place * 3 + step], order_ref[...], preferred_element_type=jnp.float32
                ).astype(jnp.bfloat16)
                taps_ref[place, step * width : (step + 1) * width, :width] = block
                taps_ref[place, (step + 1) * width : (step + 2) * width, width:] = block

        def widen(at_x, carry):
            rows[0, at_x] = below_ref[at_x].astype(jnp.float32)
            rows[1, at_x] = above_ref[at_x].astype(jnp.float32)
            return carry

        lax.fori_loop(0, side, widen, 0)

    scale = jnp.broadcast_to(scale_ref[...], (8, width))
    shift = jnp.broadcast_to(shift_ref[...], (8, width))
    row = lax.broadcasted_iota(jnp.int32, (8, width), 0)
    first = jnp.where(row == 0, shift * inside_ref[2], shift)
    last = jnp.where(row == side + 1 - 20, shift * inside_ref[3], shift)
    chunks = [(0, first), (8, shift), (16, shift), (4, shift), (12, shift), (20, last)]

    def split(cell_x, carry):
        at_x = phase_x + STRIDE * cell_x
        outside = jnp.logical_or(at_x == 0, at_x == side + 1)

        @pl.when(jnp.logical_not(outside))
        def _():
            at = at_x - 1
            for at_z in range(depth + 2):
                if at_z == 0:
                    flag, value, place = inside_ref[4], layer_ref[at], depth
                elif at_z == depth + 1:
                    flag, value, place = inside_ref[5], layer_ref[at], depth
                else:
                    flag, value, place = None, block_ref[at, at_z - 1], at_z - 1
                value = value.astype(jnp.float32)
                low, high = rows[0, at, place : place + 1, :], rows[1, at, place : place + 1, :]
                if flag is not None:
                    value, low, high = value * flag, low * flag, high * flag
                line[at_z, 7:8, :] = low
                line[at_z, 8 : side + 8, :] = value
                line[at_z, side + 8 : side + 9, :] = high

        @pl.when(outside)
        def _():
            end = jnp.where(at_x == 0, 0, 1)
            for at_z in range(depth + 2):
                value = outer_ref[end, at_z].astype(jnp.float32)
                line[at_z, 0:8, :] = value[side : side + 8]
                line[at_z, 8 : side + 8, :] = value[:side]
                line[at_z, side + 8 : side + 16, :] = value[side : side + 8]

        within = jnp.where(at_x == 0, inside_ref[0], 1.0)
        within = jnp.where(at_x == side + 1, inside_ref[1], within)
        for at_z in range(depth + 2):
            if at_z == 0:
                factor = within * inside_ref[4]
            elif at_z == depth + 1:
                factor = within * inside_ref[5]
            else:
                factor = within
            for number, (start, added) in enumerate(chunks):
                value = line[at_z, pl.ds(start + 7, 8), :]
                base = number // 3 * half + number % 3 * 8
                base = pl.multiple_of(base + cell_x * side, 8)
                layers[at_z, pl.ds(base, 8), :] = value
                layers[at_z, pl.ds(base + half // 2, 8), :] = value * scale + added * factor
        return carry

    lax.fori_loop(0, ACROSS, split, 0)
    for phase_y in range(PHASES):
        start = phase_y if phase_y < STRIDE else half + phase_y - STRIDE
        for phase_z in range(PHASES):
            parts = [
                layers[phase_z + STRIDE * cell, pl.ds(start, PLANE, stride=STRIDE), :]
                for cell in range(CELLS)
            ]
            parts.append(jnp.zeros((PADDED - ROWS, width), jnp.float32))
            windows_ref[0, phase_y, :, phase_z * width : (phase_z + 1) * width] = jnp.concatenate(
                parts, axis=0
            ).astype(jnp.bfloat16)


def make_windows(inside, *arrays):
    width, side = FINE_WIDTH, 2 * TILE_SIDE

    def whole(array):
        return pl.BlockSpec(array.shape, lambda i: (0,) * array.ndim)

    return pl.pallas_call(
        window_kernel,
        out_shape=(
            jax.ShapeDtypeStruct((PHASES, PHASES, PADDED, PHASES * width), jnp.bfloat16),
            jax.ShapeDtypeStruct((9, 4 * width, 2 * width), jnp.bfloat16),
        ),
        grid=(PHASES,),
        in_specs=[pl.BlockSpec(memory_space=pltpu.SMEM)] + [whole(array) for array in arrays],
        out_specs=(
            pl.BlockSpec((1, PHASES, PADDED, PHASES * width), lambda i: (i, 0, 0, 0)),
            pl.BlockSpec((9, 4 * width, 2 * width), lambda i: (0, 0, 0)),
        ),
        scratch_shapes=[
            pltpu.VMEM((2, side, 16, width), jnp.float32),
            pltpu.VMEM((TILE_SIDE + 2, side + 16, width), jnp.float32),
            pltpu.VMEM((TILE_SIDE + 2, 4 * ACROSS * side, width), jnp.float32),
        ],
        compiler_params=pltpu.CompilerParams(vmem_limit_bytes=28 * MIB),
        cost_estimate=pl.CostEstimate(flops=10**10, bytes_accessed=16 * MIB, transcendentals=0),
        name="windows",
    )(inside, *arrays)


def convolve_kernel(first_ref, second_ref, third_ref, taps_ref, bias_ref, out_ref):
    width = FINE_WIDTH
    bias = bias_ref[...]

    def convolve(at_y, carry):
        total = jnp.zeros((2 * PADDED, 2 * width), jnp.float32)
        for step_x, windows_ref in enumerate((first_ref, second_ref, third_ref)):
            for step_y in range(3):
                taken = [
                    windows_ref[0, at_y + step_y, :, pair * 2 * width : (pair * 2 + 4) * width]
                    for pair in range(2)
                ]
                total += jnp.dot(
                    jnp.concatenate(taken, axis=0),
                    taps_ref[step_x * 3 + step_y],
                    preferred_element_type=jnp.float32,
                )
        total = total + bias
        hidden = (total / (1.0 + jnp.exp(-total))).astype(jnp.bfloat16)
        for pair in range(2):
            out_ref[at_y * 2 + pair] = hidden[pair * PADDED : (pair + 1) * PADDED]
        return carry

    lax.fori_loop(0, STRIDE, convolve, 0)


def convolve(windows, taps, bias, start, count):
    width = FINE_WIDTH
    each = STRIDE * STRIDE // 2
    block = (1, PHASES, PADDED, PHASES * width)
    return pl.pallas_call(
        convolve_kernel,
        out_shape=jax.ShapeDtypeStruct((count * each, PADDED, 2 * width), jnp.bfloat16),
        grid=(count,),
        in_specs=[
            pl.BlockSpec(block, lambda i, step=step: (i + start + step, 0, 0, 0)) for step in range(3)
        ]
        + [
            pl.BlockSpec(taps.shape, lambda i: (0, 0, 0)),
            pl.BlockSpec(bias.shape, lambda i: (0, 0)),
        ],
        out_specs=pl.BlockSpec((each, PADDED, 2 * width), lambda i: (i, 0, 0)),
        compiler_params=pltpu.CompilerParams(vmem_limit_bytes=28 * MIB),
        cost_estimate=pl.CostEstimate(
            flops=2 * count * each * PADDED * 36 * width * 2 * width,
            bytes_accessed=16 * MIB,
            transcendentals=count * each * PADDED * 2 * width,
        ),
        name="convolve",
    )(windows, windows, windows, taps, bias)


def project_kernel(split, place_ref, early_ref, late_ref, *refs):
    weight_refs, bias_ref, out_ref = refs[:-2], refs[-2], refs[-1]
    width = out_ref.shape[1]
    start = pl.multiple_of(place_ref[0] * width, width)
    total = jnp.broadcast_to(bias_ref[:, pl.ds(start, width)], out_ref.shape)
    pairs = early_ref.shape[0]
    for number, hidden_ref in enumerate((early_ref, late_ref)):
        used = weight_refs[:-2] + (weight_refs[len(weight_refs) - 2 + number],) if split else weight_refs
        for pair in range(pairs):
            weight = jnp.concatenate(
                [
                    ref[2 * pair + item + (number * 2 * pairs if ref.shape[0] == OFFSETS else 0)]
                    for item in range(2)
                    for ref in used
                ],
                axis=0,
            )
            total += jnp.dot(hidden_ref[pair], weight, preferred_element_type=jnp.float32)
    out_ref[...] = total.astype(jnp.bfloat16)


def project(place, early, late, weights, split, bias):
    pairs, rows, depth = early.shape
    width = weights[0].shape[2]
    return pl.pallas_call(
        functools.partial(project_kernel, split),
        out_shape=jax.ShapeDtypeStruct((rows, width), jnp.bfloat16),
        in_specs=[pl.BlockSpec(memory_space=pltpu.SMEM)] + vmem(len(weights) + 3),
        out_specs=vmem(1)[0],
        compiler_params=pltpu.CompilerParams(vmem_limit_bytes=24 * MIB),
        cost_estimate=pl.CostEstimate(
            flops=4 * pairs * rows * depth * width, bytes_accessed=8 * MIB, transcendentals=0
        ),
        name="project",
    )(place, early, late, *weights, bias)


def bottle_kernel(far, place_ref, field_ref, weight_ref, *refs):
    out_refs, (held, total, packed, dense, sems) = refs[:-5], refs[-5:]
    width = field_ref.shape[4]
    share = out_refs[0].shape[1]
    span = held.shape[2]
    frame = ACROSS + 2
    rows = CELLS * 2 * ACROSS * frame
    chunk = 256
    owners = 2 * len(out_refs)
    first = pl.multiple_of((place_ref[0] // len(out_refs) ^ far) * span, span)

    def copy_of(step_y, place):
        tap = (place // 3 * 3 + step_y) * 3 + place % 3
        return pltpu.make_async_copy(
            weight_ref.at[tap, :, pl.ds(first, span)],
            held.at[step_y, pl.ds(place * width, width)],
            sems.at[step_y, place],
        )

    for step_y in range(3):
        for place in range(9):
            copy_of(step_y, place).start()

    for step_x in range(3):
        for step_z in range(3):
            place = step_x * 3 + step_z
            packed[:, place * width : (place + 1) * width] = (
                field_ref[step_z : step_z + CELLS, :, step_x : step_x + ACROSS]
                .astype(jnp.float32)
                .reshape(rows, width)
                .astype(jnp.bfloat16)
            )

    for step_x in range(3):
        for step_z in range(3):
            copy_of(0, step_x * 3 + step_z).wait()
        depth = slice(step_x * 3 * width, (step_x + 1) * 3 * width)
        for start in range(0, span, chunk):
            columns = slice(start, start + chunk)
            terms = jnp.dot(
                packed[:, depth], held[0, depth, columns], preferred_element_type=jnp.float32
            )
            total[0, :, columns] = terms if step_x == 0 else total[0, :, columns] + terms

    def rest(step_y, carry):
        for place in range(9):
            copy_of(step_y, place).wait()
        for start in range(0, span, chunk):
            columns = slice(start, start + chunk)
            total[step_y, :, columns] = jnp.dot(
                packed[...], held[step_y, :, columns], preferred_element_type=jnp.float32
            )
        return carry

    lax.fori_loop(1, 3, rest, 0)

    for number, out_ref in enumerate(out_refs):
        distance = number + far * owners // 2
        start = pl.multiple_of((place_ref[0] ^ distance) % len(out_refs) * share, share)
        for group in range(rows // frame):
            at = group * frame
            dense[group * ACROSS : (group + 1) * ACROSS, :] = sum(
                total[item, at + item : at + item + ACROSS, pl.ds(start, share)]
                for item in range(3)
            )
        out_ref[...] = dense[...].astype(out_ref.dtype)


def bottle_terms(place, field, weight, owners, far):
    frame = ACROSS + 2
    rows = CELLS * 2 * ACROSS * frame
    width = weight.shape[1]
    share = COARSE_WIDTH // owners
    span = COARSE_WIDTH // 2
    return pl.pallas_call(
        functools.partial(bottle_kernel, int(far)),
        out_shape=[
            jax.ShapeDtypeStruct((ROWS, share), jnp.bfloat16 if far or number else jnp.float32)
            for number in range(owners // 2)
        ],
        in_specs=[
            pl.BlockSpec(memory_space=pltpu.SMEM),
            pl.BlockSpec(memory_space=pltpu.VMEM),
            pl.BlockSpec(memory_space=pltpu.HBM),
        ],
        out_specs=vmem(owners // 2),
        scratch_shapes=[
            pltpu.VMEM((3, 9 * width, span), jnp.bfloat16),
            pltpu.VMEM((3, rows, span), jnp.float32),
            pltpu.VMEM((rows, 9 * width), jnp.bfloat16),
            pltpu.VMEM((ROWS, share), jnp.float32),
            pltpu.SemaphoreType.DMA((3, 9)),
        ],
        compiler_params=pltpu.CompilerParams(vmem_limit_bytes=51 * MIB),
        cost_estimate=pl.CostEstimate(
            flops=2 * rows * 27 * width * span, bytes_accessed=8 * MIB, transcendentals=0
        ),
        name="bottle_far" if far else "bottle_near",
    )(place, field, weight)


def finish_kernel(place_ref, guide_ref, own_ref, *refs):
    other_refs, bias_ref, out_ref, spread = refs[:-3], refs[-3], refs[-2], refs[-1]
    share = own_ref.shape[1]
    start = pl.multiple_of(place_ref[0] * share, share)
    value = own_ref[...] + bias_ref[:, pl.ds(start, share)]
    for other_ref in other_refs:
        value = value + other_ref[...].astype(jnp.float32)
    value = value / (1.0 + jnp.exp(-value))
    half = PLANE // 2
    for cell in range(CELLS):
        plain = value[cell * PLANE : cell * PLANE + half]
        guided = value[cell * PLANE + half : (cell + 1) * PLANE]
        mixed = plain + guide_ref[0] * (guided - plain)
        for lane in range(spread.shape[0]):
            spread[lane, pl.ds(cell, half, stride=SPREAD), :] = mixed[:, lane * LANES : (lane + 1) * LANES]
    for lane in range(spread.shape[0]):
        for cell in range(half):
            out_ref[cell, :, lane * LANES : (lane + 1) * LANES] = spread[
                lane, cell * SPREAD : cell * SPREAD + CELLS, :
            ].astype(jnp.bfloat16)


def finish(place, guide, terms, bias):
    share = terms[0].shape[1]
    return pl.pallas_call(
        finish_kernel,
        out_shape=jax.ShapeDtypeStruct((PLANE // 2, CELLS, share), jnp.bfloat16),
        in_specs=[pl.BlockSpec(memory_space=pltpu.SMEM)] * 2 + vmem(len(terms) + 1),
        out_specs=vmem(1)[0],
        scratch_shapes=[pltpu.VMEM((share // LANES, PLANE // 2 * SPREAD, LANES), jnp.float32)],
        compiler_params=pltpu.CompilerParams(vmem_limit_bytes=8 * MIB),
        name="finish",
    )(place, guide, *terms, bias)


def passed(value, steps):
    count = lax.axis_size("region")
    return lax.ppermute(
        value, "region", [(at, at + steps) for at in range(max(0, -steps), min(count, count - steps))]
    )


def across_z(value):
    count = lax.axis_size("region")
    return lax.ppermute(value, "region", [(at, at ^ 1) for at in range(count)])


def y_halos(first, last):
    place = lax.axis_index("region") // REGIONS_Z % REGIONS_Y
    upper = is_upper()
    ahead = hop(jnp.where(upper, first, last), True)
    back = hop(jnp.where(upper, last, first), False)
    zero = jnp.zeros_like(ahead)
    below = jnp.where(place > 0, jnp.where(upper, back, ahead), zero)
    above = jnp.where(place < REGIONS_Y - 1, jnp.where(upper, ahead, back), zero)
    return below, above


def with_halos(value, dim_x, dim_y, dim_z):
    value = jnp.concatenate(z_ends(z_layer(value, dim_z), value, dim_z), axis=dim_z)
    below, above = y_halos(edge(value, dim_y, False), edge(value, dim_y, True))
    value = jnp.concatenate([below, value, above], axis=dim_y)
    low, high = x_layers(edge(value, dim_x, False), edge(value, dim_x, True))
    return jnp.concatenate([low, value, high], axis=dim_x)


def edge(array, dim, last):
    size = array.shape[dim]
    return lax.slice_in_dim(array, size - 1 if last else 0, size if last else 1, axis=dim)


def is_upper():
    return lax.axis_index("region") % REGIONS_Z == 1


def z_layer(value, dim):
    return across_z(jnp.where(is_upper(), edge(value, dim, False), edge(value, dim, True)))


def z_ends(layer, value, dim):
    zero = jnp.zeros_like(layer)
    return [jnp.where(is_upper(), layer, zero), value, jnp.where(is_upper(), zero, layer)]


def x_layers(first, last):
    count = lax.axis_size("region") // (REGIONS_Y * REGIONS_Z)
    if count == 1:
        return jnp.zeros_like(last), jnp.zeros_like(first)
    return passed(last, REGIONS_Y * REGIONS_Z), passed(first, -REGIONS_Y * REGIONS_Z)


def chan_swap(value, distance):
    return lax.ppermute(value, "chan", [(at, at ^ distance) for at in range(lax.axis_size("chan"))])


def exchange(piece_at):
    chans = lax.axis_size("chan")
    return [piece_at(0)] + [chan_swap(piece_at(distance), distance) for distance in range(1, chans)]


def ring_of(count):
    return list(range(0, count, 2)) + list(range(1, count, 2))[::-1]


def hop(value, ahead):
    ring = ring_of(lax.axis_size("region"))
    following = ring[1:] + ring[:1]
    return lax.ppermute(value, "region", list(zip(ring, following) if ahead else zip(following, ring)))


def after(value, other):
    return lax.optimization_barrier((value, other))[0]


def piece_channels(each):
    chans, regions = lax.axis_size("chan"), lax.axis_size("region")
    region = lax.axis_index("region")
    lane = lax.broadcasted_iota(jnp.int32, (1, FINE_WIDTH), 1)
    piece, distance, member = lane // (chans * each), lane // each % chans, lane % each
    place = jnp.where(region % 2 == 0, region // 2, regions - 1 - region // 2)
    shift = jnp.where(piece % 2 == 0, piece // 2, -((piece + 1) // 2))
    at = (place + shift + regions) % regions
    origin = jnp.where(at < regions // 2, 2 * at, 2 * (regions - 1 - at) + 1)
    return ((lax.axis_index("chan") ^ distance) * regions + origin) * each + member


def ring_pieces(piece, milestones):
    regions = lax.axis_size("region")
    forward = backward = piece
    held = [piece]
    for step in range(1, regions // 2 + 1):
        if step > 1 and step - 2 < len(milestones):
            forward, backward = (after(value, milestones[step - 2]) for value in (forward, backward))
        if step == regions // 2:
            held += [hop(forward[: OFFSETS // 2], True), hop(backward[OFFSETS // 2 :], False)]
        else:
            forward, backward = hop(forward, True), hop(backward, False)
            held += [forward, backward]
    return held


def whole_columns(proj_weight):
    chans, held = lax.axis_size("chan"), proj_weight.shape[0]
    width = COARSE_WIDTH // chans
    mine = lax.all_to_all(proj_weight, "chan", split_axis=1, concat_axis=0, tiled=True)
    whole = lax.all_gather(mine.reshape(chans, held, width), "region", axis=1, tiled=True)
    return whole.reshape(FINE_WIDTH, OFFSETS, width).transpose(1, 0, 2)


def shards(
    latent,
    cond_scale,
    cond_shift,
    fine_weight,
    fine_bias,
    proj_weight,
    proj_bias,
    bottle_weight,
    bottle_bias,
    guide,
):
    chans = lax.axis_size("chan")
    chan_place = lax.axis_index("chan")
    region = lax.axis_index("region")
    width = COARSE_WIDTH // chans
    side = 2 * TILE_SIDE
    count_x = lax.axis_size("region") // (REGIONS_Y * REGIONS_Z)
    steps = (REGIONS_Y * REGIONS_Z, REGIONS_Z, 1)
    counts = (count_x, REGIONS_Y, REGIONS_Z)
    places = [region // step % count for step, count in zip(steps, counts)]
    inside = jnp.stack(
        [
            flag
            for place, count in zip(places, counts)
            for flag in ((place > 0).astype(jnp.float32), (place < count - 1).astype(jnp.float32))
        ]
    )

    place = chan_place[None]
    each, rest = divmod(proj_weight.shape[0], OFFSETS)
    by_ring = rest == 0 and chans * each % 16 == 0
    if by_ring:
        split = split_columns(place, proj_weight, chans)
        mine = exchange(lambda distance: split[distance])
        piece = regroup(mine)
        channel = piece_channels(each)
    else:
        channel = jnp.arange(FINE_WIDTH, dtype=jnp.int32)[None]
    order = lax.broadcasted_iota(jnp.int32, (FINE_WIDTH, FINE_WIDTH), 0) == channel

    block = latent[0].transpose(0, 2, 1, 3)
    face = lax.dynamic_index_in_dim(
        block, jnp.where(is_upper(), 0, TILE_SIDE - 1), axis=1, keepdims=False
    )
    first, last = y_rows(block)
    layer = across_z(face)
    corner = lax.broadcasted_iota(jnp.int32, first.shape, 1) == TILE_SIDE
    below, above = y_halos(
        jnp.where(corner, layer[:, :1], first), jnp.where(corner, layer[:, -1:], last)
    )
    ends = []
    for at in (0, -1):
        plane = jnp.concatenate(z_ends(layer[at][None], block[at], 0), axis=0)
        low, high = [
            jnp.concatenate(
                z_ends(part[at, TILE_SIDE : TILE_SIDE + 1], part[at, :TILE_SIDE], 0), axis=0
            )[:, None]
            for part in (below, above)
        ]
        spare = jnp.zeros((TILE_SIDE + 2, 6, FINE_WIDTH), plane.dtype)
        ends.append(jnp.concatenate([plane, high, spare, low], axis=1))
    outer = jnp.stack(x_layers(*ends))

    bias = jnp.sum(jnp.where(order, fine_bias[:, None], 0.0), axis=0)
    windows, taps = make_windows(
        inside,
        block,
        layer,
        below,
        above,
        outer,
        cond_scale[None],
        cond_shift[None],
        fine_weight.reshape(27, FINE_WIDTH, FINE_WIDTH),
        order.astype(jnp.bfloat16),
    )
    bias = jnp.concatenate([bias, bias])[None]
    half = STRIDE // 2
    early = convolve(windows, taps, bias, 0, half)
    late = convolve(windows, taps, bias, half, half)
    columns = ring_pieces(piece, [taps, early, late]) if by_ring else [whole_columns(proj_weight)]
    coarse = project(place, early, late, columns, by_ring, proj_bias[None])

    grid = coarse[:ROWS].reshape(CELLS, 2, ACROSS, ACROSS, width)
    field = with_halos(grid, 2, 3, 0)
    far = bottle_terms(place, field, bottle_weight, chans, True)
    swapped = [chan_swap(value, chans // 2 + number) for number, value in enumerate(far)]
    own, *near = bottle_terms(after(place, far), field, bottle_weight, chans, False)
    near = [chan_swap(value, 1 + number) for number, value in enumerate(near)]
    terms = [own, sum(value.astype(jnp.float32) for value in swapped)] + near
    guided = finish(place, guide, terms, bottle_bias[None])
    return guided.reshape(1, ACROSS, ACROSS, CELLS, width)


def solution(mesh):
    placed = (
        P("region", None, None, None, None),
        P(),
        P(),
        P(),
        P(),
        P(("chan", "region"), None),
        P(),
        P(None, "chan", None),
        P(),
        P(),
    )
    return jax.shard_map(
        shards,
        mesh=mesh,
        in_specs=placed,
        out_specs=P("region", None, None, None, "chan"),
        check_vma=False,
    )
```

```python
import functools

import numpy as np

import jax
import jax.numpy as jnp
from jax import lax
from jax.experimental import pallas as pl
from jax.experimental.pallas import tpu as pltpu
from jax.sharding import PartitionSpec as P

FINE_WIDTH = 128
COARSE_WIDTH = 1024
TILE_SIDE = 12
STRIDE = 4
REGIONS_Y = 4
REGIONS_Z = 2

CELLS = TILE_SIDE // STRIDE
ACROSS = 2 * CELLS
PLANE = 2 * ACROSS * ACROSS
ROWS = CELLS * PLANE
PADDED = -(-ROWS // 16) * 16
PHASES = STRIDE + 2
OFFSETS = STRIDE**3
LANES = 128
SPREAD = 8
MIB = 2**20


def vmem(count):
    return [pl.BlockSpec(memory_space=pltpu.VMEM) for _ in range(count)]


def regroup_kernel(*refs):
    rows_refs, out_ref, wide = refs[:-2], refs[-2], refs[-1]
    held = rows_refs[0].shape[0]
    groups = out_ref.shape[1]
    for lane in range(wide.shape[0]):
        columns = slice(lane * LANES, (lane + 1) * LANES)
        for number, rows_ref in enumerate(rows_refs):
            wide[lane, number * held : (number + 1) * held, :] = rows_ref[:, columns].astype(jnp.float32)
        for offset in range(OFFSETS):
            out_ref[offset, :, columns] = wide[
                lane, pl.ds(offset, groups, stride=OFFSETS), :
            ].astype(jnp.bfloat16)


def regroup(pieces):
    held, width = pieces[0].shape
    total = len(pieces) * held
    return pl.pallas_call(
        regroup_kernel,
        out_shape=jax.ShapeDtypeStruct((OFFSETS, total // OFFSETS, width), jnp.bfloat16),
        in_specs=vmem(len(pieces)),
        out_specs=vmem(1)[0],
        scratch_shapes=[pltpu.VMEM((width // LANES, total, LANES), jnp.float32)],
        compiler_params=pltpu.CompilerParams(vmem_limit_bytes=8 * MIB),
        name="regroup",
    )(*pieces)


def split_kernel(place_ref, rows_ref, *out_refs):
    width = out_refs[0].shape[1]
    for distance, out_ref in enumerate(out_refs):
        start = pl.multiple_of((place_ref[0] ^ distance) * width, width)
        out_ref[...] = rows_ref[:, pl.ds(start, width)]


def split_columns(place, rows, owners):
    held, width = rows.shape[0], rows.shape[1] // owners
    return pl.pallas_call(
        split_kernel,
        out_shape=[jax.ShapeDtypeStruct((held, width), rows.dtype)] * owners,
        in_specs=[pl.BlockSpec(memory_space=pltpu.SMEM)] + vmem(1),
        out_specs=vmem(owners),
        compiler_params=pltpu.CompilerParams(vmem_limit_bytes=4 * MIB),
        name="split_columns",
    )(place, rows)


def rows_kernel(first_ref, last_ref, low_ref, high_ref, wide):
    def take(at_x, carry):
        for rows_ref, row, out_ref in ((first_ref, 0, low_ref), (last_ref, 7, high_ref)):
            for at_z in range(TILE_SIDE):
                wide[at_z : at_z + 1, :] = rows_ref[at_x, at_z].astype(jnp.float32)[row : row + 1]
            out_ref[at_x] = wide[...].astype(jnp.bfloat16)
        return carry

    wide[...] = jnp.zeros_like(wide)
    lax.fori_loop(0, first_ref.shape[0], take, 0)


def y_rows(block):
    side_x, depth, side_y, width = block.shape
    return pl.pallas_call(
        rows_kernel,
        out_shape=(
            jax.ShapeDtypeStruct((side_x, 16, width), block.dtype),
            jax.ShapeDtypeStruct((side_x, 16, width), block.dtype),
        ),
        grid=(1,),
        in_specs=[
            pl.BlockSpec((side_x, depth, 8, width), lambda i: (0, 0, 0, 0)),
            pl.BlockSpec((side_x, depth, 8, width), lambda i: (0, 0, side_y // 8 - 1, 0)),
        ],
        out_specs=(
            pl.BlockSpec((side_x, 16, width), lambda i: (0, 0, 0)),
            pl.BlockSpec((side_x, 16, width), lambda i: (0, 0, 0)),
        ),
        scratch_shapes=[pltpu.VMEM((16, width), jnp.float32)],
        compiler_params=pltpu.CompilerParams(vmem_limit_bytes=12 * MIB),
        name="y_rows",
    )(block, block)


def window_kernel(
    inside_ref, block_ref, layer_ref, below_ref, above_ref, outer_ref, scale_ref, shift_ref,
    weight_ref, order_ref, windows_ref, taps_ref, rows, line, layers,
):
    phase_x = pl.program_id(0)
    side, depth, width = 2 * TILE_SIDE, TILE_SIDE, FINE_WIDTH
    half = 2 * ACROSS * side

    @pl.when(phase_x == 0)
    def _():
        zero = jnp.zeros((width, width), jnp.bfloat16)
        for place in range(9):
            taps_ref[place, 3 * width :, :width] = zero
            taps_ref[place, :width, width:] = zero
            for step in range(3):
                block = jnp.dot(
                    weight_ref[place * 3 + step], order_ref[...], preferred_element_type=jnp.float32
                ).astype(jnp.bfloat16)
                taps_ref[place, step * width : (step + 1) * width, :width] = block
                taps_ref[place, (step + 1) * width : (step + 2) * width, width:] = block

        def widen(at_x, carry):
            rows[0, at_x] = below_ref[at_x].astype(jnp.float32)
            rows[1, at_x] = above_ref[at_x].astype(jnp.float32)
            return carry

        lax.fori_loop(0, side, widen, 0)

    scale = jnp.broadcast_to(scale_ref[...], (8, width))
    shift = jnp.broadcast_to(shift_ref[...], (8, width))
    row = lax.broadcasted_iota(jnp.int32, (8, width), 0)
    first = jnp.where(row == 0, shift * inside_ref[2], shift)
    last = jnp.where(row == side + 1 - 20, shift * inside_ref[3], shift)
    chunks = [(0, first), (8, shift), (16, shift), (4, shift), (12, shift), (20, last)]

    def split(cell_x, carry):
        at_x = phase_x + STRIDE * cell_x
        outside = jnp.logical_or(at_x == 0, at_x == side + 1)

        @pl.when(jnp.logical_not(outside))
        def _():
            at = at_x - 1
            for at_z in range(depth + 2):
                if at_z == 0:
                    flag, value, place = inside_ref[4], layer_ref[at], depth
                elif at_z == depth + 1:
                    flag, value, place = inside_ref[5], layer_ref[at], depth
                else:
                    flag, value, place = None, block_ref[at, at_z - 1], at_z - 1
                value = value.astype(jnp.float32)
                low, high = rows[0, at, place : place + 1, :], rows[1, at, place : place + 1, :]
                if flag is not None:
                    value, low, high = value * flag, low * flag, high * flag
                line[at_z, 7:8, :] = low
                line[at_z, 8 : side + 8, :] = value
                line[at_z, side + 8 : side + 9, :] = high

        @pl.when(outside)
        def _():
            end = jnp.where(at_x == 0, 0, 1)
            for at_z in range(depth + 2):
                value = outer_ref[end, at_z].astype(jnp.float32)
                line[at_z, 0:8, :] = value[side : side + 8]
                line[at_z, 8 : side + 8, :] = value[:side]
                line[at_z, side + 8 : side + 16, :] = value[side : side + 8]

        within = jnp.where(at_x == 0, inside_ref[0], 1.0)
        within = jnp.where(at_x == side + 1, inside_ref[1], within)
        for at_z in range(depth + 2):
            if at_z == 0:
                factor = within * inside_ref[4]
            elif at_z == depth + 1:
                factor = within * inside_ref[5]
            else:
                factor = within
            for number, (start, added) in enumerate(chunks):
                value = line[at_z, pl.ds(start + 7, 8), :]
                base = number // 3 * half + number % 3 * 8
                base = pl.multiple_of(base + cell_x * side, 8)
                layers[at_z, pl.ds(base, 8), :] = value
                layers[at_z, pl.ds(base + half // 2, 8), :] = value * scale + added * factor
        return carry

    lax.fori_loop(0, ACROSS, split, 0)
    for phase_y in range(PHASES):
        start = phase_y if phase_y < STRIDE else half + phase_y - STRIDE
        for phase_z in range(PHASES):
            parts = [
                layers[phase_z + STRIDE * cell, pl.ds(start, PLANE, stride=STRIDE), :]
                for cell in range(CELLS)
            ]
            parts.append(jnp.zeros((PADDED - ROWS, width), jnp.float32))
            windows_ref[0, phase_y, :, phase_z * width : (phase_z + 1) * width] = jnp.concatenate(
                parts, axis=0
            ).astype(jnp.bfloat16)


def make_windows(inside, *arrays):
    width, side = FINE_WIDTH, 2 * TILE_SIDE

    def whole(array):
        return pl.BlockSpec(array.shape, lambda i: (0,) * array.ndim)

    return pl.pallas_call(
        window_kernel,
        out_shape=(
            jax.ShapeDtypeStruct((PHASES, PHASES, PADDED, PHASES * width), jnp.bfloat16),
            jax.ShapeDtypeStruct((9, 4 * width, 2 * width), jnp.bfloat16),
        ),
        grid=(PHASES,),
        in_specs=[pl.BlockSpec(memory_space=pltpu.SMEM)] + [whole(array) for array in arrays],
        out_specs=(
            pl.BlockSpec((1, PHASES, PADDED, PHASES * width), lambda i: (i, 0, 0, 0)),
            pl.BlockSpec((9, 4 * width, 2 * width), lambda i: (0, 0, 0)),
        ),
        scratch_shapes=[
            pltpu.VMEM((2, side, 16, width), jnp.float32),
            pltpu.VMEM((TILE_SIDE + 2, side + 16, width), jnp.float32),
            pltpu.VMEM((TILE_SIDE + 2, 4 * ACROSS * side, width), jnp.float32),
        ],
        compiler_params=pltpu.CompilerParams(vmem_limit_bytes=28 * MIB),
        cost_estimate=pl.CostEstimate(flops=10**10, bytes_accessed=16 * MIB, transcendentals=0),
        name="windows",
    )(inside, *arrays)


def convolve_kernel(first_ref, second_ref, third_ref, taps_ref, bias_ref, out_ref):
    width = FINE_WIDTH
    bias = bias_ref[...]

    def convolve(at_y, carry):
        total = jnp.zeros((2 * PADDED, 2 * width), jnp.float32)
        for step_x, windows_ref in enumerate((first_ref, second_ref, third_ref)):
            for step_y in range(3):
                taken = [
                    windows_ref[0, at_y + step_y, :, pair * 2 * width : (pair * 2 + 4) * width]
                    for pair in range(2)
                ]
                total += jnp.dot(
                    jnp.concatenate(taken, axis=0),
                    taps_ref[step_x * 3 + step_y],
                    preferred_element_type=jnp.float32,
                )
        total = total + bias
        hidden = (total / (1.0 + jnp.exp(-total))).astype(jnp.bfloat16)
        for pair in range(2):
            out_ref[at_y * 2 + pair] = hidden[pair * PADDED : (pair + 1) * PADDED]
        return carry

    lax.fori_loop(0, STRIDE, convolve, 0)


def convolve(windows, taps, bias, start, count):
    width = FINE_WIDTH
    each = STRIDE * STRIDE // 2
    block = (1, PHASES, PADDED, PHASES * width)
    return pl.pallas_call(
        convolve_kernel,
        out_shape=jax.ShapeDtypeStruct((count * each, PADDED, 2 * width), jnp.bfloat16),
        grid=(count,),
        in_specs=[
            pl.BlockSpec(block, lambda i, step=step: (i + start + step, 0, 0, 0)) for step in range(3)
        ]
        + [
            pl.BlockSpec(taps.shape, lambda i: (0, 0, 0)),
            pl.BlockSpec(bias.shape, lambda i: (0, 0)),
        ],
        out_specs=pl.BlockSpec((each, PADDED, 2 * width), lambda i: (i, 0, 0)),
        compiler_params=pltpu.CompilerParams(vmem_limit_bytes=28 * MIB),
        cost_estimate=pl.CostEstimate(
            flops=2 * count * each * PADDED * 36 * width * 2 * width,
            bytes_accessed=16 * MIB,
            transcendentals=count * each * PADDED * 2 * width,
        ),
        name="convolve",
    )(windows, windows, windows, taps, bias)


def project_kernel(split, place_ref, early_ref, late_ref, *refs):
    weight_refs, bias_ref, out_ref = refs[:-2], refs[-2], refs[-1]
    width = out_ref.shape[1]
    start = pl.multiple_of(place_ref[0] * width, width)
    total = jnp.broadcast_to(bias_ref[:, pl.ds(start, width)], out_ref.shape)
    pairs = early_ref.shape[0]
    for number, hidden_ref in enumerate((early_ref, late_ref)):
        used = weight_refs[:-2] + (weight_refs[len(weight_refs) - 2 + number],) if split else weight_refs
        for pair in range(pairs):
            weight = jnp.concatenate(
                [
                    ref[2 * pair + item + (number * 2 * pairs if ref.shape[0] == OFFSETS else 0)]
                    for item in range(2)
                    for ref in used
                ],
                axis=0,
            )
            total += jnp.dot(hidden_ref[pair], weight, preferred_element_type=jnp.float32)
    out_ref[...] = total.astype(jnp.bfloat16)


def project(place, early, late, weights, split, bias):
    pairs, rows, depth = early.shape
    width = weights[0].shape[2]
    return pl.pallas_call(
        functools.partial(project_kernel, split),
        out_shape=jax.ShapeDtypeStruct((rows, width), jnp.bfloat16),
        in_specs=[pl.BlockSpec(memory_space=pltpu.SMEM)] + vmem(len(weights) + 3),
        out_specs=vmem(1)[0],
        compiler_params=pltpu.CompilerParams(vmem_limit_bytes=24 * MIB),
        cost_estimate=pl.CostEstimate(
            flops=4 * pairs * rows * depth * width, bytes_accessed=8 * MIB, transcendentals=0
        ),
        name="project",
    )(place, early, late, *weights, bias)


def bottle_kernel(far, place_ref, field_ref, weight_ref, *refs):
    out_refs, (held, total, packed, dense, sems) = refs[:-5], refs[-5:]
    width = field_ref.shape[4]
    share = out_refs[0].shape[1]
    span = held.shape[2]
    frame = ACROSS + 2
    rows = CELLS * 2 * ACROSS * frame
    chunk = 256
    owners = 2 * len(out_refs)
    first = pl.multiple_of((place_ref[0] // len(out_refs) ^ far) * span, span)

    def copy_of(step_y, place):
        tap = (place // 3 * 3 + step_y) * 3 + place % 3
        return pltpu.make_async_copy(
            weight_ref.at[tap, :, pl.ds(first, span)],
            held.at[step_y, pl.ds(place * width, width)],
            sems.at[step_y, place],
        )

    for step_y in range(3):
        for place in range(9):
            copy_of(step_y, place).start()

    for step_x in range(3):
        for step_z in range(3):
            place = step_x * 3 + step_z
            packed[:, place * width : (place + 1) * width] = (
                field_ref[step_z : step_z + CELLS, :, step_x : step_x + ACROSS]
                .astype(jnp.float32)
                .reshape(rows, width)
                .astype(jnp.bfloat16)
            )

    for step_x in range(3):
        for step_z in range(3):
            copy_of(0, step_x * 3 + step_z).wait()
        depth = slice(step_x * 3 * width, (step_x + 1) * 3 * width)
        for start in range(0, span, chunk):
            columns = slice(start, start + chunk)
            terms = jnp.dot(
                packed[:, depth], held[0, depth, columns], preferred_element_type=jnp.float32
            )
            total[0, :, columns] = terms if step_x == 0 else total[0, :, columns] + terms

    def rest(step_y, carry):
        for place in range(9):
            copy_of(step_y, place).wait()
        for start in range(0, span, chunk):
            columns = slice(start, start + chunk)
            total[step_y, :, columns] = jnp.dot(
                packed[...], held[step_y, :, columns], preferred_element_type=jnp.float32
            )
        return carry

    lax.fori_loop(1, 3, rest, 0)

    for number, out_ref in enumerate(out_refs):
        distance = number + far * owners // 2
        start = pl.multiple_of((place_ref[0] ^ distance) % len(out_refs) * share, share)
        for group in range(rows // frame):
            at = group * frame
            dense[group * ACROSS : (group + 1) * ACROSS, :] = sum(
                total[item, at + item : at + item + ACROSS, pl.ds(start, share)]
                for item in range(3)
            )
        out_ref[...] = dense[...].astype(out_ref.dtype)


def bottle_terms(place, field, weight, owners, far):
    frame = ACROSS + 2
    rows = CELLS * 2 * ACROSS * frame
    width = weight.shape[1]
    share = COARSE_WIDTH // owners
    span = COARSE_WIDTH // 2
    return pl.pallas_call(
        functools.partial(bottle_kernel, int(far)),
        out_shape=[
            jax.ShapeDtypeStruct((ROWS, share), jnp.bfloat16 if far or number else jnp.float32)
            for number in range(owners // 2)
        ],
        in_specs=[
            pl.BlockSpec(memory_space=pltpu.SMEM),
            pl.BlockSpec(memory_space=pltpu.VMEM),
            pl.BlockSpec(memory_space=pltpu.HBM),
        ],
        out_specs=vmem(owners // 2),
        scratch_shapes=[
            pltpu.VMEM((3, 9 * width, span), jnp.bfloat16),
            pltpu.VMEM((3, rows, span), jnp.float32),
            pltpu.VMEM((rows, 9 * width), jnp.bfloat16),
            pltpu.VMEM((ROWS, share), jnp.float32),
            pltpu.SemaphoreType.DMA((3, 9)),
        ],
        compiler_params=pltpu.CompilerParams(vmem_limit_bytes=51 * MIB),
        cost_estimate=pl.CostEstimate(
            flops=2 * rows * 27 * width * span, bytes_accessed=8 * MIB, transcendentals=0
        ),
        name="bottle_far" if far else "bottle_near",
    )(place, field, weight)


def finish_kernel(place_ref, guide_ref, own_ref, *refs):
    other_refs, bias_ref, out_ref, spread = refs[:-3], refs[-3], refs[-2], refs[-1]
    share = own_ref.shape[1]
    start = pl.multiple_of(place_ref[0] * share, share)
    value = own_ref[...] + bias_ref[:, pl.ds(start, share)]
    for other_ref in other_refs:
        value = value + other_ref[...].astype(jnp.float32)
    value = value / (1.0 + jnp.exp(-value))
    half = PLANE // 2
    for cell in range(CELLS):
        plain = value[cell * PLANE : cell * PLANE + half]
        guided = value[cell * PLANE + half : (cell + 1) * PLANE]
        mixed = plain + guide_ref[0] * (guided - plain)
        for lane in range(spread.shape[0]):
            spread[lane, pl.ds(cell, half, stride=SPREAD), :] = mixed[:, lane * LANES : (lane + 1) * LANES]
    for lane in range(spread.shape[0]):
        for cell in range(half):
            out_ref[cell, :, lane * LANES : (lane + 1) * LANES] = spread[
                lane, cell * SPREAD : cell * SPREAD + CELLS, :
            ].astype(jnp.bfloat16)


def finish(place, guide, terms, bias):
    share = terms[0].shape[1]
    return pl.pallas_call(
        finish_kernel,
        out_shape=jax.ShapeDtypeStruct((PLANE // 2, CELLS, share), jnp.bfloat16),
        in_specs=[pl.BlockSpec(memory_space=pltpu.SMEM)] * 2 + vmem(len(terms) + 1),
        out_specs=vmem(1)[0],
        scratch_shapes=[pltpu.VMEM((share // LANES, PLANE // 2 * SPREAD, LANES), jnp.float32)],
        compiler_params=pltpu.CompilerParams(vmem_limit_bytes=8 * MIB),
        name="finish",
    )(place, guide, *terms, bias)


def passed(value, steps):
    count = lax.axis_size("region")
    return lax.ppermute(
        value, "region", [(at, at + steps) for at in range(max(0, -steps), min(count, count - steps))]
    )


def across_z(value):
    count = lax.axis_size("region")
    return lax.ppermute(value, "region", [(at, at ^ 1) for at in range(count)])


def y_halos(first, last):
    place = lax.axis_index("region") // REGIONS_Z % REGIONS_Y
    upper = is_upper()
    ahead = hop(jnp.where(upper, first, last), True)
    back = hop(jnp.where(upper, last, first), False)
    zero = jnp.zeros_like(ahead)
    below = jnp.where(place > 0, jnp.where(upper, back, ahead), zero)
    above = jnp.where(place < REGIONS_Y - 1, jnp.where(upper, ahead, back), zero)
    return below, above


def with_halos(value, dim_x, dim_y, dim_z):
    value = jnp.concatenate(z_ends(z_layer(value, dim_z), value, dim_z), axis=dim_z)
    below, above = y_halos(edge(value, dim_y, False), edge(value, dim_y, True))
    value = jnp.concatenate([below, value, above], axis=dim_y)
    low, high = x_layers(edge(value, dim_x, False), edge(value, dim_x, True))
    return jnp.concatenate([low, value, high], axis=dim_x)


def edge(array, dim, last):
    size = array.shape[dim]
    return lax.slice_in_dim(array, size - 1 if last else 0, size if last else 1, axis=dim)


def is_upper():
    return lax.axis_index("region") % REGIONS_Z == 1


def z_layer(value, dim):
    return across_z(jnp.where(is_upper(), edge(value, dim, False), edge(value, dim, True)))


def z_ends(layer, value, dim):
    zero = jnp.zeros_like(layer)
    return [jnp.where(is_upper(), layer, zero), value, jnp.where(is_upper(), zero, layer)]


def x_layers(first, last):
    count = lax.axis_size("region") // (REGIONS_Y * REGIONS_Z)
    if count == 1:
        return jnp.zeros_like(last), jnp.zeros_like(first)
    return passed(last, REGIONS_Y * REGIONS_Z), passed(first, -REGIONS_Y * REGIONS_Z)


def chan_swap(value, distance):
    return lax.ppermute(value, "chan", [(at, at ^ distance) for at in range(lax.axis_size("chan"))])


def exchange(piece_at):
    chans = lax.axis_size("chan")
    return [piece_at(0)] + [chan_swap(piece_at(distance), distance) for distance in range(1, chans)]


def ring_of(count):
    return list(range(0, count, 2)) + list(range(1, count, 2))[::-1]


def hop(value, ahead):
    ring = ring_of(lax.axis_size("region"))
    following = ring[1:] + ring[:1]
    return lax.ppermute(value, "region", list(zip(ring, following) if ahead else zip(following, ring)))


def after(value, other):
    return lax.optimization_barrier((value, other))[0]


def piece_channels(each):
    chans, regions = lax.axis_size("chan"), lax.axis_size("region")
    ring = ring_of(regions)
    shifts = [0]
    for step in range(1, regions // 2 + 1):
        shifts += [-step] + [step] * (step < regions // 2)
    origin = np.array(
        [[ring[(ring.index(region) + shift) % regions] for shift in shifts] for region in range(regions)]
    )
    table = np.zeros((chans, regions, regions, chans, each), np.int32)
    for chan in range(chans):
        for distance in range(chans):
            first = (chan ^ distance) * regions + origin
            table[chan, :, :, distance] = first[:, :, None] * each + np.arange(each)
    table = jnp.asarray(table.reshape(chans * regions, FINE_WIDTH))
    device = lax.axis_index("chan") * regions + lax.axis_index("region")
    return lax.dynamic_index_in_dim(table, device, 0, keepdims=True)


def ring_pieces(piece, milestones):
    regions = lax.axis_size("region")
    forward = backward = piece
    held = [piece]
    for step in range(1, regions // 2 + 1):
        if step > 1 and step - 2 < len(milestones):
            forward, backward = (after(value, milestones[step - 2]) for value in (forward, backward))
        if step == regions // 2:
            held += [hop(forward[: OFFSETS // 2], True), hop(backward[OFFSETS // 2 :], False)]
        else:
            forward, backward = hop(forward, True), hop(backward, False)
            held += [forward, backward]
    return held


def whole_columns(proj_weight):
    chans, held = lax.axis_size("chan"), proj_weight.shape[0]
    width = COARSE_WIDTH // chans
    mine = lax.all_to_all(proj_weight, "chan", split_axis=1, concat_axis=0, tiled=True)
    whole = lax.all_gather(mine.reshape(chans, held, width), "region", axis=1, tiled=True)
    return whole.reshape(FINE_WIDTH, OFFSETS, width).transpose(1, 0, 2)


def shards(
    latent,
    cond_scale,
    cond_shift,
    fine_weight,
    fine_bias,
    proj_weight,
    proj_bias,
    bottle_weight,
    bottle_bias,
    guide,
):
    chans = lax.axis_size("chan")
    chan_place = lax.axis_index("chan")
    region = lax.axis_index("region")
    width = COARSE_WIDTH // chans
    side = 2 * TILE_SIDE
    count_x = lax.axis_size("region") // (REGIONS_Y * REGIONS_Z)
    steps = (REGIONS_Y * REGIONS_Z, REGIONS_Z, 1)
    counts = (count_x, REGIONS_Y, REGIONS_Z)
    places = [region // step % count for step, count in zip(steps, counts)]
    inside = jnp.stack(
        [
            flag
            for place, count in zip(places, counts)
            for flag in ((place > 0).astype(jnp.float32), (place < count - 1).astype(jnp.float32))
        ]
    )

    place = chan_place[None]
    each, rest = divmod(proj_weight.shape[0], OFFSETS)
    by_ring = rest == 0 and chans * each % 16 == 0
    if by_ring:
        split = split_columns(place, proj_weight, chans)
        mine = exchange(lambda distance: split[distance])
        piece = regroup(mine)
        channel = piece_channels(each)
    else:
        channel = jnp.arange(FINE_WIDTH, dtype=jnp.int32)[None]
    order = lax.broadcasted_iota(jnp.int32, (FINE_WIDTH, FINE_WIDTH), 0) == channel

    block = latent[0].transpose(0, 2, 1, 3)
    outermost = jnp.where(is_upper(), 0, TILE_SIDE - 1)
    if by_ring:
        outermost = after(outermost, mine[1])
    face = lax.dynamic_index_in_dim(block, outermost, axis=1, keepdims=False)
    first, last = y_rows(block)
    layer = across_z(face)
    corner = lax.broadcasted_iota(jnp.int32, first.shape, 1) == TILE_SIDE
    below, above = y_halos(
        jnp.where(corner, layer[:, :1], first), jnp.where(corner, layer[:, -1:], last)
    )
    ends = []
    for at in (0, -1):
        plane = jnp.concatenate(z_ends(layer[at][None], block[at], 0), axis=0)
        low, high = [
            jnp.concatenate(
                z_ends(part[at, TILE_SIDE : TILE_SIDE + 1], part[at, :TILE_SIDE], 0), axis=0
            )[:, None]
            for part in (below, above)
        ]
        spare = jnp.zeros((TILE_SIDE + 2, 6, FINE_WIDTH), plane.dtype)
        ends.append(jnp.concatenate([plane, high, spare, low], axis=1))
    outer = jnp.stack(x_layers(*ends))

    bias = jnp.sum(jnp.where(order, fine_bias[:, None], 0.0), axis=0)
    windows, taps = make_windows(
        inside,
        block,
        layer,
        below,
        above,
        outer,
        cond_scale[None],
        cond_shift[None],
        fine_weight.reshape(27, FINE_WIDTH, FINE_WIDTH),
        order.astype(jnp.bfloat16),
    )
    bias = jnp.concatenate([bias, bias])[None]
    half = STRIDE // 2
    early = convolve(windows, taps, bias, 0, half)
    late = convolve(windows, taps, bias, half, half)
    columns = ring_pieces(piece, [taps, early, late]) if by_ring else [whole_columns(proj_weight)]
    coarse = project(place, early, late, columns, by_ring, proj_bias[None])

    grid = coarse[:ROWS].reshape(CELLS, 2, ACROSS, ACROSS, width)
    field = with_halos(grid, 2, 3, 0)
    far = bottle_terms(place, field, bottle_weight, chans, True)
    swapped = [chan_swap(value, chans // 2 + number) for number, value in enumerate(far)]
    own, *near = bottle_terms(after(place, far), field, bottle_weight, chans, False)
    near = [chan_swap(value, 1 + number) for number, value in enumerate(near)]
    terms = [own, sum(value.astype(jnp.float32) for value in swapped)] + near
    guided = finish(place, guide, terms, bottle_bias[None])
    return guided.reshape(1, ACROSS, ACROSS, CELLS, width)


def solution(mesh):
    placed = (
        P("region", None, None, None, None),
        P(),
        P(),
        P(),
        P(),
        P(("chan", "region"), None),
        P(),
        P(None, "chan", None),
        P(),
        P(),
    )
    return jax.shard_map(
        shards,
        mesh=mesh,
        in_specs=placed,
        out_specs=P("region", None, None, None, "chan"),
        check_vma=False,
    )
```

```python
import functools

import numpy as np

import jax
import jax.numpy as jnp
from jax import lax
from jax.experimental import pallas as pl
from jax.experimental.pallas import tpu as pltpu
from jax.sharding import PartitionSpec as P

FINE_WIDTH = 128
COARSE_WIDTH = 1024
TILE_SIDE = 12
STRIDE = 4
REGIONS_Y = 4
REGIONS_Z = 2

CELLS = TILE_SIDE // STRIDE
ACROSS = 2 * CELLS
PLANE = 2 * ACROSS * ACROSS
ROWS = CELLS * PLANE
PADDED = -(-ROWS // 16) * 16
PHASES = STRIDE + 2
OFFSETS = STRIDE**3
LANES = 128
SPREAD = 8
MIB = 2**20


def vmem(count):
    return [pl.BlockSpec(memory_space=pltpu.VMEM) for _ in range(count)]


def regroup_kernel(*refs):
    rows_refs, out_ref, wide = refs[:-2], refs[-2], refs[-1]
    held = rows_refs[0].shape[0]
    groups = out_ref.shape[1]
    for lane in range(wide.shape[0]):
        columns = slice(lane * LANES, (lane + 1) * LANES)
        for number, rows_ref in enumerate(rows_refs):
            wide[lane, number * held : (number + 1) * held, :] = rows_ref[:, columns].astype(jnp.float32)
        for offset in range(OFFSETS):
            out_ref[offset, :, columns] = wide[
                lane, pl.ds(offset, groups, stride=OFFSETS), :
            ].astype(jnp.bfloat16)


def regroup(pieces):
    held, width = pieces[0].shape
    total = len(pieces) * held
    return pl.pallas_call(
        regroup_kernel,
        out_shape=jax.ShapeDtypeStruct((OFFSETS, total // OFFSETS, width), jnp.bfloat16),
        in_specs=vmem(len(pieces)),
        out_specs=vmem(1)[0],
        scratch_shapes=[pltpu.VMEM((width // LANES, total, LANES), jnp.float32)],
        compiler_params=pltpu.CompilerParams(vmem_limit_bytes=8 * MIB),
        name="regroup",
    )(*pieces)


def split_kernel(place_ref, rows_ref, *out_refs):
    width = out_refs[0].shape[1]
    for distance, out_ref in enumerate(out_refs):
        start = pl.multiple_of((place_ref[0] ^ distance) * width, width)
        out_ref[...] = rows_ref[:, pl.ds(start, width)]


def split_columns(place, rows, owners):
    held, width = rows.shape[0], rows.shape[1] // owners
    return pl.pallas_call(
        split_kernel,
        out_shape=[jax.ShapeDtypeStruct((held, width), rows.dtype)] * owners,
        in_specs=[pl.BlockSpec(memory_space=pltpu.SMEM)] + vmem(1),
        out_specs=vmem(owners),
        compiler_params=pltpu.CompilerParams(vmem_limit_bytes=4 * MIB),
        name="split_columns",
    )(place, rows)


def rows_kernel(first_ref, last_ref, low_ref, high_ref, wide):
    def take(at_x, carry):
        for rows_ref, row, out_ref in ((first_ref, 0, low_ref), (last_ref, 7, high_ref)):
            for at_z in range(TILE_SIDE):
                wide[at_z : at_z + 1, :] = rows_ref[at_x, at_z].astype(jnp.float32)[row : row + 1]
            out_ref[at_x] = wide[...].astype(jnp.bfloat16)
        return carry

    wide[...] = jnp.zeros_like(wide)
    lax.fori_loop(0, first_ref.shape[0], take, 0)


def y_rows(block):
    side_x, depth, side_y, width = block.shape
    return pl.pallas_call(
        rows_kernel,
        out_shape=(
            jax.ShapeDtypeStruct((side_x, 16, width), block.dtype),
            jax.ShapeDtypeStruct((side_x, 16, width), block.dtype),
        ),
        grid=(1,),
        in_specs=[
            pl.BlockSpec((side_x, depth, 8, width), lambda i: (0, 0, 0, 0)),
            pl.BlockSpec((side_x, depth, 8, width), lambda i: (0, 0, side_y // 8 - 1, 0)),
        ],
        out_specs=(
            pl.BlockSpec((side_x, 16, width), lambda i: (0, 0, 0)),
            pl.BlockSpec((side_x, 16, width), lambda i: (0, 0, 0)),
        ),
        scratch_shapes=[pltpu.VMEM((16, width), jnp.float32)],
        compiler_params=pltpu.CompilerParams(vmem_limit_bytes=12 * MIB),
        name="y_rows",
    )(block, block)


def window_kernel(
    inside_ref, block_ref, layer_ref, below_ref, above_ref, outer_ref, scale_ref, shift_ref,
    weight_ref, order_ref, windows_ref, taps_ref, rows, line, layers,
):
    phase_x = pl.program_id(0)
    side, depth, width = 2 * TILE_SIDE, TILE_SIDE, FINE_WIDTH
    half = 2 * ACROSS * side

    @pl.when(phase_x == 0)
    def _():
        zero = jnp.zeros((width, width), jnp.bfloat16)
        for place in range(9):
            taps_ref[place, 3 * width :, :width] = zero
            taps_ref[place, :width, width:] = zero
            for step in range(3):
                block = jnp.dot(
                    weight_ref[place * 3 + step], order_ref[...], preferred_element_type=jnp.float32
                ).astype(jnp.bfloat16)
                taps_ref[place, step * width : (step + 1) * width, :width] = block
                taps_ref[place, (step + 1) * width : (step + 2) * width, width:] = block

        def widen(at_x, carry):
            rows[0, at_x] = below_ref[at_x].astype(jnp.float32)
            rows[1, at_x] = above_ref[at_x].astype(jnp.float32)
            return carry

        lax.fori_loop(0, side, widen, 0)

    scale = jnp.broadcast_to(scale_ref[...], (8, width))
    shift = jnp.broadcast_to(shift_ref[...], (8, width))
    row = lax.broadcasted_iota(jnp.int32, (8, width), 0)
    first = jnp.where(row == 0, shift * inside_ref[2], shift)
    last = jnp.where(row == side + 1 - 20, shift * inside_ref[3], shift)
    chunks = [(0, first), (8, shift), (16, shift), (4, shift), (12, shift), (20, last)]

    def split(cell_x, carry):
        at_x = phase_x + STRIDE * cell_x
        outside = jnp.logical_or(at_x == 0, at_x == side + 1)

        @pl.when(jnp.logical_not(outside))
        def _():
            at = at_x - 1
            for at_z in range(depth + 2):
                if at_z == 0:
                    flag, value, place = inside_ref[4], layer_ref[at], depth
                elif at_z == depth + 1:
                    flag, value, place = inside_ref[5], layer_ref[at], depth
                else:
                    flag, value, place = None, block_ref[at, at_z - 1], at_z - 1
                value = value.astype(jnp.float32)
                low, high = rows[0, at, place : place + 1, :], rows[1, at, place : place + 1, :]
                if flag is not None:
                    value, low, high = value * flag, low * flag, high * flag
                line[at_z, 7:8, :] = low
                line[at_z, 8 : side + 8, :] = value
                line[at_z, side + 8 : side + 9, :] = high

        @pl.when(outside)
        def _():
            end = jnp.where(at_x == 0, 0, 1)
            for at_z in range(depth + 2):
                value = outer_ref[end, at_z].astype(jnp.float32)
                line[at_z, 0:8, :] = value[side : side + 8]
                line[at_z, 8 : side + 8, :] = value[:side]
                line[at_z, side + 8 : side + 16, :] = value[side : side + 8]

        within = jnp.where(at_x == 0, inside_ref[0], 1.0)
        within = jnp.where(at_x == side + 1, inside_ref[1], within)
        for at_z in range(depth + 2):
            if at_z == 0:
                factor = within * inside_ref[4]
            elif at_z == depth + 1:
                factor = within * inside_ref[5]
            else:
                factor = within
            for number, (start, added) in enumerate(chunks):
                value = line[at_z, pl.ds(start + 7, 8), :]
                base = number // 3 * half + number % 3 * 8
                base = pl.multiple_of(base + cell_x * side, 8)
                layers[at_z, pl.ds(base, 8), :] = value
                layers[at_z, pl.ds(base + half // 2, 8), :] = value * scale + added * factor
        return carry

    lax.fori_loop(0, ACROSS, split, 0)
    for phase_y in range(PHASES):
        start = phase_y if phase_y < STRIDE else half + phase_y - STRIDE
        for phase_z in range(PHASES):
            parts = [
                layers[phase_z + STRIDE * cell, pl.ds(start, PLANE, stride=STRIDE), :]
                for cell in range(CELLS)
            ]
            parts.append(jnp.zeros((PADDED - ROWS, width), jnp.float32))
            windows_ref[0, phase_y, :, phase_z * width : (phase_z + 1) * width] = jnp.concatenate(
                parts, axis=0
            ).astype(jnp.bfloat16)


def make_windows(inside, *arrays):
    width, side = FINE_WIDTH, 2 * TILE_SIDE

    def whole(array):
        return pl.BlockSpec(array.shape, lambda i: (0,) * array.ndim)

    return pl.pallas_call(
        window_kernel,
        out_shape=(
            jax.ShapeDtypeStruct((PHASES, PHASES, PADDED, PHASES * width), jnp.bfloat16),
            jax.ShapeDtypeStruct((9, 4 * width, 2 * width), jnp.bfloat16),
        ),
        grid=(PHASES,),
        in_specs=[pl.BlockSpec(memory_space=pltpu.SMEM)] + [whole(array) for array in arrays],
        out_specs=(
            pl.BlockSpec((1, PHASES, PADDED, PHASES * width), lambda i: (i, 0, 0, 0)),
            pl.BlockSpec((9, 4 * width, 2 * width), lambda i: (0, 0, 0)),
        ),
        scratch_shapes=[
            pltpu.VMEM((2, side, 16, width), jnp.float32),
            pltpu.VMEM((TILE_SIDE + 2, side + 16, width), jnp.float32),
            pltpu.VMEM((TILE_SIDE + 2, 4 * ACROSS * side, width), jnp.float32),
        ],
        compiler_params=pltpu.CompilerParams(vmem_limit_bytes=28 * MIB),
        cost_estimate=pl.CostEstimate(flops=10**10, bytes_accessed=16 * MIB, transcendentals=0),
        name="windows",
    )(inside, *arrays)


def convolve_kernel(first_ref, second_ref, third_ref, taps_ref, bias_ref, out_ref):
    width = FINE_WIDTH
    bias = bias_ref[...]

    def convolve(at_y, carry):
        total = jnp.zeros((2 * PADDED, 2 * width), jnp.float32)
        for step_x, windows_ref in enumerate((first_ref, second_ref, third_ref)):
            for step_y in range(3):
                taken = [
                    windows_ref[0, at_y + step_y, :, pair * 2 * width : (pair * 2 + 4) * width]
                    for pair in range(2)
                ]
                total += jnp.dot(
                    jnp.concatenate(taken, axis=0),
                    taps_ref[step_x * 3 + step_y],
                    preferred_element_type=jnp.float32,
                )
        total = total + bias
        hidden = (total / (1.0 + jnp.exp(-total))).astype(jnp.bfloat16)
        for pair in range(2):
            out_ref[at_y * 2 + pair] = hidden[pair * PADDED : (pair + 1) * PADDED]
        return carry

    lax.fori_loop(0, STRIDE, convolve, 0)


def convolve(windows, taps, bias, start, count):
    width = FINE_WIDTH
    each = STRIDE * STRIDE // 2
    block = (1, PHASES, PADDED, PHASES * width)
    return pl.pallas_call(
        convolve_kernel,
        out_shape=jax.ShapeDtypeStruct((count * each, PADDED, 2 * width), jnp.bfloat16),
        grid=(count,),
        in_specs=[
            pl.BlockSpec(block, lambda i, step=step: (i + start + step, 0, 0, 0)) for step in range(3)
        ]
        + [
            pl.BlockSpec(taps.shape, lambda i: (0, 0, 0)),
            pl.BlockSpec(bias.shape, lambda i: (0, 0)),
        ],
        out_specs=pl.BlockSpec((each, PADDED, 2 * width), lambda i: (i, 0, 0)),
        compiler_params=pltpu.CompilerParams(vmem_limit_bytes=28 * MIB),
        cost_estimate=pl.CostEstimate(
            flops=2 * count * each * PADDED * 36 * width * 2 * width,
            bytes_accessed=16 * MIB,
            transcendentals=count * each * PADDED * 2 * width,
        ),
        name="convolve",
    )(windows, windows, windows, taps, bias)


def project_kernel(split, place_ref, early_ref, late_ref, *refs):
    weight_refs, bias_ref, out_ref = refs[:-2], refs[-2], refs[-1]
    width = out_ref.shape[1]
    start = pl.multiple_of(place_ref[0] * width, width)
    total = jnp.broadcast_to(bias_ref[:, pl.ds(start, width)], out_ref.shape)
    pairs = early_ref.shape[0]
    for number, hidden_ref in enumerate((early_ref, late_ref)):
        used = weight_refs[:-2] + (weight_refs[len(weight_refs) - 2 + number],) if split else weight_refs
        for pair in range(pairs):
            weight = jnp.concatenate(
                [
                    ref[2 * pair + item + (number * 2 * pairs if ref.shape[0] == OFFSETS else 0)]
                    for item in range(2)
                    for ref in used
                ],
                axis=0,
            )
            total += jnp.dot(hidden_ref[pair], weight, preferred_element_type=jnp.float32)
    out_ref[...] = total.astype(jnp.bfloat16)


def project(place, early, late, weights, split, bias):
    pairs, rows, depth = early.shape
    width = weights[0].shape[2]
    return pl.pallas_call(
        functools.partial(project_kernel, split),
        out_shape=jax.ShapeDtypeStruct((rows, width), jnp.bfloat16),
        in_specs=[pl.BlockSpec(memory_space=pltpu.SMEM)] + vmem(len(weights) + 3),
        out_specs=vmem(1)[0],
        compiler_params=pltpu.CompilerParams(vmem_limit_bytes=24 * MIB),
        cost_estimate=pl.CostEstimate(
            flops=4 * pairs * rows * depth * width, bytes_accessed=8 * MIB, transcendentals=0
        ),
        name="project",
    )(place, early, late, *weights, bias)


def bottle_kernel(far, place_ref, field_ref, weight_ref, *refs):
    out_refs, (held, total, packed, dense, sems) = refs[:-5], refs[-5:]
    width = field_ref.shape[4]
    share = out_refs[0].shape[1]
    span = held.shape[2]
    frame = ACROSS + 2
    rows = CELLS * 2 * ACROSS * frame
    chunk = 256
    owners = 2 * len(out_refs)
    first = pl.multiple_of((place_ref[0] // len(out_refs) ^ far) * span, span)

    def copy_of(step_y, place):
        tap = (place // 3 * 3 + step_y) * 3 + place % 3
        return pltpu.make_async_copy(
            weight_ref.at[tap, :, pl.ds(first, span)],
            held.at[step_y, pl.ds(place * width, width)],
            sems.at[step_y, place],
        )

    for step_y in range(3):
        for place in range(9):
            copy_of(step_y, place).start()

    for step_x in range(3):
        for step_z in range(3):
            place = step_x * 3 + step_z
            packed[:, place * width : (place + 1) * width] = (
                field_ref[step_z : step_z + CELLS, :, step_x : step_x + ACROSS]
                .astype(jnp.float32)
                .reshape(rows, width)
                .astype(jnp.bfloat16)
            )

    for step_x in range(3):
        for step_z in range(3):
            copy_of(0, step_x * 3 + step_z).wait()
        depth = slice(step_x * 3 * width, (step_x + 1) * 3 * width)
        for start in range(0, span, chunk):
            columns = slice(start, start + chunk)
            terms = jnp.dot(
                packed[:, depth], held[0, depth, columns], preferred_element_type=jnp.float32
            )
            total[0, :, columns] = terms if step_x == 0 else total[0, :, columns] + terms

    def rest(step_y, carry):
        for place in range(9):
            copy_of(step_y, place).wait()
        for start in range(0, span, chunk):
            columns = slice(start, start + chunk)
            total[step_y, :, columns] = jnp.dot(
                packed[...], held[step_y, :, columns], preferred_element_type=jnp.float32
            )
        return carry

    lax.fori_loop(1, 3, rest, 0)

    for number, out_ref in enumerate(out_refs):
        distance = number + far * owners // 2
        start = pl.multiple_of((place_ref[0] ^ distance) % len(out_refs) * share, share)
        for group in range(rows // frame):
            at = group * frame
            dense[group * ACROSS : (group + 1) * ACROSS, :] = sum(
                total[item, at + item : at + item + ACROSS, pl.ds(start, share)]
                for item in range(3)
            )
        out_ref[...] = dense[...].astype(out_ref.dtype)


def bottle_terms(place, field, weight, owners, far):
    frame = ACROSS + 2
    rows = CELLS * 2 * ACROSS * frame
    width = weight.shape[1]
    share = COARSE_WIDTH // owners
    span = COARSE_WIDTH // 2
    return pl.pallas_call(
        functools.partial(bottle_kernel, int(far)),
        out_shape=[
            jax.ShapeDtypeStruct((ROWS, share), jnp.bfloat16 if far or number else jnp.float32)
            for number in range(owners // 2)
        ],
        in_specs=[
            pl.BlockSpec(memory_space=pltpu.SMEM),
            pl.BlockSpec(memory_space=pltpu.VMEM),
            pl.BlockSpec(memory_space=pltpu.HBM),
        ],
        out_specs=vmem(owners // 2),
        scratch_shapes=[
            pltpu.VMEM((3, 9 * width, span), jnp.bfloat16),
            pltpu.VMEM((3, rows, span), jnp.float32),
            pltpu.VMEM((rows, 9 * width), jnp.bfloat16),
            pltpu.VMEM((ROWS, share), jnp.float32),
            pltpu.SemaphoreType.DMA((3, 9)),
        ],
        compiler_params=pltpu.CompilerParams(vmem_limit_bytes=51 * MIB),
        cost_estimate=pl.CostEstimate(
            flops=2 * rows * 27 * width * span, bytes_accessed=8 * MIB, transcendentals=0
        ),
        name="bottle_far" if far else "bottle_near",
    )(place, field, weight)


def finish_kernel(place_ref, guide_ref, own_ref, *refs):
    other_refs, bias_ref, out_ref, spread = refs[:-3], refs[-3], refs[-2], refs[-1]
    share = own_ref.shape[1]
    start = pl.multiple_of(place_ref[0] * share, share)
    value = own_ref[...] + bias_ref[:, pl.ds(start, share)]
    for other_ref in other_refs:
        value = value + other_ref[...].astype(jnp.float32)
    value = value / (1.0 + jnp.exp(-value))
    half = PLANE // 2
    for cell in range(CELLS):
        plain = value[cell * PLANE : cell * PLANE + half]
        guided = value[cell * PLANE + half : (cell + 1) * PLANE]
        mixed = plain + guide_ref[0] * (guided - plain)
        for lane in range(spread.shape[0]):
            spread[lane, pl.ds(cell, half, stride=SPREAD), :] = mixed[:, lane * LANES : (lane + 1) * LANES]
    for lane in range(spread.shape[0]):
        for cell in range(half):
            out_ref[cell, :, lane * LANES : (lane + 1) * LANES] = spread[
                lane, cell * SPREAD : cell * SPREAD + CELLS, :
            ].astype(jnp.bfloat16)


def finish(place, guide, terms, bias):
    share = terms[0].shape[1]
    return pl.pallas_call(
        finish_kernel,
        out_shape=jax.ShapeDtypeStruct((PLANE // 2, CELLS, share), jnp.bfloat16),
        in_specs=[pl.BlockSpec(memory_space=pltpu.SMEM)] * 2 + vmem(len(terms) + 1),
        out_specs=vmem(1)[0],
        scratch_shapes=[pltpu.VMEM((share // LANES, PLANE // 2 * SPREAD, LANES), jnp.float32)],
        compiler_params=pltpu.CompilerParams(vmem_limit_bytes=8 * MIB),
        name="finish",
    )(place, guide, *terms, bias)


def passed(value, steps):
    count = lax.axis_size("region")
    return lax.ppermute(
        value, "region", [(at, at + steps) for at in range(max(0, -steps), min(count, count - steps))]
    )


def across_z(value):
    count = lax.axis_size("region")
    return lax.ppermute(value, "region", [(at, at ^ 1) for at in range(count)])


def y_halos(first, last):
    place = lax.axis_index("region") // REGIONS_Z % REGIONS_Y
    upper = is_upper()
    ahead = hop(jnp.where(upper, first, last), True)
    back = hop(jnp.where(upper, last, first), False)
    zero = jnp.zeros_like(ahead)
    below = jnp.where(place > 0, jnp.where(upper, back, ahead), zero)
    above = jnp.where(place < REGIONS_Y - 1, jnp.where(upper, ahead, back), zero)
    return below, above


def with_halos(value, dim_x, dim_y, dim_z):
    value = jnp.concatenate(z_ends(z_layer(value, dim_z), value, dim_z), axis=dim_z)
    below, above = y_halos(edge(value, dim_y, False), edge(value, dim_y, True))
    value = jnp.concatenate([below, value, above], axis=dim_y)
    low, high = x_layers(edge(value, dim_x, False), edge(value, dim_x, True))
    return jnp.concatenate([low, value, high], axis=dim_x)


def edge(array, dim, last):
    size = array.shape[dim]
    return lax.slice_in_dim(array, size - 1 if last else 0, size if last else 1, axis=dim)


def is_upper():
    return lax.axis_index("region") % REGIONS_Z == 1


def z_layer(value, dim):
    return across_z(jnp.where(is_upper(), edge(value, dim, False), edge(value, dim, True)))


def z_ends(layer, value, dim):
    zero = jnp.zeros_like(layer)
    return [jnp.where(is_upper(), layer, zero), value, jnp.where(is_upper(), zero, layer)]


def x_layers(first, last):
    count = lax.axis_size("region") // (REGIONS_Y * REGIONS_Z)
    if count == 1:
        return jnp.zeros_like(last), jnp.zeros_like(first)
    return passed(last, REGIONS_Y * REGIONS_Z), passed(first, -REGIONS_Y * REGIONS_Z)


def chan_swap(value, distance):
    return lax.ppermute(value, "chan", [(at, at ^ distance) for at in range(lax.axis_size("chan"))])


def exchange(piece_at):
    chans = lax.axis_size("chan")
    return [piece_at(0)] + [chan_swap(piece_at(distance), distance) for distance in range(1, chans)]


def ring_of(count):
    return list(range(0, count, 2)) + list(range(1, count, 2))[::-1]


def hop(value, ahead):
    ring = ring_of(lax.axis_size("region"))
    following = ring[1:] + ring[:1]
    return lax.ppermute(value, "region", list(zip(ring, following) if ahead else zip(following, ring)))


def after(value, other):
    return lax.optimization_barrier((value, other))[0]


def piece_channels(each):
    chans, regions = lax.axis_size("chan"), lax.axis_size("region")
    region = lax.axis_index("region")
    lane = lax.broadcasted_iota(jnp.int32, (1, FINE_WIDTH), 1)
    piece, distance, member = lane // (chans * each), lane // each % chans, lane % each
    place = jnp.where(region % 2 == 0, region // 2, regions - 1 - region // 2)
    shift = jnp.where(piece % 2 == 0, piece // 2, -((piece + 1) // 2))
    at = (place + shift + regions) % regions
    origin = jnp.where(at < regions // 2, 2 * at, 2 * (regions - 1 - at) + 1)
    return ((lax.axis_index("chan") ^ distance) * regions + origin) * each + member


def ring_pieces(piece, milestones):
    regions = lax.axis_size("region")
    forward = backward = piece
    held = [piece]
    for step in range(1, regions // 2 + 1):
        if step > 1 and step - 2 < len(milestones):
            forward, backward = (after(value, milestones[step - 2]) for value in (forward, backward))
        if step == regions // 2:
            held += [hop(forward[: OFFSETS // 2], True), hop(backward[OFFSETS // 2 :], False)]
        else:
            forward, backward = hop(forward, True), hop(backward, False)
            held += [forward, backward]
    return held


def whole_columns(proj_weight):
    chans, held = lax.axis_size("chan"), proj_weight.shape[0]
    width = COARSE_WIDTH // chans
    mine = lax.all_to_all(proj_weight, "chan", split_axis=1, concat_axis=0, tiled=True)
    whole = lax.all_gather(mine.reshape(chans, held, width), "region", axis=1, tiled=True)
    return whole.reshape(FINE_WIDTH, OFFSETS, width).transpose(1, 0, 2)


def shards(
    latent,
    cond_scale,
    cond_shift,
    fine_weight,
    fine_bias,
    proj_weight,
    proj_bias,
    bottle_weight,
    bottle_bias,
    guide,
):
    chans = lax.axis_size("chan")
    chan_place = lax.axis_index("chan")
    region = lax.axis_index("region")
    width = COARSE_WIDTH // chans
    side = 2 * TILE_SIDE
    count_x = lax.axis_size("region") // (REGIONS_Y * REGIONS_Z)
    steps = (REGIONS_Y * REGIONS_Z, REGIONS_Z, 1)
    counts = (count_x, REGIONS_Y, REGIONS_Z)
    places = [region // step % count for step, count in zip(steps, counts)]
    inside = jnp.stack(
        [
            flag
            for place, count in zip(places, counts)
            for flag in ((place > 0).astype(jnp.float32), (place < count - 1).astype(jnp.float32))
        ]
    )

    place = chan_place[None]
    each, rest = divmod(proj_weight.shape[0], OFFSETS)
    by_ring = rest == 0 and chans * each % 16 == 0
    if by_ring:
        split = split_columns(place, proj_weight, chans)
        mine = exchange(lambda distance: split[distance])
        piece = regroup(mine)
        channel = piece_channels(each)
    else:
        channel = jnp.arange(FINE_WIDTH, dtype=jnp.int32)[None]
    order = lax.broadcasted_iota(jnp.int32, (FINE_WIDTH, FINE_WIDTH), 0) == channel

    block = latent[0].transpose(0, 2, 1, 3)
    outermost = jnp.where(is_upper(), 0, TILE_SIDE - 1)
    if by_ring:
        outermost = after(outermost, mine[1])
    face = lax.dynamic_index_in_dim(block, outermost, axis=1, keepdims=False)
    first, last = y_rows(block)
    layer = across_z(face)
    corner = lax.broadcasted_iota(jnp.int32, first.shape, 1) == TILE_SIDE
    below, above = y_halos(
        jnp.where(corner, layer[:, :1], first), jnp.where(corner, layer[:, -1:], last)
    )
    ends = []
    for at in (0, -1):
        plane = jnp.concatenate(z_ends(layer[at][None], block[at], 0), axis=0)
        low, high = [
            jnp.concatenate(
                z_ends(part[at, TILE_SIDE : TILE_SIDE + 1], part[at, :TILE_SIDE], 0), axis=0
            )[:, None]
            for part in (below, above)
        ]
        spare = jnp.zeros((TILE_SIDE + 2, 6, FINE_WIDTH), plane.dtype)
        ends.append(jnp.concatenate([plane, high, spare, low], axis=1))
    outer = jnp.stack(x_layers(*ends))

    bias = jnp.sum(jnp.where(order, fine_bias[:, None], 0.0), axis=0)
    windows, taps = make_windows(
        inside,
        block,
        layer,
        below,
        above,
        outer,
        cond_scale[None],
        cond_shift[None],
        fine_weight.reshape(27, FINE_WIDTH, FINE_WIDTH),
        order.astype(jnp.bfloat16),
    )
    bias = jnp.concatenate([bias, bias])[None]
    half = STRIDE // 2
    early = convolve(windows, taps, bias, 0, half)
    late = convolve(windows, taps, bias, half, half)
    columns = ring_pieces(piece, [taps, early, late]) if by_ring else [whole_columns(proj_weight)]
    coarse = project(place, early, late, columns, by_ring, proj_bias[None])

    grid = coarse[:ROWS].reshape(CELLS, 2, ACROSS, ACROSS, width)
    field = with_halos(grid, 2, 3, 0)
    far = bottle_terms(place, field, bottle_weight, chans, True)
    swapped = [chan_swap(value, chans // 2 + number) for number, value in enumerate(far)]
    own, *near = bottle_terms(after(place, far), field, bottle_weight, chans, False)
    near = [chan_swap(value, 1 + number) for number, value in enumerate(near)]
    terms = [own, sum(value.astype(jnp.float32) for value in swapped)] + near
    guided = finish(place, guide, terms, bottle_bias[None])
    return guided.reshape(1, ACROSS, ACROSS, CELLS, width)


def solution(mesh):
    placed = (
        P("region", None, None, None, None),
        P(),
        P(),
        P(),
        P(),
        P(("chan", "region"), None),
        P(),
        P(None, "chan", None),
        P(),
        P(),
    )
    return jax.shard_map(
        shards,
        mesh=mesh,
        in_specs=placed,
        out_specs=P("region", None, None, None, "chan"),
        check_vma=False,
    )
```

```python
import functools

import numpy as np

import jax
import jax.numpy as jnp
from jax import lax
from jax.experimental import pallas as pl
from jax.experimental.pallas import tpu as pltpu
from jax.sharding import PartitionSpec as P

FINE_WIDTH = 128
COARSE_WIDTH = 1024
TILE_SIDE = 12
STRIDE = 4
REGIONS_Y = 4
REGIONS_Z = 2

CELLS = TILE_SIDE // STRIDE
ACROSS = 2 * CELLS
PLANE = 2 * ACROSS * ACROSS
ROWS = CELLS * PLANE
PADDED = -(-ROWS // 16) * 16
PHASES = STRIDE + 2
OFFSETS = STRIDE**3
LANES = 128
SPREAD = 8
MIB = 2**20


def vmem(count):
    return [pl.BlockSpec(memory_space=pltpu.VMEM) for _ in range(count)]


def regroup_kernel(*refs):
    rows_refs, out_ref, wide = refs[:-2], refs[-2], refs[-1]
    held = rows_refs[0].shape[0]
    groups = out_ref.shape[1]
    for lane in range(wide.shape[0]):
        columns = slice(lane * LANES, (lane + 1) * LANES)
        for number, rows_ref in enumerate(rows_refs):
            wide[lane, number * held : (number + 1) * held, :] = rows_ref[:, columns].astype(jnp.float32)
        for offset in range(OFFSETS):
            out_ref[offset, :, columns] = wide[
                lane, pl.ds(offset, groups, stride=OFFSETS), :
            ].astype(jnp.bfloat16)


def regroup(pieces):
    held, width = pieces[0].shape
    total = len(pieces) * held
    return pl.pallas_call(
        regroup_kernel,
        out_shape=jax.ShapeDtypeStruct((OFFSETS, total // OFFSETS, width), jnp.bfloat16),
        in_specs=vmem(len(pieces)),
        out_specs=vmem(1)[0],
        scratch_shapes=[pltpu.VMEM((width // LANES, total, LANES), jnp.float32)],
        compiler_params=pltpu.CompilerParams(vmem_limit_bytes=8 * MIB),
        name="regroup",
    )(*pieces)


def split_kernel(place_ref, rows_ref, *out_refs):
    width = out_refs[0].shape[1]
    for distance, out_ref in enumerate(out_refs):
        start = pl.multiple_of((place_ref[0] ^ distance) * width, width)
        out_ref[...] = rows_ref[:, pl.ds(start, width)]


def split_columns(place, rows, owners):
    held, width = rows.shape[0], rows.shape[1] // owners
    return pl.pallas_call(
        split_kernel,
        out_shape=[jax.ShapeDtypeStruct((held, width), rows.dtype)] * owners,
        in_specs=[pl.BlockSpec(memory_space=pltpu.SMEM)] + vmem(1),
        out_specs=vmem(owners),
        compiler_params=pltpu.CompilerParams(vmem_limit_bytes=4 * MIB),
        name="split_columns",
    )(place, rows)


def window_kernel(
    inside_ref, block_ref, layer_ref, below_ref, above_ref, outer_ref, scale_ref, shift_ref,
    weight_ref, order_ref, windows_ref, taps_ref, rows, line, layers,
):
    phase_x = pl.program_id(0)
    side, depth, width = 2 * TILE_SIDE, TILE_SIDE, FINE_WIDTH
    half = 2 * ACROSS * side

    @pl.when(phase_x == 0)
    def _():
        zero = jnp.zeros((width, width), jnp.bfloat16)
        for place in range(9):
            taps_ref[place, 3 * width :, :width] = zero
            taps_ref[place, :width, width:] = zero
            for step in range(3):
                block = jnp.dot(
                    weight_ref[place * 3 + step], order_ref[...], preferred_element_type=jnp.float32
                ).astype(jnp.bfloat16)
                taps_ref[place, step * width : (step + 1) * width, :width] = block
                taps_ref[place, (step + 1) * width : (step + 2) * width, width:] = block

        def widen(at_x, carry):
            rows[0, at_x] = below_ref[at_x].astype(jnp.float32)
            rows[1, at_x] = above_ref[at_x].astype(jnp.float32)
            return carry

        lax.fori_loop(0, side, widen, 0)

    scale = jnp.broadcast_to(scale_ref[...], (8, width))
    shift = jnp.broadcast_to(shift_ref[...], (8, width))
    row = lax.broadcasted_iota(jnp.int32, (8, width), 0)
    first = jnp.where(row == 0, shift * inside_ref[2], shift)
    last = jnp.where(row == side + 1 - 20, shift * inside_ref[3], shift)
    chunks = [(0, first), (8, shift), (16, shift), (4, shift), (12, shift), (20, last)]

    def split(cell_x, carry):
        at_x = phase_x + STRIDE * cell_x
        outside = jnp.logical_or(at_x == 0, at_x == side + 1)

        @pl.when(jnp.logical_not(outside))
        def _():
            at = at_x - 1
            for at_z in range(depth + 2):
                if at_z == 0:
                    flag, value, place = inside_ref[4], layer_ref[at], depth
                elif at_z == depth + 1:
                    flag, value, place = inside_ref[5], layer_ref[at], depth
                else:
                    flag, value, place = None, block_ref[at, at_z - 1], at_z - 1
                value = value.astype(jnp.float32)
                low, high = rows[0, at, place : place + 1, :], rows[1, at, place : place + 1, :]
                if flag is not None:
                    value, low, high = value * flag, low * flag, high * flag
                line[at_z, 7:8, :] = low
                line[at_z, 8 : side + 8, :] = value
                line[at_z, side + 8 : side + 9, :] = high

        @pl.when(outside)
        def _():
            end = jnp.where(at_x == 0, 0, 1)
            for at_z in range(depth + 2):
                value = outer_ref[end, at_z].astype(jnp.float32)
                line[at_z, 0:8, :] = value[side : side + 8]
                line[at_z, 8 : side + 8, :] = value[:side]
                line[at_z, side + 8 : side + 16, :] = value[side : side + 8]

        within = jnp.where(at_x == 0, inside_ref[0], 1.0)
        within = jnp.where(at_x == side + 1, inside_ref[1], within)
        for at_z in range(depth + 2):
            if at_z == 0:
                factor = within * inside_ref[4]
            elif at_z == depth + 1:
                factor = within * inside_ref[5]
            else:
                factor = within
            for number, (start, added) in enumerate(chunks):
                value = line[at_z, pl.ds(start + 7, 8), :]
                base = number // 3 * half + number % 3 * 8
                base = pl.multiple_of(base + cell_x * side, 8)
                layers[at_z, pl.ds(base, 8), :] = value
                layers[at_z, pl.ds(base + half // 2, 8), :] = value * scale + added * factor
        return carry

    lax.fori_loop(0, ACROSS, split, 0)
    for phase_y in range(PHASES):
        start = phase_y if phase_y < STRIDE else half + phase_y - STRIDE
        for phase_z in range(PHASES):
            parts = [
                layers[phase_z + STRIDE * cell, pl.ds(start, PLANE, stride=STRIDE), :]
                for cell in range(CELLS)
            ]
            parts.append(jnp.zeros((PADDED - ROWS, width), jnp.float32))
            windows_ref[0, phase_y, :, phase_z * width : (phase_z + 1) * width] = jnp.concatenate(
                parts, axis=0
            ).astype(jnp.bfloat16)


def make_windows(inside, *arrays):
    width, side = FINE_WIDTH, 2 * TILE_SIDE

    def whole(array):
        return pl.BlockSpec(array.shape, lambda i: (0,) * array.ndim)

    return pl.pallas_call(
        window_kernel,
        out_shape=(
            jax.ShapeDtypeStruct((PHASES, PHASES, PADDED, PHASES * width), jnp.bfloat16),
            jax.ShapeDtypeStruct((9, 4 * width, 2 * width), jnp.bfloat16),
        ),
        grid=(PHASES,),
        in_specs=[pl.BlockSpec(memory_space=pltpu.SMEM)] + [whole(array) for array in arrays],
        out_specs=(
            pl.BlockSpec((1, PHASES, PADDED, PHASES * width), lambda i: (i, 0, 0, 0)),
            pl.BlockSpec((9, 4 * width, 2 * width), lambda i: (0, 0, 0)),
        ),
        scratch_shapes=[
            pltpu.VMEM((2, side, 16, width), jnp.float32),
            pltpu.VMEM((TILE_SIDE + 2, side + 16, width), jnp.float32),
            pltpu.VMEM((TILE_SIDE + 2, 4 * ACROSS * side, width), jnp.float32),
        ],
        compiler_params=pltpu.CompilerParams(vmem_limit_bytes=28 * MIB),
        cost_estimate=pl.CostEstimate(flops=10**10, bytes_accessed=16 * MIB, transcendentals=0),
        name="windows",
    )(inside, *arrays)


def convolve_kernel(first_ref, second_ref, third_ref, taps_ref, bias_ref, out_ref):
    width = FINE_WIDTH
    bias = bias_ref[...]

    def convolve(at_y, carry):
        total = jnp.zeros((2 * PADDED, 2 * width), jnp.float32)
        for step_x, windows_ref in enumerate((first_ref, second_ref, third_ref)):
            for step_y in range(3):
                taken = [
                    windows_ref[0, at_y + step_y, :, pair * 2 * width : (pair * 2 + 4) * width]
                    for pair in range(2)
                ]
                total += jnp.dot(
                    jnp.concatenate(taken, axis=0),
                    taps_ref[step_x * 3 + step_y],
                    preferred_element_type=jnp.float32,
                )
        total = total + bias
        hidden = (total / (1.0 + jnp.exp(-total))).astype(jnp.bfloat16)
        for pair in range(2):
            out_ref[at_y * 2 + pair] = hidden[pair * PADDED : (pair + 1) * PADDED]
        return carry

    lax.fori_loop(0, STRIDE, convolve, 0)


def convolve(windows, taps, bias, start, count):
    width = FINE_WIDTH
    each = STRIDE * STRIDE // 2
    block = (1, PHASES, PADDED, PHASES * width)
    return pl.pallas_call(
        convolve_kernel,
        out_shape=jax.ShapeDtypeStruct((count * each, PADDED, 2 * width), jnp.bfloat16),
        grid=(count,),
        in_specs=[
            pl.BlockSpec(block, lambda i, step=step: (i + start + step, 0, 0, 0)) for step in range(3)
        ]
        + [
            pl.BlockSpec(taps.shape, lambda i: (0, 0, 0)),
            pl.BlockSpec(bias.shape, lambda i: (0, 0)),
        ],
        out_specs=pl.BlockSpec((each, PADDED, 2 * width), lambda i: (i, 0, 0)),
        compiler_params=pltpu.CompilerParams(vmem_limit_bytes=28 * MIB),
        cost_estimate=pl.CostEstimate(
            flops=2 * count * each * PADDED * 36 * width * 2 * width,
            bytes_accessed=16 * MIB,
            transcendentals=count * each * PADDED * 2 * width,
        ),
        name="convolve",
    )(windows, windows, windows, taps, bias)


def project_kernel(split, place_ref, early_ref, late_ref, *refs):
    weight_refs, bias_ref, out_ref = refs[:-2], refs[-2], refs[-1]
    width = out_ref.shape[1]
    start = pl.multiple_of(place_ref[0] * width, width)
    total = jnp.broadcast_to(bias_ref[:, pl.ds(start, width)], out_ref.shape)
    pairs = early_ref.shape[0]
    for number, hidden_ref in enumerate((early_ref, late_ref)):
        used = weight_refs[:-2] + (weight_refs[len(weight_refs) - 2 + number],) if split else weight_refs
        for pair in range(pairs):
            weight = jnp.concatenate(
                [
                    ref[2 * pair + item + (number * 2 * pairs if ref.shape[0] == OFFSETS else 0)]
                    for item in range(2)
                    for ref in used
                ],
                axis=0,
            )
            total += jnp.dot(hidden_ref[pair], weight, preferred_element_type=jnp.float32)
    out_ref[...] = total.astype(jnp.bfloat16)


def project(place, early, late, weights, split, bias):
    pairs, rows, depth = early.shape
    width = weights[0].shape[2]
    return pl.pallas_call(
        functools.partial(project_kernel, split),
        out_shape=jax.ShapeDtypeStruct((rows, width), jnp.bfloat16),
        in_specs=[pl.BlockSpec(memory_space=pltpu.SMEM)] + vmem(len(weights) + 3),
        out_specs=vmem(1)[0],
        compiler_params=pltpu.CompilerParams(vmem_limit_bytes=24 * MIB),
        cost_estimate=pl.CostEstimate(
            flops=4 * pairs * rows * depth * width, bytes_accessed=8 * MIB, transcendentals=0
        ),
        name="project",
    )(place, early, late, *weights, bias)


def bottle_kernel(far, place_ref, field_ref, weight_ref, *refs):
    out_refs, (held, total, packed, dense, sems) = refs[:-5], refs[-5:]
    width = field_ref.shape[4]
    share = out_refs[0].shape[1]
    span = held.shape[2]
    frame = ACROSS + 2
    rows = CELLS * 2 * ACROSS * frame
    chunk = 256
    owners = 2 * len(out_refs)
    first = pl.multiple_of((place_ref[0] // len(out_refs) ^ far) * span, span)

    def copy_of(step_y, place):
        tap = (place // 3 * 3 + step_y) * 3 + place % 3
        return pltpu.make_async_copy(
            weight_ref.at[tap, :, pl.ds(first, span)],
            held.at[step_y, pl.ds(place * width, width)],
            sems.at[step_y, place],
        )

    for step_y in range(3):
        for place in range(9):
            copy_of(step_y, place).start()

    for step_x in range(3):
        for step_z in range(3):
            place = step_x * 3 + step_z
            packed[:, place * width : (place + 1) * width] = (
                field_ref[step_z : step_z + CELLS, :, step_x : step_x + ACROSS]
                .astype(jnp.float32)
                .reshape(rows, width)
                .astype(jnp.bfloat16)
            )

    for step_x in range(3):
        for step_z in range(3):
            copy_of(0, step_x * 3 + step_z).wait()
        depth = slice(step_x * 3 * width, (step_x + 1) * 3 * width)
        for start in range(0, span, chunk):
            columns = slice(start, start + chunk)
            terms = jnp.dot(
                packed[:, depth], held[0, depth, columns], preferred_element_type=jnp.float32
            )
            total[0, :, columns] = terms if step_x == 0 else total[0, :, columns] + terms

    def rest(step_y, carry):
        for place in range(9):
            copy_of(step_y, place).wait()
        for start in range(0, span, chunk):
            columns = slice(start, start + chunk)
            total[step_y, :, columns] = jnp.dot(
                packed[...], held[step_y, :, columns], preferred_element_type=jnp.float32
            )
        return carry

    lax.fori_loop(1, 3, rest, 0)

    for number, out_ref in enumerate(out_refs):
        distance = number + far * owners // 2
        start = pl.multiple_of((place_ref[0] ^ distance) % len(out_refs) * share, share)
        for group in range(rows // frame):
            at = group * frame
            dense[group * ACROSS : (group + 1) * ACROSS, :] = sum(
                total[item, at + item : at + item + ACROSS, pl.ds(start, share)]
                for item in range(3)
            )
        out_ref[...] = dense[...].astype(out_ref.dtype)


def bottle_terms(place, field, weight, owners, far):
    frame = ACROSS + 2
    rows = CELLS * 2 * ACROSS * frame
    width = weight.shape[1]
    share = COARSE_WIDTH // owners
    span = COARSE_WIDTH // 2
    return pl.pallas_call(
        functools.partial(bottle_kernel, int(far)),
        out_shape=[
            jax.ShapeDtypeStruct((ROWS, share), jnp.bfloat16 if far or number else jnp.float32)
            for number in range(owners // 2)
        ],
        in_specs=[
            pl.BlockSpec(memory_space=pltpu.SMEM),
            pl.BlockSpec(memory_space=pltpu.VMEM),
            pl.BlockSpec(memory_space=pltpu.HBM),
        ],
        out_specs=vmem(owners // 2),
        scratch_shapes=[
            pltpu.VMEM((3, 9 * width, span), jnp.bfloat16),
            pltpu.VMEM((3, rows, span), jnp.float32),
            pltpu.VMEM((rows, 9 * width), jnp.bfloat16),
            pltpu.VMEM((ROWS, share), jnp.float32),
            pltpu.SemaphoreType.DMA((3, 9)),
        ],
        compiler_params=pltpu.CompilerParams(vmem_limit_bytes=51 * MIB),
        cost_estimate=pl.CostEstimate(
            flops=2 * rows * 27 * width * span, bytes_accessed=8 * MIB, transcendentals=0
        ),
        name="bottle_far" if far else "bottle_near",
    )(place, field, weight)


def finish_kernel(place_ref, guide_ref, own_ref, *refs):
    other_refs, bias_ref, out_ref, spread = refs[:-3], refs[-3], refs[-2], refs[-1]
    share = own_ref.shape[1]
    start = pl.multiple_of(place_ref[0] * share, share)
    value = own_ref[...] + bias_ref[:, pl.ds(start, share)]
    for other_ref in other_refs:
        value = value + other_ref[...].astype(jnp.float32)
    value = value / (1.0 + jnp.exp(-value))
    half = PLANE // 2
    for cell in range(CELLS):
        plain = value[cell * PLANE : cell * PLANE + half]
        guided = value[cell * PLANE + half : (cell + 1) * PLANE]
        mixed = plain + guide_ref[0] * (guided - plain)
        for lane in range(spread.shape[0]):
            spread[lane, pl.ds(cell, half, stride=SPREAD), :] = mixed[:, lane * LANES : (lane + 1) * LANES]
    for lane in range(spread.shape[0]):
        for cell in range(half):
            out_ref[cell, :, lane * LANES : (lane + 1) * LANES] = spread[
                lane, cell * SPREAD : cell * SPREAD + CELLS, :
            ].astype(jnp.bfloat16)


def finish(place, guide, terms, bias):
    share = terms[0].shape[1]
    return pl.pallas_call(
        finish_kernel,
        out_shape=jax.ShapeDtypeStruct((PLANE // 2, CELLS, share), jnp.bfloat16),
        in_specs=[pl.BlockSpec(memory_space=pltpu.SMEM)] * 2 + vmem(len(terms) + 1),
        out_specs=vmem(1)[0],
        scratch_shapes=[pltpu.VMEM((share // LANES, PLANE // 2 * SPREAD, LANES), jnp.float32)],
        compiler_params=pltpu.CompilerParams(vmem_limit_bytes=8 * MIB),
        name="finish",
    )(place, guide, *terms, bias)


def passed(value, steps):
    count = lax.axis_size("region")
    return lax.ppermute(
        value, "region", [(at, at + steps) for at in range(max(0, -steps), min(count, count - steps))]
    )


def across_z(value):
    count = lax.axis_size("region")
    return lax.ppermute(value, "region", [(at, at ^ 1) for at in range(count)])


def y_arrivals(ahead, back):
    place = lax.axis_index("region") // REGIONS_Z % REGIONS_Y
    upper = is_upper()
    ahead, back = hop(ahead, True), hop(back, False)
    zero = jnp.zeros_like(ahead)
    below = jnp.where(place > 0, jnp.where(upper, back, ahead), zero)
    above = jnp.where(place < REGIONS_Y - 1, jnp.where(upper, ahead, back), zero)
    return below, above


def y_halos(first, last):
    upper = is_upper()
    return y_arrivals(jnp.where(upper, first, last), jnp.where(upper, last, first))


def with_halos(value, dim_x, dim_y, dim_z):
    value = jnp.concatenate(z_ends(z_layer(value, dim_z), value, dim_z), axis=dim_z)
    below, above = y_halos(edge(value, dim_y, False), edge(value, dim_y, True))
    value = jnp.concatenate([below, value, above], axis=dim_y)
    low, high = x_layers(edge(value, dim_x, False), edge(value, dim_x, True))
    return jnp.concatenate([low, value, high], axis=dim_x)


def edge(array, dim, last):
    size = array.shape[dim]
    return lax.slice_in_dim(array, size - 1 if last else 0, size if last else 1, axis=dim)


def is_upper():
    return lax.axis_index("region") % REGIONS_Z == 1


def z_layer(value, dim):
    return across_z(jnp.where(is_upper(), edge(value, dim, False), edge(value, dim, True)))


def z_ends(layer, value, dim):
    zero = jnp.zeros_like(layer)
    return [jnp.where(is_upper(), layer, zero), value, jnp.where(is_upper(), zero, layer)]


def x_layers(first, last):
    count = lax.axis_size("region") // (REGIONS_Y * REGIONS_Z)
    if count == 1:
        return jnp.zeros_like(last), jnp.zeros_like(first)
    return passed(last, REGIONS_Y * REGIONS_Z), passed(first, -REGIONS_Y * REGIONS_Z)


def chan_swap(value, distance):
    return lax.ppermute(value, "chan", [(at, at ^ distance) for at in range(lax.axis_size("chan"))])


def exchange(piece_at):
    chans = lax.axis_size("chan")
    return [piece_at(0)] + [chan_swap(piece_at(distance), distance) for distance in range(1, chans)]


def ring_of(count):
    return list(range(0, count, 2)) + list(range(1, count, 2))[::-1]


def hop(value, ahead):
    ring = ring_of(lax.axis_size("region"))
    following = ring[1:] + ring[:1]
    return lax.ppermute(value, "region", list(zip(ring, following) if ahead else zip(following, ring)))


def after(value, other):
    return lax.optimization_barrier((value, other))[0]


def piece_channels(each):
    chans, regions = lax.axis_size("chan"), lax.axis_size("region")
    region = lax.axis_index("region")
    lane = lax.broadcasted_iota(jnp.int32, (1, FINE_WIDTH), 1)
    piece, distance, member = lane // (chans * each), lane // each % chans, lane % each
    place = jnp.where(region % 2 == 0, region // 2, regions - 1 - region // 2)
    shift = jnp.where(piece % 2 == 0, piece // 2, -((piece + 1) // 2))
    at = (place + shift + regions) % regions
    origin = jnp.where(at < regions // 2, 2 * at, 2 * (regions - 1 - at) + 1)
    return ((lax.axis_index("chan") ^ distance) * regions + origin) * each + member


def ring_pieces(piece, milestones):
    regions = lax.axis_size("region")
    forward = backward = piece
    held = [piece]
    for step in range(1, regions // 2 + 1):
        if step > 1 and step - 2 < len(milestones):
            forward, backward = (after(value, milestones[step - 2]) for value in (forward, backward))
        if step == regions // 2:
            held += [hop(forward[: OFFSETS // 2], True), hop(backward[OFFSETS // 2 :], False)]
        else:
            forward, backward = hop(forward, True), hop(backward, False)
            held += [forward, backward]
    return held


def whole_columns(proj_weight):
    chans, held = lax.axis_size("chan"), proj_weight.shape[0]
    width = COARSE_WIDTH // chans
    mine = lax.all_to_all(proj_weight, "chan", split_axis=1, concat_axis=0, tiled=True)
    whole = lax.all_gather(mine.reshape(chans, held, width), "region", axis=1, tiled=True)
    return whole.reshape(FINE_WIDTH, OFFSETS, width).transpose(1, 0, 2)


def shards(
    latent,
    cond_scale,
    cond_shift,
    fine_weight,
    fine_bias,
    proj_weight,
    proj_bias,
    bottle_weight,
    bottle_bias,
    guide,
):
    chans = lax.axis_size("chan")
    chan_place = lax.axis_index("chan")
    region = lax.axis_index("region")
    width = COARSE_WIDTH // chans
    side = 2 * TILE_SIDE
    count_x = lax.axis_size("region") // (REGIONS_Y * REGIONS_Z)
    steps = (REGIONS_Y * REGIONS_Z, REGIONS_Z, 1)
    counts = (count_x, REGIONS_Y, REGIONS_Z)
    places = [region // step % count for step, count in zip(steps, counts)]
    inside = jnp.stack(
        [
            flag
            for place, count in zip(places, counts)
            for flag in ((place > 0).astype(jnp.float32), (place < count - 1).astype(jnp.float32))
        ]
    )

    place = chan_place[None]
    each, rest = divmod(proj_weight.shape[0], OFFSETS)
    by_ring = rest == 0 and chans * each % 16 == 0
    if by_ring:
        split = split_columns(place, proj_weight, chans)
        mine = exchange(lambda distance: split[distance])
        piece = regroup(mine)
        channel = piece_channels(each)
    else:
        channel = jnp.arange(FINE_WIDTH, dtype=jnp.int32)[None]
    order = lax.broadcasted_iota(jnp.int32, (FINE_WIDTH, FINE_WIDTH), 0) == channel

    block = latent[0].transpose(0, 2, 1, 3)
    outermost = jnp.where(is_upper(), 0, TILE_SIDE - 1)
    if by_ring:
        outermost = after(outermost, mine[1])
    face = lax.dynamic_index_in_dim(block, outermost, axis=1, keepdims=False)
    layer = across_z(face)
    spare = jnp.zeros((block.shape[0], 16 - TILE_SIDE - 1, FINE_WIDTH), block.dtype)

    def rows_at(row):
        rows = lax.dynamic_index_in_dim(block, row, axis=2, keepdims=False)
        corner = lax.dynamic_slice_in_dim(layer, row, 1, axis=1)
        return jnp.concatenate([rows, corner, spare], axis=1)

    top = 2 * TILE_SIDE - 1
    below, above = y_arrivals(
        rows_at(jnp.where(is_upper(), 0, top)), rows_at(jnp.where(is_upper(), top, 0))
    )
    ends = []
    for at in (0, -1):
        plane = jnp.concatenate(z_ends(layer[at][None], block[at], 0), axis=0)
        low, high = [
            jnp.concatenate(
                z_ends(part[at, TILE_SIDE : TILE_SIDE + 1], part[at, :TILE_SIDE], 0), axis=0
            )[:, None]
            for part in (below, above)
        ]
        spare = jnp.zeros((TILE_SIDE + 2, 6, FINE_WIDTH), plane.dtype)
        ends.append(jnp.concatenate([plane, high, spare, low], axis=1))
    outer = jnp.stack(x_layers(*ends))

    bias = jnp.sum(jnp.where(order, fine_bias[:, None], 0.0), axis=0)
    windows, taps = make_windows(
        inside,
        block,
        layer,
        below,
        above,
        outer,
        cond_scale[None],
        cond_shift[None],
        fine_weight.reshape(27, FINE_WIDTH, FINE_WIDTH),
        order.astype(jnp.bfloat16),
    )
    bias = jnp.concatenate([bias, bias])[None]
    half = STRIDE // 2
    early = convolve(windows, taps, bias, 0, half)
    late = convolve(windows, taps, bias, half, half)
    columns = ring_pieces(piece, [taps, early, late]) if by_ring else [whole_columns(proj_weight)]
    coarse = project(place, early, late, columns, by_ring, proj_bias[None])

    grid = coarse[:ROWS].reshape(CELLS, 2, ACROSS, ACROSS, width)
    field = with_halos(grid, 2, 3, 0)
    far = bottle_terms(place, field, bottle_weight, chans, True)
    swapped = [chan_swap(value, chans // 2 + number) for number, value in enumerate(far)]
    own, *near = bottle_terms(after(place, far), field, bottle_weight, chans, False)
    near = [chan_swap(value, 1 + number) for number, value in enumerate(near)]
    terms = [own, sum(value.astype(jnp.float32) for value in swapped)] + near
    guided = finish(place, guide, terms, bottle_bias[None])
    return guided.reshape(1, ACROSS, ACROSS, CELLS, width)


def solution(mesh):
    placed = (
        P("region", None, None, None, None),
        P(),
        P(),
        P(),
        P(),
        P(("chan", "region"), None),
        P(),
        P(None, "chan", None),
        P(),
        P(),
    )
    return jax.shard_map(
        shards,
        mesh=mesh,
        in_specs=placed,
        out_specs=P("region", None, None, None, "chan"),
        check_vma=False,
    )
```
